32 devices in a mesh: dp: 16 (over z, y, x), mp: 2 (over core).
Axes of the slice: x: 2, y: 2, z: 4, core: 2. Of those that a mesh axis runs over, the one named last changes fastest.
Arguments:
- patches: bfloat16 [32, 28, 14, 768], P('dp', 'mp'), may hold values from -6 to 6
- norm1_gain: bfloat16 [768], P(('dp', 'mp')), may hold values from 0.099609375 to 1.8984375
- norm1_bias: bfloat16 [768], P(('dp', 'mp')), may hold values from -1.75 to 1.75
- qkv_weight: bfloat16 [768, 2304], P(('dp', 'mp')), may hold values from -0.21875 to 0.21875
- qv_bias: bfloat16 [2, 768], P(None, ('dp', 'mp')), may hold values from -1.75 to 1.75
- rel_pos_h: bfloat16 [27, 64], replicated, may hold values from -0.75 to 0.75
- rel_pos_w: bfloat16 [27, 64], replicated, may hold values from -0.75 to 0.75
- proj_weight: bfloat16 [768, 768], P(('dp', 'mp')), may hold values from -0.875 to 0.875
- proj_bias: bfloat16 [768], P(('dp', 'mp')), may hold values from -1.75 to 1.75
- norm2_gain: bfloat16 [768], P(('dp', 'mp')), may hold values from 0.099609375 to 1.8984375
- norm2_bias: bfloat16 [768], P(('dp', 'mp')), may hold values from -1.75 to 1.75
- fc1_weight: bfloat16 [768, 3072], P('dp', 'mp'), may hold values from -0.21875 to 0.21875
- fc1_bias: bfloat16 [3072], P('mp'), may hold values from -1.75 to 1.75
- fc2_weight: bfloat16 [3072, 768], P('mp', 'dp'), may hold values from -0.109375 to 0.109375
- fc2_bias: bfloat16 [768], P(('dp', 'mp')), may hold values from -1.75 to 1.75
- heights: int32 [32], P('dp'), may hold values from 15 to 28, as said below
- widths: int32 [32], P('dp'), may hold values from 8 to 14, as said below
- out_grad: bfloat16 [32, 28, 14, 768], P('dp', 'mp'), may hold values from -8 to 8
Outputs:
- block_out: bfloat16 [32, 28, 14, 768], P('dp', 'mp')
- patches_grad: float32 [32, 28, 14, 768], P('dp', 'mp')
- norm1_gain_grad: float32 [768], P(('dp', 'mp'))
- norm1_bias_grad: float32 [768], P(('dp', 'mp'))
- qkv_weight_grad: float32 [768, 2304], P(('dp', 'mp'))
- qv_bias_grad: float32 [2, 768], P(None, ('dp', 'mp'))
- rel_pos_h_grad: float32 [27, 64], replicated
- rel_pos_w_grad: float32 [27, 64], replicated
- proj_weight_grad: float32 [768, 768], P(('dp', 'mp'))
- proj_bias_grad: float32 [768], P(('dp', 'mp'))
- norm2_gain_grad: float32 [768], P(('dp', 'mp'))
- norm2_bias_grad: float32 [768], P(('dp', 'mp'))
- fc1_weight_grad: float32 [768, 3072], P('dp', 'mp')
- fc1_bias_grad: float32 [3072], P('mp')
- fc2_weight_grad: float32 [3072, 768], P('mp', 'dp')
- fc2_bias_grad: float32 [768], P(('dp', 'mp'))
The draws below stay inside these ranges and needn't reach their ends.
Inputs may be any that keep to these rules, and one draw needn't show every extreme that they name: `heights`: some image has the full height and some the least one. `widths`: some image has the full width and some the least one.
All inputs are finite; a program needn't handle non-finite values.
Results may differ from the reference program's by a relative error of at most 0.012.
The reference program's roundings to bfloat16 on the way count: a program that leaves them out, or rounds other values in their place, can miss the bound.
Values may be sent and summed in bfloat16 or wider, within the bound.
No kernel may reach another device: no remote copies, remote signals or barrier semaphores. Data moves between devices by JAX's collectives and lax.ppermute only.
A program may use at most 128 MiB of HBM per device.

```python
import jax
import jax.numpy as jnp
from jax import lax

D = 768
HEADS = 12
HDIM = 64
FF = 3072
WIN = 14
WROWS = 2
RELS = 27
IMAGES = 32


def ragged_sizes(key, lowest, beyond):
    key_one, key_two, key_three = jax.random.split(key, 3)
    sizes_drawn = jax.random.randint(key_one, (IMAGES,), lowest, beyond)
    top_slot = jax.random.randint(key_two, (), 0, IMAGES)
    low_slot = (top_slot + 1 + jax.random.randint(key_three, (), 0, IMAGES - 1)) % IMAGES
    slot_index = jnp.arange(IMAGES)
    sizes_drawn = jnp.where(slot_index == top_slot, beyond - 1, sizes_drawn)
    return jnp.where(slot_index == low_slot, lowest, sizes_drawn).astype(jnp.int32)


def draw_heights(key, part):
    key = jax.random.fold_in(key, 11)
    return ragged_sizes(key, (WROWS - 1) * WIN + 1, WROWS * WIN + 1)


def draw_widths(key, part):
    key = jax.random.fold_in(key, 23)
    return ragged_sizes(key, WIN // 2 + 1, WIN + 1)


def raised(entries, key, source, target, parts, factor):
    def block_of(dim):
        return (jnp.arange(entries.shape[dim]) // (entries.shape[dim] // parts)).reshape((-1,) + (1,) * (entries.ndim - 1 - dim))

    one_side = jax.random.permutation(key, parts)[block_of(target)]
    other_side = (block_of(target) + parts // 2) % parts
    return jnp.where((block_of(source) == one_side) | (block_of(source) == other_side), factor * entries, entries)


def level_of(stream_key, dims, cuts, low, top_value):
    def one(axis_at, parts):
        steps = jax.random.uniform(jax.random.fold_in(jax.random.fold_in(stream_key, 6), axis_at), (parts,), jnp.float32, low / len(cuts), top_value / len(cuts))
        return jnp.repeat(jnp.exp(steps), dims[axis_at] // parts).reshape((-1,) + (1,) * (len(dims) - axis_at - 1))

    level = one(*cuts[0])
    for cut in cuts[1:]:
        level = level * one(*cut)
    return level


def normal_values(stream_key, shape, width, reach, cuts=(), dtype=jnp.bfloat16):
    loudness = level_of(stream_key, shape, cuts, -0.22, 0.18) if cuts else 1.0
    entries = jax.random.normal(stream_key, shape, jnp.float32) * width * loudness
    return jnp.minimum(jnp.maximum(entries, -reach), reach).astype(dtype)


def bell_draw_with(stream_key, extent, width, bound, cuts, heavy, kind=jnp.bfloat16):
    entries = width * jax.random.normal(stream_key, extent, jnp.float32)
    if cuts:
        entries = entries * level_of(stream_key, extent, cuts, -0.22, 0.18)
    return jnp.clip(raised(entries, jax.random.fold_in(stream_key, 3), *heavy), -bound, bound).astype(kind)


def setup_inputs(seed: int = 0) -> dict:
    key_of = jax.random.split(jax.random.key(seed), 19)
    patches = normal_values(key_of[0], (IMAGES, WROWS * WIN, WIN, D), 1.0, 6.0, ((0, 16), (1, 2)))
    norm1_gain = jnp.clip(1.0 + 0.18 * jax.random.normal(key_of[1], (D,), jnp.float32), 0.099609375, 1.8984375).astype(jnp.bfloat16)
    norm1_bias = normal_values(key_of[2], (D,), 0.3, 1.75, ((0, 32),))
    qkv_weight = normal_values(key_of[3], (D, 3 * D), D ** -0.5, 0.21875, ((0, 32),))
    qv_bias = normal_values(key_of[4], (2, D), 0.3, 1.75, ((1, 32),))
    rel_pos_h = normal_values(key_of[5], (RELS, HDIM), 0.12, 0.75)
    rel_pos_w = normal_values(key_of[6], (RELS, HDIM), 0.12, 0.75)
    proj_weight = normal_values(key_of[7], (D, D), (D // WIN) ** -0.5, 0.875, ((0, 32),))
    proj_bias = normal_values(key_of[8], (D,), 0.3, 1.75, ((0, 32),))
    norm2_gain = jnp.clip(1.0 + 0.18 * jax.random.normal(key_of[9], (D,), jnp.float32), 0.099609375, 1.8984375).astype(jnp.bfloat16)
    norm2_bias = normal_values(key_of[10], (D,), 0.3, 1.75, ((0, 32),))
    fc1_weight = normal_values(key_of[11], (D, FF), D ** -0.5, 0.21875, ((0, 16), (1, 2)))
    fc1_bias = normal_values(key_of[12], (FF,), 0.3, 1.75, ((0, 2),))
    fc2_weight = normal_values(key_of[13], (FF, D), FF ** -0.5, 0.109375, ((0, 2), (1, 16)))
    fc2_bias = normal_values(key_of[14], (D,), 0.3, 1.75, ((0, 32),))
    heights = draw_heights(jax.random.fold_in(key_of[18], 71), 0)
    widths = draw_widths(jax.random.fold_in(key_of[18], 71), 0)
    out_grad = bell_draw_with(key_of[17], (IMAGES, WROWS * WIN, WIN, D), 1.0, 8.0, ((0, 16), (1, 2)), (0, 3, 16, 2.0))
    return {"patches": patches, "norm1_gain": norm1_gain, "norm1_bias": norm1_bias, "qkv_weight": qkv_weight, "qv_bias": qv_bias, "rel_pos_h": rel_pos_h, "rel_pos_w": rel_pos_w, "proj_weight": proj_weight, "proj_bias": proj_bias, "norm2_gain": norm2_gain, "norm2_bias": norm2_bias, "fc1_weight": fc1_weight, "fc1_bias": fc1_bias, "fc2_weight": fc2_weight, "fc2_bias": fc2_bias, "heights": heights, "widths": widths, "out_grad": out_grad}


@jax.custom_vjp
def low(v):
    return lax.optimization_barrier(v.astype(jnp.bfloat16)).astype(jnp.float32)

@jax.custom_vjp
def low_back(v):
    return v

def low_keep(v):
    return (low(v), None)

def low_pass(kept, grad):
    return (grad,)

def back_keep(v):
    return (v, None)

def back_low(kept, grad):
    return (low(grad),)
low.defvjp(low_keep, low_pass)
low_back.defvjp(back_keep, back_low)
EPSILON = 1e-06
MASKED_SCORE = -1e+30
HIGHEST = lax.Precision.HIGHEST

def table_rows(rel_table, window):
    offsets = jnp.arange(window)
    rel_index = (offsets[:, None] - offsets[None, :] + window - 1).astype(jnp.int32)
    return rel_table[rel_index]

def layer_norm(values, gain_vec, shift_vec):
    row_mean = lax.optimization_barrier(jnp.mean(values, axis=-1, keepdims=True))
    centered = values - row_mean
    variance = lax.optimization_barrier(jnp.mean(centered * centered, axis=-1, keepdims=True))
    return centered * lax.rsqrt(variance + EPSILON) * gain_vec + shift_vec

def attend(tokens_win, key_mask, norm1_gain, norm1_bias, qkv_weight, qv_bias, rel_pos_h, rel_pos_w, proj_weight, proj_bias):
    win_count, win_tokens, model_width = tokens_win.shape
    window = (rel_pos_h.shape[0] + 1) // 2
    normed = low(layer_norm(tokens_win, norm1_gain, norm1_bias))
    projected = jnp.einsum('bnd,de->bne', normed, qkv_weight, precision=HIGHEST)
    queries = projected[..., :model_width] + qv_bias[0]
    key_rows = projected[..., model_width:2 * model_width]
    value_rows = projected[..., 2 * model_width:] + qv_bias[1]

    def split_heads(inner_val):
        return low_back(low(inner_val)).reshape(win_count, win_tokens, HEADS, HDIM).transpose(0, 2, 1, 3)
    queries, key_rows, value_rows = (split_heads(queries), split_heads(key_rows), split_heads(value_rows))
    score_scale = HDIM ** (-0.5)
    scores = jnp.einsum('bhqc,bhkc->bhqk', queries, key_rows, precision=HIGHEST) * score_scale
    query_grid = queries.reshape(win_count, HEADS, window, window, HDIM)
    along_h = low_back(jnp.einsum('bhyxc,ykc->bhyxk', query_grid, table_rows(rel_pos_h, window), precision=HIGHEST))
    along_w = low_back(jnp.einsum('bhyxc,xkc->bhyxk', query_grid, table_rows(rel_pos_w, window), precision=HIGHEST))
    scores = scores.reshape(win_count, HEADS, window, window, window, window)
    scores = scores + along_h[:, :, :, :, :, None] + along_w[:, :, :, :, None, :]
    scores = low_back(scores.reshape(win_count, HEADS, win_tokens, win_tokens))
    scores = jnp.where(key_mask[:, None, None, :], scores, MASKED_SCORE)
    row_max = lax.optimization_barrier(jnp.max(scores, axis=-1, keepdims=True))
    exp_terms = jnp.exp(scores - row_max)
    soft_weights = exp_terms / lax.optimization_barrier(jnp.sum(exp_terms, axis=-1, keepdims=True))
    attended = jnp.einsum('bhqk,bhkc->bhqc', low(soft_weights), value_rows, precision=HIGHEST)
    attended = low_back(low(attended.transpose(0, 2, 1, 3).reshape(win_count, win_tokens, model_width)))
    branch = low_back(jnp.einsum('bnd,de->bne', attended, proj_weight, precision=HIGHEST) + proj_bias)
    return tokens_win + branch

def reference(patches, norm1_gain, norm1_bias, qkv_weight, qv_bias, rel_pos_h, rel_pos_w, proj_weight, proj_bias, norm2_gain, norm2_bias, fc1_weight, fc1_bias, fc2_weight, fc2_bias, heights, widths, out_grad):
    canvas_rows = WROWS * WIN
    row_index = jnp.arange(canvas_rows)[None, :, None]
    col_index = jnp.arange(WIN)[None, None, :]
    valid = (row_index < heights[:, None, None]) & (col_index < widths[:, None, None])

    def to_windows(values):
        return values.reshape(IMAGES // 8, 8 * WROWS, WIN * WIN, values.shape[-1])

    def from_windows(values):
        return values.reshape(IMAGES, canvas_rows, WIN, values.shape[-1])
    key_mask = to_windows(valid[..., None])[..., 0]
    floats = tuple((argument.astype(jnp.float32) for argument in (patches, norm1_gain, norm1_bias, qkv_weight, qv_bias, rel_pos_h, rel_pos_w, proj_weight, proj_bias, norm2_gain, norm2_bias, fc1_weight, fc1_bias, fc2_weight, fc2_bias)))

    def forward(tokens, gain_one, shift_one, weight_qkv, bias_qv, table_h, table_w, weight_proj, bias_proj, gain_two, shift_two, weight_in, bias_in, weight_out, bias_out):

        def block_group(group):
            tokens_win, mask_win = group
            resid = attend(tokens_win, mask_win, gain_one, shift_one, weight_qkv, bias_qv, table_h, table_w, weight_proj, bias_proj)
            normed = low(layer_norm(resid, gain_two, shift_two))
            hidden = low_back(jnp.einsum('bnd,df->bnf', normed, weight_in, precision=HIGHEST) + bias_in)
            active = low(jax.nn.gelu(hidden, approximate=False))
            branch = low_back(jnp.einsum('bnf,fd->bnd', active, weight_out, precision=HIGHEST) + bias_out)
            return jnp.where(mask_win[..., None], resid + branch, 0.0)
        outputs = lax.map(jax.checkpoint(block_group), (to_windows(tokens), key_mask))
        return from_windows(outputs)
    block_out, pullback = jax.vjp(forward, *floats)
    grads = pullback(out_grad.astype(jnp.float32))
    return (block_out.astype(jnp.bfloat16), grads[0], grads[1], grads[2], grads[3], grads[4], grads[5], grads[6], grads[7], grads[8], grads[9], grads[10], grads[11], grads[12], grads[13], grads[14])
```

```python
from functools import partial

import jax
import jax.numpy as jnp
import numpy as np
from jax import lax
from jax.experimental import pallas as pl
from jax.experimental.pallas import tpu as pltpu
from jax.sharding import PartitionSpec as P

HEADS = 12
HDIM = 64
LANES = 128
PAIRS = HEADS // 2
WIN = 14
SIDE = 16
TOK = WIN * SIDE
KEYS = 256
PIECES = 16
EPSILON = 1e-06
MASKED_SCORE = -1e30
MASK_LANE = 60
FFN_CHUNKS = 3
BACK_CHUNKS = 1
F32 = jnp.float32
BF16 = jnp.bfloat16
SMEM = pl.BlockSpec(memory_space=pltpu.SMEM)
HBM = pl.BlockSpec(memory_space=pl.ANY)
WHOLE = pl.BlockSpec(memory_space=pltpu.VMEM)
VMEM_BYTES = 52 * 2**20


def params():
    return pltpu.CompilerParams(vmem_limit_bytes=VMEM_BYTES)


def shape(dims, dtype):
    return jax.ShapeDtypeStruct(dims, dtype)


def dot(a, b):
    return jnp.dot(a, b, preferred_element_type=F32)


def dot_nt(a, b):
    return lax.dot_general(a, b, (((1,), (1,)), ((), ())), preferred_element_type=F32)


def dot_tn(a, b):
    return lax.dot_general(a, b, (((0,), (0,)), ((), ())), preferred_element_type=F32)


def lanes(rows):
    return lax.broadcasted_iota(jnp.int32, (rows, LANES), 1)


def moments(values):
    centered = values - jnp.mean(values, axis=-1, keepdims=True)
    inverse = lax.rsqrt(jnp.mean(centered * centered, axis=-1, keepdims=True) + EPSILON)
    return centered * inverse, inverse


def norm_back(grad, xhat, inverse, gain):
    scaled = grad * gain
    first = jnp.mean(scaled, axis=-1, keepdims=True)
    second = jnp.mean(scaled * xhat, axis=-1, keepdims=True)
    return inverse * (scaled - first - xhat * second)


def pieces_in(meta, at, refs, rows, cols, dest, sems, first):
    copies = []
    for ref in refs:
        for part in range(ref.shape[0] // rows):
            place = pl.multiple_of(meta[at + len(copies)] * rows, rows)
            copy = pltpu.make_async_copy(
                ref.at[pl.ds(part * rows, rows), cols],
                dest.at[pl.ds(place, rows), :],
                sems.at[first + len(copies)],
            )
            copy.start()
            copies.append(copy)
    return copies


def row_valid(meta, core, window, rows, width):
    place = lax.broadcasted_iota(jnp.int32, (rows, width), 0)
    row, col = place // SIDE, place % SIDE
    inside = (row < WIN) & (col < WIN)
    return inside & (core * WIN + row < meta[33 + window]) & (col < meta[35 + window])


def relative(turned):
    out = []
    for row in range(WIN):
        slab = turned[row * SIDE : (row + 1) * SIDE]
        down = pltpu.roll(slab, row, 1) if row else slab
        across = pltpu.roll(slab, 0, 1, stride=1, stride_axis=0)
        out.append(jnp.where(lanes(SIDE) % 64 < 32, down, across))
    return jnp.concatenate(out, axis=0)


def attend_kernel(count, meta, tok, table, spread, *refs):
    own0, own1 = refs[:count], refs[count : 2 * count]
    other0, other1 = refs[2 * count : 3 * count], refs[3 * count : 4 * count]
    (n1, q_out, k_out, v_out, p_out, att, x1, n2, vecs, w_out) = refs[4 * count : 4 * count + 10]
    weights, small, aug, sems, out_sem = refs[4 * count + 10 :]
    width = weights.shape[1]
    rows = width // PIECES
    core = meta[32]
    copies = []
    for refs_here, at, which, extra in (
        (own0, 0, 2 * core, True),
        (own1, 16, 2 * core + 1, False),
        (other0, 0, 2 - 2 * core, False),
        (other1, 16, 3 - 2 * core, False),
    ):
        copies += pieces_in(
            meta, at, refs_here, rows, pl.ds(0, width), weights.at[which], sems, len(copies)
        )
        if extra:
            copies += pieces_in(
                meta, at, refs_here, rows, pl.ds(width, LANES), small, sems, len(copies)
            )
    for window in range(2):
        keys = lanes(KEYS)
        valid = row_valid(meta, core, window, KEYS, LANES)
        aug[window] = jnp.where(
            (keys == MASK_LANE) & ~valid, MASKED_SCORE, spread[...].astype(F32)
        ).astype(BF16)
        k_out[window, TOK:] = jnp.zeros((KEYS - TOK, width), BF16)
        v_out[window, TOK:] = jnp.zeros((KEYS - TOK, width), BF16)
    tokens = tok[...].reshape(2 * TOK, width).astype(F32)
    xhat, _ = moments(tokens)
    for copy in copies:
        copy.wait()
    out_copy = pltpu.make_async_copy(weights, w_out, out_sem)
    out_copy.start()
    vecs[...] = small[...].astype(F32).T[:8]
    normed = (xhat * vecs[0:1] + vecs[1:2]).astype(BF16)
    n1[...] = normed.reshape(2, TOK, width)
    for mat, dest in enumerate((q_out, k_out, v_out)):
        for start in range(0, width, 256):
            cols = pl.ds(start, 256)
            made = dot(normed, weights[mat, :, cols])
            if mat != 1:
                made = made + vecs[2 + mat // 2 : 3 + mat // 2, cols]
            made = made.astype(BF16)
            dest[0, :TOK, cols] = made[:TOK]
            dest[1, :TOK, cols] = made[TOK:]

    def heads_of(step, _):
        window, pair = step // PAIRS, step % PAIRS
        cols = pl.ds(pl.multiple_of(pair * LANES, LANES), LANES)
        q2, k2, v2 = q_out[window, :, cols], k_out[window, :, cols], v_out[window, :, cols]
        turned = dot(q2, table[...])
        place = lanes(TOK)
        keys_aug = jnp.concatenate([k2, aug[window]], axis=1)
        parts = []
        for half in range(2):
            rel = relative(turned[:, half * LANES : (half + 1) * LANES])
            high = rel.astype(BF16).astype(F32)
            rel = jnp.where(place < 64, high, rel - high)
            rel = jnp.where(place == MASK_LANE, 1.0, rel).astype(BF16)
            mine = jnp.where(place // 64 == half, q2.astype(F32) * HDIM**-0.5, 0.0).astype(BF16)
            scores = dot_nt(jnp.concatenate([mine, rel], axis=1), keys_aug)
            terms = jnp.exp(scores - jnp.max(scores, axis=-1, keepdims=True))
            soft = terms * (1.0 / jnp.sum(terms, axis=-1, keepdims=True))
            soft = soft.astype(BF16)
            p_out[window, 2 * pair + half] = soft
            parts.append(dot(soft, v2))
        att[window, :, cols] = jnp.where(place < 64, parts[0], parts[1]).astype(BF16)
        return 0

    lax.fori_loop(0, 2 * PAIRS, heads_of, 0)
    attended = att[...].reshape(2 * TOK, width)
    tokens = tok[...].reshape(2 * TOK, width).astype(F32)
    resid = tokens + (dot(attended, weights[3]) + vecs[4:5])
    x1[...] = resid.reshape(2, TOK, width)
    xhat2, _ = moments(resid)
    n2[...] = (xhat2 * vecs[5:6] + vecs[6:7]).astype(BF16).reshape(2, TOK, width)
    out_copy.wait()


def attend(meta, tok, table, spread, own0, own1, other0, other1):
    count, width = len(own0), tok.shape[-1]
    rows = (2, TOK, width)
    keys = (2, KEYS, width)
    return pl.pallas_call(
        partial(attend_kernel, count),
        out_shape=[
            shape(rows, BF16),
            shape(rows, BF16),
            shape(keys, BF16),
            shape(keys, BF16),
            shape((2, HEADS, TOK, KEYS), BF16),
            shape(rows, BF16),
            shape(rows, F32),
            shape(rows, BF16),
            shape((8, width), F32),
            shape((4, width, width), BF16),
        ],
        in_specs=[SMEM, WHOLE, WHOLE, WHOLE] + [HBM] * (4 * count),
        out_specs=[WHOLE] * 9 + [HBM],
        scratch_shapes=[
            pltpu.VMEM((4, width, width), BF16),
            pltpu.VMEM((width, LANES), BF16),
            pltpu.VMEM((2, KEYS, LANES), BF16),
            pltpu.SemaphoreType.DMA((5 * PIECES,)),
            pltpu.SemaphoreType.DMA,
        ],
        compiler_params=params(),
        cost_estimate=pl.CostEstimate(
            flops=6_000_000_000, bytes_accessed=20_000_000, transcendentals=1_500_000
        ),
        name="attend",
    )(meta, tok, table, spread, *own0, *own1, *other0, *other1)


def hidden_kernel(count, first, last, meta, n2a, n2b, dma, dmb, bias, *refs):
    refs = list(refs)
    in0, in1 = refs[:count], refs[count : 2 * count]
    refs = refs[2 * count :]
    if not first:
        out_in, back_in = refs[:2]
        refs = refs[2:]
    g0_keep, g0_send, g1_keep, g1_send, bias_grad = refs[:5]
    refs = refs[5:]
    if last:
        out_own, out_far, back_own, back_far = refs[:4]
        refs = refs[4:]
    else:
        out_acc, back_acc = refs[:2]
        refs = refs[2:]
    w0, w1, n2s, dms, acts, backs, g0, g1, sems, out_sems = refs
    width, cols_here = w0.shape
    rows = width // PIECES
    copies = pieces_in(meta, 0, in0, rows, pl.ds(0, cols_here), w0, sems, 0)
    copies += pieces_in(meta, 16, in1, rows, pl.ds(0, cols_here), w1, sems, PIECES)
    n2s[: 2 * TOK] = n2a[...].reshape(2 * TOK, width)
    n2s[2 * TOK :] = n2b[...].reshape(2 * TOK, width)
    dms[: 2 * TOK] = dma[...].reshape(2 * TOK, width)
    dms[2 * TOK :] = dmb[...].reshape(2 * TOK, width)
    for copy in copies:
        copy.wait()
    outs = []
    for start in range(0, cols_here, 256):
        cols = pl.ds(start, 256)
        inner = dot(n2s[...], w0[:, cols]) + bias[:, cols]
        back = dot(dms[...], w1[:, cols])
        cdf = 0.5 + 0.5 * lax.erf(inner * 0.7071067811865476)
        density = jnp.exp(inner * inner * -0.5) * 0.3989422804014327
        acts[:, cols] = (inner * cdf).astype(BF16)
        back_pre = (back * (cdf + inner * density)).astype(BF16)
        backs[:, cols] = back_pre
        bias_grad[:, cols] = jnp.sum(back_pre.astype(F32), axis=0, keepdims=True)
        g0[:, cols] = dot_tn(n2s[...], back_pre).astype(BF16)
        g1[:, cols] = dot_tn(dms[...], acts[:, cols]).astype(BF16)
        for which, (made, keep, send) in enumerate(((g0, g0_keep, g0_send), (g1, g1_keep, g1_send))):
            for piece in range(PIECES):
                dest = keep if piece < PIECES // 2 else send
                place = pl.multiple_of(meta[16 * which + piece] * rows, rows)
                at = (piece % (PIECES // 2)) * rows
                copy = pltpu.make_async_copy(
                    made.at[pl.ds(place, rows), cols],
                    dest.at[pl.ds(at, rows), cols],
                    out_sems.at[len(outs)],
                )
                copy.start()
                outs.append(copy)
    made_out = dot_nt(acts[...], w1[...])
    made_back = dot_nt(backs[...], w0[...])
    if not first:
        made_out = made_out + out_in[...]
        made_back = made_back + back_in[...]
    if last:
        out_own[...] = made_out[: 2 * TOK]
        out_far[...] = made_out[2 * TOK :].astype(BF16)
        back_own[...] = made_back[: 2 * TOK]
        back_far[...] = made_back[2 * TOK :].astype(BF16)
    else:
        out_acc[...] = made_out
        back_acc[...] = made_back
    for copy in outs:
        copy.wait()


def hidden(meta, n2a, n2b, dma, dmb, bias, in0, in1, carried, last):
    count, width, cols_here = len(in0), n2a.shape[-1], bias.shape[-1]
    first = carried is None
    half = (width // 2, cols_here)
    out_shape = [shape(half, BF16)] * 4 + [shape((1, cols_here), F32)]
    if last:
        one = (2 * TOK, width)
        out_shape += [shape(one, F32), shape(one, BF16), shape(one, F32), shape(one, BF16)]
    else:
        out_shape += [shape((4 * TOK, width), F32)] * 2
    carried = () if first else carried
    return pl.pallas_call(
        partial(hidden_kernel, count, first, last),
        out_shape=out_shape,
        in_specs=[SMEM] + [WHOLE] * 5 + [HBM] * (2 * count) + [WHOLE] * len(carried),
        out_specs=[HBM] * 4 + [WHOLE] * (len(out_shape) - 4),
        scratch_shapes=[
            pltpu.VMEM((width, cols_here), BF16),
            pltpu.VMEM((width, cols_here), BF16),
            pltpu.VMEM((4 * TOK, width), BF16),
            pltpu.VMEM((4 * TOK, width), BF16),
            pltpu.VMEM((4 * TOK, cols_here), BF16),
            pltpu.VMEM((4 * TOK, cols_here), BF16),
            pltpu.VMEM((width, cols_here), BF16),
            pltpu.VMEM((width, cols_here), BF16),
            pltpu.SemaphoreType.DMA((2 * PIECES,)),
            pltpu.SemaphoreType.DMA((2 * PIECES * (cols_here // 256),)),
        ],
        compiler_params=params(),
        cost_estimate=pl.CostEstimate(
            flops=12 * 4 * TOK * width * cols_here,
            bytes_accessed=20_000_000,
            transcendentals=8 * TOK * cols_here,
        ),
        name="hidden",
    )(meta, n2a, n2b, dma, dmb, bias, *in0, *in1, *carried)


def middle_kernel(meta, out_own, out_far, back_own, back_far, x1, dm, vecs, block, dx1, da, sums):
    width = x1.shape[-1]
    core = meta[32]
    total = [jnp.zeros((1, width), F32) for _ in range(4)]
    for window in range(2):
        rows = pl.ds(window * TOK, TOK)
        resid = x1[window]
        valid = row_valid(meta, core, window, TOK, width)
        branch = out_own[rows] + out_far[rows].astype(F32) + vecs[7:8]
        block[window] = jnp.where(valid, resid + branch, 0.0).astype(BF16)
        grad = back_own[rows] + back_far[rows].astype(F32)
        xhat, inverse = moments(resid)
        out_grad = dm[window].astype(F32)
        dresid = out_grad + norm_back(grad, xhat, inverse, vecs[5:6])
        dx1[window] = dresid
        rounded = dresid.astype(BF16)
        da[window] = rounded
        for slot, value in enumerate((rounded.astype(F32), grad * xhat, grad, out_grad)):
            total[slot] = total[slot] + jnp.sum(value, axis=0, keepdims=True)
    sums[...] = jnp.concatenate([jnp.zeros((4, width), F32)] + total, axis=0)


def middle(meta, out_own, out_far, back_own, back_far, x1, dm, vecs):
    rows = x1.shape
    return pl.pallas_call(
        middle_kernel,
        out_shape=[
            shape(rows, BF16),
            shape(rows, F32),
            shape(rows, BF16),
            shape((8, rows[-1]), F32),
        ],
        in_specs=[SMEM] + [WHOLE] * 7,
        out_specs=[WHOLE] * 4,
        compiler_params=params(),
        cost_estimate=pl.CostEstimate(
            flops=20_000_000, bytes_accessed=9_000_000, transcendentals=0
        ),
        name="middle",
    )(meta, out_own, out_far, back_own, back_far, x1, dm, vecs)


def unrelative(grads):
    out = []
    for row in range(WIN):
        slab = grads[row * SIDE : (row + 1) * SIDE]
        down = pltpu.roll(slab, row, 1) if row else slab
        across = pltpu.roll(slab, 0, 1, stride=1, stride_axis=0)
        out.append(jnp.where(lanes(SIDE) < 32, down, across))
    return jnp.concatenate(out, axis=0)


def attend_back_kernel(
    first, last, meta, q, k, v, p, wqkv, wproj, da, da_cols, att, n1, tok, dx1, vecs, gather, table, *refs
):
    refs = list(refs)
    if not first:
        dn1_in = refs.pop(0)
    mine0, mine1, theirs0, theirs1, bias_sums, table_grad, result = refs[:7]
    refs = refs[7:]
    if last:
        norm_sums = refs.pop(0)
    dat, dqkv, grads, sems = refs
    core = meta[32]
    width, cols_here = da.shape[-1], q.shape[-1]
    pairs, rows = cols_here // LANES, width // PIECES
    dat[...] = (
        dot_nt(da[...].reshape(2 * TOK, width), wproj[0]).astype(BF16).reshape(2, TOK, cols_here)
    )
    table_grad[...] = jnp.zeros_like(table_grad)
    outs = []

    def send(mat, made):
        grads[mat] = made.astype(BF16)
        own, far = (mine0, theirs0) if mat % 2 == 0 else (mine1, theirs1)
        for piece in range(PIECES):
            place = pl.multiple_of(meta[16 * (mat % 2) + piece] * rows, rows)
            source = grads.at[mat, pl.ds(place, rows), :]
            to, sem = pl.ds(piece * rows, rows), sems.at[len(outs)]
            copies = [pltpu.make_async_copy(source, ref.at[to, :], sem) for ref in (own, far)]
            pl.when(core == mat // 2)(copies[0].start)
            pl.when(core != mat // 2)(copies[1].start)
            outs.append(copies[0])

    send(3, dot_tn(att[...].reshape(2 * TOK, width), da_cols[...].reshape(2 * TOK, cols_here)))

    def heads_of(step, _):
        window, pair = step // pairs, step % pairs
        cols = pl.ds(pl.multiple_of(pair * LANES, LANES), LANES)
        q2, k2, v2 = q[window, :, cols], k[window, :, cols], v[window, :, cols]
        dat2 = dat[window, :, cols]
        place = lanes(TOK)
        q8 = (q2.astype(F32) * HDIM**-0.5).astype(BF16)
        k8 = (k2.astype(F32) * HDIM**-0.5).astype(BF16)
        dqs, dks, dvs, dts = [], [], [], []
        for half in range(2):
            soft = p[window, 2 * pair + half]
            soft32 = soft.astype(F32)
            mine = jnp.where(place // 64 == half, dat2.astype(F32), 0.0).astype(BF16)
            weighted = soft32 * dot_nt(mine, v2)
            ds = (weighted - soft32 * jnp.sum(weighted, axis=-1, keepdims=True)).astype(BF16)
            turned = dot(ds, gather[...]).astype(BF16).astype(F32)
            turned = unrelative(turned).astype(BF16)
            dqs.append(dot(ds, k8) + dot(turned, table[half]))
            dks.append(dot_tn(ds, q8))
            dvs.append(dot_tn(soft, dat2))
            dts.append(dot_tn(turned, q2))
        key_place = lanes(TOK)
        dqkv[0, window, :, cols] = jnp.where(place < 64, dqs[0], dqs[1]).astype(BF16)
        dqkv[1, window, :, cols] = jnp.where(key_place < 64, dks[0][:TOK], dks[1][:TOK]).astype(BF16)
        dqkv[2, window, :, cols] = jnp.where(key_place < 64, dvs[0][:TOK], dvs[1][:TOK]).astype(BF16)
        table_grad[...] += jnp.where(lanes(LANES) < 64, dts[0], dts[1])
        return 0

    lax.fori_loop(0, 2 * pairs, heads_of, 0)
    normed = n1[...].reshape(2 * TOK, width)
    dn1 = jnp.zeros((2 * TOK, width), F32) if first else dn1_in[...].reshape(2 * TOK, width)
    for mat in range(3):
        change = dqkv[mat].reshape(2 * TOK, cols_here)
        send(mat, dot_tn(normed, change))
        dn1 = dn1 + dot_nt(change, wqkv[mat])
        if mat != 1:
            bias_sums[mat // 2 : mat // 2 + 1] = jnp.sum(change.astype(F32), axis=0, keepdims=True)
    if last:
        xhat, inverse = moments(tok[...].reshape(2 * TOK, width).astype(F32))
        norm_sums[0:1] = jnp.sum(dn1 * xhat, axis=0, keepdims=True)
        norm_sums[1:2] = jnp.sum(dn1, axis=0, keepdims=True)
        back = norm_back(dn1, xhat, inverse, vecs[0:1])
        result[...] = dx1[...] + back.reshape(2, TOK, width)
    else:
        result[...] = dn1.reshape(2, TOK, width)
    for copy in outs:
        copy.wait()


def attend_back(chunk, chunks, meta, q, k, v, p, weights, da, att, n1, tok, dx1, vecs, gather, table, dn1):
    width = q.shape[-1]
    cols_here, heads_here = width // chunks, HEADS // chunks
    first, last = chunk == 0, chunk == chunks - 1
    part = lambda rows: pl.BlockSpec((2, rows, cols_here), lambda i: (0, 0, chunk))
    out_shape = [shape((width, cols_here), BF16)] * 4 + [
        shape((2, cols_here), F32),
        shape((LANES, LANES), F32),
        shape((2, TOK, width), F32),
    ]
    if last:
        out_shape.append(shape((2, width), F32))
    extra = () if first else (dn1,)
    return pl.pallas_call(
        partial(attend_back_kernel, first, last),
        out_shape=out_shape,
        grid=(1,),
        in_specs=[
            SMEM,
            part(TOK),
            part(KEYS),
            part(KEYS),
            pl.BlockSpec((2, heads_here, TOK, KEYS), lambda i: (0, chunk, 0, 0)),
            pl.BlockSpec((3, width, cols_here), lambda i: (0, 0, chunk)),
            pl.BlockSpec((1, cols_here, width), lambda i: (3, chunk, 0)),
            WHOLE,
            part(TOK),
        ]
        + [WHOLE] * (7 + len(extra)),
        out_specs=[HBM] * 4 + [WHOLE] * (len(out_shape) - 4),
        scratch_shapes=[
            pltpu.VMEM((2, TOK, cols_here), BF16),
            pltpu.VMEM((3, 2, TOK, cols_here), BF16),
            pltpu.VMEM((4, width, cols_here), BF16),
            pltpu.SemaphoreType.DMA((4 * PIECES,)),
        ],
        compiler_params=params(),
        cost_estimate=pl.CostEstimate(
            flops=12_000_000_000 // chunks, bytes_accessed=24_000_000 // chunks, transcendentals=0
        ),
        name="attend_back",
    )(meta, q, k, v, p, weights, weights, da, da, att, n1, tok, dx1, vecs, gather, table, *extra)


def grid_of(count):
    return (4, 2, 2) if count == 16 else None


def turn(values, dims, axis, by):
    pairs = []
    for chip in range(dims[0] * dims[1] * dims[2]):
        place = list(np.unravel_index(chip, dims))
        place[axis] = (place[axis] + by) % dims[axis]
        pairs.append((chip, int(np.ravel_multi_index(place, dims))))
    return lax.ppermute(values, "dp", pairs)


def other_core(values):
    return lax.ppermute(values, "mp", [(0, 1), (1, 0)])


def place_order(dims, first, second):
    here = lax.axis_index("dp")
    z, y, x = here // (dims[1] * dims[2]), here // dims[2] % dims[1], here % dims[2]
    found = []
    for outer in range(2):
        for inner in range(2):
            at = [z, y, x]
            at[first] = (at[first] + inner) % 2
            at[second] = (at[second] + outer) % 2
            for step in range(dims[0]):
                found.append(((z - step) % dims[0] * dims[1] + at[1]) * dims[2] + at[2])
    return jnp.stack(found).astype(jnp.int32)


def gather_rows(block, dims, first, second):
    near = jnp.concatenate(
        [block] + [turn(block, dims, 0, step) for step in range(1, dims[0])], axis=0
    )
    beside = turn(near, dims, first, 1)
    return [near, beside, turn(near, dims, second, 1), turn(beside, dims, second, 1)]


def add(a, b):
    return a.astype(F32) + b.astype(F32)


def scatter_rows(keep, far, dims, first, second):
    half = keep.shape[0] // 2
    came = turn(far, dims, second, 1)
    beside = turn(add(keep[half:], came[half:]).astype(BF16), dims, first, 1)
    near = add(keep[:half], came[:half]) + beside.astype(F32)
    rows = half // dims[0]
    total = near[:rows]
    for step in range(1, dims[0]):
        part = near[step * rows : (step + 1) * rows].astype(BF16)
        total = total + turn(part, dims, 0, dims[0] - step).astype(F32)
    return total


def add_all(values, dims):
    values = values + other_core(values)
    if dims is None:
        return lax.psum(values, "dp")
    values = values + turn(values, dims, 2, 1)
    values = values + turn(values, dims, 1, 1)
    return values + sum(turn(values, dims, 0, step) for step in range(1, dims[0]))


def constants():
    key = np.arange(KEYS)
    row, col = key // SIDE, key % SIDE
    inside = (row < WIN) & (col < WIN)
    spread = np.zeros((KEYS, LANES), np.float32)
    gather = np.zeros((KEYS, LANES), np.float32)
    for place in key[inside]:
        for base in (0, 64):
            spread[place, base + WIN - 1 + row[place]] = 1.0
            spread[place, base + 32 + WIN - 1 + col[place]] = 1.0
        gather[place, WIN - 1 - row[place]] = 1.0
        gather[place, 32 + WIN - 1 - col[place]] = 1.0
    return spread, gather


def tables(rel_pos_h, rel_pos_w):
    count = rel_pos_h.shape[0]
    gap = jnp.zeros((32 - count, HDIM), BF16)
    turned = jnp.concatenate([rel_pos_h[::-1], gap, rel_pos_w[::-1], gap], axis=0)
    turned = jnp.concatenate([turned, turned], axis=0).T
    none = jnp.zeros_like(turned)
    forward = jnp.concatenate(
        [jnp.concatenate([turned, none], axis=0), jnp.concatenate([none, turned], axis=0)], axis=1
    )
    straight = jnp.concatenate([rel_pos_h, gap, rel_pos_w, gap], axis=0)
    straight = jnp.concatenate([straight, jnp.zeros_like(straight)], axis=0)
    none = jnp.zeros_like(straight)
    backward = jnp.stack(
        [
            jnp.concatenate([straight, none], axis=1),
            jnp.concatenate([none, straight], axis=1),
        ]
    )
    return forward, backward


def padded(values):
    images, rows, _, width = values.shape
    values = jnp.pad(values, ((0, 0), (0, 0), (0, SIDE - WIN), (0, 0)))
    return values.reshape(images, rows * SIDE, width)


def unpadded(values):
    images, _, width = values.shape
    return values.reshape(images, WIN, SIDE, width)[:, :, :WIN]


def local(
    patches,
    norm1_gain,
    norm1_bias,
    qkv_weight,
    qv_bias,
    rel_pos_h,
    rel_pos_w,
    proj_weight,
    proj_bias,
    norm2_gain,
    norm2_bias,
    fc1_weight,
    fc1_bias,
    fc2_weight,
    fc2_bias,
    heights,
    widths,
    out_grad,
):
    width = patches.shape[-1]
    dims = grid_of(lax.axis_size("dp"))
    core = lax.axis_index("mp")
    is_first = core == 0
    if dims is None:
        order = jnp.tile(jnp.arange(PIECES, dtype=jnp.int32), 2)
    else:
        order = jnp.concatenate([place_order(dims, 2, 1), place_order(dims, 1, 2)])
    meta = jnp.concatenate(
        [order, core.astype(jnp.int32)[None], heights, widths, jnp.zeros((27,), jnp.int32)]
    )

    vectors = (norm1_gain, norm1_bias, qv_bias[0], qv_bias[1], proj_bias, norm2_gain, norm2_bias, fc2_bias)
    small = jnp.pad(jnp.stack(vectors, axis=1), ((0, 0), (0, LANES - len(vectors))))
    qk = jnp.concatenate([qkv_weight[:, :width], small, qkv_weight[:, width : 2 * width]], axis=1)
    vp = jnp.concatenate([qkv_weight[:, 2 * width :], small, proj_weight], axis=1)
    if dims is None:
        qk = lax.all_gather(qk, ("dp", "mp"), axis=0, tiled=True)
        vp = lax.all_gather(vp, ("dp", "mp"), axis=0, tiled=True)
        own = jnp.where(is_first, qk, vp)
        far = jnp.where(is_first, vp, qk)
        own0, own1 = [own[:, : width + LANES]], [own[:, width + LANES :]]
        far0, far1 = [far[:, : width + LANES]], [far[:, width + LANES :]]
        hidden_in = [
            (
                [lax.all_gather(fc1_weight, "dp", axis=0, tiled=True)],
                [lax.all_gather(fc2_weight.T, "dp", axis=0, tiled=True)],
            )
        ]
    else:
        near = jnp.where(is_first, qk, vp)
        came = other_core(jnp.where(is_first, vp, qk))
        block = jnp.concatenate(
            [jnp.where(is_first, near, came), jnp.where(is_first, came, near)], axis=0
        )
        own0 = gather_rows(block[:, : width + LANES], dims, 2, 1)
        own1 = gather_rows(block[:, width + LANES :], dims, 1, 2)
        far0 = [other_core(part) for part in own0]
        far1 = [other_core(part) for part in own1]
        hidden_in = []
        part = fc1_weight.shape[1] // FFN_CHUNKS
        for chunk in range(FFN_CHUNKS):
            cols = slice(chunk * part, (chunk + 1) * part)
            hidden_in.append(
                (
                    gather_rows(fc1_weight[:, cols], dims, 2, 1),
                    gather_rows(fc2_weight.T[:, cols], dims, 1, 2),
                )
            )

    tok = padded(patches)
    row_index = core * WIN + jnp.arange(WIN)
    valid = (row_index[None, :, None] < heights[:, None, None]) & (
        jnp.arange(WIN)[None, None, :] < widths[:, None, None]
    )
    dm = padded(jnp.where(valid[..., None], out_grad, jnp.zeros_like(out_grad)))
    dm_far = other_core(dm)
    spread, gather = constants()
    table, table_back = tables(rel_pos_h, rel_pos_w)

    n1, q, k, v, p, att, x1, n2, vecs, weights = attend(
        meta, tok, table, jnp.asarray(spread, BF16), own0, own1, far0, far1
    )
    n2_far = other_core(n2)

    carried = None
    hidden_grads, bias_grads = [], []
    part = fc1_weight.shape[1] // len(hidden_in)
    for chunk, (in0, in1) in enumerate(hidden_in):
        bias = fc1_bias[None, chunk * part : (chunk + 1) * part].astype(F32)
        last = chunk == len(hidden_in) - 1
        made = hidden(meta, n2, n2_far, dm, dm_far, bias, in0, in1, carried, last)
        bias_grads.append(made[4])
        carried = made[5:]
        if dims is None:
            hidden_grads.append(
                [
                    lax.psum_scatter(
                        jnp.concatenate(pair, axis=0).astype(F32), "dp", scatter_dimension=0, tiled=True
                    )
                    for pair in (made[0:2], made[2:4])
                ]
            )
        else:
            hidden_grads.append(
                (
                    scatter_rows(made[0], made[1], dims, 2, 1),
                    scatter_rows(made[2], made[3], dims, 1, 2),
                )
            )
    out_own, out_far, back_own, back_far = carried
    block_out, dx1, da, sums2 = middle(
        meta, out_own, other_core(out_far), back_own, other_core(back_far), x1, dm, vecs
    )

    dn1 = None
    bias_sums, table_grad, attend_grads = [], 0.0, []
    for chunk in range(BACK_CHUNKS):
        made = attend_back(
            chunk,
            BACK_CHUNKS,
            meta,
            q,
            k,
            v,
            p,
            weights,
            da,
            att,
            n1,
            tok,
            dx1,
            vecs,
            jnp.asarray(gather, BF16),
            table_back,
            dn1,
        )
        bias_sums.append(made[4])
        table_grad = table_grad + made[5]
        dn1 = made[6]
        if chunk == BACK_CHUNKS - 1:
            sums1 = made[7]
        halves = []
        for mine, theirs, axes in ((made[0], made[2], (2, 1)), (made[1], made[3], (1, 2))):
            if dims is None:
                whole = lax.psum_scatter(
                    add(mine, other_core(theirs)), "dp", scatter_dimension=0, tiled=True
                )
            else:
                came = other_core(theirs)
                half = width // 2
                whole = scatter_rows(
                    add(mine[:half], came[:half]).astype(BF16),
                    add(mine[half:], came[half:]).astype(BF16),
                    dims,
                    *axes,
                )
            halves.append(whole)
        whole = jnp.stack(halves)
        rows = whole.shape[1] // 2
        near = jnp.where(is_first, whole[:, :rows], whole[:, rows:])
        came = other_core(jnp.where(is_first, whole[:, rows:], whole[:, :rows]))
        attend_grads.append((jnp.where(is_first, near, came), jnp.where(is_first, came, near)))
    qk_grad = [jnp.concatenate([g[0][i] for g in attend_grads], axis=1) for i in range(2)]
    vp_grad = [jnp.concatenate([g[1][i] for g in attend_grads], axis=1) for i in range(2)]
    qkv_grad = jnp.concatenate([qk_grad[0], qk_grad[1], vp_grad[0]], axis=1)

    qv_sums = jnp.concatenate(bias_sums, axis=1)
    rel_sums = table_grad[:64, :HDIM] + table_grad[:64, HDIM:]
    fc1_sums = jnp.concatenate(bias_grads, axis=1)
    fc1_sums = jnp.concatenate(
        [jnp.where(is_first, fc1_sums, 0.0), jnp.where(is_first, 0.0, fc1_sums)], axis=1
    )
    flat = jnp.concatenate(
        [
            jnp.concatenate([sums1, qv_sums, sums2[4:]], axis=0).reshape(-1, LANES),
            rel_sums.reshape(-1, LANES),
            fc1_sums.reshape(-1, LANES),
        ],
        axis=0,
    )
    flat = add_all(flat, dims)
    at = 8 * width // LANES
    vec_sums = flat[:at].reshape(8, width)
    rel = flat[at : at + 32].reshape(64, HDIM)
    fc1_bias_grad = lax.dynamic_index_in_dim(flat[at + 32 :].reshape(2, -1), core, 0, keepdims=False)
    share = norm1_gain.shape[0]
    device = lax.axis_index("dp") * 2 + core
    mine = lax.dynamic_slice_in_dim(vec_sums, device * share, share, axis=1)
    rels = rel_pos_h.shape[0]
    return (
        unpadded(block_out),
        unpadded(dn1),
        mine[0],
        mine[1],
        qkv_grad,
        mine[2:4],
        rel[:rels],
        rel[32 : 32 + rels],
        vp_grad[1],
        mine[4],
        mine[5],
        mine[6],
        jnp.concatenate([g[0] for g in hidden_grads], axis=1),
        fc1_bias_grad,
        jnp.concatenate([g[1] for g in hidden_grads], axis=1).T,
        mine[7],
    )


def solution(mesh):
    return jax.shard_map(
        local,
        mesh=mesh,
        in_specs=(
            P("dp", "mp", None, None),
            P(("dp", "mp")),
            P(("dp", "mp")),
            P(("dp", "mp"), None),
            P(None, ("dp", "mp")),
            P(),
            P(),
            P(("dp", "mp"), None),
            P(("dp", "mp")),
            P(("dp", "mp")),
            P(("dp", "mp")),
            P("dp", "mp"),
            P("mp"),
            P("mp", "dp"),
            P(("dp", "mp")),
            P("dp"),
            P("dp"),
            P("dp", "mp", None, None),
        ),
        out_specs=(
            P("dp", "mp", None, None),
            P("dp", "mp", None, None),
            P(("dp", "mp")),
            P(("dp", "mp")),
            P(("dp", "mp"), None),
            P(None, ("dp", "mp")),
            P(),
            P(),
            P(("dp", "mp"), None),
            P(("dp", "mp")),
            P(("dp", "mp")),
            P(("dp", "mp")),
            P("dp", "mp"),
            P("mp"),
            P("mp", "dp"),
            P(("dp", "mp")),
        ),
        check_vma=False,
    )
```

```python
from functools import partial

import jax
import jax.numpy as jnp
import numpy as np
from jax import lax
from jax.experimental import pallas as pl
from jax.experimental.pallas import tpu as pltpu
from jax.sharding import PartitionSpec as P

HEADS = 12
HDIM = 64
LANES = 128
PAIRS = HEADS // 2
WIN = 14
SIDE = 16
TOK = WIN * SIDE
KEYS = 256
PIECES = 16
EPSILON = 1e-06
MASKED_SCORE = -1e30
MASK_LANE = 60
FFN_CHUNKS = 2
BACK_PARTS = ((0, 4), (4, 2))
F32 = jnp.float32
BF16 = jnp.bfloat16
SMEM = pl.BlockSpec(memory_space=pltpu.SMEM)
HBM = pl.BlockSpec(memory_space=pl.ANY)
WHOLE = pl.BlockSpec(memory_space=pltpu.VMEM)
VMEM_BYTES = 52 * 2**20


def params():
    return pltpu.CompilerParams(vmem_limit_bytes=VMEM_BYTES)


def shape(dims, dtype):
    return jax.ShapeDtypeStruct(dims, dtype)


def dot(a, b):
    return jnp.dot(a, b, preferred_element_type=F32)


def dot_nt(a, b):
    return lax.dot_general(a, b, (((1,), (1,)), ((), ())), preferred_element_type=F32)


def dot_tn(a, b):
    return lax.dot_general(a, b, (((0,), (0,)), ((), ())), preferred_element_type=F32)


def lanes(rows):
    return lax.broadcasted_iota(jnp.int32, (rows, LANES), 1)


def moments(values):
    centered = values - jnp.mean(values, axis=-1, keepdims=True)
    inverse = lax.rsqrt(jnp.mean(centered * centered, axis=-1, keepdims=True) + EPSILON)
    return centered * inverse, inverse


def norm_back(grad, xhat, inverse, gain):
    scaled = grad * gain
    first = jnp.mean(scaled, axis=-1, keepdims=True)
    second = jnp.mean(scaled * xhat, axis=-1, keepdims=True)
    return inverse * (scaled - first - xhat * second)


def pieces_in(meta, at, refs, rows, cols, dest, sems, first):
    copies = []
    for ref in refs:
        for part in range(ref.shape[0] // rows):
            place = pl.multiple_of(meta[at + len(copies)] * rows, rows)
            copy = pltpu.make_async_copy(
                ref.at[pl.ds(part * rows, rows), cols],
                dest.at[pl.ds(place, rows), :],
                sems.at[first + len(copies)],
            )
            copy.start()
            copies.append(copy)
    return copies


def row_valid(meta, core, window, rows, width):
    place = lax.broadcasted_iota(jnp.int32, (rows, width), 0)
    row, col = place // SIDE, place % SIDE
    inside = (row < WIN) & (col < WIN)
    return inside & (core * WIN + row < meta[65 + window]) & (col < meta[67 + window])


def relative(turned):
    out = []
    for row in range(WIN):
        slab = turned[row * SIDE : (row + 1) * SIDE]
        down = pltpu.roll(slab, row, 1) if row else slab
        across = pltpu.roll(slab, 0, 1, stride=1, stride_axis=0)
        out.append(jnp.where(lanes(SIDE) % 64 < 32, down, across))
    return jnp.concatenate(out, axis=0)


def attend_kernel(count, meta, tok, table, spread, *refs):
    own, other = refs[:count], refs[count : 2 * count]
    n1, q_out, k_out, v_out, p_out, att, vecs, w_out = refs[2 * count : 2 * count + 8]
    weights, small, aug, sems, out_sem = refs[2 * count + 8 :]
    width = weights.shape[1]
    rows = width // PIECES
    core = meta[64]
    copies = []
    for refs_here, at, half, extra in ((own, 0, core, True), (other, 16, 1 - core, False)):
        places = [(0, width, weights.at[2 * half]), (width + LANES, width, weights.at[2 * half + 1])]
        if extra:
            places.append((width, LANES, small))
        for start, size, dest in places:
            copies += pieces_in(
                meta, at, refs_here, rows, pl.ds(start, size), dest, sems, len(copies)
            )
    for window in range(2):
        keys = lanes(KEYS)
        valid = row_valid(meta, core, window, KEYS, LANES)
        aug[window] = jnp.where(
            (keys == MASK_LANE) & ~valid, MASKED_SCORE, spread[...].astype(F32)
        ).astype(BF16)
        k_out[window, TOK:] = jnp.zeros((KEYS - TOK, width), BF16)
        v_out[window, TOK:] = jnp.zeros((KEYS - TOK, width), BF16)
    tokens = tok[...].reshape(2 * TOK, width).astype(F32)
    xhat, _ = moments(tokens)
    for copy in copies:
        copy.wait()
    out_copy = pltpu.make_async_copy(weights, w_out, out_sem)
    out_copy.start()
    vecs[...] = small[...].astype(F32).T[:8]
    normed = (xhat * vecs[0:1] + vecs[1:2]).astype(BF16)
    n1[...] = normed.reshape(2, TOK, width)
    for mat, dest in enumerate((q_out, k_out, v_out)):
        for start in range(0, width, 256):
            cols = pl.ds(start, 256)
            made = dot(normed, weights[mat, :, cols])
            if mat != 1:
                made = made + vecs[2 + mat // 2 : 3 + mat // 2, cols]
            made = made.astype(BF16)
            dest[0, :TOK, cols] = made[:TOK]
            dest[1, :TOK, cols] = made[TOK:]

    def heads_of(step, _):
        window, pair = step // PAIRS, step % PAIRS
        cols = pl.ds(pl.multiple_of(pair * LANES, LANES), LANES)
        q2, k2, v2 = q_out[window, :, cols], k_out[window, :, cols], v_out[window, :, cols]
        turned = dot(q2, table[...])
        place = lanes(TOK)
        keys_aug = jnp.concatenate([k2, aug[window]], axis=1)
        parts = []
        for half in range(2):
            rel = relative(turned[:, half * LANES : (half + 1) * LANES])
            high = rel.astype(BF16).astype(F32)
            rel = jnp.where(place < 64, high, rel - high)
            rel = jnp.where(place == MASK_LANE, 1.0, rel).astype(BF16)
            mine = jnp.where(place // 64 == half, q2.astype(F32) * HDIM**-0.5, 0.0).astype(BF16)
            scores = dot_nt(jnp.concatenate([mine, rel], axis=1), keys_aug)
            terms = jnp.exp(scores - jnp.max(scores, axis=-1, keepdims=True))
            soft = terms * (1.0 / jnp.sum(terms, axis=-1, keepdims=True))
            soft = soft.astype(BF16)
            p_out[window, 2 * pair + half] = soft
            parts.append(dot(soft, v2))
        att[window, :, cols] = jnp.where(place < 64, parts[0], parts[1]).astype(BF16)
        return 0

    lax.fori_loop(0, 2 * PAIRS, heads_of, 0)
    out_copy.wait()


def attend(meta, tok, table, spread, own, other):
    count, width = len(own), tok.shape[-1]
    rows = (2, TOK, width)
    keys = (2, KEYS, width)
    return pl.pallas_call(
        partial(attend_kernel, count),
        out_shape=[
            shape(rows, BF16),
            shape(rows, BF16),
            shape(keys, BF16),
            shape(keys, BF16),
            shape((2, HEADS, TOK, KEYS), BF16),
            shape(rows, BF16),
            shape((8, width), F32),
            shape((4, width, width), BF16),
        ],
        in_specs=[SMEM, WHOLE, WHOLE, WHOLE] + [HBM] * (2 * count),
        out_specs=[WHOLE] * 7 + [HBM],
        scratch_shapes=[
            pltpu.VMEM((4, width, width), BF16),
            pltpu.VMEM((width, LANES), BF16),
            pltpu.VMEM((2, KEYS, LANES), BF16),
            pltpu.SemaphoreType.DMA((5 * PIECES,)),
            pltpu.SemaphoreType.DMA,
        ],
        compiler_params=params(),
        cost_estimate=pl.CostEstimate(
            flops=6_000_000_000, bytes_accessed=60_000_000, transcendentals=1_500_000
        ),
        name="attend",
    )(meta, tok, table, spread, *own, *other)


def join_kernel(tok, att, weights, vecs, x1, n2):
    width = tok.shape[-1]
    for window in range(2):
        resid = tok[window].astype(F32) + (dot(att[window], weights[0]) + vecs[4:5])
        x1[window] = resid
        xhat, _ = moments(resid)
        n2[window] = (xhat * vecs[5:6] + vecs[6:7]).astype(BF16)


def join(tok, att, weights, vecs):
    width = tok.shape[-1]
    return pl.pallas_call(
        join_kernel,
        out_shape=[shape(tok.shape, F32), shape(tok.shape, BF16)],
        grid=(1,),
        in_specs=[
            WHOLE,
            WHOLE,
            pl.BlockSpec((1, width, width), lambda i: (3, 0, 0)),
            WHOLE,
        ],
        out_specs=[WHOLE] * 2,
        compiler_params=params(),
        cost_estimate=pl.CostEstimate(
            flops=600_000_000, bytes_accessed=9_000_000, transcendentals=0
        ),
        name="join",
    )(tok, att, weights, vecs)


def hidden_kernel(count, starts, first, last, meta, n2a, n2b, dma, dmb, bias, *refs):
    refs = list(refs)
    ins, refs = refs[:count], refs[count:]
    if not first:
        out_in, back_in = refs[:2]
        refs = refs[2:]
    keep, send, bias_grad = refs[:3]
    refs = refs[3:]
    if last:
        out_own, out_far, back_own, back_far = refs[:4]
        refs = refs[4:]
    else:
        out_acc, back_acc = refs[:2]
        refs = refs[2:]
    w0, w1, n2s, dms, acts, backs, g0, g1, sems, out_sems = refs
    width, cols_here = w0.shape
    rows = width // PIECES
    copies = []
    for start, dest in zip(starts, (w0, w1)):
        copies += pieces_in(meta, 0, ins, rows, pl.ds(start, cols_here), dest, sems, len(copies))
    n2s[: 2 * TOK] = n2a[...].reshape(2 * TOK, width)
    n2s[2 * TOK :] = n2b[...].reshape(2 * TOK, width)
    dms[: 2 * TOK] = dma[...].reshape(2 * TOK, width)
    dms[2 * TOK :] = dmb[...].reshape(2 * TOK, width)
    for copy in copies:
        copy.wait()
    outs = []
    for start in range(0, cols_here, 256):
        cols = pl.ds(start, 256)
        inner = dot(n2s[...], w0[:, cols]) + bias[:, cols]
        back = dot(dms[...], w1[:, cols])
        cdf = 0.5 + 0.5 * lax.erf(inner * 0.7071067811865476)
        density = jnp.exp(inner * inner * -0.5) * 0.3989422804014327
        acts[:, cols] = (inner * cdf).astype(BF16)
        back_pre = (back * (cdf + inner * density)).astype(BF16)
        backs[:, cols] = back_pre
        bias_grad[:, cols] = jnp.sum(back_pre.astype(F32), axis=0, keepdims=True)
        g0[:, cols] = dot_tn(n2s[...], back_pre).astype(BF16)
        g1[:, cols] = dot_tn(dms[...], acts[:, cols]).astype(BF16)
        for which, made in enumerate((g0, g1)):
            for piece in range(PIECES):
                dest = keep if piece < PIECES // 2 else send
                place = pl.multiple_of(meta[32 + piece] * rows, rows)
                at = (piece % (PIECES // 2)) * rows
                copy = pltpu.make_async_copy(
                    made.at[pl.ds(place, rows), cols],
                    dest.at[pl.ds(at, rows), pl.ds(which * cols_here + start, 256)],
                    out_sems.at[len(outs)],
                )
                copy.start()
                outs.append(copy)
    made_out = dot_nt(acts[...], w1[...])
    made_back = dot_nt(backs[...], w0[...])
    if not first:
        made_out = made_out + out_in[...]
        made_back = made_back + back_in[...]
    if last:
        out_own[...] = made_out[: 2 * TOK]
        out_far[...] = made_out[2 * TOK :].astype(BF16)
        back_own[...] = made_back[: 2 * TOK]
        back_far[...] = made_back[2 * TOK :].astype(BF16)
    else:
        out_acc[...] = made_out
        back_acc[...] = made_back
    for copy in outs:
        copy.wait()


def hidden(meta, n2a, n2b, dma, dmb, bias, ins, starts, carried, last):
    count, width, cols_here = len(ins), n2a.shape[-1], bias.shape[-1]
    first = carried is None
    out_shape = [shape((width // 2, 2 * cols_here), BF16)] * 2 + [shape((1, cols_here), F32)]
    if last:
        one = (2 * TOK, width)
        out_shape += [shape(one, F32), shape(one, BF16), shape(one, F32), shape(one, BF16)]
    else:
        out_shape += [shape((4 * TOK, width), F32)] * 2
    carried = () if first else carried
    return pl.pallas_call(
        partial(hidden_kernel, count, starts, first, last),
        out_shape=out_shape,
        in_specs=[SMEM] + [WHOLE] * 5 + [HBM] * count + [WHOLE] * len(carried),
        out_specs=[HBM] * 2 + [WHOLE] * (len(out_shape) - 2),
        scratch_shapes=[
            pltpu.VMEM((width, cols_here), BF16),
            pltpu.VMEM((width, cols_here), BF16),
            pltpu.VMEM((4 * TOK, width), BF16),
            pltpu.VMEM((4 * TOK, width), BF16),
            pltpu.VMEM((4 * TOK, cols_here), BF16),
            pltpu.VMEM((4 * TOK, cols_here), BF16),
            pltpu.VMEM((width, cols_here), BF16),
            pltpu.VMEM((width, cols_here), BF16),
            pltpu.SemaphoreType.DMA((2 * PIECES,)),
            pltpu.SemaphoreType.DMA((2 * PIECES * (cols_here // 256),)),
        ],
        compiler_params=params(),
        cost_estimate=pl.CostEstimate(
            flops=12 * 4 * TOK * width * cols_here,
            bytes_accessed=20_000_000,
            transcendentals=8 * TOK * cols_here,
        ),
        name="hidden",
    )(meta, n2a, n2b, dma, dmb, bias, *ins, *carried)


def middle_kernel(meta, out_own, out_far, back_own, back_far, x1, dm, vecs, block, dx1, da, sums):
    width = x1.shape[-1]
    core = meta[64]
    total = [jnp.zeros((1, width), F32) for _ in range(4)]
    for window in range(2):
        rows = pl.ds(window * TOK, TOK)
        resid = x1[window]
        valid = row_valid(meta, core, window, TOK, width)
        branch = out_own[rows] + out_far[rows].astype(F32) + vecs[7:8]
        block[window] = jnp.where(valid, resid + branch, 0.0).astype(BF16)
        grad = back_own[rows] + back_far[rows].astype(F32)
        xhat, inverse = moments(resid)
        out_grad = dm[window].astype(F32)
        dresid = out_grad + norm_back(grad, xhat, inverse, vecs[5:6])
        dx1[window] = dresid
        rounded = dresid.astype(BF16)
        da[window] = rounded
        for slot, value in enumerate((rounded.astype(F32), grad * xhat, grad, out_grad)):
            total[slot] = total[slot] + jnp.sum(value, axis=0, keepdims=True)
    sums[...] = jnp.concatenate([jnp.zeros((4, width), F32)] + total, axis=0)


def middle(meta, out_own, out_far, back_own, back_far, x1, dm, vecs):
    rows = x1.shape
    return pl.pallas_call(
        middle_kernel,
        out_shape=[
            shape(rows, BF16),
            shape(rows, F32),
            shape(rows, BF16),
            shape((8, rows[-1]), F32),
        ],
        in_specs=[SMEM] + [WHOLE] * 7,
        out_specs=[WHOLE] * 4,
        compiler_params=params(),
        cost_estimate=pl.CostEstimate(
            flops=20_000_000, bytes_accessed=9_000_000, transcendentals=0
        ),
        name="middle",
    )(meta, out_own, out_far, back_own, back_far, x1, dm, vecs)


def unrelative(grads):
    out = []
    for row in range(WIN):
        slab = grads[row * SIDE : (row + 1) * SIDE]
        down = pltpu.roll(slab, row, 1) if row else slab
        across = pltpu.roll(slab, 0, 1, stride=1, stride_axis=0)
        out.append(jnp.where(lanes(SIDE) < 32, down, across))
    return jnp.concatenate(out, axis=0)


def attend_back_kernel(
    first, last, meta, q, k, v, p, wqkv, wproj, da, da_cols, att, n1, tok, dx1, vecs, gather, table, *refs
):
    refs = list(refs)
    if not first:
        dn1_in = refs.pop(0)
    mine, theirs, bias_sums, table_grad, result = refs[:5]
    refs = refs[5:]
    if last:
        norm_sums = refs.pop(0)
    dat, dqkv, grads, sems = refs
    core = meta[64]
    width, cols_here = da.shape[-1], q.shape[-1]
    pairs, rows = cols_here // LANES, width // PIECES
    dat[...] = (
        dot_nt(da[...].reshape(2 * TOK, width), wproj[0]).astype(BF16).reshape(2, TOK, cols_here)
    )
    table_grad[...] = jnp.zeros_like(table_grad)
    outs = []

    def send(mat, made):
        grads[mat] = made.astype(BF16)
        is_own = core == mat // 2
        at = jnp.where(is_own, 32, 48)
        for piece in range(PIECES):
            place = pl.multiple_of(meta[at + piece] * rows, rows)
            source = grads.at[mat, pl.ds(place, rows), :]
            to = pl.ds(piece * rows, rows), pl.ds(mat % 2 * cols_here, cols_here)
            sem = sems.at[len(outs)]
            copies = [pltpu.make_async_copy(source, ref.at[to], sem) for ref in (mine, theirs)]
            pl.when(is_own)(copies[0].start)
            pl.when(~is_own)(copies[1].start)
            outs.append(copies[0])

    send(3, dot_tn(att[...].reshape(2 * TOK, width), da_cols[...].reshape(2 * TOK, cols_here)))

    def heads_of(step, _):
        window, pair = step // pairs, step % pairs
        cols = pl.ds(pl.multiple_of(pair * LANES, LANES), LANES)
        q2, k2, v2 = q[window, :, cols], k[window, :, cols], v[window, :, cols]
        dat2 = dat[window, :, cols]
        place = lanes(TOK)
        q8 = (q2.astype(F32) * HDIM**-0.5).astype(BF16)
        k8 = (k2.astype(F32) * HDIM**-0.5).astype(BF16)
        dqs, dks, dvs, dts = [], [], [], []
        for half in range(2):
            soft = p[window, 2 * pair + half]
            soft32 = soft.astype(F32)
            mine = jnp.where(place // 64 == half, dat2.astype(F32), 0.0).astype(BF16)
            weighted = soft32 * dot_nt(mine, v2)
            ds = (weighted - soft32 * jnp.sum(weighted, axis=-1, keepdims=True)).astype(BF16)
            turned = dot(ds, gather[...]).astype(BF16).astype(F32)
            turned = unrelative(turned).astype(BF16)
            dqs.append(dot(ds, k8) + dot(turned, table[half]))
            dks.append(dot_tn(ds, q8))
            dvs.append(dot_tn(soft, dat2))
            dts.append(dot_tn(turned, q2))
        key_place = lanes(TOK)
        dqkv[0, window, :, cols] = jnp.where(place < 64, dqs[0], dqs[1]).astype(BF16)
        dqkv[1, window, :, cols] = jnp.where(key_place < 64, dks[0][:TOK], dks[1][:TOK]).astype(BF16)
        dqkv[2, window, :, cols] = jnp.where(key_place < 64, dvs[0][:TOK], dvs[1][:TOK]).astype(BF16)
        table_grad[...] += jnp.where(lanes(LANES) < 64, dts[0], dts[1])
        return 0

    lax.fori_loop(0, 2 * pairs, heads_of, 0)
    normed = n1[...].reshape(2 * TOK, width)
    dn1 = jnp.zeros((2 * TOK, width), F32) if first else dn1_in[...].reshape(2 * TOK, width)
    for mat in range(3):
        change = dqkv[mat].reshape(2 * TOK, cols_here)
        send(mat, dot_tn(normed, change))
        dn1 = dn1 + dot_nt(change, wqkv[mat])
        if mat != 1:
            bias_sums[mat // 2 : mat // 2 + 1] = jnp.sum(change.astype(F32), axis=0, keepdims=True)
    if last:
        xhat, inverse = moments(tok[...].reshape(2 * TOK, width).astype(F32))
        norm_sums[0:1] = jnp.sum(dn1 * xhat, axis=0, keepdims=True)
        norm_sums[1:2] = jnp.sum(dn1, axis=0, keepdims=True)
        back = norm_back(dn1, xhat, inverse, vecs[0:1])
        result[...] = dx1[...] + back.reshape(2, TOK, width)
    else:
        result[...] = dn1.reshape(2, TOK, width)
    for copy in outs:
        copy.wait()


def attend_back(start, count, meta, q, k, v, p, weights, da, att, n1, tok, dx1, vecs, gather, table, dn1):
    width = q.shape[-1]
    cols_here, heads_here = count * LANES, 2 * count
    first, last, chunk = start == 0, start + count == PAIRS, start // count
    part = lambda rows: pl.BlockSpec((2, rows, cols_here), lambda i: (0, 0, chunk))
    out_shape = [shape((width, 2 * cols_here), BF16)] * 2 + [
        shape((2, cols_here), F32),
        shape((LANES, LANES), F32),
        shape((2, TOK, width), F32),
    ]
    if last:
        out_shape.append(shape((2, width), F32))
    extra = () if first else (dn1,)
    return pl.pallas_call(
        partial(attend_back_kernel, first, last),
        out_shape=out_shape,
        grid=(1,),
        in_specs=[
            SMEM,
            part(TOK),
            part(KEYS),
            part(KEYS),
            pl.BlockSpec((2, heads_here, TOK, KEYS), lambda i: (0, chunk, 0, 0)),
            pl.BlockSpec((3, width, cols_here), lambda i: (0, 0, chunk)),
            pl.BlockSpec((1, cols_here, width), lambda i: (3, chunk, 0)),
            WHOLE,
            part(TOK),
        ]
        + [WHOLE] * (7 + len(extra)),
        out_specs=[HBM] * 2 + [WHOLE] * (len(out_shape) - 2),
        scratch_shapes=[
            pltpu.VMEM((2, TOK, cols_here), BF16),
            pltpu.VMEM((3, 2, TOK, cols_here), BF16),
            pltpu.VMEM((4, width, cols_here), BF16),
            pltpu.SemaphoreType.DMA((4 * PIECES,)),
        ],
        compiler_params=params(),
        cost_estimate=pl.CostEstimate(
            flops=2_000_000_000 * count, bytes_accessed=10_000_000 * count, transcendentals=0
        ),
        name="attend_back",
    )(meta, q, k, v, p, weights, weights, da, da, att, n1, tok, dx1, vecs, gather, table, *extra)


def grid_of(count):
    return (4, 2, 2) if count == 16 else None


def turn(values, dims, moves):
    pairs = []
    for chip in range(dims[0] * dims[1] * dims[2]):
        for core, (axis, by) in enumerate(moves):
            place = list(np.unravel_index(chip, dims))
            place[axis] = (place[axis] + by) % dims[axis]
            pairs.append((2 * chip + core, 2 * int(np.ravel_multi_index(place, dims)) + core))
    return lax.ppermute(values, ("dp", "mp"), pairs)


ALONG_X, ALONG_Y = ((2, 1),) * 2, ((1, 1),) * 2
FIRST, SECOND = ((2, 1), (1, 1)), ((1, 1), (2, 1))


def along_z(values, dims):
    return [turn(values, dims, ((0, step),) * 2) for step in range(1, dims[0])]


def other_core(values):
    return lax.ppermute(values, "mp", [(0, 1), (1, 0)])


def after(values, *others):
    return lax.optimization_barrier((values, *others))[0]


def place_orders(dims, core):
    here = lax.axis_index("dp")
    z, y, x = here // (dims[1] * dims[2]), here // dims[2] % dims[1], here % dims[2]

    def chip(step, inner, outer):
        by_x = jnp.where(core == 0, inner, outer)
        by_y = jnp.where(core == 0, outer, inner)
        return ((z - step) % dims[0] * dims[1] + (y + by_y) % 2) * dims[2] + (x + by_x) % 2

    square = [(inner, outer) for outer in range(2) for inner in range(2)]
    gather = [chip(0, *at) for at in square]
    gather += [chip(step, *at) for at in square for step in range(1, dims[0])]
    scatter = [chip(step, *at) for at in square for step in range(dims[0])]
    return [jnp.stack(found).astype(jnp.int32) for found in (gather, scatter)]


def add(a, b):
    return a.astype(F32) + b.astype(F32)


class Scatter:
    def __init__(self, keep, far, dims):
        self.keep, self.dims = keep, dims
        self.came = turn(far, dims, SECOND)

    def second(self, *others):
        half = self.keep.shape[0] // 2
        came = after(self.came, *others)
        send = add(self.keep[half:], came[half:]).astype(BF16)
        self.near = add(self.keep[:half], came[:half])
        self.came = turn(send, self.dims, FIRST)
        return send

    def third(self, *others):
        near = self.near + after(self.came, *others).astype(F32)
        rows = near.shape[0] // self.dims[0]
        self.near = near[:rows]
        sends = [near[at * rows : (at + 1) * rows].astype(BF16) for at in range(1, self.dims[0])]
        self.came = [
            turn(part, self.dims, ((0, self.dims[0] - step),) * 2)
            for step, part in enumerate(sends, 1)
        ]
        return sends[0]

    def last(self, *others):
        total = self.near
        for part in self.came:
            total = total + after(part, *others).astype(F32)
        return total


def constants():
    key = np.arange(KEYS)
    row, col = key // SIDE, key % SIDE
    inside = (row < WIN) & (col < WIN)
    spread = np.zeros((KEYS, LANES), np.float32)
    gather = np.zeros((KEYS, LANES), np.float32)
    for place in key[inside]:
        for base in (0, 64):
            spread[place, base + WIN - 1 + row[place]] = 1.0
            spread[place, base + 32 + WIN - 1 + col[place]] = 1.0
        gather[place, WIN - 1 - row[place]] = 1.0
        gather[place, 32 + WIN - 1 - col[place]] = 1.0
    return spread, gather


def tables(rel_pos_h, rel_pos_w):
    count = rel_pos_h.shape[0]
    gap = jnp.zeros((32 - count, HDIM), BF16)
    turned = jnp.concatenate([rel_pos_h[::-1], gap, rel_pos_w[::-1], gap], axis=0)
    turned = jnp.concatenate([turned, turned], axis=0).T
    none = jnp.zeros_like(turned)
    forward = jnp.concatenate(
        [jnp.concatenate([turned, none], axis=0), jnp.concatenate([none, turned], axis=0)], axis=1
    )
    straight = jnp.concatenate([rel_pos_h, gap, rel_pos_w, gap], axis=0)
    straight = jnp.concatenate([straight, jnp.zeros_like(straight)], axis=0)
    none = jnp.zeros_like(straight)
    backward = jnp.stack(
        [
            jnp.concatenate([straight, none], axis=1),
            jnp.concatenate([none, straight], axis=1),
        ]
    )
    return forward, backward


def padded(values):
    images, rows, _, width = values.shape
    values = jnp.pad(values, ((0, 0), (0, 0), (0, SIDE - WIN), (0, 0)))
    return values.reshape(images, rows * SIDE, width)


def unpadded(values):
    images, _, width = values.shape
    return values.reshape(images, WIN, SIDE, width)[:, :, :WIN]


def local(
    patches,
    norm1_gain,
    norm1_bias,
    qkv_weight,
    qv_bias,
    rel_pos_h,
    rel_pos_w,
    proj_weight,
    proj_bias,
    norm2_gain,
    norm2_bias,
    fc1_weight,
    fc1_bias,
    fc2_weight,
    fc2_bias,
    heights,
    widths,
    out_grad,
):
    width = patches.shape[-1]
    dims = grid_of(lax.axis_size("dp"))
    core = lax.axis_index("mp")
    is_first = core == 0
    if dims is None:
        orders = [jnp.tile(jnp.arange(PIECES, dtype=jnp.int32), 4)]
    else:
        own, far = place_orders(dims, core), place_orders(dims, 1 - core)
        orders = [own[0], far[0], own[1], far[1]]
    meta = jnp.concatenate(
        orders + [core.astype(jnp.int32)[None], heights, widths, jnp.zeros((11,), jnp.int32)]
    )
    hidden_count = fc1_weight.shape[1]

    vectors = (norm1_gain, norm1_bias, qv_bias[0], qv_bias[1], proj_bias, norm2_gain, norm2_bias, fc2_bias)
    small = jnp.pad(jnp.stack(vectors, axis=1), ((0, 0), (0, LANES - len(vectors))))
    qk = jnp.concatenate([qkv_weight[:, :width], small, qkv_weight[:, width : 2 * width]], axis=1)
    vp = jnp.concatenate([qkv_weight[:, 2 * width :], small, proj_weight], axis=1)
    if dims is None:
        qk = lax.all_gather(qk, ("dp", "mp"), axis=0, tiled=True)
        vp = lax.all_gather(vp, ("dp", "mp"), axis=0, tiled=True)
        attend_own = [jnp.where(is_first, qk, vp)]
        attend_far = [jnp.where(is_first, vp, qk)]
        hidden_in = [
            jnp.concatenate(
                [
                    lax.all_gather(fc1_weight, "dp", axis=0, tiled=True),
                    lax.all_gather(fc2_weight.T, "dp", axis=0, tiled=True),
                ],
                axis=1,
            )
        ]
    else:
        came = other_core(jnp.where(is_first, vp, qk))
        hidden_block = jnp.concatenate([fc1_weight, fc2_weight.T], axis=1)
        hidden_beside = turn(hidden_block, dims, FIRST)
        near = jnp.where(is_first, qk, vp)
        block = jnp.concatenate(
            [jnp.where(is_first, near, came), jnp.where(is_first, came, near)], axis=0
        )
        attend_z = along_z(block, dims)
        beside = turn(block, dims, FIRST)
        both = jnp.concatenate([block, beside], axis=0)
        over = turn(both, dims, SECOND)
        both = jnp.concatenate([hidden_block, after(hidden_beside, both)], axis=0)
        hidden_over = turn(both, dims, SECOND)
        attend_z = jnp.concatenate([after(attend_z[0], both)] + attend_z[1:], axis=0)
        z_beside = turn(attend_z, dims, FIRST)
        hidden_z = along_z(after(hidden_block, attend_z), dims)
        both = jnp.concatenate([attend_z, z_beside], axis=0)
        z_over = turn(both, dims, SECOND)
        attend_own = [block, beside, over, attend_z, z_beside, z_over]
        attend_far = [other_core(part) for part in attend_own]
        hidden_z = jnp.concatenate([after(hidden_z[0], both)] + hidden_z[1:], axis=0)
        hidden_z_beside = turn(hidden_z, dims, FIRST)
        hidden_z_over = turn(hidden_z, dims, SECOND)

    tok = padded(patches)
    row_index = core * WIN + jnp.arange(WIN)
    valid = (row_index[None, :, None] < heights[:, None, None]) & (
        jnp.arange(WIN)[None, None, :] < widths[:, None, None]
    )
    dm = padded(jnp.where(valid[..., None], out_grad, jnp.zeros_like(out_grad)))
    dm_far = other_core(dm)
    spread, gather = constants()
    table, table_back = tables(rel_pos_h, rel_pos_w)

    if dims is not None:
        tok = after(tok, hidden_z)
    n1, q, k, v, p, att, vecs, weights = attend(
        meta, tok, table, jnp.asarray(spread, BF16), attend_own, attend_far
    )
    if dims is not None:
        hidden_z_both = turn(after(hidden_z_beside, att), dims, SECOND)
        hidden_in = [
            hidden_block, hidden_beside, hidden_over, hidden_z, hidden_z_beside, hidden_z_over, hidden_z_both,
        ]
    x1, n2 = join(tok, att, weights, vecs)
    n2_far = other_core(n2)

    carried = None
    hidden_sums, bias_grads = [], []
    part = hidden_count // FFN_CHUNKS
    for chunk in range(FFN_CHUNKS):
        bias = fc1_bias[None, chunk * part : (chunk + 1) * part].astype(F32)
        last = chunk == FFN_CHUNKS - 1
        starts = (chunk * part, hidden_count + chunk * part)
        made = hidden(meta, n2, n2_far, dm, dm_far, bias, hidden_in, starts, carried, last)
        bias_grads.append(made[2])
        carried = made[3:]
        if dims is None:
            hidden_sums.append(
                lax.psum_scatter(
                    jnp.concatenate(made[:2], axis=0).astype(F32), "dp", scatter_dimension=0, tiled=True
                )
            )
        else:
            if chunk:
                sent = hidden_sums[-1].second(made[2])
                made = [made[0], after(made[1], sent)]
            hidden_sums.append(Scatter(made[0], made[1], dims))
    out_own, out_far, back_own, back_far = carried
    back_far = other_core(back_far)
    block_out, dx1, da, sums2 = middle(
        meta, out_own, other_core(out_far), back_own, back_far, x1, dm, vecs
    )

    dn1 = None
    bias_sums, table_grad, attend_sums = [], 0.0, []
    for start, count in BACK_PARTS:
        made = attend_back(
            start,
            count,
            meta,
            q,
            k,
            v,
            p,
            weights,
            da,
            att,
            n1,
            tok,
            dx1,
            vecs,
            jnp.asarray(gather, BF16),
            table_back,
            dn1,
        )
        bias_sums.append(made[2])
        table_grad = table_grad + made[3]
        dn1 = made[4]
        mine, theirs = made[0], made[1]
        came = other_core(theirs)
        if dims is None:
            attend_sums.append(
                lax.psum_scatter(add(mine, came), "dp", scatter_dimension=0, tiled=True)
            )
            continue
        half = width // 2
        if start == 0:
            sent = hidden_sums[0].third(dn1)
            sent = hidden_sums[1].second(sent)
            both = add(mine, after(came, sent)).astype(BF16)
            attend_sums.append(Scatter(both[:half], both[half:], dims))
            da = after(da, both)
    sums1 = made[5]

    qv_sums = jnp.concatenate(bias_sums, axis=1)
    rel_sums = table_grad[:64, :HDIM] + table_grad[:64, HDIM:]
    fc1_sums = jnp.concatenate(bias_grads, axis=1)
    fc1_sums = jnp.concatenate(
        [jnp.where(is_first, fc1_sums, 0.0), jnp.where(is_first, 0.0, fc1_sums)], axis=1
    )
    flat = jnp.concatenate(
        [
            jnp.concatenate([sums1, qv_sums, sums2[4:]], axis=0).reshape(-1, LANES),
            rel_sums.reshape(-1, LANES),
            fc1_sums.reshape(-1, LANES),
        ],
        axis=0,
    )
    if dims is None:
        flat = lax.psum(flat + other_core(flat), "dp")
    else:
        flat_came = other_core(flat)
        sent = hidden_sums[1].third(dn1)
        sent = attend_sums[0].second(sent)
        both = add(mine, after(came, sent)).astype(BF16)
        attend_sums.append(Scatter(both[:half], both[half:], dims))
        flat = flat + after(flat_came, both)
        flat_came = turn(flat, dims, SECOND)
        sent = attend_sums[0].third(flat)
        flat = flat + after(flat_came, sent)
        flat_came = turn(flat, dims, FIRST)
        sent = attend_sums[1].second(flat)
        flat = flat + after(flat_came, sent)
        flat_came = along_z(flat, dims)
        hidden_sums = [found.last(sent) for found in hidden_sums]
        sent = attend_sums[1].third(flat, *hidden_sums)
        attend_sums[0] = attend_sums[0].last(sent)
        flat = flat + sum(flat_came)
        attend_sums[1] = attend_sums[1].last(flat, attend_sums[0])

    whole = jnp.concatenate(attend_sums, axis=1)
    rows = whole.shape[0] // 2
    near = jnp.where(is_first, whole[:rows], whole[rows:])
    came = other_core(jnp.where(is_first, whole[rows:], whole[:rows]))
    halves = [[], []]
    at = 0
    for _, count in BACK_PARTS:
        for half in range(2):
            halves[half].append(slice(at, at + count * LANES))
            at += count * LANES
    qk, vp = jnp.where(is_first, near, came), jnp.where(is_first, came, near)
    q_grad, k_grad, v_grad, proj_grad = (
        jnp.concatenate([found[:, cols] for cols in half], axis=1)
        for found in (qk, vp)
        for half in halves
    )
    qkv_grad = jnp.concatenate([q_grad, k_grad, v_grad], axis=1)
    cols = hidden_sums[0].shape[1] // 2
    fc1_grad = jnp.concatenate([found[:, :cols] for found in hidden_sums], axis=1)
    fc2_grad = jnp.concatenate([found[:, cols:] for found in hidden_sums], axis=1).T

    at = 8 * width // LANES
    vec_sums = flat[:at].reshape(8, width)
    rel = flat[at : at + 32].reshape(64, HDIM)
    fc1_bias_grad = lax.dynamic_index_in_dim(flat[at + 32 :].reshape(2, -1), core, 0, keepdims=False)
    share = norm1_gain.shape[0]
    device = lax.axis_index("dp") * 2 + core
    mine = lax.dynamic_slice_in_dim(vec_sums, device * share, share, axis=1)
    rels = rel_pos_h.shape[0]
    return (
        unpadded(block_out),
        unpadded(dn1),
        mine[0],
        mine[1],
        qkv_grad,
        mine[2:4],
        rel[:rels],
        rel[32 : 32 + rels],
        proj_grad,
        mine[4],
        mine[5],
        mine[6],
        fc1_grad,
        fc1_bias_grad,
        fc2_grad,
        mine[7],
    )


def solution(mesh):
    return jax.shard_map(
        local,
        mesh=mesh,
        in_specs=(
            P("dp", "mp", None, None),
            P(("dp", "mp")),
            P(("dp", "mp")),
            P(("dp", "mp"), None),
            P(None, ("dp", "mp")),
            P(),
            P(),
            P(("dp", "mp"), None),
            P(("dp", "mp")),
            P(("dp", "mp")),
            P(("dp", "mp")),
            P("dp", "mp"),
            P("mp"),
            P("mp", "dp"),
            P(("dp", "mp")),
            P("dp"),
            P("dp"),
            P("dp", "mp", None, None),
        ),
        out_specs=(
            P("dp", "mp", None, None),
            P("dp", "mp", None, None),
            P(("dp", "mp")),
            P(("dp", "mp")),
            P(("dp", "mp"), None),
            P(None, ("dp", "mp")),
            P(),
            P(),
            P(("dp", "mp"), None),
            P(("dp", "mp")),
            P(("dp", "mp")),
            P(("dp", "mp")),
            P("dp", "mp"),
            P("mp"),
            P("mp", "dp"),
            P(("dp", "mp")),
        ),
        check_vma=False,
    )
```

```python
from functools import partial

import jax
import jax.numpy as jnp
import numpy as np
from jax import lax
from jax.experimental import pallas as pl
from jax.experimental.pallas import tpu as pltpu
from jax.sharding import PartitionSpec as P

HEADS = 12
HDIM = 64
LANES = 128
PAIRS = HEADS // 2
WIN = 14
SIDE = 16
TOK = WIN * SIDE
KEYS = 256
PIECES = 16
EPSILON = 1e-06
MASKED_SCORE = -1e30
MASK_LANE = 60
CHUNK = 512
BACK_PARTS = ((0, 2), (2, 2), (4, 2))
F32 = jnp.float32
BF16 = jnp.bfloat16
SMEM = pl.BlockSpec(memory_space=pltpu.SMEM)
HBM = pl.BlockSpec(memory_space=pl.ANY)
WHOLE = pl.BlockSpec(memory_space=pltpu.VMEM)
VMEM_BYTES = 52 * 2**20


def params():
    return pltpu.CompilerParams(vmem_limit_bytes=VMEM_BYTES)


def shape(dims, dtype):
    return jax.ShapeDtypeStruct(dims, dtype)


def dot(a, b):
    return jnp.dot(a, b, preferred_element_type=F32)


def dot_nt(a, b):
    return lax.dot_general(a, b, (((1,), (1,)), ((), ())), preferred_element_type=F32)


def dot_tn(a, b):
    return lax.dot_general(a, b, (((0,), (0,)), ((), ())), preferred_element_type=F32)


def lanes(rows):
    return lax.broadcasted_iota(jnp.int32, (rows, LANES), 1)


def moments(values):
    centered = values - jnp.mean(values, axis=-1, keepdims=True)
    inverse = lax.rsqrt(jnp.mean(centered * centered, axis=-1, keepdims=True) + EPSILON)
    return centered * inverse, inverse


def norm_back(grad, xhat, inverse, gain):
    scaled = grad * gain
    first = jnp.mean(scaled, axis=-1, keepdims=True)
    second = jnp.mean(scaled * xhat, axis=-1, keepdims=True)
    return inverse * (scaled - first - xhat * second)


def begin(source, dest, sem):
    copy = pltpu.make_async_copy(source, dest, sem)
    copy.start()
    return copy


def finish(copies):
    for copy in copies:
        copy.wait()


def pieces_in(meta, at, ins, start, dest, sems, first):
    rows, cols = dest.shape[0] // PIECES, dest.shape[1]
    copies = []
    for ref, base in ins:
        for part in range(ref.shape[0] // rows):
            place = pl.multiple_of(meta[at + len(copies)] * rows, rows)
            source = ref.at[pl.ds(part * rows, rows), pl.ds(base + start, cols)]
            copies.append(begin(source, dest.at[pl.ds(place, rows), :], sems.at[first + len(copies)]))
    return copies


def row_valid(meta, core, window, rows, width):
    place = lax.broadcasted_iota(jnp.int32, (rows, width), 0)
    row, col = place // SIDE, place % SIDE
    inside = (row < WIN) & (col < WIN)
    return inside & (core * WIN + row < meta[65 + window]) & (col < meta[67 + window])


def relative(turned):
    out = []
    for row in range(WIN):
        slab = turned[row * SIDE : (row + 1) * SIDE]
        down = pltpu.roll(slab, row, 1) if row else slab
        across = pltpu.roll(slab, 0, 1, stride=1, stride_axis=0)
        out.append(jnp.where(lanes(SIDE) % 64 < 32, down, across))
    return jnp.concatenate(out, axis=0)


def attend_kernel(count, total, meta, tok, table, spread, *refs):
    own, other = refs[:count], refs[count:total]
    vecs, n1, q, k, v, p, att, w_out = refs[total : total + 8]
    toks, weights, small, aug, n1s, qs, ks, vs, ps, atts, sems, out_sems = refs[total + 8 :]
    width = weights.shape[1]
    core = meta[64]
    tok_copy = begin(tok, toks, sems.at[5 * PIECES])
    own, other = ([(ref, 0) for ref in found] for found in (own, other))
    copies = pieces_in(meta, 0, own, width, small, sems, 0)
    for found, at, half in ((own, 0, core), (other, 16, 1 - core)):
        for start, mat in ((0, 2 * half), (width + LANES, 2 * half + 1)):
            copies += pieces_in(meta, at, found, start, weights.at[mat], sems, len(copies))
    for window in range(2):
        valid = row_valid(meta, core, window, KEYS, LANES)
        aug[window] = jnp.where(
            (lanes(KEYS) == MASK_LANE) & ~valid, MASKED_SCORE, spread[...].astype(F32)
        ).astype(BF16)
        ks[window, TOK:] = jnp.zeros((KEYS - TOK, width), BF16)
        vs[window, TOK:] = jnp.zeros((KEYS - TOK, width), BF16)
    tok_copy.wait()
    xhat, _ = moments(toks[...].reshape(2 * TOK, width).astype(F32))
    finish(copies)
    outs = [begin(weights, w_out, out_sems.at[0])]
    vecs[...] = small[...].astype(F32).T[:8]
    normed = (xhat * vecs[0:1] + vecs[1:2]).astype(BF16)
    n1s[...] = normed.reshape(2, TOK, width)
    outs.append(begin(n1s, n1, out_sems.at[1]))
    for mat, (made_in, dest) in enumerate(((qs, q), (ks, k), (vs, v))):
        for start in range(0, width, 256):
            cols = pl.ds(start, 256)
            made = dot(normed, weights[mat, :, cols])
            if mat != 1:
                made = made + vecs[2 + mat // 2 : 3 + mat // 2, cols]
            made = made.astype(BF16)
            made_in[0, :TOK, cols] = made[:TOK]
            made_in[1, :TOK, cols] = made[TOK:]
        outs.append(begin(made_in, dest, out_sems.at[2 + mat]))

    place = lanes(TOK)
    for step in range(2 * PAIRS):
        window, pair = step // PAIRS, step % PAIRS
        cols = pl.ds(pair * LANES, LANES)
        q2, k2, v2 = qs[window, :, cols], ks[window, :, cols], vs[window, :, cols]
        turned = dot(q2, table[...])
        keys_aug = jnp.concatenate([k2, aug[window]], axis=1)
        parts = []
        for half in range(2):
            rel = relative(turned[:, half * LANES : (half + 1) * LANES])
            high = rel.astype(BF16).astype(F32)
            rel = jnp.where(place < 64, high, rel - high)
            rel = jnp.where(place == MASK_LANE, 1.0, rel).astype(BF16)
            mine = jnp.where(place // 64 == half, q2.astype(F32) * HDIM**-0.5, 0.0).astype(BF16)
            scores = dot_nt(jnp.concatenate([mine, rel], axis=1), keys_aug)
            terms = jnp.exp(scores - jnp.max(scores, axis=-1, keepdims=True))
            soft = terms * (1.0 / jnp.sum(terms, axis=-1, keepdims=True))
            soft = soft.astype(BF16)
            ps[window, 2 * pair + half] = soft
            parts.append(dot(soft, v2))
        atts[window, :, cols] = jnp.where(place < 64, parts[0], parts[1]).astype(BF16)
        heads = pl.ds(2 * pair, 2)
        outs.append(begin(ps.at[window, heads], p.at[window, heads], out_sems.at[len(outs)]))
    outs.append(begin(atts, att, out_sems.at[len(outs)]))
    finish(outs)


def attend(meta, tok, table, spread, own, other):
    count, total, width = len(own), len(own) + len(other), tok.shape[-1]
    rows, keys, heads = (2, TOK, width), (2, KEYS, width), (2, HEADS, TOK, KEYS)
    mats = (4, width, width)
    outs = (rows, rows, keys, keys, heads, rows, mats)
    return pl.pallas_call(
        partial(attend_kernel, count, total),
        out_shape=[shape((8, width), F32)] + [shape(dims, BF16) for dims in outs],
        in_specs=[SMEM, HBM, WHOLE, WHOLE] + [HBM] * total,
        out_specs=[WHOLE] + [HBM] * len(outs),
        scratch_shapes=[
            pltpu.VMEM(dims, BF16)
            for dims in (rows, mats, (width, LANES), (2, KEYS, LANES), rows, rows, keys, keys, heads, rows)
        ]
        + [
            pltpu.SemaphoreType.DMA((5 * PIECES + 1,)),
            pltpu.SemaphoreType.DMA((6 + 2 * PAIRS,)),
        ],
        compiler_params=params(),
        cost_estimate=pl.CostEstimate(
            flops=20_000_000_000, bytes_accessed=40_000_000, transcendentals=1_500_000
        ),
        name="attend",
    )(meta, tok, table, spread, *own, *other)


def join_kernel(tok, att, weights, vecs, x1, n2):
    for window in range(2):
        resid = tok[window].astype(F32) + (dot(att[window], weights[0]) + vecs[4:5])
        x1[window] = resid
        xhat, _ = moments(resid)
        n2[window] = (xhat * vecs[5:6] + vecs[6:7]).astype(BF16)


def join(tok, att, weights, vecs):
    width = tok.shape[-1]
    return pl.pallas_call(
        join_kernel,
        out_shape=[shape(tok.shape, F32), shape(tok.shape, BF16)],
        grid=(1,),
        in_specs=[
            WHOLE,
            WHOLE,
            pl.BlockSpec((1, width, width), lambda i: (3, 0, 0)),
            WHOLE,
        ],
        out_specs=[WHOLE] * 2,
        compiler_params=params(),
        cost_estimate=pl.CostEstimate(
            flops=600_000_000, bytes_accessed=9_000_000, transcendentals=0
        ),
        name="join",
    )(tok, att, weights, vecs)


def pieces_out(meta, made, cols, keep, send, sems, first):
    rows = made.shape[0] // PIECES
    copies = []
    for piece in range(PIECES):
        dest = keep if piece < PIECES // 2 else send
        place = pl.multiple_of(meta[32 + piece] * rows, rows)
        at = pl.ds(piece % (PIECES // 2) * rows, rows)
        source = made.at[pl.ds(place, rows), cols]
        copies.append(begin(source, dest.at[at, cols], sems.at[first + len(copies)]))
    return copies


def hidden_fwd_kernel(bases, meta, n2a, n2b, dm_turned, bias, *refs):
    count = len(bases)
    ins, (keep, send) = list(zip(refs[:count], bases)), refs[count : count + 2]
    w0, n2s, dms, grad, sems, out_sems = refs[count + 2 :]
    width, hidden = w0.shape
    starts = range(0, hidden, CHUNK)
    at = PIECES * len(starts)
    n2_copies = [
        begin(n2a, n2s.at[: 2 * TOK], sems.at[at]),
        begin(n2b, n2s.at[2 * TOK :], sems.at[at + 1]),
    ]
    copies = [
        pieces_in(meta, 0, ins, start, w0.at[:, pl.ds(start, CHUNK)], sems, PIECES * step)
        for step, start in enumerate(starts)
    ]
    dm_copy = begin(dm_turned, dms, sems.at[at + 2])
    finish(n2_copies)
    outs = []
    for step, start in enumerate(starts):
        cols = pl.ds(start, CHUNK)
        finish(copies[step])
        inner = dot(n2s[...], w0[:, cols]) + bias[:, cols]
        act = (inner * (0.5 + 0.5 * lax.erf(inner * 0.7071067811865476))).astype(BF16)
        if step == 0:
            dm_copy.wait()
        grad[:, cols] = dot(dms[...], act).astype(BF16)
        outs += pieces_out(meta, grad, cols, keep, send, out_sems, len(outs))
    finish(outs)


def hidden_fwd(meta, n2a, n2b, dm_turned, bias, ins):
    refs, bases = zip(*ins)
    width, hidden = n2a.shape[-1], bias.shape[-1]
    steps = hidden // CHUNK
    return pl.pallas_call(
        partial(hidden_fwd_kernel, bases),
        out_shape=[shape((width // 2, hidden), BF16)] * 2,
        in_specs=[SMEM] + [HBM] * 3 + [WHOLE] + [HBM] * len(refs),
        out_specs=[HBM] * 2,
        scratch_shapes=[
            pltpu.VMEM((width, hidden), BF16),
            pltpu.VMEM((4 * TOK, width), BF16),
            pltpu.VMEM((width, 4 * TOK), BF16),
            pltpu.VMEM((width, hidden), BF16),
            pltpu.SemaphoreType.DMA((PIECES * steps + 3,)),
            pltpu.SemaphoreType.DMA((PIECES * steps,)),
        ],
        compiler_params=params(),
        cost_estimate=pl.CostEstimate(
            flops=12 * 4 * TOK * width * hidden,
            bytes_accessed=12_000_000,
            transcendentals=4 * TOK * hidden,
        ),
        name="hidden_fwd",
    )(meta, n2a, n2b, dm_turned, bias, *refs)


def hidden_back_kernel(bases0, bases1, meta, n2a, n2b, dma, dmb, bias, *refs):
    count = len(bases0)
    ins0, ins1 = list(zip(refs[:count], bases0)), list(zip(refs[count : 2 * count], bases1))
    refs = refs[2 * count :]
    bias_grad, keep, send, back_own, back_far, out_own, out_far = refs[:7]
    w0, w1, n2s, n2t, dms, acts, backs, grad, big, small, sems, out_sems = refs[7:]
    width, hidden = w0.shape
    starts = range(0, hidden, CHUNK)
    halves = (pl.ds(0, 2 * TOK), pl.ds(2 * TOK, 2 * TOK))
    at = 2 * PIECES * len(starts)
    n2_copies = [
        begin(ref, n2s.at[half], sems.at[at + i]) for i, (ref, half) in enumerate(zip((n2a, n2b), halves))
    ]
    copies = []
    for step, start in enumerate(starts):
        cols = pl.ds(start, CHUNK)
        copies.append(pieces_in(meta, 0, ins0, start, w0.at[:, cols], sems, 2 * PIECES * step))
        if step == 0:
            dm_copies = [
                begin(ref, dms.at[half], sems.at[at + 2 + i])
                for i, (ref, half) in enumerate(zip((dma, dmb), halves))
            ]
        copies.append(pieces_in(meta, 0, ins1, start, w1.at[:, cols], sems, 2 * PIECES * step + PIECES))
    finish(n2_copies)
    n2t[...] = n2s[...].T
    outs = []
    for step, start in enumerate(starts):
        cols = pl.ds(start, CHUNK)
        finish(copies[2 * step])
        inner = dot(n2s[...], w0[:, cols]) + bias[:, cols]
        if step == 0:
            finish(dm_copies)
        finish(copies[2 * step + 1])
        back = dot(dms[...], w1[:, cols])
        cdf = 0.5 + 0.5 * lax.erf(inner * 0.7071067811865476)
        density = jnp.exp(inner * inner * -0.5) * 0.3989422804014327
        acts[:, cols] = (inner * cdf).astype(BF16)
        back_pre = (back * (cdf + inner * density)).astype(BF16)
        backs[:, cols] = back_pre
        bias_grad[:, cols] = jnp.sum(back_pre.astype(F32), axis=0, keepdims=True)
        grad[:, cols] = dot(n2t[...], back_pre).astype(BF16)
        outs += pieces_out(meta, grad, cols, keep, send, out_sems, len(outs))
    for which, (left, right, own, far) in enumerate(
        ((backs, w0, back_own, back_far), (acts, w1, out_own, out_far))
    ):
        small[which] = dot_nt(left[halves[1]], right[...]).astype(BF16)
        outs.append(begin(small.at[which], far, out_sems.at[len(outs)]))
        big[which] = dot_nt(left[halves[0]], right[...])
        outs.append(begin(big.at[which], own, out_sems.at[len(outs)]))
    finish(outs)


def hidden_back(meta, n2a, n2b, dma, dmb, bias, ins0, ins1):
    (refs0, bases0), (refs1, bases1) = zip(*ins0), zip(*ins1)
    width, hidden = n2a.shape[-1], bias.shape[-1]
    steps = hidden // CHUNK
    one = (2 * TOK, width)
    tall = pltpu.VMEM((4 * TOK, width), BF16)
    wide = pltpu.VMEM((width, hidden), BF16)
    return pl.pallas_call(
        partial(hidden_back_kernel, bases0, bases1),
        out_shape=[shape((1, hidden), F32)]
        + [shape((width // 2, hidden), BF16)] * 2
        + [shape(one, F32), shape(one, BF16)] * 2,
        in_specs=[SMEM] + [HBM] * 4 + [WHOLE] + [HBM] * (2 * len(refs0)),
        out_specs=[WHOLE] + [HBM] * 6,
        scratch_shapes=[
            wide,
            wide,
            tall,
            pltpu.VMEM((width, 4 * TOK), BF16),
            tall,
            pltpu.VMEM((4 * TOK, hidden), BF16),
            pltpu.VMEM((4 * TOK, hidden), BF16),
            wide,
            pltpu.VMEM((2,) + one, F32),
            pltpu.VMEM((2,) + one, BF16),
            pltpu.SemaphoreType.DMA((2 * PIECES * steps + 4,)),
            pltpu.SemaphoreType.DMA((PIECES * steps + 4,)),
        ],
        compiler_params=params(),
        cost_estimate=pl.CostEstimate(
            flops=24 * 4 * TOK * width * hidden,
            bytes_accessed=20_000_000,
            transcendentals=8 * TOK * hidden,
        ),
        name="hidden_back",
    )(meta, n2a, n2b, dma, dmb, bias, *refs0, *refs1)


def unrelative(grads):
    out = []
    for row in range(WIN):
        slab = grads[row * SIDE : (row + 1) * SIDE]
        down = pltpu.roll(slab, row, 1) if row else slab
        across = pltpu.roll(slab, 0, 1, stride=1, stride_axis=0)
        out.append(jnp.where(lanes(SIDE) < 32, down, across))
    return jnp.concatenate(out, axis=0)


def attend_back_kernel(start, count, meta, vecs, gather, table, q, k, v, p, weights, att, n1, *refs):
    first, last = start == 0, start + count == PAIRS
    parts = start // count
    if first:
        back_own, back_far, x1, dm = refs[:4]
        norm_sums, bias_sums, table_grad, mine, theirs, dqkv_out, dx1, da = refs[4:12]
        refs = refs[12:]
        owns, fars, x1s, dms, dx1s = refs[-5:]
        refs = refs[:-5]
    else:
        da, refs = refs[0], refs[1:]
        if last:
            tok, dx1, *changes = refs[: 2 + parts]
            norm_sums, bias_sums, table_grad, mine, theirs, result = refs[2 + parts : 8 + parts]
            refs = refs[8 + parts :]
            wqkv, toks, dx1s, results, *changed = refs[-4 - parts :]
            refs = refs[: -4 - parts]
        else:
            bias_sums, table_grad, mine, theirs, dqkv_out = refs[:5]
            refs = refs[5:]
    das, wproj, atts, n1s, qs, ks, vs, ps, dat, dqkv, grads, turned_in, sems, out_sems = refs
    core = meta[64]
    width, cols_here = das.shape[-1], qs.shape[-1]
    rows = width // PIECES
    columns = pl.ds(start * LANES, cols_here)
    tokens = (2 * TOK, width)
    early = []
    if first:
        early = [(back_own, owns), (back_far, fars), (x1, x1s), (dm, dms)]
    else:
        early = [(da, das)]
    early = [begin(ref, dest, sems.at[at]) for at, (ref, dest) in enumerate(early)]
    wait_proj = begin(weights.at[3, columns, :], wproj, sems.at[4])
    wait_att = begin(att, atts, sems.at[5])
    wait_v = begin(v.at[:, :, columns], vs, sems.at[6])
    wait_p = []
    for window in range(2):
        for pair in range(count):
            heads = pl.ds(2 * (start + pair), 2)
            wait_p.append(
                begin(p.at[window, heads], ps.at[window, pl.ds(2 * pair, 2)], sems.at[10 + len(wait_p)])
            )
        if window == 0:
            wait_qk = [
                begin(ref.at[:, :, columns], dest, sems.at[7 + at])
                for at, (ref, dest) in enumerate(((q, qs), (k, ks)))
            ]
    wait_n1 = begin(n1, n1s, sems.at[9])
    if last:
        at = 10 + 2 * count
        ends = [begin(tok, toks, sems.at[at]), begin(dx1, dx1s, sems.at[at + 1])]
        ends += [begin(weights.at[mat], wqkv.at[mat], sems.at[at + 2 + mat]) for mat in range(3)]
        for part in range(parts):
            ends.append(begin(changes[part], changed[part], sems.at[at + 5 + part]))
    outs = []
    finish(early)
    if first:
        total = [jnp.zeros((1, width), F32) for _ in range(4)]
        for window in range(2):
            here = pl.ds(window * TOK, TOK)
            grad = owns[here] + fars[here].astype(F32)
            xhat, inverse = moments(x1s[window])
            out_grad = dms[window].astype(F32)
            dresid = out_grad + norm_back(grad, xhat, inverse, vecs[5:6])
            dx1s[window] = dresid
            rounded = dresid.astype(BF16)
            das[window] = rounded
            for slot, value in enumerate((rounded.astype(F32), grad * xhat, grad, out_grad)):
                total[slot] = total[slot] + jnp.sum(value, axis=0, keepdims=True)
        norm_sums[...] = jnp.concatenate(total, axis=0)
        outs.append(begin(dx1s, dx1, out_sems.at[4 * PIECES]))
        outs.append(begin(das, da, out_sems.at[4 * PIECES + 1]))
    wait_proj.wait()
    dat[...] = dot_nt(das[...].reshape(tokens), wproj[...]).astype(BF16).reshape(2, TOK, cols_here)

    def send(mat, made):
        grads[mat] = made.astype(BF16)
        is_own = core == mat // 2
        at = jnp.where(is_own, 32, 48)
        for piece in range(PIECES):
            place = pl.multiple_of(meta[at + piece] * rows, rows)
            source = grads.at[mat, pl.ds(place, rows), :]
            to = pl.ds(piece * rows, rows), pl.ds(mat % 2 * cols_here, cols_here)
            sem = out_sems.at[mat * PIECES + piece]
            copies = [pltpu.make_async_copy(source, ref.at[to], sem) for ref in (mine, theirs)]
            pl.when(is_own)(copies[0].start)
            pl.when(~is_own)(copies[1].start)
            outs.append(copies[0])

    wait_att.wait()
    turned_in[...] = atts[...].reshape(tokens).T
    send(3, dot(turned_in[...], das[:, :, columns].reshape(2 * TOK, cols_here)))
    finish(wait_qk + [wait_v])
    place = lanes(TOK)
    table_sum = jnp.zeros((LANES, LANES), F32)
    for step in range(2 * count):
        window, pair = step // count, step % count
        cols = pl.ds(pair * LANES, LANES)
        q2, k2, v2, dat2 = (ref[window, :, cols] for ref in (qs, ks, vs, dat))
        q8 = (q2.astype(F32) * HDIM**-0.5).astype(BF16)
        k8 = (k2.astype(F32) * HDIM**-0.5).astype(BF16)
        wait_p[step].wait()
        dqs, dks, dvs, dts = [], [], [], []
        for half in range(2):
            soft = ps[window, 2 * pair + half]
            soft32 = soft.astype(F32)
            own_lanes = jnp.where(place // 64 == half, dat2.astype(F32), 0.0).astype(BF16)
            weighted = soft32 * dot_nt(own_lanes, v2)
            ds = (weighted - soft32 * jnp.sum(weighted, axis=-1, keepdims=True)).astype(BF16)
            turned = dot(ds, gather[...]).astype(BF16).astype(F32)
            turned = unrelative(turned).astype(BF16)
            dqs.append(dot(ds, k8) + dot(turned, table[half]))
            dks.append(dot_tn(ds, q8))
            dvs.append(dot_tn(soft, dat2))
            dts.append(dot_tn(turned, q2))
        dqkv[0, window, :, cols] = jnp.where(place < 64, dqs[0], dqs[1]).astype(BF16)
        dqkv[1, window, :, cols] = jnp.where(place < 64, dks[0][:TOK], dks[1][:TOK]).astype(BF16)
        dqkv[2, window, :, cols] = jnp.where(place < 64, dvs[0][:TOK], dvs[1][:TOK]).astype(BF16)
        table_sum = table_sum + jnp.where(lanes(LANES) < 64, dts[0], dts[1])
    table_grad[...] = table_sum
    if not last:
        outs.append(begin(dqkv, dqkv_out, out_sems.at[4 * PIECES + 2]))
    wait_n1.wait()
    turned_in[...] = n1s[...].reshape(tokens).T
    for mat in range(3):
        change = dqkv[mat].reshape(2 * TOK, cols_here)
        send(mat, dot(turned_in[...], change))
        if mat != 1:
            bias_sums[mat // 2 : mat // 2 + 1] = jnp.sum(change.astype(F32), axis=0, keepdims=True)
    if last:
        finish(ends)
        total = [jnp.zeros((1, width), F32) for _ in range(2)]
        for window in range(2):
            grad = jnp.zeros((TOK, width), F32)
            for part, change in enumerate([*changed, dqkv]):
                here = pl.ds(part * cols_here, cols_here)
                for mat in range(3):
                    grad = grad + dot_nt(change[mat, window], wqkv[mat, :, here])
            xhat, inverse = moments(toks[window].astype(F32))
            results[window] = dx1s[window] + norm_back(grad, xhat, inverse, vecs[0:1])
            outs.append(begin(results.at[window], result.at[window], out_sems.at[4 * PIECES + window]))
            for slot, value in enumerate((grad * xhat, grad)):
                total[slot] = total[slot] + jnp.sum(value, axis=0, keepdims=True)
        norm_sums[...] = jnp.concatenate(total, axis=0)
    finish(outs)


def attend_back(start, count, meta, vecs, gather, table, q, k, v, p, weights, att, n1, ins):
    width, cols_here = q.shape[-1], count * LANES
    first, last, parts = start == 0, start + count == PAIRS, start // count
    rows, keys = (2, TOK, width), (2, KEYS, cols_here)
    part, flat = (2, TOK, cols_here), (2 * TOK, width)
    heads = (2, 2 * count, TOK, KEYS)
    small = [shape((2, cols_here), F32), shape((LANES, LANES), F32)]
    large = [shape((width, 2 * cols_here), BF16)] * 2
    large.append(shape(rows, F32) if last else shape((3,) + part, BF16))
    if last:
        small = [shape((2, width), F32)] + small
    if first:
        small = [shape((4, width), F32)] + small
        large += [shape(rows, F32), shape(rows, BF16)]
    scratch = [rows, (cols_here, width), rows, rows, part, keys, keys, heads, part, (3,) + part]
    scratch += [(4, width, cols_here), (width, 2 * TOK)]
    scratch = [pltpu.VMEM(dims, BF16) for dims in scratch]
    scratch += [pltpu.SemaphoreType.DMA((15 + 2 * count + parts,)), pltpu.SemaphoreType.DMA((4 * PIECES + 3,))]
    if first:
        scratch += [
            pltpu.VMEM(flat, F32),
            pltpu.VMEM(flat, BF16),
            pltpu.VMEM(rows, F32),
            pltpu.VMEM(rows, BF16),
            pltpu.VMEM(rows, F32),
        ]
    if last:
        scratch += [
            pltpu.VMEM((3, width, width), BF16),
            pltpu.VMEM(rows, BF16),
            pltpu.VMEM(rows, F32),
            pltpu.VMEM(rows, F32),
        ] + [pltpu.VMEM((3,) + part, BF16)] * parts
    return pl.pallas_call(
        partial(attend_back_kernel, start, count),
        out_shape=small + large,
        in_specs=[SMEM] + [WHOLE] * 3 + [HBM] * (7 + len(ins)),
        out_specs=[WHOLE] * len(small) + [HBM] * len(large),
        scratch_shapes=scratch,
        compiler_params=params(),
        cost_estimate=pl.CostEstimate(
            flops=8_000_000_000 * count, bytes_accessed=10_000_000 * count, transcendentals=0
        ),
        name="attend_back",
    )(meta, vecs, gather, table, q, k, v, p, weights, att, n1, *ins)


def grid_of(count):
    return (4, 2, 2) if count == 16 else None


def turn(values, dims, moves):
    pairs = []
    for chip in range(dims[0] * dims[1] * dims[2]):
        for core, (axis, by) in enumerate(moves):
            place = list(np.unravel_index(chip, dims))
            place[axis] = (place[axis] + by) % dims[axis]
            pairs.append((2 * chip + core, 2 * int(np.ravel_multi_index(place, dims)) + core))
    return lax.ppermute(values, ("dp", "mp"), pairs)


ALONG_X, ALONG_Y = ((2, 1),) * 2, ((1, 1),) * 2
FIRST, SECOND = ((2, 1), (1, 1)), ((1, 1), (2, 1))


def along_z(values, dims):
    return [turn(values, dims, ((0, step),) * 2) for step in range(1, dims[0])]


def swap_z(values, dims, by):
    chips = dims[1] * dims[2]
    pairs = [(chip, (chip // chips ^ by) * chips + chip % chips) for chip in range(dims[0] * chips)]
    return lax.ppermute(values, "dp", pairs)


def other_core(values):
    return lax.ppermute(values, "mp", [(0, 1), (1, 0)])


def after(values, *others):
    return lax.optimization_barrier((values, *others))[0]


class Flow:
    def __init__(self, *came):
        self.came = list(came)


def meet(flows, *values):
    sizes = [len(flow.came) for flow in flows]
    found = list(lax.optimization_barrier((*(part for flow in flows for part in flow.came), *values)))
    for flow, size in zip(flows, sizes):
        flow.came, found = found[:size], found[size:]
    return found


def place_orders(dims, core):
    here = lax.axis_index("dp")
    z, y, x = here // (dims[1] * dims[2]), here // dims[2] % dims[1], here % dims[2]

    def chip(step, inner, outer):
        by_x = jnp.where(core == 0, inner, outer)
        by_y = jnp.where(core == 0, outer, inner)
        return ((z - step) % dims[0] * dims[1] + (y + by_y) % 2) * dims[2] + (x + by_x) % 2

    square = [(inner, outer) for outer in range(2) for inner in range(2)]
    gather = [chip(0, *at) for at in square]
    gather += [chip(step, *at) for at in square for step in range(1, dims[0])]
    scatter = [chip(step, *at) for at in square for step in range(dims[0])]
    return [jnp.stack(found).astype(jnp.int32) for found in (gather, scatter)]


def add(a, b):
    return a.astype(F32) + b.astype(F32)


class Scatter(Flow):
    def __init__(self, keep, far, dims):
        super().__init__(turn(far, dims, SECOND))
        self.keep, self.dims = keep, dims

    def second(self):
        half = self.keep.shape[0] // 2
        send = add(self.keep[half:], self.came[0][half:]).astype(BF16)
        self.near = add(self.keep[:half], self.came[0][:half])
        self.came = [turn(send, self.dims, FIRST)]

    def third(self):
        near = self.near + self.came[0].astype(F32)
        rows = near.shape[0] // self.dims[0]
        self.near = near[:rows]
        self.came = [
            turn(near[step * rows : (step + 1) * rows].astype(BF16), self.dims, ((0, self.dims[0] - step),) * 2)
            for step in range(1, self.dims[0])
        ]

    def last(self):
        return sum((part.astype(F32) for part in self.came), self.near)


def constants():
    key = np.arange(KEYS)
    row, col = key // SIDE, key % SIDE
    inside = (row < WIN) & (col < WIN)
    spread = np.zeros((KEYS, LANES), np.float32)
    gather = np.zeros((KEYS, LANES), np.float32)
    for place in key[inside]:
        for base in (0, 64):
            spread[place, base + WIN - 1 + row[place]] = 1.0
            spread[place, base + 32 + WIN - 1 + col[place]] = 1.0
        gather[place, WIN - 1 - row[place]] = 1.0
        gather[place, 32 + WIN - 1 - col[place]] = 1.0
    return spread, gather


def tables(rel_pos_h, rel_pos_w):
    count = rel_pos_h.shape[0]
    gap = jnp.zeros((32 - count, HDIM), BF16)
    turned = jnp.concatenate([rel_pos_h[::-1], gap, rel_pos_w[::-1], gap], axis=0)
    turned = jnp.concatenate([turned, turned], axis=0).T
    none = jnp.zeros_like(turned)
    forward = jnp.concatenate(
        [jnp.concatenate([turned, none], axis=0), jnp.concatenate([none, turned], axis=0)], axis=1
    )
    straight = jnp.concatenate([rel_pos_h, gap, rel_pos_w, gap], axis=0)
    straight = jnp.concatenate([straight, jnp.zeros_like(straight)], axis=0)
    none = jnp.zeros_like(straight)
    backward = jnp.stack(
        [
            jnp.concatenate([straight, none], axis=1),
            jnp.concatenate([none, straight], axis=1),
        ]
    )
    return forward, backward


def padded(values):
    images, rows, _, width = values.shape
    values = jnp.pad(values, ((0, 0), (0, 0), (0, SIDE - WIN), (0, 0)))
    return values.reshape(images, rows * SIDE, width)


def unpadded(values):
    images, _, width = values.shape
    return values.reshape(images, WIN, SIDE, width)[:, :, :WIN]


def local(
    patches,
    norm1_gain,
    norm1_bias,
    qkv_weight,
    qv_bias,
    rel_pos_h,
    rel_pos_w,
    proj_weight,
    proj_bias,
    norm2_gain,
    norm2_bias,
    fc1_weight,
    fc1_bias,
    fc2_weight,
    fc2_bias,
    heights,
    widths,
    out_grad,
):
    width = patches.shape[-1]
    dims = grid_of(lax.axis_size("dp"))
    core = lax.axis_index("mp")
    is_first = core == 0
    if dims is None:
        orders = [jnp.tile(jnp.arange(PIECES, dtype=jnp.int32), 4)]
    else:
        own, far = place_orders(dims, core), place_orders(dims, 1 - core)
        orders = [own[0], far[0], own[1], far[1]]
    meta = jnp.concatenate(
        orders + [core.astype(jnp.int32)[None], heights, widths, jnp.zeros((11,), jnp.int32)]
    )

    tok = padded(patches)
    row_index = core * WIN + jnp.arange(WIN)
    valid = (row_index[None, :, None] < heights[:, None, None]) & (
        jnp.arange(WIN)[None, None, :] < widths[:, None, None]
    )
    dm = padded(jnp.where(valid[..., None], out_grad, jnp.zeros_like(out_grad)))
    dm_far = other_core(dm)

    vectors = (norm1_gain, norm1_bias, qv_bias[0], qv_bias[1], proj_bias, norm2_gain, norm2_bias, fc2_bias)
    small = jnp.pad(jnp.stack(vectors, axis=1), ((0, 0), (0, LANES - len(vectors))))
    qk = jnp.concatenate([qkv_weight[:, :width], small, qkv_weight[:, width : 2 * width]], axis=1)
    vp = jnp.concatenate([qkv_weight[:, 2 * width :], small, proj_weight], axis=1)
    if dims is None:
        qk = lax.all_gather(qk, ("dp", "mp"), axis=0, tiled=True)
        vp = lax.all_gather(vp, ("dp", "mp"), axis=0, tiled=True)
        attend_own = [jnp.where(is_first, qk, vp)]
        attend_far = [jnp.where(is_first, vp, qk)]
        hidden_in = tuple(
            ((lax.all_gather(part, "dp", axis=0, tiled=True), 0),) for part in (fc1_weight, fc2_weight.T)
        )
    else:
        fc1, fc2 = fc1_weight, fc2_weight.T
        came = other_core(jnp.where(is_first, vp, qk))
        near = jnp.where(is_first, qk, vp)
        block = jnp.concatenate(
            [jnp.where(is_first, near, came), jnp.where(is_first, came, near)], axis=0
        )
        attend_size, hidden_size = block.shape[1], fc1.shape[1]
        own = jnp.concatenate([block, fc1, fc2], axis=1)
        attend_z, beside = Flow(*along_z(block, dims)), Flow(turn(own, dims, FIRST))
        dm_flow = Flow(dm_far)
        fc1, fc2 = meet([attend_z, beside, dm_flow], fc1, fc2)
        dm_far = dm_flow.came[0]

        own = jnp.concatenate([own, *beside.came], axis=0)
        over = Flow(turn(own, dims, SECOND))
        attend_z = jnp.concatenate(attend_z.came, axis=0)
        z_beside, fc1_z = Flow(turn(attend_z, dims, FIRST)), Flow(*along_z(fc1, dims))
        (fc2,) = meet([over, z_beside, fc1_z], fc2)

        over = over.came[0]
        attend_z = jnp.concatenate([attend_z, *z_beside.came], axis=0)
        fc1_z = jnp.concatenate(fc1_z.came, axis=0)
        z_over, fc1_beside = Flow(turn(attend_z, dims, SECOND)), Flow(turn(fc1_z, dims, FIRST))
        fc2_z = Flow(*along_z(fc2, dims))
        own_attend = jnp.concatenate([own[:, :attend_size], over[:, :attend_size]], axis=0)
        own_attend, attend_z = meet([z_over, fc1_beside, fc2_z], own_attend, attend_z)

        z_over = z_over.came[0]
        far = Flow(*(other_core(part) for part in (own_attend, attend_z, z_over)))
        fc1_z = jnp.concatenate([fc1_z, *fc1_beside.came], axis=0)
        fc1_over = Flow(turn(fc1_z, dims, SECOND))
        fc2_z = jnp.concatenate(fc2_z.came, axis=0)
        fc2_beside = Flow(turn(fc2_z, dims, FIRST))
        tok, fc1_z, fc2_z = meet([far], tok, fc1_z, fc2_z)
        attend_own, attend_far = [own, over, attend_z, z_over], far.came

    dm_flat, dm_far = dm.reshape(-1, width), dm_far.reshape(-1, width)
    dm_turned = jnp.concatenate([dm_flat, dm_far], axis=0).T
    spread, gather = constants()
    table, table_back = tables(rel_pos_h, rel_pos_w)

    vecs, n1, q, k, v, p, att, weights = attend(
        meta, tok, table, jnp.asarray(spread, BF16), attend_own, attend_far
    )
    if dims is not None:
        (att,) = meet([fc1_over, fc2_beside], att)
        fc2_z = jnp.concatenate([fc2_z, *fc2_beside.came], axis=0)
        fc2_over = Flow(turn(fc2_z, dims, SECOND))
        att = after(att, fc2_z)
    x1, n2 = join(tok, att, weights, vecs)
    n2_far = other_core(n2).reshape(-1, width)
    n2 = n2.reshape(-1, width)
    bias = fc1_bias[None].astype(F32)
    if dims is not None:
        places = (attend_size, attend_size), (attend_size + hidden_size,) * 2
        hidden_in = [tuple(zip((own, over, fc1_z, *fc1_over.came), (*places[0], 0, 0)))]
    fc2_part = hidden_fwd(meta, n2, n2_far, dm_turned, bias, hidden_in[0])
    if dims is not None:
        fc2_part = meet([fc2_over], *fc2_part)
        hidden_in.append(tuple(zip((own, over, fc2_z, *fc2_over.came), (*places[1], 0, 0))))
        fc2_sum = Scatter(*fc2_part, dims)
    fc1_bias_part, *fc1_part, back_own, back_far, out_own, out_far = hidden_back(
        meta, n2, n2_far, dm_flat, dm_far, bias, *hidden_in
    )
    back_far = other_core(back_far)
    if dims is not None:
        fc1_part = meet([fc2_sum], *fc1_part)
        fc2_sum.second()
        fc1_sum = Scatter(*fc1_part, dims)
    out_far = other_core(out_far)

    shared = (meta, vecs, jnp.asarray(gather, BF16), table_back, q, k, v, p, weights, att, n1)
    bias_sums, table_grad, attend_sums, changes = [], 0.0, [], []
    ins = (back_own, back_far, x1, dm)
    half = width // 2
    for start, count in BACK_PARTS:
        made = attend_back(start, count, *shared, ins)
        if start == 0:
            sums2, *made, dx1, da = made
        if start + count == PAIRS:
            sums1, *made = made
        bias_sums.append(made[0])
        table_grad = table_grad + made[1]
        mine, theirs, change = made[2:]
        changes.append(change)
        if dims is None:
            attend_sums.append(
                lax.psum_scatter(add(mine, other_core(theirs)), "dp", scatter_dimension=0, tiled=True)
            )
        elif start + count < PAIRS:
            came = Flow(other_core(theirs))
            if start == 0:
                da, mine = meet([fc2_sum, fc1_sum], da, mine)
                fc2_sum.third()
                fc1_sum.second()
            else:
                da, mine = meet([fc2_sum, fc1_sum, *attend_sums], da, mine)
                fc2_sum = fc2_sum.last()
                fc1_sum.third()
                attend_sums[0].second()
            both = add(mine, came.came[0]).astype(BF16)
            attend_sums.append(Scatter(both[:half], both[half:], dims))
            da = after(da, both)
        ins = (da,) if start + 2 * count < PAIRS else (da, tok, dx1, *changes)
    result = change
    branch = add(out_own, out_far).reshape(x1.shape) + vecs[7]
    block_out = unpadded(x1 + branch)
    block_out = jnp.where(valid[..., None], block_out, 0.0).astype(BF16)

    qv_sums = jnp.concatenate(bias_sums, axis=1)
    rel_sums = table_grad[:64, :HDIM] + table_grad[:64, HDIM:]
    fc1_sums = jnp.concatenate(
        [jnp.where(is_first, fc1_bias_part, 0.0), jnp.where(is_first, 0.0, fc1_bias_part)], axis=1
    )
    flat = jnp.concatenate(
        [
            jnp.concatenate([sums1, qv_sums, sums2], axis=0).reshape(-1, LANES),
            rel_sums.reshape(-1, LANES),
            fc1_sums.reshape(-1, LANES),
        ],
        axis=0,
    )
    if dims is None:
        flat = lax.psum(flat + other_core(flat), "dp")
        fc1_sum, fc2_sum = (
            lax.psum_scatter(
                jnp.concatenate(parts, axis=0).astype(F32), "dp", scatter_dimension=0, tiled=True
            )
            for parts in (fc1_part, fc2_part)
        )
    else:
        mine, theirs, flat = meet([fc1_sum, *attend_sums], mine, theirs, flat)
        came, flat_came = Flow(other_core(theirs)), Flow(other_core(flat))
        attend_sums[1].second()
        fc1_sum = fc1_sum.last()
        mine, flat = meet([came, flat_came, attend_sums[1]], mine, flat)
        both = add(mine, came.came[0]).astype(BF16)
        attend_sums.append(Scatter(both[:half], both[half:], dims))
        flat = flat + flat_came.came[0]
        flat_came = Flow(turn(flat, dims, SECOND))
        attend_sums[0].third()
        (flat,) = meet([flat_came, attend_sums[0], attend_sums[2]], flat)
        flat = flat + flat_came.came[0]
        flat_came = Flow(turn(flat, dims, FIRST))
        attend_sums[2].second()
        attend_sums[1].third()
        attend_sums[0] = attend_sums[0].last()
        (flat,) = meet([flat_came, attend_sums[1], attend_sums[2]], flat)
        flat = flat + flat_came.came[0]
        flat_came = Flow(swap_z(flat, dims, 2))
        attend_sums[2].third()
        attend_sums[1] = attend_sums[1].last()
        (flat,) = meet([flat_came, attend_sums[2]], flat)
        flat = flat + flat_came.came[0]
        flat = flat + swap_z(flat, dims, 1)
        attend_sums[2] = attend_sums[2].last()

    whole = jnp.concatenate(attend_sums, axis=1)
    rows = whole.shape[0] // 2
    near = jnp.where(is_first, whole[:rows], whole[rows:])
    came = other_core(jnp.where(is_first, whole[rows:], whole[:rows]))
    halves = [[], []]
    at = 0
    for _, count in BACK_PARTS:
        for half in range(2):
            halves[half].append(slice(at, at + count * LANES))
            at += count * LANES
    qk, vp = jnp.where(is_first, near, came), jnp.where(is_first, came, near)
    q_grad, k_grad, v_grad, proj_grad = (
        jnp.concatenate([found[:, cols] for cols in half], axis=1)
        for found in (qk, vp)
        for half in halves
    )
    qkv_grad = jnp.concatenate([q_grad, k_grad, v_grad], axis=1)
    at = 8 * width // LANES
    vec_sums = flat[:at].reshape(8, width)
    rel = flat[at : at + 32].reshape(64, HDIM)
    fc1_bias_grad = lax.dynamic_index_in_dim(flat[at + 32 :].reshape(2, -1), core, 0, keepdims=False)
    share = norm1_gain.shape[0]
    device = lax.axis_index("dp") * 2 + core
    mine = lax.dynamic_slice_in_dim(vec_sums, device * share, share, axis=1)
    rels = rel_pos_h.shape[0]
    return (
        block_out,
        unpadded(result),
        mine[0],
        mine[1],
        qkv_grad,
        mine[2:4],
        rel[:rels],
        rel[32 : 32 + rels],
        proj_grad,
        mine[4],
        mine[5],
        mine[6],
        fc1_sum,
        fc1_bias_grad,
        fc2_sum.T,
        mine[7],
    )


def solution(mesh):
    return jax.shard_map(
        local,
        mesh=mesh,
        in_specs=(
            P("dp", "mp", None, None),
            P(("dp", "mp")),
            P(("dp", "mp")),
            P(("dp", "mp"), None),
            P(None, ("dp", "mp")),
            P(),
            P(),
            P(("dp", "mp"), None),
            P(("dp", "mp")),
            P(("dp", "mp")),
            P(("dp", "mp")),
            P("dp", "mp"),
            P("mp"),
            P("mp", "dp"),
            P(("dp", "mp")),
            P("dp"),
            P("dp"),
            P("dp", "mp", None, None),
        ),
        out_specs=(
            P("dp", "mp", None, None),
            P("dp", "mp", None, None),
            P(("dp", "mp")),
            P(("dp", "mp")),
            P(("dp", "mp"), None),
            P(None, ("dp", "mp")),
            P(),
            P(),
            P(("dp", "mp"), None),
            P(("dp", "mp")),
            P(("dp", "mp")),
            P(("dp", "mp")),
            P("dp", "mp"),
            P("mp"),
            P("mp", "dp"),
            P(("dp", "mp")),
        ),
        check_vma=False,
    )
```

```python
from functools import partial

import jax
import jax.numpy as jnp
import numpy as np
from jax import lax
from jax.experimental import pallas as pl
from jax.experimental.pallas import tpu as pltpu
from jax.sharding import PartitionSpec as P

HEADS = 12
HDIM = 64
LANES = 128
PAIRS = HEADS // 2
WIN = 14
SIDE = 16
TOK = WIN * SIDE
KEYS = 256
PIECES = 16
EPSILON = 1e-06
MASKED_SCORE = -1e30
MASK_LANE = 60
CHUNK = 512
BACK_PARTS = (4, 2)
F32 = jnp.float32
BF16 = jnp.bfloat16
SMEM = pl.BlockSpec(memory_space=pltpu.SMEM)
HBM = pl.BlockSpec(memory_space=pl.ANY)
WHOLE = pl.BlockSpec(memory_space=pltpu.VMEM)
VMEM_BYTES = 52 * 2**20
COST = pl.CostEstimate(flops=1000, bytes_accessed=1000, transcendentals=0)


def params():
    return pltpu.CompilerParams(vmem_limit_bytes=VMEM_BYTES)


def shape(dims, dtype):
    return jax.ShapeDtypeStruct(dims, dtype)


def dot(a, b):
    return jnp.dot(a, b, preferred_element_type=F32)


def dot_nt(a, b):
    return lax.dot_general(a, b, (((1,), (1,)), ((), ())), preferred_element_type=F32)


def dot_tn(a, b):
    return lax.dot_general(a, b, (((0,), (0,)), ((), ())), preferred_element_type=F32)


def lanes(rows):
    return lax.broadcasted_iota(jnp.int32, (rows, LANES), 1)


def moments(values):
    centered = values - jnp.mean(values, axis=-1, keepdims=True)
    inverse = lax.rsqrt(jnp.mean(centered * centered, axis=-1, keepdims=True) + EPSILON)
    return centered * inverse, inverse


def norm_back(grad, xhat, inverse, gain):
    scaled = grad * gain
    first = jnp.mean(scaled, axis=-1, keepdims=True)
    second = jnp.mean(scaled * xhat, axis=-1, keepdims=True)
    return inverse * (scaled - first - xhat * second)


def begin(source, dest, sem):
    copy = pltpu.make_async_copy(source, dest, sem)
    copy.start()
    return copy


def finish(copies):
    for copy in copies:
        copy.wait()


def pieces_in(meta, at, ins, start, dest, sems, first):
    rows, cols = dest.shape[0] // PIECES, dest.shape[1]
    copies = []
    for ref, base in ins:
        for part in range(ref.shape[0] // rows):
            place = pl.multiple_of(meta[at + len(copies)] * rows, rows)
            source = ref.at[pl.ds(part * rows, rows), pl.ds(base + start, cols)]
            copies.append(begin(source, dest.at[pl.ds(place, rows), :], sems.at[first + len(copies)]))
    return copies


def row_valid(meta, core, window, rows, width):
    place = lax.broadcasted_iota(jnp.int32, (rows, width), 0)
    row, col = place // SIDE, place % SIDE
    inside = (row < WIN) & (col < WIN)
    return inside & (core * WIN + row < meta[65 + window]) & (col < meta[67 + window])


def relative(turned):
    out = []
    for row in range(WIN):
        slab = turned[row * SIDE : (row + 1) * SIDE]
        down = pltpu.roll(slab, row, 1) if row else slab
        across = pltpu.roll(slab, 0, 1, stride=1, stride_axis=0)
        out.append(jnp.where(lanes(SIDE) % 64 < 32, down, across))
    return jnp.concatenate(out, axis=0)


def columns_of(mat, width, start=0, size=None):
    return mat // 2, pl.ds(mat % 2 * (width + LANES) + start, width if size is None else size)


def attend_kernel(count, total, meta, tok, table, spread, *refs):
    own, other = refs[:count], refs[count:total]
    vecs, n1, q, k, v, p, att, w_out, x1, n2 = refs[total : total + 10]
    toks, weights, aug, n1s, qs, ks, vs, ps, atts, x1s, n2s, sems, out_sems = refs[total + 10 :]
    width = toks.shape[-1]
    core = meta[64]
    copies = [begin(tok, toks, sems.at[2 * PIECES])]
    for found, at, half in ((own, 0, core), (other, 16, 1 - core)):
        found = [(ref, 0) for ref in found]
        copies += pieces_in(meta, at, found, 0, weights.at[half], sems, at)
    for window in range(2):
        valid = row_valid(meta, core, window, KEYS, LANES)
        aug[window] = jnp.where(
            (lanes(KEYS) == MASK_LANE) & ~valid, MASKED_SCORE, spread[...].astype(F32)
        ).astype(BF16)
        ks[window, TOK:] = jnp.zeros((KEYS - TOK, width), BF16)
        vs[window, TOK:] = jnp.zeros((KEYS - TOK, width), BF16)
    copies[0].wait()
    tokens = toks[...].reshape(2 * TOK, width).astype(F32)
    xhat, _ = moments(tokens)
    finish(copies[1:])
    outs = [begin(weights, w_out, out_sems.at[0])]
    vecs[...] = weights[0, :, width : width + LANES].astype(F32).T[:8]
    normed = (xhat * vecs[0:1] + vecs[1:2]).astype(BF16)
    n1s[...] = normed.reshape(2, TOK, width)
    outs.append(begin(n1s, n1, out_sems.at[1]))
    for mat, (made_in, dest) in enumerate(((qs, q), (ks, k), (vs, v))):
        for start in range(0, width, 256):
            cols = pl.ds(start, 256)
            half, here = columns_of(mat, width, start, 256)
            made = dot(normed, weights[half, :, here])
            if mat != 1:
                made = made + vecs[2 + mat // 2 : 3 + mat // 2, cols]
            made = made.astype(BF16)
            made_in[0, :TOK, cols] = made[:TOK]
            made_in[1, :TOK, cols] = made[TOK:]
        outs.append(begin(made_in, dest, out_sems.at[2 + mat]))

    place = lanes(TOK)
    for step in range(2 * PAIRS):
        window, pair = step // PAIRS, step % PAIRS
        cols = pl.ds(pair * LANES, LANES)
        q2, k2, v2 = qs[window, :, cols], ks[window, :, cols], vs[window, :, cols]
        turned = dot(q2, table[...])
        keys_aug = jnp.concatenate([k2, aug[window]], axis=1)
        parts = []
        for half in range(2):
            rel = relative(turned[:, half * LANES : (half + 1) * LANES])
            high = rel.astype(BF16).astype(F32)
            rel = jnp.where(place < 64, high, rel - high)
            rel = jnp.where(place == MASK_LANE, 1.0, rel).astype(BF16)
            mine = jnp.where(place // 64 == half, q2.astype(F32) * HDIM**-0.5, 0.0).astype(BF16)
            scores = dot_nt(jnp.concatenate([mine, rel], axis=1), keys_aug)
            terms = jnp.exp(scores - jnp.max(scores, axis=-1, keepdims=True))
            soft = terms * (1.0 / jnp.sum(terms, axis=-1, keepdims=True))
            soft = soft.astype(BF16)
            ps[window, 2 * pair + half] = soft
            parts.append(dot(soft, v2))
        atts[window, :, cols] = jnp.where(place < 64, parts[0], parts[1]).astype(BF16)
        heads = pl.ds(2 * pair, 2)
        outs.append(begin(ps.at[window, heads], p.at[window, heads], out_sems.at[len(outs)]))
    outs.append(begin(atts, att, out_sems.at[len(outs)]))
    half, here = columns_of(3, width)
    for window in range(2):
        resid = toks[window].astype(F32) + (dot(atts[window], weights[half, :, here]) + vecs[4:5])
        x1s[window] = resid
        xhat, _ = moments(resid)
        n2s[window] = (xhat * vecs[5:6] + vecs[6:7]).astype(BF16)
        outs.append(begin(x1s.at[window], x1.at[window], out_sems.at[len(outs)]))
        outs.append(begin(n2s.at[window], n2.at[window], out_sems.at[len(outs)]))
    finish(outs)


def attend(meta, tok, table, spread, own, other):
    count, total, width = len(own), len(own) + len(other), tok.shape[-1]
    rows, keys, heads = (2, TOK, width), (2, KEYS, width), (2, HEADS, TOK, KEYS)
    halves = (2, width, 2 * width + LANES)
    outs = [shape(dims, BF16) for dims in (rows, rows, keys, keys, heads, rows, halves)]
    outs += [shape(rows, F32), shape(rows, BF16)]
    scratch = (rows, halves, (2, KEYS, LANES), rows, rows, keys, keys, heads, rows)
    return pl.pallas_call(
        partial(attend_kernel, count, total),
        out_shape=[shape((8, width), F32)] + outs,
        in_specs=[SMEM, HBM, WHOLE, WHOLE] + [HBM] * total,
        out_specs=[WHOLE] + [HBM] * len(outs),
        scratch_shapes=[pltpu.VMEM(dims, BF16) for dims in scratch]
        + [
            pltpu.VMEM(rows, F32),
            pltpu.VMEM(rows, BF16),
            pltpu.SemaphoreType.DMA((2 * PIECES + 1,)),
            pltpu.SemaphoreType.DMA((10 + 2 * PAIRS,)),
        ],
        compiler_params=params(),
        cost_estimate=COST,
        name="attend",
    )(meta, tok, table, spread, *own, *other)


def pieces_out(meta, made, cols, keep, send, sems, first):
    rows = made.shape[0] // PIECES
    copies = []
    for piece in range(PIECES):
        dest = keep if piece < PIECES // 2 else send
        place = pl.multiple_of(meta[32 + piece] * rows, rows)
        at = pl.ds(piece % (PIECES // 2) * rows, rows)
        source = made.at[pl.ds(place, rows), cols]
        copies.append(begin(source, dest.at[at, cols], sems.at[first + len(copies)]))
    return copies


def hidden_fwd_kernel(bases, meta, n2a, n2b, dma, dmb, bias, *refs):
    count = len(bases)
    ins, (keep, send) = list(zip(refs[:count], bases)), refs[count : count + 2]
    w0, n2s, dms, grad, sems, out_sems = refs[count + 2 :]
    width, hidden = w0.shape
    at = PIECES
    copies = [begin(n2a, n2s.at[: 2 * TOK], sems.at[at]), begin(n2b, n2s.at[2 * TOK :], sems.at[at + 1])]
    copies += pieces_in(meta, 0, ins, 0, w0, sems, 0)
    dm_copies = [
        begin(dma, dms.at[: 2 * TOK], sems.at[at + 2]),
        begin(dmb, dms.at[2 * TOK :], sems.at[at + 3]),
    ]
    finish(copies)
    outs = []
    for start in range(0, hidden, CHUNK):
        cols = pl.ds(start, CHUNK)
        inner = dot(n2s[...], w0[:, cols]) + bias[:, cols]
        act = (inner * (0.5 + 0.5 * lax.erf(inner * 0.7071067811865476))).astype(BF16)
        if start == 0:
            finish(dm_copies)
        grad[:, cols] = dot_tn(dms[...], act).astype(BF16)
        if start + CHUNK == hidden - CHUNK:
            outs += pieces_out(meta, grad, pl.ds(0, hidden - CHUNK), keep, send, out_sems, 0)
    outs += pieces_out(meta, grad, pl.ds(hidden - CHUNK, CHUNK), keep, send, out_sems, PIECES)
    finish(outs)


def hidden_fwd(meta, n2a, n2b, dma, dmb, bias, ins):
    refs, bases = zip(*ins)
    width, hidden = n2a.shape[-1], bias.shape[-1]
    return pl.pallas_call(
        partial(hidden_fwd_kernel, bases),
        out_shape=[shape((width // 2, hidden), BF16)] * 2,
        in_specs=[SMEM] + [HBM] * 4 + [WHOLE] + [HBM] * len(refs),
        out_specs=[HBM] * 2,
        scratch_shapes=[
            pltpu.VMEM((width, hidden), BF16),
            pltpu.VMEM((4 * TOK, width), BF16),
            pltpu.VMEM((4 * TOK, width), BF16),
            pltpu.VMEM((width, hidden), BF16),
            pltpu.SemaphoreType.DMA((PIECES + 4,)),
            pltpu.SemaphoreType.DMA((2 * PIECES,)),
        ],
        compiler_params=params(),
        cost_estimate=COST,
        name="hidden_fwd",
    )(meta, n2a, n2b, dma, dmb, bias, *refs)


def hidden_back_kernel(bases0, bases1, meta, n2a, n2b, dma, dmb, bias, *refs):
    count = len(bases0)
    ins0, ins1 = list(zip(refs[:count], bases0)), list(zip(refs[count : 2 * count], bases1))
    refs = refs[2 * count :]
    bias_grad, keep, send, back_own, back_far, out_own, out_far = refs[:7]
    w0, w1, n2s, dms, acts, backs, grad, big, small, sems, out_sems = refs[7:]
    width, hidden = w0.shape
    halves = (pl.ds(0, 2 * TOK), pl.ds(2 * TOK, 2 * TOK))
    at = 2 * PIECES
    copies = [begin(ref, n2s.at[half], sems.at[at + i]) for i, (ref, half) in enumerate(zip((n2a, n2b), halves))]
    copies += pieces_in(meta, 0, ins0, 0, w0, sems, 0)
    at += 2
    later = [begin(ref, dms.at[half], sems.at[at + i]) for i, (ref, half) in enumerate(zip((dma, dmb), halves))]
    later += pieces_in(meta, 0, ins1, 0, w1, sems, PIECES)
    finish(copies)
    outs = []
    for start in range(0, hidden, CHUNK):
        cols = pl.ds(start, CHUNK)
        inner = dot(n2s[...], w0[:, cols]) + bias[:, cols]
        if start == 0:
            finish(later)
        back = dot(dms[...], w1[:, cols])
        cdf = 0.5 + 0.5 * lax.erf(inner * 0.7071067811865476)
        density = jnp.exp(inner * inner * -0.5) * 0.3989422804014327
        acts[:, cols] = (inner * cdf).astype(BF16)
        back_pre = (back * (cdf + inner * density)).astype(BF16)
        backs[:, cols] = back_pre
        bias_grad[:, cols] = jnp.sum(back_pre.astype(F32), axis=0, keepdims=True)
        grad[:, cols] = dot_tn(n2s[...], back_pre).astype(BF16)
    outs = pieces_out(meta, grad, pl.ds(0, hidden), keep, send, out_sems, 0)
    for which, (left, right, own, far) in enumerate(
        ((backs, w0, back_own, back_far), (acts, w1, out_own, out_far))
    ):
        small[which] = dot_nt(left[halves[1]], right[...]).astype(BF16)
        outs.append(begin(small.at[which], far, out_sems.at[len(outs)]))
        big[which] = dot_nt(left[halves[0]], right[...])
        outs.append(begin(big.at[which], own, out_sems.at[len(outs)]))
    finish(outs)


def hidden_back(meta, n2a, n2b, dma, dmb, bias, ins0, ins1):
    (refs0, bases0), (refs1, bases1) = zip(*ins0), zip(*ins1)
    width, hidden = n2a.shape[-1], bias.shape[-1]
    one = (2 * TOK, width)
    tall = pltpu.VMEM((4 * TOK, width), BF16)
    wide = pltpu.VMEM((width, hidden), BF16)
    return pl.pallas_call(
        partial(hidden_back_kernel, bases0, bases1),
        out_shape=[shape((1, hidden), F32)]
        + [shape((width // 2, hidden), BF16)] * 2
        + [shape(one, F32), shape(one, BF16)] * 2,
        in_specs=[SMEM] + [HBM] * 4 + [WHOLE] + [HBM] * (2 * len(refs0)),
        out_specs=[WHOLE] + [HBM] * 6,
        scratch_shapes=[
            wide,
            wide,
            tall,
            tall,
            pltpu.VMEM((4 * TOK, hidden), BF16),
            pltpu.VMEM((4 * TOK, hidden), BF16),
            wide,
            pltpu.VMEM((2,) + one, F32),
            pltpu.VMEM((2,) + one, BF16),
            pltpu.SemaphoreType.DMA((2 * PIECES + 4,)),
            pltpu.SemaphoreType.DMA((PIECES + 4,)),
        ],
        compiler_params=params(),
        cost_estimate=COST,
        name="hidden_back",
    )(meta, n2a, n2b, dma, dmb, bias, *refs0, *refs1)


def unrelative(grads):
    out = []
    for row in range(WIN):
        slab = grads[row * SIDE : (row + 1) * SIDE]
        down = pltpu.roll(slab, row, 1) if row else slab
        across = pltpu.roll(slab, 0, 1, stride=1, stride_axis=0)
        out.append(jnp.where(lanes(SIDE) < 32, down, across))
    return jnp.concatenate(out, axis=0)


def attend_back_kernel(before, count, meta, vecs, gather, table, q, k, v, p, weights, att, n1, *refs):
    start, parts = sum(before), len(before)
    first, last = start == 0, start + count == PAIRS
    if first:
        back_own, back_far, x1, dm = refs[:4]
        norm_sums, bias_sums, table_grad, mine, theirs, dqkv_out, dx1, da = refs[4:12]
        refs = refs[12:]
        owns, fars, x1s, dms, dx1s = refs[-5:]
        refs = refs[:-5]
    else:
        da, refs = refs[0], refs[1:]
        if last:
            tok, dx1, *changes = refs[: 2 + parts]
            norm_sums, bias_sums, table_grad, mine, theirs, result = refs[2 + parts : 8 + parts]
            refs = refs[8 + parts :]
            wqkv, toks, dx1s, results, *changed = refs[-4 - parts :]
            refs = refs[: -4 - parts]
        else:
            bias_sums, table_grad, mine, theirs, dqkv_out = refs[:5]
            refs = refs[5:]
    das, wproj, atts, n1s, qs, ks, vs, ps, dat, dqkv, grads, sems, out_sems = refs
    core = meta[64]
    width, cols_here = das.shape[-1], qs.shape[-1]
    rows = width // PIECES
    columns = pl.ds(start * LANES, cols_here)
    tokens = (2 * TOK, width)
    early = []
    if first:
        early = [(back_own, owns), (back_far, fars), (x1, x1s), (dm, dms)]
    else:
        early = [(da, das)]
    early = [begin(ref, dest, sems.at[at]) for at, (ref, dest) in enumerate(early)]
    half, here = columns_of(3, width)
    wait_proj = begin(weights.at[half, columns, here], wproj, sems.at[4])
    wait_att = begin(att, atts, sems.at[5])
    wait_v = begin(v.at[:, :, columns], vs, sems.at[6])
    wait_p = []
    for window in range(2):
        for pair in range(count):
            heads = pl.ds(2 * (start + pair), 2)
            wait_p.append(
                begin(p.at[window, heads], ps.at[window, pl.ds(2 * pair, 2)], sems.at[10 + len(wait_p)])
            )
        if window == 0:
            wait_qk = [
                begin(ref.at[:, :, columns], dest, sems.at[7 + at])
                for at, (ref, dest) in enumerate(((q, qs), (k, ks)))
            ]
    wait_n1 = begin(n1, n1s, sems.at[9])
    if last:
        at = 10 + 2 * count
        ends = [begin(tok, toks, sems.at[at]), begin(dx1, dx1s, sems.at[at + 1])]
        for mat in range(3):
            half, here = columns_of(mat, width)
            ends.append(begin(weights.at[half, :, here], wqkv.at[mat], sems.at[at + 2 + mat]))
        for part in range(parts):
            ends.append(begin(changes[part], changed[part], sems.at[at + 5 + part]))
    outs = []
    finish(early)
    if first:
        total = [jnp.zeros((1, width), F32) for _ in range(4)]
        for window in range(2):
            here = pl.ds(window * TOK, TOK)
            grad = owns[here] + fars[here].astype(F32)
            xhat, inverse = moments(x1s[window])
            out_grad = dms[window].astype(F32)
            dresid = out_grad + norm_back(grad, xhat, inverse, vecs[5:6])
            dx1s[window] = dresid
            rounded = dresid.astype(BF16)
            das[window] = rounded
            for slot, value in enumerate((rounded.astype(F32), grad * xhat, grad, out_grad)):
                total[slot] = total[slot] + jnp.sum(value, axis=0, keepdims=True)
        norm_sums[...] = jnp.concatenate(total, axis=0)
        outs.append(begin(dx1s, dx1, out_sems.at[2 * PIECES]))
        outs.append(begin(das, da, out_sems.at[2 * PIECES + 1]))
    wait_proj.wait()
    dat[...] = dot_nt(das[...].reshape(tokens), wproj[...]).astype(BF16).reshape(2, TOK, cols_here)

    def send(half):
        is_own = core == half
        at = jnp.where(is_own, 32, 48)
        for piece in range(PIECES):
            place = pl.multiple_of(meta[at + piece] * rows, rows)
            source, to = grads.at[half, pl.ds(place, rows), :], pl.ds(piece * rows, rows)
            sem = out_sems.at[half * PIECES + piece]
            copies = [pltpu.make_async_copy(source, ref.at[to, :], sem) for ref in (mine, theirs)]
            pl.when(is_own)(copies[0].start)
            pl.when(~is_own)(copies[1].start)
            outs.append(copies[0])

    wait_att.wait()
    made = dot_tn(atts[...].reshape(tokens), das[:, :, columns].reshape(2 * TOK, cols_here))
    grads[1, :, cols_here:] = made.astype(BF16)
    finish(wait_qk + [wait_v])
    place = lanes(TOK)
    table_sum = jnp.zeros((LANES, LANES), F32)
    for step in range(2 * count):
        window, pair = step // count, step % count
        cols = pl.ds(pair * LANES, LANES)
        q2, k2, v2, dat2 = (ref[window, :, cols] for ref in (qs, ks, vs, dat))
        q8 = (q2.astype(F32) * HDIM**-0.5).astype(BF16)
        k8 = (k2.astype(F32) * HDIM**-0.5).astype(BF16)
        wait_p[step].wait()
        dqs, dks, dvs, dts = [], [], [], []
        for half in range(2):
            soft = ps[window, 2 * pair + half]
            soft32 = soft.astype(F32)
            own_lanes = jnp.where(place // 64 == half, dat2.astype(F32), 0.0).astype(BF16)
            weighted = soft32 * dot_nt(own_lanes, v2)
            ds = (weighted - soft32 * jnp.sum(weighted, axis=-1, keepdims=True)).astype(BF16)
            turned = dot(ds, gather[...]).astype(BF16).astype(F32)
            turned = unrelative(turned).astype(BF16)
            dqs.append(dot(ds, k8) + dot(turned, table[half]))
            dks.append(dot_tn(ds, q8))
            dvs.append(dot_tn(soft, dat2))
            dts.append(dot_tn(turned, q2))
        dqkv[0, window, :, cols] = jnp.where(place < 64, dqs[0], dqs[1]).astype(BF16)
        dqkv[1, window, :, cols] = jnp.where(place < 64, dks[0][:TOK], dks[1][:TOK]).astype(BF16)
        dqkv[2, window, :, cols] = jnp.where(place < 64, dvs[0][:TOK], dvs[1][:TOK]).astype(BF16)
        table_sum = table_sum + jnp.where(lanes(LANES) < 64, dts[0], dts[1])
    table_grad[...] = table_sum
    if not last:
        outs.append(begin(dqkv, dqkv_out, out_sems.at[2 * PIECES + 2]))
    wait_n1.wait()
    for mat in (2, 0, 1):
        change = dqkv[mat].reshape(2 * TOK, cols_here)
        made = dot_tn(n1s[...].reshape(tokens), change)
        grads[mat // 2, :, pl.ds(mat % 2 * cols_here, cols_here)] = made.astype(BF16)
        if mat != 0:
            send(mat // 2)
        if mat != 1:
            bias_sums[mat // 2 : mat // 2 + 1] = jnp.sum(change.astype(F32), axis=0, keepdims=True)
    if last:
        finish(ends)
        total = [jnp.zeros((1, width), F32) for _ in range(2)]
        for window in range(2):
            grad = jnp.zeros((TOK, width), F32)
            at = 0
            for change in (*changed, dqkv):
                here = pl.ds(at, change.shape[-1])
                for mat in range(3):
                    grad = grad + dot_nt(change[mat, window], wqkv[mat, :, here])
                at += change.shape[-1]
            xhat, inverse = moments(toks[window].astype(F32))
            results[window] = dx1s[window] + norm_back(grad, xhat, inverse, vecs[0:1])
            outs.append(begin(results.at[window], result.at[window], out_sems.at[2 * PIECES + window]))
            for slot, value in enumerate((grad * xhat, grad)):
                total[slot] = total[slot] + jnp.sum(value, axis=0, keepdims=True)
        norm_sums[...] = jnp.concatenate(total, axis=0)
    finish(outs)


def attend_back(before, count, meta, vecs, gather, table, q, k, v, p, weights, att, n1, ins):
    width, cols_here = q.shape[-1], count * LANES
    start, parts = sum(before), len(before)
    first, last = start == 0, start + count == PAIRS
    rows, keys = (2, TOK, width), (2, KEYS, cols_here)
    part, flat = (2, TOK, cols_here), (2 * TOK, width)
    heads = (2, 2 * count, TOK, KEYS)
    small = [shape((2, cols_here), F32), shape((LANES, LANES), F32)]
    large = [shape((width, 2 * cols_here), BF16)] * 2
    large.append(shape(rows, F32) if last else shape((3,) + part, BF16))
    if last:
        small = [shape((2, width), F32)] + small
    if first:
        small = [shape((4, width), F32)] + small
        large += [shape(rows, F32), shape(rows, BF16)]
    scratch = [rows, (cols_here, width), rows, rows, part, keys, keys, heads, part, (3,) + part]
    scratch.append((2, width, 2 * cols_here))
    scratch = [pltpu.VMEM(dims, BF16) for dims in scratch]
    scratch += [pltpu.SemaphoreType.DMA((15 + 2 * count + parts,)), pltpu.SemaphoreType.DMA((2 * PIECES + 3,))]
    if first:
        scratch += [
            pltpu.VMEM(flat, F32),
            pltpu.VMEM(flat, BF16),
            pltpu.VMEM(rows, F32),
            pltpu.VMEM(rows, BF16),
            pltpu.VMEM(rows, F32),
        ]
    if last:
        scratch += [
            pltpu.VMEM((3, width, width), BF16),
            pltpu.VMEM(rows, BF16),
            pltpu.VMEM(rows, F32),
            pltpu.VMEM(rows, F32),
        ] + [pltpu.VMEM((3, 2, TOK, size * LANES), BF16) for size in before]
    return pl.pallas_call(
        partial(attend_back_kernel, before, count),
        out_shape=small + large,
        in_specs=[SMEM] + [WHOLE] * 3 + [HBM] * (7 + len(ins)),
        out_specs=[WHOLE] * len(small) + [HBM] * len(large),
        scratch_shapes=scratch,
        compiler_params=params(),
        cost_estimate=COST,
        name="attend_back",
    )(meta, vecs, gather, table, q, k, v, p, weights, att, n1, *ins)


def grid_of(count):
    return (4, 2, 2) if count == 16 else None


def turn(values, dims, moves):
    pairs = []
    for chip in range(dims[0] * dims[1] * dims[2]):
        for core, (axis, by) in enumerate(moves):
            place = list(np.unravel_index(chip, dims))
            place[axis] = (place[axis] + by) % dims[axis]
            pairs.append((2 * chip + core, 2 * int(np.ravel_multi_index(place, dims)) + core))
    return lax.ppermute(values, ("dp", "mp"), pairs)


ALONG_X, ALONG_Y = ((2, 1),) * 2, ((1, 1),) * 2
FIRST, SECOND = ((2, 1), (1, 1)), ((1, 1), (2, 1))


def along_z(values, dims):
    return [turn(values, dims, ((0, step),) * 2) for step in range(1, dims[0])]


def swap_z(values, dims, by):
    chips = dims[1] * dims[2]
    pairs = [(chip, (chip // chips ^ by) * chips + chip % chips) for chip in range(dims[0] * chips)]
    return lax.ppermute(values, "dp", pairs)


def other_core(values):
    return lax.ppermute(values, "mp", [(0, 1), (1, 0)])


def after(values, *others):
    return lax.optimization_barrier((values, *others))[0]


class Flow:
    def __init__(self, *came):
        self.came = list(came)


def meet(flows, *values):
    sizes = [len(flow.came) for flow in flows]
    found = list(lax.optimization_barrier((*(part for flow in flows for part in flow.came), *values)))
    for flow, size in zip(flows, sizes):
        flow.came, found = found[:size], found[size:]
    return found


def place_orders(dims, core):
    here = lax.axis_index("dp")
    z, y, x = here // (dims[1] * dims[2]), here // dims[2] % dims[1], here % dims[2]

    def chip(step, inner, outer):
        by_x = jnp.where(core == 0, inner, outer)
        by_y = jnp.where(core == 0, outer, inner)
        return ((z - step) % dims[0] * dims[1] + (y + by_y) % 2) * dims[2] + (x + by_x) % 2

    square = [(inner, outer) for outer in range(2) for inner in range(2)]
    gather = [chip(0, *at) for at in square]
    gather += [chip(step, *at) for at in square for step in range(1, dims[0])]
    scatter = [chip(step, *at) for at in square for step in range(dims[0])]
    return [jnp.stack(found).astype(jnp.int32) for found in (gather, scatter)]


def add(a, b):
    return a.astype(F32) + b.astype(F32)


class Scatter(Flow):
    def __init__(self, keep, far, dims):
        super().__init__(turn(far, dims, SECOND))
        self.keep, self.dims = keep, dims

    def second(self):
        half = self.keep.shape[0] // 2
        send = add(self.keep[half:], self.came[0][half:]).astype(BF16)
        self.near = add(self.keep[:half], self.came[0][:half])
        self.sent = send
        self.came = [turn(send, self.dims, FIRST)]

    def third(self):
        near = self.near + self.came[0].astype(F32)
        rows = near.shape[0] // self.dims[0]
        self.near = near[:rows]
        self.came = [
            turn(near[step * rows : (step + 1) * rows].astype(BF16), self.dims, ((0, self.dims[0] - step),) * 2)
            for step in range(1, self.dims[0])
        ]

    def halve(self):
        near = self.near + self.came[0].astype(F32)
        rows = near.shape[0] // self.dims[0]
        parts = [near[step * rows : (step + 1) * rows] for step in range(self.dims[0])]
        even = lax.axis_index("dp") // (self.dims[1] * self.dims[2]) % 2 == 0
        self.near = parts[0]
        self.beside = jnp.where(even, parts[3], parts[1])
        send = jnp.concatenate([parts[2], jnp.where(even, parts[1], parts[3])], axis=0).astype(BF16)
        self.came = [swap_z(send, self.dims, 2)]

    def quarter(self):
        rows = self.near.shape[0]
        came = self.came[0]
        self.near = self.near + came[:rows].astype(F32)
        self.came = [swap_z((self.beside + came[rows:].astype(F32)).astype(BF16), self.dims, 1)]

    def last(self):
        return sum((part.astype(F32) for part in self.came), self.near)


def constants():
    key = np.arange(KEYS)
    row, col = key // SIDE, key % SIDE
    inside = (row < WIN) & (col < WIN)
    spread = np.zeros((KEYS, LANES), np.float32)
    gather = np.zeros((KEYS, LANES), np.float32)
    for place in key[inside]:
        for base in (0, 64):
            spread[place, base + WIN - 1 + row[place]] = 1.0
            spread[place, base + 32 + WIN - 1 + col[place]] = 1.0
        gather[place, WIN - 1 - row[place]] = 1.0
        gather[place, 32 + WIN - 1 - col[place]] = 1.0
    return spread, gather


def tables(rel_pos_h, rel_pos_w):
    count = rel_pos_h.shape[0]
    gap = jnp.zeros((32 - count, HDIM), BF16)
    turned = jnp.concatenate([rel_pos_h[::-1], gap, rel_pos_w[::-1], gap], axis=0)
    turned = jnp.concatenate([turned, turned], axis=0).T
    none = jnp.zeros_like(turned)
    forward = jnp.concatenate(
        [jnp.concatenate([turned, none], axis=0), jnp.concatenate([none, turned], axis=0)], axis=1
    )
    straight = jnp.concatenate([rel_pos_h, gap, rel_pos_w, gap], axis=0)
    straight = jnp.concatenate([straight, jnp.zeros_like(straight)], axis=0)
    none = jnp.zeros_like(straight)
    backward = jnp.stack(
        [
            jnp.concatenate([straight, none], axis=1),
            jnp.concatenate([none, straight], axis=1),
        ]
    )
    return forward, backward


def padded(values):
    images, rows, _, width = values.shape
    values = jnp.pad(values, ((0, 0), (0, 0), (0, SIDE - WIN), (0, 0)))
    return values.reshape(images, rows * SIDE, width)


def unpadded(values):
    images, _, width = values.shape
    return values.reshape(images, WIN, SIDE, width)[:, :, :WIN]


def local(
    patches,
    norm1_gain,
    norm1_bias,
    qkv_weight,
    qv_bias,
    rel_pos_h,
    rel_pos_w,
    proj_weight,
    proj_bias,
    norm2_gain,
    norm2_bias,
    fc1_weight,
    fc1_bias,
    fc2_weight,
    fc2_bias,
    heights,
    widths,
    out_grad,
):
    width = patches.shape[-1]
    dims = grid_of(lax.axis_size("dp"))
    core = lax.axis_index("mp")
    is_first = core == 0
    if dims is None:
        orders = [jnp.tile(jnp.arange(PIECES, dtype=jnp.int32), 4)]
    else:
        own, far = place_orders(dims, core), place_orders(dims, 1 - core)
        orders = [own[0], far[0], own[1], far[1]]
    meta = jnp.concatenate(
        orders + [core.astype(jnp.int32)[None], heights, widths, jnp.zeros((11,), jnp.int32)]
    )

    tok = padded(patches)
    row_index = core * WIN + jnp.arange(WIN)
    valid = (row_index[None, :, None] < heights[:, None, None]) & (
        jnp.arange(WIN)[None, None, :] < widths[:, None, None]
    )
    dm = padded(jnp.where(valid[..., None], out_grad, jnp.zeros_like(out_grad)))
    vectors = (norm1_gain, norm1_bias, qv_bias[0], qv_bias[1], proj_bias, norm2_gain, norm2_bias, fc2_bias)
    small = jnp.pad(jnp.stack(vectors, axis=1), ((0, 0), (0, LANES - len(vectors))))
    qk = jnp.concatenate([qkv_weight[:, :width], small, qkv_weight[:, width : 2 * width]], axis=1)
    vp = jnp.concatenate([qkv_weight[:, 2 * width :], small, proj_weight], axis=1)
    if dims is None:
        qk = lax.all_gather(qk, ("dp", "mp"), axis=0, tiled=True)
        vp = lax.all_gather(vp, ("dp", "mp"), axis=0, tiled=True)
        attend_own = [jnp.where(is_first, qk, vp)]
        attend_far = [jnp.where(is_first, vp, qk)]
        dm_far = other_core(dm)
        hidden_in = tuple(
            ((lax.all_gather(part, "dp", axis=0, tiled=True), 0),) for part in (fc1_weight, fc2_weight.T)
        )
    else:
        fc1, fc2 = fc1_weight, fc2_weight.T
        came = other_core(jnp.where(is_first, vp, qk))
        own_h = jnp.concatenate([fc1, fc2], axis=1)
        beside_h = turn(own_h, dims, FIRST)
        near = jnp.where(is_first, qk, vp)
        block = jnp.concatenate(
            [jnp.where(is_first, near, came), jnp.where(is_first, came, near)], axis=0
        )
        attend_z = along_z(block, dims)
        beside = turn(block, dims, FIRST)
        own_h = jnp.concatenate([own_h, beside_h], axis=0)
        over_h = turn(own_h, dims, SECOND)
        own = jnp.concatenate([block, after(beside, own_h)], axis=0)
        over = turn(own, dims, SECOND)
        attend_z = jnp.concatenate([after(attend_z[0], own)] + attend_z[1:], axis=0)
        z_beside = turn(attend_z, dims, FIRST)
        fc1_z = along_z(after(fc1, attend_z), dims)
        over, over_h, z_beside = meet([], over, over_h, z_beside)
        own = jnp.concatenate([own, over], axis=0)
        far = [other_core(own)]
        attend_z = jnp.concatenate([attend_z, z_beside], axis=0)
        z_over = turn(attend_z, dims, SECOND)
        fc1_z = jnp.concatenate([after(fc1_z[0], attend_z)] + fc1_z[1:], axis=0)
        fc1_beside = turn(fc1_z, dims, FIRST)
        fc2_z = along_z(after(fc2, fc1_z), dims)
        far.append(other_core(after(attend_z, fc1_z)))
        z_over = after(z_over, fc1_z)
        far.append(other_core(z_over))
        fc1_z = jnp.concatenate([fc1_z, after(fc1_beside, z_over)], axis=0)
        fc1_over = turn(fc1_z, dims, SECOND)
        attend_own, attend_far = [own, attend_z, z_over], far
        dm_far = other_core(after(dm, z_over))
        tok = after(tok, fc1_z)

    dm_flat, dm_far = dm.reshape(-1, width), dm_far.reshape(-1, width)
    spread, gather = constants()
    table, table_back = tables(rel_pos_h, rel_pos_w)

    vecs, n1, q, k, v, p, att, weights, x1, n2 = attend(
        meta, tok, table, jnp.asarray(spread, BF16), attend_own, attend_far
    )
    if dims is not None:
        fc2_z = jnp.concatenate([after(fc2_z[0], n2)] + fc2_z[1:], axis=0)
        fc2_beside = turn(fc2_z, dims, FIRST)
    n2_far = other_core(n2).reshape(-1, width)
    n2 = n2.reshape(-1, width)
    bias = fc1_bias[None].astype(F32)
    if dims is not None:
        fc2_z = jnp.concatenate([fc2_z, after(fc2_beside, n2)], axis=0)
        fc2_over = turn(fc2_z, dims, SECOND)
        n2 = after(n2, fc2_z)
        size = fc1.shape[1]
        hidden_in = [
            ((own_h, 0), (over_h, 0), (fc1_z, 0), (fc1_over, 0)),
            ((own_h, size), (over_h, size), (fc2_z, 0), (fc2_over, 0)),
        ]
    fc2_part = hidden_fwd(meta, n2, n2_far, dm_flat, dm_far, bias, hidden_in[0])
    if dims is not None:
        fc2_part = meet([], *fc2_part, fc2_over)[:2]
        fc2_sum = Scatter(*fc2_part, dims)
    fc1_bias_part, *fc1_part, back_own, back_far, out_own, out_far = hidden_back(
        meta, n2, n2_far, dm_flat, dm_far, bias, *hidden_in
    )
    back_far = other_core(back_far)
    if dims is not None:
        fc1_part = meet([fc2_sum], *fc1_part)
        fc2_sum.second()
        fc1_sum = Scatter(*fc1_part, dims)
        back_own = after(back_own, fc2_sum.sent)

    shared = (meta, vecs, jnp.asarray(gather, BF16), table_back, q, k, v, p, weights, att, n1)
    bias_sums, table_grad, attend_sums, changes = [], 0.0, [], []
    ins = (back_own, back_far, x1, dm)
    half = width // 2
    for part, count in enumerate(BACK_PARTS):
        last = part == len(BACK_PARTS) - 1
        made = attend_back(BACK_PARTS[:part], count, *shared, ins)
        if part == 0:
            sums2, *made, dx1, da = made
        if last:
            sums1, *made = made
        bias_sums.append(made[0])
        table_grad = table_grad + made[1]
        mine, theirs, change = made[2:]
        changes.append(change)
        if dims is None:
            attend_sums.append(
                lax.psum_scatter(add(mine, other_core(theirs)), "dp", scatter_dimension=0, tiled=True)
            )
        elif not last:
            came = Flow(other_core(theirs))
            da, mine = meet([fc2_sum, fc1_sum], da, mine)
            fc2_sum.third()
            fc1_sum.second()
            both = add(mine, came.came[0]).astype(BF16)
            first = Scatter(both[:half], both[half:], dims)
            da = after(da, both)
        ins = (da, tok, dx1, *changes)
    result = change
    qv_sums = jnp.concatenate(bias_sums, axis=1)
    rel_sums = table_grad[:64, :HDIM] + table_grad[:64, HDIM:]
    fc1_sums = jnp.concatenate(
        [jnp.where(is_first, fc1_bias_part, 0.0), jnp.where(is_first, 0.0, fc1_bias_part)], axis=1
    )
    flat = jnp.concatenate(
        [
            jnp.concatenate([sums1, qv_sums, sums2], axis=0).reshape(-1, LANES),
            rel_sums.reshape(-1, LANES),
            fc1_sums.reshape(-1, LANES),
        ],
        axis=0,
    )
    if dims is None:
        flat = lax.psum(flat + other_core(flat), "dp")
        out_far = other_core(out_far)
        fc1_sum, fc2_sum = (
            lax.psum_scatter(
                jnp.concatenate(parts, axis=0).astype(F32), "dp", scatter_dimension=0, tiled=True
            )
            for parts in (fc1_part, fc2_part)
        )
    else:
        mine, theirs, flat, out_far = meet([fc2_sum, fc1_sum, first], mine, theirs, flat, out_far)
        came, flat_came = Flow(other_core(theirs)), Flow(other_core(flat))
        first.second()
        fc1_sum.halve()
        mine, flat, out_far = meet([came, flat_came, first], mine, flat, out_far)
        both = add(mine, came.came[0]).astype(BF16)
        second = Scatter(both[:half], both[half:], dims)
        flat = flat + flat_came.came[0]
        flat_came = Flow(turn(flat, dims, SECOND))
        first.halve()
        fc2_sum = fc2_sum.last()
        out_far = other_core(out_far)
        flat, result = meet([flat_came, second, fc1_sum], flat, result)
        flat = flat + flat_came.came[0]
        flat_came = Flow(turn(flat, dims, FIRST))
        second.second()
        fc1_sum.quarter()
        flat, out_far = meet([flat_came, first, second, fc1_sum], flat, out_far)
        flat = flat + flat_came.came[0]
        flat_came = Flow(swap_z(flat, dims, 2))
        second.third()
        first.quarter()
        fc1_sum = fc1_sum.last()
        flat, fc1_sum = meet([flat_came, second, first], flat, fc1_sum)
        flat = flat + flat_came.came[0]
        flat = flat + swap_z(flat, dims, 1)
        attend_sums = [first.last(), second.last()]
    branch = add(out_own, out_far).reshape(x1.shape) + vecs[7]
    block_out = unpadded(x1 + branch)
    block_out = jnp.where(valid[..., None], block_out, 0.0).astype(BF16)

    whole = jnp.stack(
        [
            jnp.concatenate([part[:, at * (part.shape[1] // 2) :][:, : part.shape[1] // 2] for part in attend_sums], axis=1)
            for at in range(2)
        ]
    )
    rows = whole.shape[1] // 2
    near = jnp.where(is_first, whole[:, :rows], whole[:, rows:])
    came = other_core(jnp.where(is_first, whole[:, rows:], whole[:, :rows]))
    (q_grad, k_grad), (v_grad, proj_grad) = jnp.where(is_first, near, came), jnp.where(is_first, came, near)
    qkv_grad = jnp.concatenate([q_grad, k_grad, v_grad], axis=1)
    at = 8 * width // LANES
    vec_sums = flat[:at].reshape(8, width)
    rel = flat[at : at + 32].reshape(64, HDIM)
    fc1_bias_grad = lax.dynamic_index_in_dim(flat[at + 32 :].reshape(2, -1), core, 0, keepdims=False)
    share = norm1_gain.shape[0]
    device = lax.axis_index("dp") * 2 + core
    mine = lax.dynamic_slice_in_dim(vec_sums, device * share, share, axis=1)
    rels = rel_pos_h.shape[0]
    return (
        block_out,
        unpadded(result),
        mine[0],
        mine[1],
        qkv_grad,
        mine[2:4],
        rel[:rels],
        rel[32 : 32 + rels],
        proj_grad,
        mine[4],
        mine[5],
        mine[6],
        fc1_sum,
        fc1_bias_grad,
        fc2_sum.T,
        mine[7],
    )


def solution(mesh):
    return jax.shard_map(
        local,
        mesh=mesh,
        in_specs=(
            P("dp", "mp", None, None),
            P(("dp", "mp")),
            P(("dp", "mp")),
            P(("dp", "mp"), None),
            P(None, ("dp", "mp")),
            P(),
            P(),
            P(("dp", "mp"), None),
            P(("dp", "mp")),
            P(("dp", "mp")),
            P(("dp", "mp")),
            P("dp", "mp"),
            P("mp"),
            P("mp", "dp"),
            P(("dp", "mp")),
            P("dp"),
            P("dp"),
            P("dp", "mp", None, None),
        ),
        out_specs=(
            P("dp", "mp", None, None),
            P("dp", "mp", None, None),
            P(("dp", "mp")),
            P(("dp", "mp")),
            P(("dp", "mp"), None),
            P(None, ("dp", "mp")),
            P(),
            P(),
            P(("dp", "mp"), None),
            P(("dp", "mp")),
            P(("dp", "mp")),
            P(("dp", "mp")),
            P("dp", "mp"),
            P("mp"),
            P("mp", "dp"),
            P(("dp", "mp")),
        ),
        check_vma=False,
    )
```

```python
from functools import partial

import jax
import jax.numpy as jnp
import numpy as np
from jax import lax
from jax.experimental import pallas as pl
from jax.experimental.pallas import tpu as pltpu
from jax.sharding import PartitionSpec as P

HEADS = 12
HDIM = 64
LANES = 128
PAIRS = HEADS // 2
WIN = 14
SIDE = 16
TOK = WIN * SIDE
KEYS = 256
PIECES = 16
EPSILON = 1e-06
MASKED_SCORE = -1e30
MASK_LANE = 60
SMALL = 48
CHUNK = 512
BACK_PARTS = (4, 2)
F32 = jnp.float32
BF16 = jnp.bfloat16
SMEM = pl.BlockSpec(memory_space=pltpu.SMEM)
HBM = pl.BlockSpec(memory_space=pl.ANY)
WHOLE = pl.BlockSpec(memory_space=pltpu.VMEM)
VMEM_BYTES = 52 * 2**20
COST = pl.CostEstimate(flops=1000, bytes_accessed=1000, transcendentals=0)


def params():
    return pltpu.CompilerParams(vmem_limit_bytes=VMEM_BYTES)


def shape(dims, dtype):
    return jax.ShapeDtypeStruct(dims, dtype)


def dot(a, b):
    return jnp.dot(a, b, preferred_element_type=F32)


def dot_nt(a, b):
    return lax.dot_general(a, b, (((1,), (1,)), ((), ())), preferred_element_type=F32)


def dot_tn(a, b):
    return lax.dot_general(a, b, (((0,), (0,)), ((), ())), preferred_element_type=F32)


def lanes(rows):
    return lax.broadcasted_iota(jnp.int32, (rows, LANES), 1)


def moments(values):
    centered = values - jnp.mean(values, axis=-1, keepdims=True)
    inverse = lax.rsqrt(jnp.mean(centered * centered, axis=-1, keepdims=True) + EPSILON)
    return centered * inverse, inverse


def norm_back(grad, xhat, inverse, gain):
    scaled = grad * gain
    first = jnp.mean(scaled, axis=-1, keepdims=True)
    second = jnp.mean(scaled * xhat, axis=-1, keepdims=True)
    return inverse * (scaled - first - xhat * second)


def begin(source, dest, sem):
    copy = pltpu.make_async_copy(source, dest, sem)
    copy.start()
    return copy


def finish(copies):
    for copy in copies:
        copy.wait()


def pieces_in(meta, at, ins, start, dest, sems, first):
    rows, cols = dest.shape[0] // PIECES, dest.shape[1]
    copies = []
    for ref, base in ins:
        for part in range(ref.shape[0] // rows):
            place = pl.multiple_of(meta[at + len(copies)] * rows, rows)
            source = ref.at[pl.ds(part * rows, rows), pl.ds(base + start, cols)]
            copies.append(begin(source, dest.at[pl.ds(place, rows), :], sems.at[first + len(copies)]))
    return copies


def row_valid(meta, core, window, rows, width):
    place = lax.broadcasted_iota(jnp.int32, (rows, width), 0)
    row, col = place // SIDE, place % SIDE
    inside = (row < WIN) & (col < WIN)
    return inside & (core * WIN + row < meta[65 + window]) & (col < meta[67 + window])


def relative(turned):
    out = []
    for row in range(WIN):
        slab = turned[row * SIDE : (row + 1) * SIDE]
        down = pltpu.roll(slab, row, 1) if row else slab
        across = pltpu.roll(slab, 0, 1, stride=1, stride_axis=0)
        out.append(jnp.where(lanes(SIDE) % 64 < 32, down, across))
    return jnp.concatenate(out, axis=0)


def columns_of(mat, width, start=0, size=None):
    return mat // 2, pl.ds(mat % 2 * (width + LANES) + start, width if size is None else size)


def attend_kernel(count, total, meta, tok, table, spread, *refs):
    own, other = refs[:count], refs[count:total]
    vecs, n1, q, k, v, p, att, w_out, x1, n2 = refs[total : total + 10]
    toks, weights, aug, n1s, qs, ks, vs, ps, atts, x1s, n2s, sems, out_sems = refs[total + 10 :]
    width = toks.shape[-1]
    core = meta[64]
    copies = [begin(tok, toks, sems.at[2 * PIECES])]
    for found, at, half in ((own, 0, core), (other, 16, 1 - core)):
        found = [(ref, 0) for ref in found]
        copies += pieces_in(meta, at, found, 0, weights.at[half], sems, at)
    for window in range(2):
        valid = row_valid(meta, core, window, KEYS, LANES)
        aug[window] = jnp.where(
            (lanes(KEYS) == MASK_LANE) & ~valid, MASKED_SCORE, spread[...].astype(F32)
        ).astype(BF16)
        ks[window, TOK:] = jnp.zeros((KEYS - TOK, width), BF16)
        vs[window, TOK:] = jnp.zeros((KEYS - TOK, width), BF16)
    copies[0].wait()
    tokens = toks[...].reshape(2 * TOK, width).astype(F32)
    xhat, _ = moments(tokens)
    finish(copies[1:])
    outs = [begin(weights, w_out, out_sems.at[0])]
    vecs[...] = weights[0, :, width : width + LANES].astype(F32).T[:8]
    normed = (xhat * vecs[0:1] + vecs[1:2]).astype(BF16)
    n1s[...] = normed.reshape(2, TOK, width)
    outs.append(begin(n1s, n1, out_sems.at[1]))
    for mat, (made_in, dest) in enumerate(((qs, q), (ks, k), (vs, v))):
        for start in range(0, width, 256):
            cols = pl.ds(start, 256)
            half, here = columns_of(mat, width, start, 256)
            made = dot(normed, weights[half, :, here])
            if mat != 1:
                made = made + vecs[2 + mat // 2 : 3 + mat // 2, cols]
            made = made.astype(BF16)
            made_in[0, :TOK, cols] = made[:TOK]
            made_in[1, :TOK, cols] = made[TOK:]
        outs.append(begin(made_in, dest, out_sems.at[2 + mat]))

    place = lanes(TOK)
    for step in range(2 * PAIRS):
        window, pair = step // PAIRS, step % PAIRS
        cols = pl.ds(pair * LANES, LANES)
        q2, k2, v2 = qs[window, :, cols], ks[window, :, cols], vs[window, :, cols]
        turned = dot(q2, table[...])
        keys_aug = jnp.concatenate([k2, aug[window]], axis=1)
        parts = []
        for half in range(2):
            rel = relative(turned[:, half * LANES : (half + 1) * LANES])
            high = rel.astype(BF16).astype(F32)
            rel = jnp.where(place < 64, high, rel - high)
            rel = jnp.where(place == MASK_LANE, 1.0, rel).astype(BF16)
            mine = jnp.where(place // 64 == half, q2.astype(F32) * HDIM**-0.5, 0.0).astype(BF16)
            scores = dot_nt(jnp.concatenate([mine, rel], axis=1), keys_aug)
            terms = jnp.exp(scores - jnp.max(scores, axis=-1, keepdims=True))
            soft = terms * (1.0 / jnp.sum(terms, axis=-1, keepdims=True))
            soft = soft.astype(BF16)
            ps[window, 2 * pair + half] = soft
            parts.append(dot(soft, v2))
        atts[window, :, cols] = jnp.where(place < 64, parts[0], parts[1]).astype(BF16)
        heads = pl.ds(2 * pair, 2)
        outs.append(begin(ps.at[window, heads], p.at[window, heads], out_sems.at[len(outs)]))
    outs.append(begin(atts, att, out_sems.at[len(outs)]))
    half, here = columns_of(3, width)
    for window in range(2):
        resid = toks[window].astype(F32) + (dot(atts[window], weights[half, :, here]) + vecs[4:5])
        x1s[window] = resid
        xhat, _ = moments(resid)
        n2s[window] = (xhat * vecs[5:6] + vecs[6:7]).astype(BF16)
        outs.append(begin(x1s.at[window], x1.at[window], out_sems.at[len(outs)]))
        outs.append(begin(n2s.at[window], n2.at[window], out_sems.at[len(outs)]))
    finish(outs)


def attend(meta, tok, table, spread, own, other):
    count, total, width = len(own), len(own) + len(other), tok.shape[-1]
    rows, keys, heads = (2, TOK, width), (2, KEYS, width), (2, HEADS, TOK, KEYS)
    halves = (2, width, 2 * width + LANES)
    outs = [shape(dims, BF16) for dims in (rows, rows, keys, keys, heads, rows, halves)]
    outs += [shape(rows, F32), shape(rows, BF16)]
    scratch = (rows, halves, (2, KEYS, LANES), rows, rows, keys, keys, heads, rows)
    return pl.pallas_call(
        partial(attend_kernel, count, total),
        out_shape=[shape((8, width), F32)] + outs,
        in_specs=[SMEM, HBM, WHOLE, WHOLE] + [HBM] * total,
        out_specs=[WHOLE] + [HBM] * len(outs),
        scratch_shapes=[pltpu.VMEM(dims, BF16) for dims in scratch]
        + [
            pltpu.VMEM(rows, F32),
            pltpu.VMEM(rows, BF16),
            pltpu.SemaphoreType.DMA((2 * PIECES + 1,)),
            pltpu.SemaphoreType.DMA((10 + 2 * PAIRS,)),
        ],
        compiler_params=params(),
        cost_estimate=COST,
        name="attend",
    )(meta, tok, table, spread, *own, *other)


def pieces_out(meta, made, cols, keep, send, sems, first):
    rows = made.shape[0] // PIECES
    copies = []
    for piece in range(PIECES):
        dest = keep if piece < PIECES // 2 else send
        place = pl.multiple_of(meta[32 + piece] * rows, rows)
        at = pl.ds(piece % (PIECES // 2) * rows, rows)
        source = made.at[pl.ds(place, rows), cols]
        copies.append(begin(source, dest.at[at, cols], sems.at[first + len(copies)]))
    return copies


def hidden_fwd_kernel(bases, meta, n2a, n2b, dma, dmb, bias, *refs):
    count = len(bases)
    ins, (keep, send) = list(zip(refs[:count], bases)), refs[count : count + 2]
    w0, n2s, dms, grad, sems, out_sems = refs[count + 2 :]
    width, hidden = w0.shape
    at = PIECES
    copies = [begin(n2a, n2s.at[: 2 * TOK], sems.at[at]), begin(n2b, n2s.at[2 * TOK :], sems.at[at + 1])]
    copies += pieces_in(meta, 0, ins, 0, w0, sems, 0)
    dm_copies = [
        begin(dma, dms.at[: 2 * TOK], sems.at[at + 2]),
        begin(dmb, dms.at[2 * TOK :], sems.at[at + 3]),
    ]
    finish(copies)
    outs = []
    for start in range(0, hidden, CHUNK):
        cols = pl.ds(start, CHUNK)
        inner = dot(n2s[...], w0[:, cols]) + bias[:, cols]
        act = (inner * (0.5 + 0.5 * lax.erf(inner * 0.7071067811865476))).astype(BF16)
        if start == 0:
            finish(dm_copies)
        grad[:, cols] = dot_tn(dms[...], act).astype(BF16)
        if start + CHUNK == hidden - CHUNK:
            outs += pieces_out(meta, grad, pl.ds(0, hidden - CHUNK), keep, send, out_sems, 0)
    outs += pieces_out(meta, grad, pl.ds(hidden - CHUNK, CHUNK), keep, send, out_sems, PIECES)
    finish(outs)


def hidden_fwd(meta, n2a, n2b, dma, dmb, bias, ins):
    refs, bases = zip(*ins)
    width, hidden = n2a.shape[-1], bias.shape[-1]
    return pl.pallas_call(
        partial(hidden_fwd_kernel, bases),
        out_shape=[shape((width // 2, hidden), BF16)] * 2,
        in_specs=[SMEM] + [HBM] * 4 + [WHOLE] + [HBM] * len(refs),
        out_specs=[HBM] * 2,
        scratch_shapes=[
            pltpu.VMEM((width, hidden), BF16),
            pltpu.VMEM((4 * TOK, width), BF16),
            pltpu.VMEM((4 * TOK, width), BF16),
            pltpu.VMEM((width, hidden), BF16),
            pltpu.SemaphoreType.DMA((PIECES + 4,)),
            pltpu.SemaphoreType.DMA((2 * PIECES,)),
        ],
        compiler_params=params(),
        cost_estimate=COST,
        name="hidden_fwd",
    )(meta, n2a, n2b, dma, dmb, bias, *refs)


def hidden_back_kernel(bases0, bases1, meta, n2a, n2b, dma, dmb, bias, *refs):
    count = len(bases0)
    ins0, ins1 = list(zip(refs[:count], bases0)), list(zip(refs[count : 2 * count], bases1))
    refs = refs[2 * count :]
    bias_grad, keep, send, back_own, back_far, out_own, out_far = refs[:7]
    w0, w1, n2s, dms, acts, backs, grad, big, small, sems, out_sems = refs[7:]
    width, hidden = w0.shape
    halves = (pl.ds(0, 2 * TOK), pl.ds(2 * TOK, 2 * TOK))
    at = 2 * PIECES
    copies = [begin(ref, n2s.at[half], sems.at[at + i]) for i, (ref, half) in enumerate(zip((n2a, n2b), halves))]
    copies += pieces_in(meta, 0, ins0, 0, w0, sems, 0)
    at += 2
    later = [begin(ref, dms.at[half], sems.at[at + i]) for i, (ref, half) in enumerate(zip((dma, dmb), halves))]
    later += pieces_in(meta, 0, ins1, 0, w1, sems, PIECES)
    finish(copies)
    outs = []
    for start in range(0, hidden, CHUNK):
        cols = pl.ds(start, CHUNK)
        inner = dot(n2s[...], w0[:, cols]) + bias[:, cols]
        if start == 0:
            finish(later)
        back = dot(dms[...], w1[:, cols])
        cdf = 0.5 + 0.5 * lax.erf(inner * 0.7071067811865476)
        density = jnp.exp(inner * inner * -0.5) * 0.3989422804014327
        acts[:, cols] = (inner * cdf).astype(BF16)
        back_pre = (back * (cdf + inner * density)).astype(BF16)
        backs[:, cols] = back_pre
        bias_grad[:, cols] = jnp.sum(back_pre.astype(F32), axis=0, keepdims=True)
        grad[:, cols] = dot_tn(n2s[...], back_pre).astype(BF16)
    outs = pieces_out(meta, grad, pl.ds(0, hidden), keep, send, out_sems, 0)
    for which, (left, right, own, far) in enumerate(
        ((backs, w0, back_own, back_far), (acts, w1, out_own, out_far))
    ):
        small[which] = dot_nt(left[halves[1]], right[...]).astype(BF16)
        outs.append(begin(small.at[which], far, out_sems.at[len(outs)]))
        big[which] = dot_nt(left[halves[0]], right[...])
        outs.append(begin(big.at[which], own, out_sems.at[len(outs)]))
    finish(outs)


def hidden_back(meta, n2a, n2b, dma, dmb, bias, ins0, ins1):
    (refs0, bases0), (refs1, bases1) = zip(*ins0), zip(*ins1)
    width, hidden = n2a.shape[-1], bias.shape[-1]
    one = (2 * TOK, width)
    tall = pltpu.VMEM((4 * TOK, width), BF16)
    wide = pltpu.VMEM((width, hidden), BF16)
    return pl.pallas_call(
        partial(hidden_back_kernel, bases0, bases1),
        out_shape=[shape((1, hidden), F32)]
        + [shape((width // 2, hidden), BF16)] * 2
        + [shape(one, F32), shape(one, BF16)] * 2,
        in_specs=[SMEM] + [HBM] * 4 + [WHOLE] + [HBM] * (2 * len(refs0)),
        out_specs=[WHOLE] + [HBM] * 6,
        scratch_shapes=[
            wide,
            wide,
            tall,
            tall,
            pltpu.VMEM((4 * TOK, hidden), BF16),
            pltpu.VMEM((4 * TOK, hidden), BF16),
            wide,
            pltpu.VMEM((2,) + one, F32),
            pltpu.VMEM((2,) + one, BF16),
            pltpu.SemaphoreType.DMA((2 * PIECES + 4,)),
            pltpu.SemaphoreType.DMA((PIECES + 4,)),
        ],
        compiler_params=params(),
        cost_estimate=COST,
        name="hidden_back",
    )(meta, n2a, n2b, dma, dmb, bias, *refs0, *refs1)


def unrelative(grads):
    out = []
    for row in range(WIN):
        slab = grads[row * SIDE : (row + 1) * SIDE]
        down = pltpu.roll(slab, row, 1) if row else slab
        across = pltpu.roll(slab, 0, 1, stride=1, stride_axis=0)
        out.append(jnp.where(lanes(SIDE) < 32, down, across))
    return jnp.concatenate(out, axis=0)


def attend_back_kernel(before, count, meta, vecs, gather, table, q, k, v, p, weights, att, n1, *refs):
    start, parts = sum(before), len(before)
    first, last = start == 0, start + count == PAIRS
    if first:
        back_own, back_far, x1, dm = refs[:4]
        norm_sums, bias_sums, table_grad, mine, theirs, dqkv_out, dx1, da = refs[4:12]
        refs = refs[12:]
        owns, fars, x1s, dms, dx1s = refs[-5:]
        refs = refs[:-5]
    else:
        da, refs = refs[0], refs[1:]
        if last:
            earlier, tok, dx1, *changes = refs[:4], *refs[4 : 6 + parts]
            flat, mine, theirs, result = refs[6 + parts : 10 + parts]
            refs = refs[10 + parts :]
            bias_sums, wqkv, toks, dx1s, results, *changed = refs[-5 - parts :]
            refs = refs[: -5 - parts]
        else:
            bias_sums, table_grad, mine, theirs, dqkv_out = refs[:5]
            refs = refs[5:]
    das, wproj, atts, n1s, qs, ks, vs, ps, dat, dqkv, grads, sems, out_sems = refs
    core = meta[64]
    width, cols_here = das.shape[-1], qs.shape[-1]
    rows = width // PIECES
    columns = pl.ds(start * LANES, cols_here)
    tokens = (2 * TOK, width)
    early = []
    if first:
        early = [(back_own, owns), (back_far, fars), (x1, x1s), (dm, dms)]
    else:
        early = [(da, das)]
    early = [begin(ref, dest, sems.at[at]) for at, (ref, dest) in enumerate(early)]
    half, here = columns_of(3, width)
    wait_proj = begin(weights.at[half, columns, here], wproj, sems.at[4])
    wait_att = begin(att, atts, sems.at[5])
    wait_v = begin(v.at[:, :, columns], vs, sems.at[6])
    wait_p = []
    for window in range(2):
        for pair in range(count):
            heads = pl.ds(2 * (start + pair), 2)
            wait_p.append(
                begin(p.at[window, heads], ps.at[window, pl.ds(2 * pair, 2)], sems.at[10 + len(wait_p)])
            )
        if window == 0:
            wait_qk = [
                begin(ref.at[:, :, columns], dest, sems.at[7 + at])
                for at, (ref, dest) in enumerate(((q, qs), (k, ks)))
            ]
    wait_n1 = begin(n1, n1s, sems.at[9])
    if last:
        at = 10 + 2 * count
        ends = [begin(tok, toks, sems.at[at]), begin(dx1, dx1s, sems.at[at + 1])]
        for mat in range(3):
            half, here = columns_of(mat, width)
            ends.append(begin(weights.at[half, :, here], wqkv.at[mat], sems.at[at + 2 + mat]))
        for part in range(parts):
            ends.append(begin(changes[part], changed[part], sems.at[at + 5 + part]))
    outs = []
    finish(early)
    if first:
        total = [jnp.zeros((1, width), F32) for _ in range(4)]
        for window in range(2):
            here = pl.ds(window * TOK, TOK)
            grad = owns[here] + fars[here].astype(F32)
            xhat, inverse = moments(x1s[window])
            out_grad = dms[window].astype(F32)
            dresid = out_grad + norm_back(grad, xhat, inverse, vecs[5:6])
            dx1s[window] = dresid
            rounded = dresid.astype(BF16)
            das[window] = rounded
            for slot, value in enumerate((rounded.astype(F32), grad * xhat, grad, out_grad)):
                total[slot] = total[slot] + jnp.sum(value, axis=0, keepdims=True)
        norm_sums[...] = jnp.concatenate(total, axis=0)
        outs.append(begin(dx1s, dx1, out_sems.at[2 * PIECES]))
        outs.append(begin(das, da, out_sems.at[2 * PIECES + 1]))
    wait_proj.wait()
    dat[...] = dot_nt(das[...].reshape(tokens), wproj[...]).astype(BF16).reshape(2, TOK, cols_here)

    def send(half):
        is_own = core == half
        at = jnp.where(is_own, 32, 48)
        for piece in range(PIECES):
            place = pl.multiple_of(meta[at + piece] * rows, rows)
            source, to = grads.at[half, pl.ds(place, rows), :], pl.ds(piece * rows, rows)
            sem = out_sems.at[half * PIECES + piece]
            copies = [pltpu.make_async_copy(source, ref.at[to, :], sem) for ref in (mine, theirs)]
            pl.when(is_own)(copies[0].start)
            pl.when(~is_own)(copies[1].start)
            outs.append(copies[0])

    wait_att.wait()
    made = dot_tn(atts[...].reshape(tokens), das[:, :, columns].reshape(2 * TOK, cols_here))
    grads[1, :, cols_here:] = made.astype(BF16)
    finish(wait_qk + [wait_v] + wait_p)
    place = lanes(TOK)
    table_sum = jnp.zeros((LANES, LANES), F32)
    for step in range(2 * count):
        window, pair = step // count, step % count
        cols = pl.ds(pair * LANES, LANES)
        q2, k2, v2, dat2 = (ref[window, :, cols] for ref in (qs, ks, vs, dat))
        q8 = (q2.astype(F32) * HDIM**-0.5).astype(BF16)
        k8 = (k2.astype(F32) * HDIM**-0.5).astype(BF16)
        dqs, dks, dvs, dts = [], [], [], []
        for half in range(2):
            soft = ps[window, 2 * pair + half]
            soft32 = soft.astype(F32)
            own_lanes = jnp.where(place // 64 == half, dat2.astype(F32), 0.0).astype(BF16)
            weighted = soft32 * dot_nt(own_lanes, v2)
            ds = (weighted - soft32 * jnp.sum(weighted, axis=-1, keepdims=True)).astype(BF16)
            turned = dot(ds, gather[...]).astype(BF16).astype(F32)
            turned = unrelative(turned).astype(BF16)
            dqs.append(dot(ds, k8) + dot(turned, table[half]))
            dks.append(dot_tn(ds, q8))
            dvs.append(dot_tn(soft, dat2))
            dts.append(dot_tn(turned, q2))
        dqkv[0, window, :, cols] = jnp.where(place < 64, dqs[0], dqs[1]).astype(BF16)
        dqkv[1, window, :, cols] = jnp.where(place < 64, dks[0][:TOK], dks[1][:TOK]).astype(BF16)
        dqkv[2, window, :, cols] = jnp.where(place < 64, dvs[0][:TOK], dvs[1][:TOK]).astype(BF16)
        table_sum = table_sum + jnp.where(lanes(LANES) < 64, dts[0], dts[1])
    if not last:
        table_grad[...] = table_sum
    if not last:
        outs.append(begin(dqkv, dqkv_out, out_sems.at[2 * PIECES + 2]))
    wait_n1.wait()
    for mat in (2, 0, 1):
        change = dqkv[mat].reshape(2 * TOK, cols_here)
        made = dot_tn(n1s[...].reshape(tokens), change)
        grads[mat // 2, :, pl.ds(mat % 2 * cols_here, cols_here)] = made.astype(BF16)
        if mat != 0:
            send(mat // 2)
        if mat != 1:
            bias_sums[mat // 2 : mat // 2 + 1] = jnp.sum(change.astype(F32), axis=0, keepdims=True)
    if last:
        finish(ends)
        total = [jnp.zeros((1, width), F32) for _ in range(2)]
        for window in range(2):
            grad = jnp.zeros((TOK, width), F32)
            at = 0
            for change in (*changed, dqkv):
                here = pl.ds(at, change.shape[-1])
                for mat in range(3):
                    grad = grad + dot_nt(change[mat, window], wqkv[mat, :, here])
                at += change.shape[-1]
            xhat, inverse = moments(toks[window].astype(F32))
            results[window] = dx1s[window] + norm_back(grad, xhat, inverse, vecs[0:1])
            outs.append(begin(results.at[window], result.at[window], out_sems.at[2 * PIECES + window]))
            for slot, value in enumerate((grad * xhat, grad)):
                total[slot] = total[slot] + jnp.sum(value, axis=0, keepdims=True)
        norm2_sums, bias0, table0, hidden_sums = earlier
        pack(meta, total, (bias0, bias_sums), norm2_sums, table0[...] + table_sum, hidden_sums, flat)
    finish(outs)


def pack(meta, norm1, biases, norm2, table, hidden, flat):
    flat[...] = jnp.zeros_like(flat)
    parts = biases[0].shape[1] // LANES
    for row in range(8):
        for at in range(6):
            cols = pl.ds(at * LANES, LANES)
            if row < 2:
                value = norm1[row][:, at * LANES : (at + 1) * LANES]
            elif row < 4:
                ref, place = (biases[0], at) if at < parts else (biases[1], at - parts)
                value = ref[row - 2 : row - 1, pl.ds(place * LANES, LANES)]
            else:
                value = norm2[row - 4 : row - 3, cols]
            block = 6 * row + at
            flat[block // 4 : block // 4 + 1, pl.ds(block % 4 * LANES, LANES)] = value
    for block in range(hidden.shape[1] // LANES):
        value = hidden[:, pl.ds(block * LANES, LANES)]
        for core in range(2):
            at = 12 + 3 * core + block // 4
            flat[at : at + 1, pl.ds(block % 4 * LANES, LANES)] = jnp.where(meta[64] == core, value, 0.0)
    both = table[:64] + pltpu.roll(table[:64], HDIM, 1)
    for group in range(4):
        flat[24:40, pl.ds(group * LANES, LANES)] = both[16 * group : 16 * group + 16]


def unpacked(flat, core):
    vectors = flat[:12].reshape(8, -1)
    hidden = lax.dynamic_slice_in_dim(flat, 12 + 3 * core, 3).reshape(-1)
    table = flat[24:40].reshape(16, 4, LANES).transpose(1, 0, 2).reshape(64, LANES)[:, :HDIM]
    return vectors, hidden, table


def attend_back(before, count, meta, vecs, gather, table, q, k, v, p, weights, att, n1, ins):
    width, cols_here = q.shape[-1], count * LANES
    start, parts = sum(before), len(before)
    first, last = start == 0, start + count == PAIRS
    rows, keys = (2, TOK, width), (2, KEYS, cols_here)
    part, flat = (2, TOK, cols_here), (2 * TOK, width)
    heads = (2, 2 * count, TOK, KEYS)
    small = [shape((2, cols_here), F32), shape((LANES, LANES), F32)]
    large = [shape((width, 2 * cols_here), BF16)] * 2
    large.append(shape(rows, F32) if last else shape((3,) + part, BF16))
    if last:
        small = [shape((SMALL, 2 * cols_here), F32)]
    if first:
        small = [shape((4, width), F32)] + small
        large += [shape(rows, F32), shape(rows, BF16)]
    scratch = [rows, (cols_here, width), rows, rows, part, keys, keys, heads, part, (3,) + part]
    scratch.append((2, width, 2 * cols_here))
    scratch = [pltpu.VMEM(dims, BF16) for dims in scratch]
    scratch += [pltpu.SemaphoreType.DMA((15 + 2 * count + parts,)), pltpu.SemaphoreType.DMA((2 * PIECES + 3,))]
    if first:
        scratch += [
            pltpu.VMEM(flat, F32),
            pltpu.VMEM(flat, BF16),
            pltpu.VMEM(rows, F32),
            pltpu.VMEM(rows, BF16),
            pltpu.VMEM(rows, F32),
        ]
    if last:
        scratch += [
            pltpu.VMEM((2, cols_here), F32),
            pltpu.VMEM((3, width, width), BF16),
            pltpu.VMEM(rows, BF16),
            pltpu.VMEM(rows, F32),
            pltpu.VMEM(rows, F32),
        ] + [pltpu.VMEM((3, 2, TOK, size * LANES), BF16) for size in before]
    return pl.pallas_call(
        partial(attend_back_kernel, before, count),
        out_shape=small + large,
        in_specs=[SMEM] + [WHOLE] * 3 + [HBM] * 8 + [WHOLE if last and at < 4 else HBM for at in range(len(ins) - 1)],
        out_specs=[WHOLE] * len(small) + [HBM] * len(large),
        scratch_shapes=scratch,
        compiler_params=params(),
        cost_estimate=COST,
        name="attend_back",
    )(meta, vecs, gather, table, q, k, v, p, weights, att, n1, *ins)


def grid_of(count):
    return (4, 2, 2) if count == 16 else None


def turn(values, dims, moves):
    pairs = []
    for chip in range(dims[0] * dims[1] * dims[2]):
        for core, (axis, by) in enumerate(moves):
            place = list(np.unravel_index(chip, dims))
            place[axis] = (place[axis] + by) % dims[axis]
            pairs.append((2 * chip + core, 2 * int(np.ravel_multi_index(place, dims)) + core))
    return lax.ppermute(values, ("dp", "mp"), pairs)


ALONG_X, ALONG_Y = ((2, 1),) * 2, ((1, 1),) * 2
FIRST, SECOND = ((2, 1), (1, 1)), ((1, 1), (2, 1))


def along_z(values, dims):
    return [turn(values, dims, ((0, step),) * 2) for step in range(1, dims[0])]


def swap_z(values, dims, by):
    chips = dims[1] * dims[2]
    pairs = [(chip, (chip // chips ^ by) * chips + chip % chips) for chip in range(dims[0] * chips)]
    return lax.ppermute(values, "dp", pairs)


def other_core(values):
    return lax.ppermute(values, "mp", [(0, 1), (1, 0)])


def after(values, *others):
    return lax.optimization_barrier((values, *others))[0]


def stack_kernel(count, *refs):
    ins, out, sems = refs[:count], refs[count], refs[count + 1]
    copies, at = [], 0
    for ref in ins:
        rows = ref.shape[0]
        copies.append(begin(ref, out.at[pl.ds(at, rows)], sems.at[len(copies)]))
        at += rows
    finish(copies)


def stack(*parts):
    rows = sum(part.shape[0] for part in parts)
    return pl.pallas_call(
        partial(stack_kernel, len(parts)),
        out_shape=shape((rows, parts[0].shape[1]), BF16),
        in_specs=[HBM] * len(parts),
        out_specs=HBM,
        scratch_shapes=[pltpu.SemaphoreType.DMA((len(parts),))],
        compiler_params=params(),
        cost_estimate=COST,
        name="stack",
    )(*parts)


class Flow:
    def __init__(self, *came):
        self.came = list(came)


def meet(flows, *values):
    sizes = [len(flow.came) for flow in flows]
    found = list(lax.optimization_barrier((*(part for flow in flows for part in flow.came), *values)))
    for flow, size in zip(flows, sizes):
        flow.came, found = found[:size], found[size:]
    return found


def place_orders(dims, core):
    here = lax.axis_index("dp")
    z, y, x = here // (dims[1] * dims[2]), here // dims[2] % dims[1], here % dims[2]

    def chip(step, inner, outer):
        by_x = jnp.where(core == 0, inner, outer)
        by_y = jnp.where(core == 0, outer, inner)
        return ((z - step) % dims[0] * dims[1] + (y + by_y) % 2) * dims[2] + (x + by_x) % 2

    square = [(inner, outer) for outer in range(2) for inner in range(2)]
    gather = [chip(0, *at) for at in square]
    gather += [chip(step, *at) for at in square for step in range(1, dims[0])]
    scatter = [chip(step, *at) for at in square for step in range(dims[0])]
    return [jnp.stack(found).astype(jnp.int32) for found in (gather, scatter)]


def add(a, b):
    return a.astype(F32) + b.astype(F32)


def staged_kernel(kernel, starts, scalars, *refs):
    count = len(starts)
    meta, refs = refs[:scalars], refs[scalars:]
    total = len(refs) // 2
    held, sems = refs[total : 2 * total], refs[2 * total]
    copies = []
    for ref, start, dest in zip(refs, starts, held):
        if start is not None:
            ref = ref.at[pl.ds(start, dest.shape[0])]
        copies.append(begin(ref, dest, sems.at[len(copies)]))
    finish(copies)
    kernel(*meta, *held)
    finish([begin(held[at], refs[at], sems.at[at]) for at in range(count, total)])


def staged(kernel, outs, *ins, meta=None):
    ins = [part if isinstance(part, tuple) else (part, None, part.shape[0]) for part in ins]
    arrays, starts, rows = zip(*ins)
    scalars = () if meta is None else (meta,)
    held = [pltpu.VMEM((count, *array.shape[1:]), array.dtype) for array, count in zip(arrays, rows)]
    held += [pltpu.VMEM(out.shape, out.dtype) for out in outs]
    return pl.pallas_call(
        partial(staged_kernel, kernel, starts, len(scalars)),
        out_shape=outs,
        in_specs=[SMEM] * len(scalars) + [HBM] * len(arrays),
        out_specs=[HBM] * len(outs),
        scratch_shapes=held + [pltpu.SemaphoreType.DMA((len(held),))],
        compiler_params=params(),
        cost_estimate=COST,
        name="staged",
    )(*scalars, *arrays)


def core_rows_kernel(count, meta, *refs):
    *terms, own, far = refs
    half, width = own.shape[1:]
    one, two = (sum(ref[...].astype(F32) for ref in part) for part in (terms[:count], terms[count:]))
    cut, last = one.shape[1] // 2, two.shape[1] // 2
    for core in range(2):

        def put(ref, at=slice(core * half, (core + 1) * half)):
            for mat in range(2):
                ref[mat, :, :cut] = one[at, mat * cut : (mat + 1) * cut]
                ref[mat, :, cut:] = two[at, mat * last : (mat + 1) * last]

        pl.when(meta[64] == core)(partial(put, own))
        pl.when(meta[64] != core)(partial(put, far))


def last_rows_kernel(meta, near, came, qkv, proj):
    width = proj.shape[1]

    def put(qk, vp):
        qkv[:, :width] = qk[0]
        qkv[:, width : 2 * width] = qk[1]
        qkv[:, 2 * width :] = vp[0]
        proj[...] = vp[1]

    pl.when(meta[64] == 0)(partial(put, near, came))
    pl.when(meta[64] != 0)(partial(put, came, near))


class Scatter(Flow):
    def __init__(self, keep, far, dims):
        super().__init__(turn(far, dims, SECOND))
        self.keep, self.dims = keep, dims

    def second(self):
        half = self.keep.shape[0] // 2
        send = add(self.keep[half:], self.came[0][half:]).astype(BF16)
        self.near = add(self.keep[:half], self.came[0][:half])
        self.sent = send
        self.came = [turn(send, self.dims, FIRST)]

    def third(self):
        near = self.near + self.came[0].astype(F32)
        rows = near.shape[0] // self.dims[0]
        self.near = near[:rows]
        sends = [near[step * rows : (step + 1) * rows].astype(BF16) for step in range(1, self.dims[0])]
        self.sent = sends[0]
        self.came = [
            turn(send, self.dims, ((0, self.dims[0] - step),) * 2) for step, send in enumerate(sends, 1)
        ]

    def halve(self):
        near = self.near + self.came[0].astype(F32)
        rows = near.shape[0] // self.dims[0]
        parts = [near[step * rows : (step + 1) * rows] for step in range(self.dims[0])]
        even = lax.axis_index("dp") // (self.dims[1] * self.dims[2]) % 2 == 0
        self.near = parts[0]
        self.beside = jnp.where(even, parts[3], parts[1])
        send = jnp.concatenate([parts[2], jnp.where(even, parts[1], parts[3])], axis=0).astype(BF16)
        self.came = [swap_z(send, self.dims, 2)]

    def quarter(self):
        rows = self.near.shape[0]
        came = self.came[0]
        self.near = self.near + came[:rows].astype(F32)
        self.sent = (self.beside + came[rows:].astype(F32)).astype(BF16)
        self.came = [swap_z(self.sent, self.dims, 1)]

    def last(self):
        return sum((part.astype(F32) for part in self.came), self.near)


def constants():
    key = np.arange(KEYS)
    row, col = key // SIDE, key % SIDE
    inside = (row < WIN) & (col < WIN)
    spread = np.zeros((KEYS, LANES), np.float32)
    gather = np.zeros((KEYS, LANES), np.float32)
    for place in key[inside]:
        for base in (0, 64):
            spread[place, base + WIN - 1 + row[place]] = 1.0
            spread[place, base + 32 + WIN - 1 + col[place]] = 1.0
        gather[place, WIN - 1 - row[place]] = 1.0
        gather[place, 32 + WIN - 1 - col[place]] = 1.0
    return spread, gather


def tables(rel_pos_h, rel_pos_w):
    count = rel_pos_h.shape[0]
    gap = jnp.zeros((32 - count, HDIM), BF16)
    turned = jnp.concatenate([rel_pos_h[::-1], gap, rel_pos_w[::-1], gap], axis=0)
    turned = jnp.concatenate([turned, turned], axis=0).T
    none = jnp.zeros_like(turned)
    forward = jnp.concatenate(
        [jnp.concatenate([turned, none], axis=0), jnp.concatenate([none, turned], axis=0)], axis=1
    )
    straight = jnp.concatenate([rel_pos_h, gap, rel_pos_w, gap], axis=0)
    straight = jnp.concatenate([straight, jnp.zeros_like(straight)], axis=0)
    none = jnp.zeros_like(straight)
    backward = jnp.stack(
        [
            jnp.concatenate([straight, none], axis=1),
            jnp.concatenate([none, straight], axis=1),
        ]
    )
    return forward, backward


def padded(values):
    images, rows, _, width = values.shape
    values = jnp.pad(values, ((0, 0), (0, 0), (0, SIDE - WIN), (0, 0)))
    return values.reshape(images, rows * SIDE, width)


def unpadded(values):
    images, _, width = values.shape
    return values.reshape(images, WIN, SIDE, width)[:, :, :WIN]


def local(
    patches,
    norm1_gain,
    norm1_bias,
    qkv_weight,
    qv_bias,
    rel_pos_h,
    rel_pos_w,
    proj_weight,
    proj_bias,
    norm2_gain,
    norm2_bias,
    fc1_weight,
    fc1_bias,
    fc2_weight,
    fc2_bias,
    heights,
    widths,
    out_grad,
):
    width = patches.shape[-1]
    dims = grid_of(lax.axis_size("dp"))
    core = lax.axis_index("mp")
    is_first = core == 0
    spread, gather = constants()

    def prepare(patches, out_grad, heights, rel_pos_h, rel_pos_w):
        if dims is None:
            orders = [jnp.tile(jnp.arange(PIECES, dtype=jnp.int32), 4)]
        else:
            own, far = place_orders(dims, core), place_orders(dims, 1 - core)
            orders = [own[0], far[0], own[1], far[1]]
        meta = jnp.concatenate(
            orders + [core.astype(jnp.int32)[None], heights, widths, jnp.zeros((11,), jnp.int32)]
        )
        row_index = core * WIN + jnp.arange(WIN)
        valid = (row_index[None, :, None] < heights[:, None, None]) & (
            jnp.arange(WIN)[None, None, :] < widths[:, None, None]
        )
        dm = padded(jnp.where(valid[..., None], out_grad, jnp.zeros_like(out_grad)))
        return padded(patches), dm, meta, *tables(rel_pos_h, rel_pos_w)

    wanted = (patches, out_grad, heights, rel_pos_h, rel_pos_w)
    vectors = (norm1_gain, norm1_bias, qv_bias[0], qv_bias[1], proj_bias, norm2_gain, norm2_bias, fc2_bias)
    small = jnp.pad(jnp.stack(vectors, axis=1), ((0, 0), (0, LANES - len(vectors))))
    qk = jnp.concatenate([qkv_weight[:, :width], small, qkv_weight[:, width : 2 * width]], axis=1)
    vp = jnp.concatenate([qkv_weight[:, 2 * width :], small, proj_weight], axis=1)
    if dims is None:
        qk = lax.all_gather(qk, ("dp", "mp"), axis=0, tiled=True)
        vp = lax.all_gather(vp, ("dp", "mp"), axis=0, tiled=True)
        attend_own = [jnp.where(is_first, qk, vp)]
        attend_far = [jnp.where(is_first, vp, qk)]
        tok, dm, meta, table, table_back = prepare(*wanted)
        hidden_in = tuple(
            ((lax.all_gather(part, "dp", axis=0, tiled=True), 0),) for part in (fc1_weight, fc2_weight.T)
        )
    else:
        fc1, fc2 = fc1_weight, fc2_weight.T
        came = other_core(jnp.where(is_first, vp, qk))
        near = jnp.where(is_first, qk, vp)
        block = jnp.concatenate(
            [jnp.where(is_first, near, came), jnp.where(is_first, came, near)], axis=0
        )
        attend_size, size = block.shape[1], fc1.shape[1]
        tok, dm, meta, table, table_back = prepare(*meet([], *wanted, block)[:5])
        own = jnp.concatenate([block, fc1, fc2], axis=1)
        attend_z, beside = Flow(*along_z(block, dims)), Flow(turn(own, dims, FIRST))
        fc1, fc2, tok, dm, table, table_back, meta = meet(
            [attend_z, beside], fc1, fc2, tok, dm, table, table_back, meta
        )

        attend_z = stack(*attend_z.came)
        z_beside = Flow(turn(attend_z, dims, FIRST))
        own = stack(own, *beside.came)
        over = Flow(turn(own, dims, SECOND))
        fc1_z = Flow(*along_z(after(fc1, own), dims))
        (fc2,) = meet([over, z_beside, fc1_z], fc2)

        over = over.came[0]
        attend_z = stack(attend_z, *z_beside.came)
        z_over = Flow(turn(attend_z, dims, SECOND))
        fc1_z = stack(after(fc1_z.came[0], attend_z), *fc1_z.came[1:])
        fc1_beside = Flow(turn(fc1_z, dims, FIRST))
        fc2_z = Flow(*along_z(after(fc2, fc1_z), dims))
        own_attend = jnp.concatenate([own[:, :attend_size], over[:, :attend_size]], axis=0)
        own_attend, attend_z = meet([z_over, fc1_beside, fc2_z], own_attend, attend_z)

        z_over = z_over.came[0]
        far = Flow(*(other_core(part) for part in (own_attend, attend_z, z_over)))
        fc1_z = stack(fc1_z, *fc1_beside.came)
        fc1_over = Flow(turn(fc1_z, dims, SECOND))
        fc2_z = stack(*fc2_z.came)
        fc2_beside = Flow(turn(fc2_z, dims, FIRST))
        tok, fc1_z, fc2_z, dm = meet([far], tok, fc1_z, fc2_z, dm)
        dm_far = Flow(other_core(dm))
        attend_own, attend_far = [own, over, attend_z, z_over], far.came

    vecs, n1, q, k, v, p, att, weights, x1, n2 = attend(
        meta, tok, table, jnp.asarray(spread, BF16), attend_own, attend_far
    )
    n2_far = other_core(n2).reshape(-1, width)
    if dims is None:
        dm_far = other_core(dm)
    else:
        (n2,) = meet([fc1_over, fc2_beside, dm_far], n2)
        (dm_far,) = dm_far.came
        fc2_z = stack(fc2_z, *fc2_beside.came)
        fc2_over = turn(fc2_z, dims, SECOND)
    dm_flat, dm_far = dm.reshape(-1, width), dm_far.reshape(-1, width)
    n2 = n2.reshape(-1, width)
    bias = fc1_bias[None].astype(F32)
    if dims is not None:
        n2 = after(n2, fc2_z)
        hidden_in = [
            ((own, attend_size), (over, attend_size), (fc1_z, 0), (*fc1_over.came, 0)),
            ((own, attend_size + size), (over, attend_size + size), (fc2_z, 0), (fc2_over, 0)),
        ]
    fc2_part = hidden_fwd(meta, n2, n2_far, dm_flat, dm_far, bias, hidden_in[0])
    if dims is not None:
        fc2_part = meet([], *fc2_part, fc2_over)[:2]
        fc2_sum = Scatter(*fc2_part, dims)
    fc1_bias_part, *fc1_part, back_own, back_far, out_own, out_far = hidden_back(
        meta, n2, n2_far, dm_flat, dm_far, bias, *hidden_in
    )
    back_far = other_core(back_far)
    if dims is not None:
        fc1_part = meet([fc2_sum], *fc1_part)
        fc2_sum.second()
        fc1_sum = Scatter(*fc1_part, dims)
        back_own = after(back_own, fc2_sum.sent)

    shared = (meta, vecs, jnp.asarray(gather, BF16), table_back, q, k, v, p, weights, att, n1)
    half = width // 2
    def block_of(out_far):
        branch = add(out_own, out_far).reshape(x1.shape) + vecs[7]
        row_index = core * WIN + jnp.arange(WIN)
        valid = (row_index[None, :, None] < heights[:, None, None]) & (
            jnp.arange(WIN)[None, None, :] < widths[:, None, None]
        )
        return jnp.where(valid[..., None], unpadded(x1 + branch), 0.0).astype(BF16)

    def core_rows(wholes):
        whole = jnp.stack(
            [
                jnp.concatenate([part.reshape(part.shape[0], 2, -1)[:, at] for part in wholes], axis=1)
                for at in range(2)
            ]
        )
        rows = whole.shape[1] // 2
        cuts = whole[:, :rows], whole[:, rows:]
        return jnp.where(is_first, *cuts), jnp.where(is_first, *cuts[::-1])

    count0, count1 = BACK_PARTS
    sums2, bias0, table0, mine0, theirs0, change, dx1, da = attend_back(
        (), count0, *shared, (back_own, back_far, x1, dm)
    )
    if dims is not None:
        da, mine0, theirs0 = meet([fc2_sum, fc1_sum], da, mine0, theirs0)
        came0 = other_core(theirs0)
        fc2_sum.third()
        fc1_sum.second()
        both = add(mine0, came0).astype(BF16)
        first = Scatter(both[:half], both[half:], dims)
        da = after(da, both)
    flat, mine, theirs, result = attend_back(
        (count0,), count1, *shared, (da, sums2, bias0, table0, fc1_bias_part, tok, dx1, change)
    )
    if dims is None:
        result, block_out = unpadded(result), block_of(other_core(out_far))
        fc1_sum, fc2_sum = (
            lax.psum_scatter(
                jnp.concatenate(parts, axis=0).astype(F32), "dp", scatter_dimension=0, tiled=True
            )
            for parts in (fc1_part, fc2_part)
        )
        wholes = [
            lax.psum_scatter(add(own, other_core(far)), "dp", scatter_dimension=0, tiled=True)
            for own, far in ((mine0, theirs0), (mine, theirs))
        ]
        near, far = core_rows(wholes)
        came = other_core(far)
        flat = lax.psum(flat, ("dp", "mp"))
    else:
        came, flat_came = Flow(other_core(theirs)), Flow(other_core(flat))
        mine, flat, out_far, result = meet([fc2_sum, fc1_sum, first], mine, flat, out_far, result)
        first.second()
        fc1_sum.halve()
        mine, flat, out_far = meet([came, flat_came, first], mine, flat, out_far)
        both = add(mine, came.came[0]).astype(BF16)
        second = Scatter(both[:half], both[half:], dims)
        flat = flat + flat_came.came[0]
        flat_came = Flow(turn(flat, dims, SECOND))
        first.halve()
        late = Flow(other_core(out_far))
        flat, result = meet([flat_came, second, fc1_sum], flat, result)
        flat = flat + flat_came.came[0]
        flat_came = Flow(turn(flat, dims, FIRST))
        second.second()
        fc1_sum.quarter()
        fc2_sum = fc2_sum.last()
        result = unpadded(result)
        flat, fc2_sum, result = meet([flat_came, first, second, fc1_sum, late], flat, fc2_sum, result)
        flat = flat + flat_came.came[0]
        flat_came = Flow(swap_z(flat, dims, 2))
        second.third()
        first.quarter()
        fc1_sum.near, late.came[0] = meet([], fc1_sum.near, late.came[0], second.sent, first.sent)[:2]
        fc1_sum = fc1_sum.last()
        block_out = block_of(late.came[0])
        flat, fc1_sum, block_out = meet([flat_came, second, first], flat, fc1_sum, block_out)

        share = shape((2, width // len(FIRST) // dims[0] // dims[1] // dims[2], width), F32)
        near, far = staged(
            partial(core_rows_kernel, 2), [share, share], first.near, *first.came, second.near, *second.came, meta=meta
        )
        came = other_core(far)
        flat = flat + flat_came.came[0]
        flat_came = swap_z(flat, dims, 1)
        flat = flat + after(flat_came, far)
    rows = near.shape[1]
    outs = [shape((rows, 3 * width), F32), shape((rows, width), F32)]
    qkv_grad, proj_grad = staged(last_rows_kernel, outs, near, came, meta=meta)
    vec_sums, fc1_bias_grad, rel = unpacked(flat, core)
    share = norm1_gain.shape[0]
    device = lax.axis_index("dp") * 2 + core
    mine = lax.dynamic_slice_in_dim(vec_sums, device * share, share, axis=1)
    rels = rel_pos_h.shape[0]
    return (
        block_out,
        result,
        mine[0],
        mine[1],
        qkv_grad,
        mine[2:4],
        rel[:rels],
        rel[32 : 32 + rels],
        proj_grad,
        mine[4],
        mine[5],
        mine[6],
        fc1_sum,
        fc1_bias_grad,
        fc2_sum.T,
        mine[7],
    )


def solution(mesh):
    return jax.shard_map(
        local,
        mesh=mesh,
        in_specs=(
            P("dp", "mp", None, None),
            P(("dp", "mp")),
            P(("dp", "mp")),
            P(("dp", "mp"), None),
            P(None, ("dp", "mp")),
            P(),
            P(),
            P(("dp", "mp"), None),
            P(("dp", "mp")),
            P(("dp", "mp")),
            P(("dp", "mp")),
            P("dp", "mp"),
            P("mp"),
            P("mp", "dp"),
            P(("dp", "mp")),
            P("dp"),
            P("dp"),
            P("dp", "mp", None, None),
        ),
        out_specs=(
            P("dp", "mp", None, None),
            P("dp", "mp", None, None),
            P(("dp", "mp")),
            P(("dp", "mp")),
            P(("dp", "mp"), None),
            P(None, ("dp", "mp")),
            P(),
            P(),
            P(("dp", "mp"), None),
            P(("dp", "mp")),
            P(("dp", "mp")),
            P(("dp", "mp")),
            P("dp", "mp"),
            P("mp"),
            P("mp", "dp"),
            P(("dp", "mp")),
        ),
        check_vma=False,
    )
```

```python
from functools import partial

import jax
import jax.numpy as jnp
import numpy as np
from jax import lax
from jax.experimental import pallas as pl
from jax.experimental.pallas import tpu as pltpu
from jax.sharding import PartitionSpec as P

HEADS = 12
HDIM = 64
LANES = 128
PAIRS = HEADS // 2
WIN = 14
SIDE = 16
TOK = WIN * SIDE
KEYS = 256
PIECES = 16
EPSILON = 1e-06
MASKED_SCORE = -1e30
MASK_LANE = 60
SMALL = 48
CHUNK = 512
BACK_PARTS = (4, 2)
F32 = jnp.float32
BF16 = jnp.bfloat16
SMEM = pl.BlockSpec(memory_space=pltpu.SMEM)
HBM = pl.BlockSpec(memory_space=pl.ANY)
WHOLE = pl.BlockSpec(memory_space=pltpu.VMEM)
VMEM_BYTES = 52 * 2**20
COST = pl.CostEstimate(flops=1000, bytes_accessed=1000, transcendentals=0)


def params():
    return pltpu.CompilerParams(vmem_limit_bytes=VMEM_BYTES)


def shape(dims, dtype):
    return jax.ShapeDtypeStruct(dims, dtype)


def dot(a, b):
    return jnp.dot(a, b, preferred_element_type=F32)


def dot_nt(a, b):
    return lax.dot_general(a, b, (((1,), (1,)), ((), ())), preferred_element_type=F32)


def dot_tn(a, b):
    return lax.dot_general(a, b, (((0,), (0,)), ((), ())), preferred_element_type=F32)


def lanes(rows):
    return lax.broadcasted_iota(jnp.int32, (rows, LANES), 1)


def moments(values):
    centered = values - jnp.mean(values, axis=-1, keepdims=True)
    inverse = lax.rsqrt(jnp.mean(centered * centered, axis=-1, keepdims=True) + EPSILON)
    return centered * inverse, inverse


def norm_back(grad, xhat, inverse, gain):
    scaled = grad * gain
    first = jnp.mean(scaled, axis=-1, keepdims=True)
    second = jnp.mean(scaled * xhat, axis=-1, keepdims=True)
    return inverse * (scaled - first - xhat * second)


def begin(source, dest, sem):
    copy = pltpu.make_async_copy(source, dest, sem)
    copy.start()
    return copy


def finish(copies):
    for copy in copies:
        copy.wait()


def pieces_in(meta, at, ins, start, dest, sems, first):
    rows, cols = dest.shape[0] // PIECES, dest.shape[1]
    copies = []
    for ref, base in ins:
        for part in range(ref.shape[0] // rows):
            place = pl.multiple_of(meta[at + len(copies)] * rows, rows)
            source = ref.at[pl.ds(part * rows, rows), pl.ds(base + start, cols)]
            copies.append(begin(source, dest.at[pl.ds(place, rows), :], sems.at[first + len(copies)]))
    return copies


def row_valid(meta, core, window, rows, width):
    place = lax.broadcasted_iota(jnp.int32, (rows, width), 0)
    row, col = place // SIDE, place % SIDE
    inside = (row < WIN) & (col < WIN)
    return inside & (core * WIN + row < meta[65 + window]) & (col < meta[67 + window])


def relative(turned):
    out = []
    for row in range(WIN):
        slab = turned[row * SIDE : (row + 1) * SIDE]
        down = pltpu.roll(slab, row, 1) if row else slab
        across = pltpu.roll(slab, 0, 1, stride=1, stride_axis=0)
        out.append(jnp.where(lanes(SIDE) % 64 < 32, down, across))
    return jnp.concatenate(out, axis=0)


def columns_of(mat, width, start=0, size=None):
    return mat // 2, pl.ds(mat % 2 * (width + LANES) + start, width if size is None else size)


def attend_kernel(count, total, meta, tok, table, spread, *refs):
    own, other = refs[:count], refs[count:total]
    vecs, n1, q, k, v, p, att, w_out, x1, n2 = refs[total : total + 10]
    toks, weights, aug, n1s, qs, ks, vs, ps, atts, x1s, n2s, sems, out_sems = refs[total + 10 :]
    width = toks.shape[-1]
    core = meta[64]
    copies = [begin(tok, toks, sems.at[2 * PIECES])]
    for found, at, half in ((own, 0, core), (other, 16, 1 - core)):
        found = [(ref, 0) for ref in found]
        copies += pieces_in(meta, at, found, 0, weights.at[half], sems, at)
    for window in range(2):
        valid = row_valid(meta, core, window, KEYS, LANES)
        aug[window] = jnp.where(
            (lanes(KEYS) == MASK_LANE) & ~valid, MASKED_SCORE, spread[...].astype(F32)
        ).astype(BF16)
        ks[window, TOK:] = jnp.zeros((KEYS - TOK, width), BF16)
        vs[window, TOK:] = jnp.zeros((KEYS - TOK, width), BF16)
    copies[0].wait()
    tokens = toks[...].reshape(2 * TOK, width).astype(F32)
    xhat, _ = moments(tokens)
    finish(copies[1:])
    outs = [begin(weights, w_out, out_sems.at[0])]
    vecs[...] = weights[0, :, width : width + LANES].astype(F32).T[:8]
    normed = (xhat * vecs[0:1] + vecs[1:2]).astype(BF16)
    n1s[...] = normed.reshape(2, TOK, width)
    outs.append(begin(n1s, n1, out_sems.at[1]))
    for mat, (made_in, dest) in enumerate(((qs, q), (ks, k), (vs, v))):
        for start in range(0, width, 256):
            cols = pl.ds(start, 256)
            half, here = columns_of(mat, width, start, 256)
            made = dot(normed, weights[half, :, here])
            if mat != 1:
                made = made + vecs[2 + mat // 2 : 3 + mat // 2, cols]
            made = made.astype(BF16)
            made_in[0, :TOK, cols] = made[:TOK]
            made_in[1, :TOK, cols] = made[TOK:]
        outs.append(begin(made_in, dest, out_sems.at[2 + mat]))

    place = lanes(TOK)
    for step in range(2 * PAIRS):
        window, pair = step // PAIRS, step % PAIRS
        cols = pl.ds(pair * LANES, LANES)
        q2, k2, v2 = qs[window, :, cols], ks[window, :, cols], vs[window, :, cols]
        turned = dot(q2, table[...])
        keys_aug = jnp.concatenate([k2, aug[window]], axis=1)
        parts = []
        for half in range(2):
            rel = relative(turned[:, half * LANES : (half + 1) * LANES])
            high = rel.astype(BF16).astype(F32)
            rel = jnp.where(place < 64, high, rel - high)
            rel = jnp.where(place == MASK_LANE, 1.0, rel).astype(BF16)
            mine = jnp.where(place // 64 == half, q2.astype(F32) * HDIM**-0.5, 0.0).astype(BF16)
            scores = dot_nt(jnp.concatenate([mine, rel], axis=1), keys_aug)
            terms = jnp.exp(scores - jnp.max(scores, axis=-1, keepdims=True))
            soft = terms * (1.0 / jnp.sum(terms, axis=-1, keepdims=True))
            soft = soft.astype(BF16)
            ps[window, 2 * pair + half] = soft
            parts.append(dot(soft, v2))
        atts[window, :, cols] = jnp.where(place < 64, parts[0], parts[1]).astype(BF16)
        heads = pl.ds(2 * pair, 2)
        outs.append(begin(ps.at[window, heads], p.at[window, heads], out_sems.at[len(outs)]))
    outs.append(begin(atts, att, out_sems.at[len(outs)]))
    half, here = columns_of(3, width)
    for window in range(2):
        resid = toks[window].astype(F32) + (dot(atts[window], weights[half, :, here]) + vecs[4:5])
        x1s[window] = resid
        xhat, _ = moments(resid)
        n2s[window] = (xhat * vecs[5:6] + vecs[6:7]).astype(BF16)
        outs.append(begin(x1s.at[window], x1.at[window], out_sems.at[len(outs)]))
        outs.append(begin(n2s.at[window], n2.at[window], out_sems.at[len(outs)]))
    finish(outs)


def attend(meta, tok, table, spread, own, other):
    count, total, width = len(own), len(own) + len(other), tok.shape[-1]
    rows, keys, heads = (2, TOK, width), (2, KEYS, width), (2, HEADS, TOK, KEYS)
    halves = (2, width, 2 * width + LANES)
    outs = [shape(dims, BF16) for dims in (rows, rows, keys, keys, heads, rows, halves)]
    outs += [shape(rows, F32), shape(rows, BF16)]
    scratch = (rows, halves, (2, KEYS, LANES), rows, rows, keys, keys, heads, rows)
    return pl.pallas_call(
        partial(attend_kernel, count, total),
        out_shape=[shape((8, width), F32)] + outs,
        in_specs=[SMEM, HBM, WHOLE, WHOLE] + [HBM] * total,
        out_specs=[WHOLE] + [HBM] * len(outs),
        scratch_shapes=[pltpu.VMEM(dims, BF16) for dims in scratch]
        + [
            pltpu.VMEM(rows, F32),
            pltpu.VMEM(rows, BF16),
            pltpu.SemaphoreType.DMA((2 * PIECES + 1,)),
            pltpu.SemaphoreType.DMA((10 + 2 * PAIRS,)),
        ],
        compiler_params=params(),
        cost_estimate=COST,
        name="attend",
    )(meta, tok, table, spread, *own, *other)


def pieces_out(meta, made, cols, keep, send, sems, first):
    rows = made.shape[0] // PIECES
    copies = []
    for piece in range(PIECES):
        dest = keep if piece < PIECES // 2 else send
        place = pl.multiple_of(meta[32 + piece] * rows, rows)
        at = pl.ds(piece % (PIECES // 2) * rows, rows)
        source = made.at[pl.ds(place, rows), cols]
        copies.append(begin(source, dest.at[at, cols], sems.at[first + len(copies)]))
    return copies


def hidden_fwd_kernel(bases, meta, n2a, n2b, dma, dmb, bias, *refs):
    count = len(bases)
    ins, (keep, send) = list(zip(refs[:count], bases)), refs[count : count + 2]
    w0, n2s, dms, grad, sems, out_sems = refs[count + 2 :]
    width, hidden = w0.shape
    at = PIECES
    copies = [begin(n2a, n2s.at[: 2 * TOK], sems.at[at]), begin(n2b, n2s.at[2 * TOK :], sems.at[at + 1])]
    copies += pieces_in(meta, 0, ins, 0, w0, sems, 0)
    dm_copies = [
        begin(dma, dms.at[: 2 * TOK], sems.at[at + 2]),
        begin(dmb, dms.at[2 * TOK :], sems.at[at + 3]),
    ]
    finish(copies)
    outs = []
    for start in range(0, hidden, CHUNK):
        cols = pl.ds(start, CHUNK)
        inner = dot(n2s[...], w0[:, cols]) + bias[:, cols]
        act = (inner * (0.5 + 0.5 * lax.erf(inner * 0.7071067811865476))).astype(BF16)
        if start == 0:
            finish(dm_copies)
        grad[:, cols] = dot_tn(dms[...], act).astype(BF16)
        if start + CHUNK == hidden - CHUNK:
            outs += pieces_out(meta, grad, pl.ds(0, hidden - CHUNK), keep, send, out_sems, 0)
    outs += pieces_out(meta, grad, pl.ds(hidden - CHUNK, CHUNK), keep, send, out_sems, PIECES)
    finish(outs)


def hidden_fwd(meta, n2a, n2b, dma, dmb, bias, ins):
    refs, bases = zip(*ins)
    width, hidden = n2a.shape[-1], bias.shape[-1]
    return pl.pallas_call(
        partial(hidden_fwd_kernel, bases),
        out_shape=[shape((width // 2, hidden), BF16)] * 2,
        in_specs=[SMEM] + [HBM] * 4 + [WHOLE] + [HBM] * len(refs),
        out_specs=[HBM] * 2,
        scratch_shapes=[
            pltpu.VMEM((width, hidden), BF16),
            pltpu.VMEM((4 * TOK, width), BF16),
            pltpu.VMEM((4 * TOK, width), BF16),
            pltpu.VMEM((width, hidden), BF16),
            pltpu.SemaphoreType.DMA((PIECES + 4,)),
            pltpu.SemaphoreType.DMA((2 * PIECES,)),
        ],
        compiler_params=params(),
        cost_estimate=COST,
        name="hidden_fwd",
    )(meta, n2a, n2b, dma, dmb, bias, *refs)


def hidden_back_kernel(bases0, bases1, meta, n2a, n2b, dma, dmb, bias, *refs):
    count = len(bases0)
    ins0, ins1 = list(zip(refs[:count], bases0)), list(zip(refs[count : 2 * count], bases1))
    refs = refs[2 * count :]
    bias_grad, keep, send, back_own, back_far, acts_out = refs[:6]
    w0, w1, n2s, dms, acts, backs, grad, big, small, sems, out_sems = refs[6:]
    width, hidden = w0.shape
    halves = (pl.ds(0, 2 * TOK), pl.ds(2 * TOK, 2 * TOK))
    at = 2 * PIECES
    copies = [begin(ref, n2s.at[half], sems.at[at + i]) for i, (ref, half) in enumerate(zip((n2a, n2b), halves))]
    copies += pieces_in(meta, 0, ins0, 0, w0, sems, 0)
    at += 2
    later = [begin(ref, dms.at[half], sems.at[at + i]) for i, (ref, half) in enumerate(zip((dma, dmb), halves))]
    later += pieces_in(meta, 0, ins1, 0, w1, sems, PIECES)
    finish(copies)
    outs = []
    for start in range(0, hidden, CHUNK):
        cols = pl.ds(start, CHUNK)
        inner = dot(n2s[...], w0[:, cols]) + bias[:, cols]
        if start == 0:
            finish(later)
        back = dot(dms[...], w1[:, cols])
        cdf = 0.5 + 0.5 * lax.erf(inner * 0.7071067811865476)
        density = jnp.exp(inner * inner * -0.5) * 0.3989422804014327
        acts[:, cols] = (inner * cdf).astype(BF16)
        back_pre = (back * (cdf + inner * density)).astype(BF16)
        backs[:, cols] = back_pre
        bias_grad[:, cols] = jnp.sum(back_pre.astype(F32), axis=0, keepdims=True)
        grad[:, cols] = dot_tn(n2s[...], back_pre).astype(BF16)
    outs = pieces_out(meta, grad, pl.ds(0, hidden), keep, send, out_sems, 0)
    outs.append(begin(acts, acts_out, out_sems.at[len(outs)]))
    small[...] = dot_nt(backs[halves[1]], w0[...]).astype(BF16)
    outs.append(begin(small, back_far, out_sems.at[len(outs)]))
    big[...] = dot_nt(backs[halves[0]], w0[...])
    outs.append(begin(big, back_own, out_sems.at[len(outs)]))
    finish(outs)


def hidden_back(meta, n2a, n2b, dma, dmb, bias, ins0, ins1):
    (refs0, bases0), (refs1, bases1) = zip(*ins0), zip(*ins1)
    width, hidden = n2a.shape[-1], bias.shape[-1]
    one = (2 * TOK, width)
    tall = pltpu.VMEM((4 * TOK, width), BF16)
    wide = pltpu.VMEM((width, hidden), BF16)
    return pl.pallas_call(
        partial(hidden_back_kernel, bases0, bases1),
        out_shape=[shape((1, hidden), F32)]
        + [shape((width // 2, hidden), BF16)] * 2
        + [shape(one, F32), shape(one, BF16), shape((4 * TOK, hidden), BF16)],
        in_specs=[SMEM] + [HBM] * 4 + [WHOLE] + [HBM] * (2 * len(refs0)),
        out_specs=[WHOLE] + [HBM] * 5,
        scratch_shapes=[
            wide,
            wide,
            tall,
            tall,
            pltpu.VMEM((4 * TOK, hidden), BF16),
            pltpu.VMEM((4 * TOK, hidden), BF16),
            wide,
            pltpu.VMEM(one, F32),
            pltpu.VMEM(one, BF16),
            pltpu.SemaphoreType.DMA((2 * PIECES + 4,)),
            pltpu.SemaphoreType.DMA((PIECES + 3,)),
        ],
        compiler_params=params(),
        cost_estimate=COST,
        name="hidden_back",
    )(meta, n2a, n2b, dma, dmb, bias, *refs0, *refs1)


def hidden_out_kernel(bases, meta, acts_in, *refs):
    count = len(bases)
    ins, (own, far) = list(zip(refs[:count], bases)), refs[count : count + 2]
    w1, acts, big, small, sems, out_sems = refs[count + 2 :]
    copies = [begin(acts_in, acts, sems.at[PIECES])]
    copies += pieces_in(meta, 0, ins, 0, w1, sems, 0)
    finish(copies)
    big[...] = dot_nt(acts[: 2 * TOK], w1[...])
    outs = [begin(big, own, out_sems.at[0])]
    small[...] = dot_nt(acts[2 * TOK :], w1[...]).astype(BF16)
    outs.append(begin(small, far, out_sems.at[1]))
    finish(outs)


def hidden_out(meta, acts, width, ins):
    refs, bases = zip(*ins)
    hidden = acts.shape[1]
    one = (2 * TOK, width)
    return pl.pallas_call(
        partial(hidden_out_kernel, bases),
        out_shape=[shape(one, F32), shape(one, BF16)],
        in_specs=[SMEM] + [HBM] * (1 + len(refs)),
        out_specs=[HBM] * 2,
        scratch_shapes=[
            pltpu.VMEM((width, hidden), BF16),
            pltpu.VMEM(acts.shape, BF16),
            pltpu.VMEM(one, F32),
            pltpu.VMEM(one, BF16),
            pltpu.SemaphoreType.DMA((PIECES + 1,)),
            pltpu.SemaphoreType.DMA((2,)),
        ],
        compiler_params=params(),
        cost_estimate=COST,
        name="hidden_out",
    )(meta, acts, *refs)


def unrelative(grads):
    out = []
    for row in range(WIN):
        slab = grads[row * SIDE : (row + 1) * SIDE]
        down = pltpu.roll(slab, row, 1) if row else slab
        across = pltpu.roll(slab, 0, 1, stride=1, stride_axis=0)
        out.append(jnp.where(lanes(SIDE) < 32, down, across))
    return jnp.concatenate(out, axis=0)


def attend_back_kernel(before, count, meta, vecs, gather, table, q, k, v, p, weights, att, n1, *refs):
    start, parts = sum(before), len(before)
    first, last = start == 0, start + count == PAIRS
    if first:
        back_own, back_far, x1, dm = refs[:4]
        norm_sums, bias_sums, table_grad, mine, theirs, dqkv_out, dx1, da = refs[4:12]
        refs = refs[12:]
        owns, fars, x1s, dms, dx1s = refs[-5:]
        refs = refs[:-5]
    else:
        da, refs = refs[0], refs[1:]
        if last:
            earlier, tok, dx1, *changes = refs[:4], *refs[4 : 6 + parts]
            flat, mine, theirs, result = refs[6 + parts : 10 + parts]
            refs = refs[10 + parts :]
            bias_sums, wqkv, toks, dx1s, results, *changed = refs[-5 - parts :]
            refs = refs[: -5 - parts]
        else:
            bias_sums, table_grad, mine, theirs, dqkv_out = refs[:5]
            refs = refs[5:]
    das, wproj, atts, n1s, qs, ks, vs, ps, dat, dqkv, grads, sems, out_sems = refs
    core = meta[64]
    width, cols_here = das.shape[-1], qs.shape[-1]
    rows = width // PIECES
    columns = pl.ds(start * LANES, cols_here)
    tokens = (2 * TOK, width)
    early = []
    if first:
        early = [(back_own, owns), (back_far, fars), (x1, x1s), (dm, dms)]
    else:
        early = [(da, das)]
    early = [begin(ref, dest, sems.at[at]) for at, (ref, dest) in enumerate(early)]
    half, here = columns_of(3, width)
    wait_proj = begin(weights.at[half, columns, here], wproj, sems.at[4])
    wait_att = begin(att, atts, sems.at[5])
    wait_v = begin(v.at[:, :, columns], vs, sems.at[6])
    wait_p = []
    for window in range(2):
        for pair in range(count):
            heads = pl.ds(2 * (start + pair), 2)
            wait_p.append(
                begin(p.at[window, heads], ps.at[window, pl.ds(2 * pair, 2)], sems.at[10 + len(wait_p)])
            )
        if window == 0:
            wait_qk = [
                begin(ref.at[:, :, columns], dest, sems.at[7 + at])
                for at, (ref, dest) in enumerate(((q, qs), (k, ks)))
            ]
    wait_n1 = begin(n1, n1s, sems.at[9])
    if last:
        at = 10 + 2 * count
        ends = [begin(tok, toks, sems.at[at]), begin(dx1, dx1s, sems.at[at + 1])]
        for mat in range(3):
            half, here = columns_of(mat, width)
            ends.append(begin(weights.at[half, :, here], wqkv.at[mat], sems.at[at + 2 + mat]))
        for part in range(parts):
            ends.append(begin(changes[part], changed[part], sems.at[at + 5 + part]))
    outs = []
    finish(early)
    if first:
        total = [jnp.zeros((1, width), F32) for _ in range(4)]
        for window in range(2):
            here = pl.ds(window * TOK, TOK)
            grad = owns[here] + fars[here].astype(F32)
            xhat, inverse = moments(x1s[window])
            out_grad = dms[window].astype(F32)
            dresid = out_grad + norm_back(grad, xhat, inverse, vecs[5:6])
            dx1s[window] = dresid
            rounded = dresid.astype(BF16)
            das[window] = rounded
            for slot, value in enumerate((rounded.astype(F32), grad * xhat, grad, out_grad)):
                total[slot] = total[slot] + jnp.sum(value, axis=0, keepdims=True)
        norm_sums[...] = jnp.concatenate(total, axis=0)
        outs.append(begin(dx1s, dx1, out_sems.at[2 * PIECES]))
        outs.append(begin(das, da, out_sems.at[2 * PIECES + 1]))
    wait_proj.wait()
    dat[...] = dot_nt(das[...].reshape(tokens), wproj[...]).astype(BF16).reshape(2, TOK, cols_here)

    def send(half):
        is_own = core == half
        at = jnp.where(is_own, 32, 48)
        for piece in range(PIECES):
            place = pl.multiple_of(meta[at + piece] * rows, rows)
            source, to = grads.at[half, pl.ds(place, rows), :], pl.ds(piece * rows, rows)
            sem = out_sems.at[half * PIECES + piece]
            copies = [pltpu.make_async_copy(source, ref.at[to, :], sem) for ref in (mine, theirs)]
            pl.when(is_own)(copies[0].start)
            pl.when(~is_own)(copies[1].start)
            outs.append(copies[0])

    wait_att.wait()
    made = dot_tn(atts[...].reshape(tokens), das[:, :, columns].reshape(2 * TOK, cols_here))
    grads[1, :, cols_here:] = made.astype(BF16)
    finish(wait_qk + [wait_v] + wait_p)
    place = lanes(TOK)
    table_sum = jnp.zeros((LANES, LANES), F32)
    for step in range(2 * count):
        window, pair = step // count, step % count
        cols = pl.ds(pair * LANES, LANES)
        q2, k2, v2, dat2 = (ref[window, :, cols] for ref in (qs, ks, vs, dat))
        q8 = (q2.astype(F32) * HDIM**-0.5).astype(BF16)
        k8 = (k2.astype(F32) * HDIM**-0.5).astype(BF16)
        dqs, dks, dvs, dts = [], [], [], []
        for half in range(2):
            soft = ps[window, 2 * pair + half]
            soft32 = soft.astype(F32)
            own_lanes = jnp.where(place // 64 == half, dat2.astype(F32), 0.0).astype(BF16)
            weighted = soft32 * dot_nt(own_lanes, v2)
            ds = (weighted - soft32 * jnp.sum(weighted, axis=-1, keepdims=True)).astype(BF16)
            turned = dot(ds, gather[...]).astype(BF16).astype(F32)
            turned = unrelative(turned).astype(BF16)
            dqs.append(dot(ds, k8) + dot(turned, table[half]))
            dks.append(dot_tn(ds, q8))
            dvs.append(dot_tn(soft, dat2))
            dts.append(dot_tn(turned, q2))
        dqkv[0, window, :, cols] = jnp.where(place < 64, dqs[0], dqs[1]).astype(BF16)
        dqkv[1, window, :, cols] = jnp.where(place < 64, dks[0][:TOK], dks[1][:TOK]).astype(BF16)
        dqkv[2, window, :, cols] = jnp.where(place < 64, dvs[0][:TOK], dvs[1][:TOK]).astype(BF16)
        table_sum = table_sum + jnp.where(lanes(LANES) < 64, dts[0], dts[1])
    if not last:
        table_grad[...] = table_sum
    if not last:
        outs.append(begin(dqkv, dqkv_out, out_sems.at[2 * PIECES + 2]))
    wait_n1.wait()
    for mat in (2, 0, 1):
        change = dqkv[mat].reshape(2 * TOK, cols_here)
        made = dot_tn(n1s[...].reshape(tokens), change)
        grads[mat // 2, :, pl.ds(mat % 2 * cols_here, cols_here)] = made.astype(BF16)
        if mat != 0:
            send(mat // 2)
        if mat != 1:
            bias_sums[mat // 2 : mat // 2 + 1] = jnp.sum(change.astype(F32), axis=0, keepdims=True)
    if last:
        finish(ends)
        total = [jnp.zeros((1, width), F32) for _ in range(2)]
        for window in range(2):
            grad = jnp.zeros((TOK, width), F32)
            at = 0
            for change in (*changed, dqkv):
                here = pl.ds(at, change.shape[-1])
                for mat in range(3):
                    grad = grad + dot_nt(change[mat, window], wqkv[mat, :, here])
                at += change.shape[-1]
            xhat, inverse = moments(toks[window].astype(F32))
            results[window] = dx1s[window] + norm_back(grad, xhat, inverse, vecs[0:1])
            outs.append(begin(results.at[window], result.at[window], out_sems.at[2 * PIECES + window]))
            for slot, value in enumerate((grad * xhat, grad)):
                total[slot] = total[slot] + jnp.sum(value, axis=0, keepdims=True)
        norm2_sums, bias0, table0, hidden_sums = earlier
        pack(meta, total, (bias0, bias_sums), norm2_sums, table0[...] + table_sum, hidden_sums, flat)
    finish(outs)


def pack(meta, norm1, biases, norm2, table, hidden, flat):
    flat[...] = jnp.zeros_like(flat)
    parts = biases[0].shape[1] // LANES
    for row in range(8):
        for at in range(6):
            cols = pl.ds(at * LANES, LANES)
            if row < 2:
                value = norm1[row][:, at * LANES : (at + 1) * LANES]
            elif row < 4:
                ref, place = (biases[0], at) if at < parts else (biases[1], at - parts)
                value = ref[row - 2 : row - 1, pl.ds(place * LANES, LANES)]
            else:
                value = norm2[row - 4 : row - 3, cols]
            block = 6 * row + at
            flat[block // 4 : block // 4 + 1, pl.ds(block % 4 * LANES, LANES)] = value
    for block in range(hidden.shape[1] // LANES):
        value = hidden[:, pl.ds(block * LANES, LANES)]
        for core in range(2):
            at = 12 + 3 * core + block // 4
            flat[at : at + 1, pl.ds(block % 4 * LANES, LANES)] = jnp.where(meta[64] == core, value, 0.0)
    both = table[:64] + pltpu.roll(table[:64], HDIM, 1)
    for group in range(4):
        flat[24:40, pl.ds(group * LANES, LANES)] = both[16 * group : 16 * group + 16]


def unpacked(flat, core):
    vectors = flat[:12].reshape(8, -1)
    hidden = lax.dynamic_slice_in_dim(flat, 12 + 3 * core, 3).reshape(-1)
    table = flat[24:40].reshape(16, 4, LANES).transpose(1, 0, 2).reshape(64, LANES)[:, :HDIM]
    return vectors, hidden, table


def attend_back(before, count, meta, vecs, gather, table, q, k, v, p, weights, att, n1, ins):
    width, cols_here = q.shape[-1], count * LANES
    start, parts = sum(before), len(before)
    first, last = start == 0, start + count == PAIRS
    rows, keys = (2, TOK, width), (2, KEYS, cols_here)
    part, flat = (2, TOK, cols_here), (2 * TOK, width)
    heads = (2, 2 * count, TOK, KEYS)
    small = [shape((2, cols_here), F32), shape((LANES, LANES), F32)]
    large = [shape((width, 2 * cols_here), BF16)] * 2
    large.append(shape(rows, F32) if last else shape((3,) + part, BF16))
    if last:
        small = [shape((SMALL, 2 * cols_here), F32)]
    if first:
        small = [shape((4, width), F32)] + small
        large += [shape(rows, F32), shape(rows, BF16)]
    scratch = [rows, (cols_here, width), rows, rows, part, keys, keys, heads, part, (3,) + part]
    scratch.append((2, width, 2 * cols_here))
    scratch = [pltpu.VMEM(dims, BF16) for dims in scratch]
    scratch += [pltpu.SemaphoreType.DMA((15 + 2 * count + parts,)), pltpu.SemaphoreType.DMA((2 * PIECES + 3,))]
    if first:
        scratch += [
            pltpu.VMEM(flat, F32),
            pltpu.VMEM(flat, BF16),
            pltpu.VMEM(rows, F32),
            pltpu.VMEM(rows, BF16),
            pltpu.VMEM(rows, F32),
        ]
    if last:
        scratch += [
            pltpu.VMEM((2, cols_here), F32),
            pltpu.VMEM((3, width, width), BF16),
            pltpu.VMEM(rows, BF16),
            pltpu.VMEM(rows, F32),
            pltpu.VMEM(rows, F32),
        ] + [pltpu.VMEM((3, 2, TOK, size * LANES), BF16) for size in before]
    return pl.pallas_call(
        partial(attend_back_kernel, before, count),
        out_shape=small + large,
        in_specs=[SMEM] + [WHOLE] * 3 + [HBM] * 8 + [WHOLE if last and at < 4 else HBM for at in range(len(ins) - 1)],
        out_specs=[WHOLE] * len(small) + [HBM] * len(large),
        scratch_shapes=scratch,
        compiler_params=params(),
        cost_estimate=COST,
        name="attend_back",
    )(meta, vecs, gather, table, q, k, v, p, weights, att, n1, *ins)


def grid_of(count):
    return (4, 2, 2) if count == 16 else None


def turn(values, dims, moves):
    pairs = []
    for chip in range(dims[0] * dims[1] * dims[2]):
        for core, (axis, by) in enumerate(moves):
            place = list(np.unravel_index(chip, dims))
            place[axis] = (place[axis] + by) % dims[axis]
            pairs.append((2 * chip + core, 2 * int(np.ravel_multi_index(place, dims)) + core))
    return lax.ppermute(values, ("dp", "mp"), pairs)


ALONG_X, ALONG_Y = ((2, 1),) * 2, ((1, 1),) * 2
FIRST, SECOND = ((2, 1), (1, 1)), ((1, 1), (2, 1))


def along_z(values, dims):
    return [turn(values, dims, ((0, step),) * 2) for step in range(1, dims[0])]


def swap_z(values, dims, by):
    chips = dims[1] * dims[2]
    pairs = [(chip, (chip // chips ^ by) * chips + chip % chips) for chip in range(dims[0] * chips)]
    return lax.ppermute(values, "dp", pairs)


def other_core(values):
    return lax.ppermute(values, "mp", [(0, 1), (1, 0)])


def after(values, *others):
    return lax.optimization_barrier((values, *others))[0]


def stack_kernel(count, *refs):
    ins, out, sems = refs[:count], refs[count], refs[count + 1]
    copies, at = [], 0
    for ref in ins:
        rows = ref.shape[0]
        copies.append(begin(ref, out.at[pl.ds(at, rows)], sems.at[len(copies)]))
        at += rows
    finish(copies)


def stack(*parts):
    rows = sum(part.shape[0] for part in parts)
    return pl.pallas_call(
        partial(stack_kernel, len(parts)),
        out_shape=shape((rows, parts[0].shape[1]), BF16),
        in_specs=[HBM] * len(parts),
        out_specs=HBM,
        scratch_shapes=[pltpu.SemaphoreType.DMA((len(parts),))],
        compiler_params=params(),
        cost_estimate=COST,
        name="stack",
    )(*parts)


class Flow:
    def __init__(self, *came):
        self.came = list(came)


def meet(flows, *values):
    sizes = [len(flow.came) for flow in flows]
    found = list(lax.optimization_barrier((*(part for flow in flows for part in flow.came), *values)))
    for flow, size in zip(flows, sizes):
        flow.came, found = found[:size], found[size:]
    return found


def place_orders(dims, core):
    here = lax.axis_index("dp")
    z, y, x = here // (dims[1] * dims[2]), here // dims[2] % dims[1], here % dims[2]

    def chip(step, inner, outer):
        by_x = jnp.where(core == 0, inner, outer)
        by_y = jnp.where(core == 0, outer, inner)
        return ((z - step) % dims[0] * dims[1] + (y + by_y) % 2) * dims[2] + (x + by_x) % 2

    square = [(inner, outer) for outer in range(2) for inner in range(2)]
    gather = [chip(0, *at) for at in square]
    gather += [chip(step, *at) for at in square for step in range(1, dims[0])]
    scatter = [chip(step, *at) for at in square for step in range(dims[0])]
    return [jnp.stack(found).astype(jnp.int32) for found in (gather, scatter)]


def add(a, b):
    return a.astype(F32) + b.astype(F32)


def staged_kernel(kernel, starts, scalars, *refs):
    count = len(starts)
    meta, refs = refs[:scalars], refs[scalars:]
    total = len(refs) // 2
    held, sems = refs[total : 2 * total], refs[2 * total]
    copies = []
    for ref, start, dest in zip(refs, starts, held):
        if start is not None:
            ref = ref.at[pl.ds(start, dest.shape[0])]
        copies.append(begin(ref, dest, sems.at[len(copies)]))
    finish(copies)
    kernel(*meta, *held)
    finish([begin(held[at], refs[at], sems.at[at]) for at in range(count, total)])


def staged(kernel, outs, *ins, meta=None):
    ins = [part if isinstance(part, tuple) else (part, None, part.shape[0]) for part in ins]
    arrays, starts, rows = zip(*ins)
    scalars = () if meta is None else (meta,)
    held = [pltpu.VMEM((count, *array.shape[1:]), array.dtype) for array, count in zip(arrays, rows)]
    held += [pltpu.VMEM(out.shape, out.dtype) for out in outs]
    return pl.pallas_call(
        partial(staged_kernel, kernel, starts, len(scalars)),
        out_shape=outs,
        in_specs=[SMEM] * len(scalars) + [HBM] * len(arrays),
        out_specs=[HBM] * len(outs),
        scratch_shapes=held + [pltpu.SemaphoreType.DMA((len(held),))],
        compiler_params=params(),
        cost_estimate=COST,
        name="staged",
    )(*scalars, *arrays)


def core_rows_kernel(count, meta, *refs):
    *terms, own, far = refs
    half, width = own.shape[1:]
    one, two = (sum(ref[...].astype(F32) for ref in part) for part in (terms[:count], terms[count:]))
    cut, last = one.shape[1] // 2, two.shape[1] // 2
    for core in range(2):

        def put(ref, at=slice(core * half, (core + 1) * half)):
            for mat in range(2):
                ref[mat, :, :cut] = one[at, mat * cut : (mat + 1) * cut]
                ref[mat, :, cut:] = two[at, mat * last : (mat + 1) * last]

        pl.when(meta[64] == core)(partial(put, own))
        pl.when(meta[64] != core)(partial(put, far))


def last_rows_kernel(meta, near, came, qkv, proj):
    width = proj.shape[1]

    def put(qk, vp):
        qkv[:, :width] = qk[0]
        qkv[:, width : 2 * width] = qk[1]
        qkv[:, 2 * width :] = vp[0]
        proj[...] = vp[1]

    pl.when(meta[64] == 0)(partial(put, near, came))
    pl.when(meta[64] != 0)(partial(put, came, near))


class Scatter(Flow):
    def __init__(self, keep, far, dims):
        super().__init__(turn(far, dims, SECOND))
        self.keep, self.dims, self.sent = keep, dims, far

    def second(self):
        half = self.keep.shape[0] // 2
        send = add(self.keep[half:], self.came[0][half:]).astype(BF16)
        self.near = add(self.keep[:half], self.came[0][:half])
        self.sent = send
        self.came = [turn(send, self.dims, FIRST)]

    def third(self):
        near = self.near + self.came[0].astype(F32)
        rows = near.shape[0] // self.dims[0]
        self.near = near[:rows]
        sends = [near[step * rows : (step + 1) * rows].astype(BF16) for step in range(1, self.dims[0])]
        self.sent = sends[0]
        self.came = [
            turn(send, self.dims, ((0, self.dims[0] - step),) * 2) for step, send in enumerate(sends, 1)
        ]

    def halve(self):
        near = self.near + self.came[0].astype(F32)
        rows = near.shape[0] // self.dims[0]
        parts = [near[step * rows : (step + 1) * rows] for step in range(self.dims[0])]
        even = lax.axis_index("dp") // (self.dims[1] * self.dims[2]) % 2 == 0
        self.near = parts[0]
        self.beside = jnp.where(even, parts[3], parts[1])
        self.sent = jnp.concatenate([parts[2], jnp.where(even, parts[1], parts[3])], axis=0).astype(BF16)
        self.came = [swap_z(self.sent, self.dims, 2)]

    def quarter(self):
        rows = self.near.shape[0]
        came = self.came[0]
        self.near = self.near + came[:rows].astype(F32)
        self.sent = (self.beside + came[rows:].astype(F32)).astype(BF16)
        self.came = [swap_z(self.sent, self.dims, 1)]

    def last(self):
        return sum((part.astype(F32) for part in self.came), self.near)


def constants():
    key = np.arange(KEYS)
    row, col = key // SIDE, key % SIDE
    inside = (row < WIN) & (col < WIN)
    spread = np.zeros((KEYS, LANES), np.float32)
    gather = np.zeros((KEYS, LANES), np.float32)
    for place in key[inside]:
        for base in (0, 64):
            spread[place, base + WIN - 1 + row[place]] = 1.0
            spread[place, base + 32 + WIN - 1 + col[place]] = 1.0
        gather[place, WIN - 1 - row[place]] = 1.0
        gather[place, 32 + WIN - 1 - col[place]] = 1.0
    return spread, gather


def tables(rel_pos_h, rel_pos_w):
    count = rel_pos_h.shape[0]
    gap = jnp.zeros((32 - count, HDIM), BF16)
    turned = jnp.concatenate([rel_pos_h[::-1], gap, rel_pos_w[::-1], gap], axis=0)
    turned = jnp.concatenate([turned, turned], axis=0).T
    none = jnp.zeros_like(turned)
    forward = jnp.concatenate(
        [jnp.concatenate([turned, none], axis=0), jnp.concatenate([none, turned], axis=0)], axis=1
    )
    straight = jnp.concatenate([rel_pos_h, gap, rel_pos_w, gap], axis=0)
    straight = jnp.concatenate([straight, jnp.zeros_like(straight)], axis=0)
    none = jnp.zeros_like(straight)
    backward = jnp.stack(
        [
            jnp.concatenate([straight, none], axis=1),
            jnp.concatenate([none, straight], axis=1),
        ]
    )
    return forward, backward


def padded(values):
    images, rows, _, width = values.shape
    values = jnp.pad(values, ((0, 0), (0, 0), (0, SIDE - WIN), (0, 0)))
    return values.reshape(images, rows * SIDE, width)


def unpadded(values):
    images, _, width = values.shape
    return values.reshape(images, WIN, SIDE, width)[:, :, :WIN]


def local(
    patches,
    norm1_gain,
    norm1_bias,
    qkv_weight,
    qv_bias,
    rel_pos_h,
    rel_pos_w,
    proj_weight,
    proj_bias,
    norm2_gain,
    norm2_bias,
    fc1_weight,
    fc1_bias,
    fc2_weight,
    fc2_bias,
    heights,
    widths,
    out_grad,
):
    width = patches.shape[-1]
    dims = grid_of(lax.axis_size("dp"))
    core = lax.axis_index("mp")
    is_first = core == 0
    spread, gather = constants()

    def prepare(patches, out_grad, heights, rel_pos_h, rel_pos_w):
        if dims is None:
            orders = [jnp.tile(jnp.arange(PIECES, dtype=jnp.int32), 4)]
        else:
            own, far = place_orders(dims, core), place_orders(dims, 1 - core)
            orders = [own[0], far[0], own[1], far[1]]
        meta = jnp.concatenate(
            orders + [core.astype(jnp.int32)[None], heights, widths, jnp.zeros((11,), jnp.int32)]
        )
        row_index = core * WIN + jnp.arange(WIN)
        valid = (row_index[None, :, None] < heights[:, None, None]) & (
            jnp.arange(WIN)[None, None, :] < widths[:, None, None]
        )
        dm = padded(jnp.where(valid[..., None], out_grad, jnp.zeros_like(out_grad)))
        return padded(patches), dm, meta, *tables(rel_pos_h, rel_pos_w)

    wanted = (patches, out_grad, heights, rel_pos_h, rel_pos_w)
    vectors = (norm1_gain, norm1_bias, qv_bias[0], qv_bias[1], proj_bias, norm2_gain, norm2_bias, fc2_bias)
    small = jnp.pad(jnp.stack(vectors, axis=1), ((0, 0), (0, LANES - len(vectors))))
    qk = jnp.concatenate([qkv_weight[:, :width], small, qkv_weight[:, width : 2 * width]], axis=1)
    vp = jnp.concatenate([qkv_weight[:, 2 * width :], small, proj_weight], axis=1)
    if dims is None:
        qk = lax.all_gather(qk, ("dp", "mp"), axis=0, tiled=True)
        vp = lax.all_gather(vp, ("dp", "mp"), axis=0, tiled=True)
        attend_own = [jnp.where(is_first, qk, vp)]
        attend_far = [jnp.where(is_first, vp, qk)]
        tok, dm, meta, table, table_back = prepare(*wanted)
        hidden_in = tuple(
            ((lax.all_gather(part, "dp", axis=0, tiled=True), 0),) for part in (fc1_weight, fc2_weight.T)
        )
    else:
        fc1, fc2 = fc1_weight, fc2_weight.T
        came = other_core(jnp.where(is_first, vp, qk))
        near = jnp.where(is_first, qk, vp)
        block = jnp.concatenate(
            [jnp.where(is_first, near, came), jnp.where(is_first, came, near)], axis=0
        )
        attend_size, size = block.shape[1], fc1.shape[1]
        tok, dm, meta, table, table_back = prepare(*meet([], *wanted, block)[:5])
        own = jnp.concatenate([block, fc1, fc2], axis=1)
        attend_z, beside = Flow(*along_z(block, dims)), Flow(turn(own, dims, FIRST))
        fc1, fc2, tok, dm, table, table_back, meta = meet(
            [attend_z, beside], fc1, fc2, tok, dm, table, table_back, meta
        )

        attend_z = stack(*attend_z.came)
        z_beside = Flow(turn(attend_z, dims, FIRST))
        own = stack(own, *beside.came)
        over = Flow(turn(own, dims, SECOND))
        fc1_z = Flow(*along_z(after(fc1, own), dims))
        (fc2,) = meet([over, z_beside, fc1_z], fc2)

        over = over.came[0]
        attend_z = stack(attend_z, *z_beside.came)
        z_over = Flow(turn(attend_z, dims, SECOND))
        fc1_z = stack(after(fc1_z.came[0], attend_z), *fc1_z.came[1:])
        fc1_beside = Flow(turn(fc1_z, dims, FIRST))
        fc2_z = Flow(*along_z(after(fc2, fc1_z), dims))
        own_attend = jnp.concatenate([own[:, :attend_size], over[:, :attend_size]], axis=0)
        own_attend, attend_z = meet([z_over, fc1_beside, fc2_z], own_attend, attend_z)

        z_over = z_over.came[0]
        far = Flow(*(other_core(part) for part in (own_attend, attend_z, z_over)))
        fc1_z = stack(fc1_z, *fc1_beside.came)
        fc1_over = Flow(turn(fc1_z, dims, SECOND))
        fc2_z = stack(*fc2_z.came)
        fc2_beside = Flow(turn(fc2_z, dims, FIRST))
        tok, fc1_z, fc2_z, dm = meet([far], tok, fc1_z, fc2_z, dm)
        dm_far = Flow(other_core(dm))
        attend_own, attend_far = [own, over, attend_z, z_over], far.came

    vecs, n1, q, k, v, p, att, weights, x1, n2 = attend(
        meta, tok, table, jnp.asarray(spread, BF16), attend_own, attend_far
    )
    n2_far = other_core(n2).reshape(-1, width)
    if dims is None:
        dm_far = other_core(dm)
    else:
        (n2,) = meet([fc1_over, fc2_beside, dm_far], n2)
        (dm_far,) = dm_far.came
        fc2_z = stack(fc2_z, *fc2_beside.came)
        fc2_over = turn(fc2_z, dims, SECOND)
    dm_flat, dm_far = dm.reshape(-1, width), dm_far.reshape(-1, width)
    n2 = n2.reshape(-1, width)
    bias = fc1_bias[None].astype(F32)
    if dims is not None:
        n2 = after(n2, fc2_z)
        hidden_in = [
            ((own, attend_size), (over, attend_size), (fc1_z, 0), (*fc1_over.came, 0)),
            ((own, attend_size + size), (over, attend_size + size), (fc2_z, 0), (fc2_over, 0)),
        ]
    fc2_part = hidden_fwd(meta, n2, n2_far, dm_flat, dm_far, bias, hidden_in[0])
    if dims is not None:
        fc2_part = meet([], *fc2_part, fc2_over)[:2]
        fc2_sum = Scatter(*fc2_part, dims)
    fc1_bias_part, *fc1_part, back_own, back_far, acts = hidden_back(
        meta, n2, n2_far, dm_flat, dm_far, bias, *hidden_in
    )
    back_far = other_core(back_far)
    if dims is not None:
        fc1_part = meet([fc2_sum], *fc1_part)
        fc2_sum.second()
        fc1_sum = Scatter(*fc1_part, dims)
        back_own = after(back_own, fc2_sum.sent)

    shared = (meta, vecs, jnp.asarray(gather, BF16), table_back, q, k, v, p, weights, att, n1)
    half = width // 2
    def block_of(out_own, out_far):
        branch = add(out_own, out_far).reshape(x1.shape) + vecs[7]
        row_index = core * WIN + jnp.arange(WIN)
        valid = (row_index[None, :, None] < heights[:, None, None]) & (
            jnp.arange(WIN)[None, None, :] < widths[:, None, None]
        )
        return jnp.where(valid[..., None], unpadded(x1 + branch), 0.0).astype(BF16)

    def core_rows(wholes):
        whole = jnp.stack(
            [
                jnp.concatenate([part.reshape(part.shape[0], 2, -1)[:, at] for part in wholes], axis=1)
                for at in range(2)
            ]
        )
        rows = whole.shape[1] // 2
        cuts = whole[:, :rows], whole[:, rows:]
        return jnp.where(is_first, *cuts), jnp.where(is_first, *cuts[::-1])

    count0, count1 = BACK_PARTS
    sums2, bias0, table0, mine0, theirs0, change, dx1, da = attend_back(
        (), count0, *shared, (back_own, back_far, x1, dm)
    )
    if dims is not None:
        da, mine0, theirs0 = meet([fc2_sum], da, mine0, theirs0)
        came0 = other_core(theirs0)
        da, mine0 = meet([fc1_sum, fc2_sum], da, mine0)
        fc2_sum.third()
        fc1_sum.second()
        both = add(mine0, came0).astype(BF16)
        first = Scatter(both[:half], both[half:], dims)
        da = after(da, both)
    flat, mine, theirs, result = attend_back(
        (count0,), count1, *shared, (da, sums2, bias0, table0, fc1_bias_part, tok, dx1, change)
    )
    if dims is None:
        out_own, out_far = hidden_out(meta, acts, width, hidden_in[1])
        result, block_out = unpadded(result), block_of(out_own, other_core(out_far))
        fc1_sum, fc2_sum = (
            lax.psum_scatter(
                jnp.concatenate(parts, axis=0).astype(F32), "dp", scatter_dimension=0, tiled=True
            )
            for parts in (fc1_part, fc2_part)
        )
        wholes = [
            lax.psum_scatter(add(own, other_core(far)), "dp", scatter_dimension=0, tiled=True)
            for own, far in ((mine0, theirs0), (mine, theirs))
        ]
        near, far = core_rows(wholes)
        came = other_core(far)
        flat = lax.psum(flat, ("dp", "mp"))
    else:
        came, flat_came = Flow(other_core(theirs)), Flow(other_core(flat))
        mine, flat, acts, result = meet([fc2_sum, fc1_sum, first], mine, flat, acts, result)
        first.second()
        fc1_sum.halve()
        mine, flat, acts = meet([came, flat_came, first], mine, flat, acts)
        both = add(mine, came.came[0]).astype(BF16)
        second = Scatter(both[:half], both[half:], dims)
        flat = flat + flat_came.came[0]
        flat_came = Flow(turn(flat, dims, SECOND))
        first.halve()
        acts = after(acts, first.sent, second.sent)
        out_own, out_far = hidden_out(meta, acts, width, hidden_in[1])
        flat, result, out_far = meet([flat_came, second, fc1_sum], flat, result, out_far)
        late = Flow(other_core(out_far))
        flat = flat + flat_came.came[0]
        flat_came = Flow(turn(flat, dims, FIRST))
        second.second()
        fc1_sum.quarter()
        fc2_sum = fc2_sum.last()
        result = unpadded(result)
        flat, fc2_sum, result = meet([flat_came, first, second, fc1_sum, late], flat, fc2_sum, result)
        flat = flat + flat_came.came[0]
        flat_came = Flow(swap_z(flat, dims, 2))
        second.third()
        first.quarter()
        fc1_sum.near, late.came[0] = meet([], fc1_sum.near, late.came[0], second.sent, first.sent)[:2]
        fc1_sum = fc1_sum.last()
        block_out = block_of(out_own, late.came[0])
        flat, fc1_sum, block_out = meet([flat_came, second, first], flat, fc1_sum, block_out)

        share = shape((2, width // len(FIRST) // dims[0] // dims[1] // dims[2], width), F32)
        near, far = staged(
            partial(core_rows_kernel, 2), [share, share], first.near, *first.came, second.near, *second.came, meta=meta
        )
        came = other_core(far)
        flat = flat + flat_came.came[0]
        flat_came = swap_z(flat, dims, 1)
        flat = flat + after(flat_came, far)
    rows = near.shape[1]
    outs = [shape((rows, 3 * width), F32), shape((rows, width), F32)]
    qkv_grad, proj_grad = staged(last_rows_kernel, outs, near, came, meta=meta)
    vec_sums, fc1_bias_grad, rel = unpacked(flat, core)
    share = norm1_gain.shape[0]
    device = lax.axis_index("dp") * 2 + core
    mine = lax.dynamic_slice_in_dim(vec_sums, device * share, share, axis=1)
    rels = rel_pos_h.shape[0]
    return (
        block_out,
        result,
        mine[0],
        mine[1],
        qkv_grad,
        mine[2:4],
        rel[:rels],
        rel[32 : 32 + rels],
        proj_grad,
        mine[4],
        mine[5],
        mine[6],
        fc1_sum,
        fc1_bias_grad,
        fc2_sum.T,
        mine[7],
    )


def solution(mesh):
    return jax.shard_map(
        local,
        mesh=mesh,
        in_specs=(
            P("dp", "mp", None, None),
            P(("dp", "mp")),
            P(("dp", "mp")),
            P(("dp", "mp"), None),
            P(None, ("dp", "mp")),
            P(),
            P(),
            P(("dp", "mp"), None),
            P(("dp", "mp")),
            P(("dp", "mp")),
            P(("dp", "mp")),
            P("dp", "mp"),
            P("mp"),
            P("mp", "dp"),
            P(("dp", "mp")),
            P("dp"),
            P("dp"),
            P("dp", "mp", None, None),
        ),
        out_specs=(
            P("dp", "mp", None, None),
            P("dp", "mp", None, None),
            P(("dp", "mp")),
            P(("dp", "mp")),
            P(("dp", "mp"), None),
            P(None, ("dp", "mp")),
            P(),
            P(),
            P(("dp", "mp"), None),
            P(("dp", "mp")),
            P(("dp", "mp")),
            P(("dp", "mp")),
            P("dp", "mp"),
            P("mp"),
            P("mp", "dp"),
            P(("dp", "mp")),
        ),
        check_vma=False,
    )
```

```python
from functools import partial

import jax
import jax.numpy as jnp
import numpy as np
from jax import lax
from jax.experimental import pallas as pl
from jax.experimental.pallas import tpu as pltpu
from jax.sharding import PartitionSpec as P

HEADS = 12
HDIM = 64
LANES = 128
PAIRS = HEADS // 2
WIN = 14
SIDE = 16
TOK = WIN * SIDE
KEYS = 256
PIECES = 16
EPSILON = 1e-06
MASKED_SCORE = -1e30
MASK_LANE = 60
SMALL = 48
CHUNK = 512
BACK_PARTS = (4, 2)
F32 = jnp.float32
BF16 = jnp.bfloat16
SMEM = pl.BlockSpec(memory_space=pltpu.SMEM)
HBM = pl.BlockSpec(memory_space=pl.ANY)
WHOLE = pl.BlockSpec(memory_space=pltpu.VMEM)
VMEM_BYTES = 52 * 2**20
COST = pl.CostEstimate(flops=1000, bytes_accessed=1000, transcendentals=0)


def params():
    return pltpu.CompilerParams(vmem_limit_bytes=VMEM_BYTES)


def shape(dims, dtype):
    return jax.ShapeDtypeStruct(dims, dtype)


def dot(a, b):
    return jnp.dot(a, b, preferred_element_type=F32)


def dot_nt(a, b):
    return lax.dot_general(a, b, (((1,), (1,)), ((), ())), preferred_element_type=F32)


def dot_tn(a, b):
    return lax.dot_general(a, b, (((0,), (0,)), ((), ())), preferred_element_type=F32)


def lanes(rows):
    return lax.broadcasted_iota(jnp.int32, (rows, LANES), 1)


def moments(values):
    centered = values - jnp.mean(values, axis=-1, keepdims=True)
    inverse = lax.rsqrt(jnp.mean(centered * centered, axis=-1, keepdims=True) + EPSILON)
    return centered * inverse, inverse


def norm_back(grad, xhat, inverse, gain):
    scaled = grad * gain
    first = jnp.mean(scaled, axis=-1, keepdims=True)
    second = jnp.mean(scaled * xhat, axis=-1, keepdims=True)
    return inverse * (scaled - first - xhat * second)


def begin(source, dest, sem):
    copy = pltpu.make_async_copy(source, dest, sem)
    copy.start()
    return copy


def finish(copies):
    for copy in copies:
        copy.wait()


def pieces_in(meta, at, ins, start, dest, sems, first):
    rows, cols = dest.shape[0] // PIECES, dest.shape[1]
    copies = []
    for ref, base in ins:
        for part in range(ref.shape[0] // rows):
            place = pl.multiple_of(meta[at + len(copies)] * rows, rows)
            source = ref.at[pl.ds(part * rows, rows), pl.ds(base + start, cols)]
            copies.append(begin(source, dest.at[pl.ds(place, rows), :], sems.at[first + len(copies)]))
    return copies


def row_valid(meta, core, window, rows, width):
    place = lax.broadcasted_iota(jnp.int32, (rows, width), 0)
    row, col = place // SIDE, place % SIDE
    inside = (row < WIN) & (col < WIN)
    return inside & (core * WIN + row < meta[65 + window]) & (col < meta[67 + window])


def relative(turned):
    out = []
    for row in range(WIN):
        slab = turned[row * SIDE : (row + 1) * SIDE]
        down = pltpu.roll(slab, row, 1) if row else slab
        across = pltpu.roll(slab, 0, 1, stride=1, stride_axis=0)
        out.append(jnp.where(lanes(SIDE) % 64 < 32, down, across))
    return jnp.concatenate(out, axis=0)


def columns_of(mat, width, start=0, size=None):
    return mat // 2, pl.ds(mat % 2 * (width + LANES) + start, width if size is None else size)


def attend_kernel(count, total, meta, tok, table, spread, *refs):
    own, other = refs[:count], refs[count:total]
    vecs, n1, q, k, v, p, att, w_out, x1, n2 = refs[total : total + 10]
    toks, weights, aug, n1s, qs, ks, vs, ps, atts, x1s, n2s, sems, out_sems = refs[total + 10 :]
    width = toks.shape[-1]
    core = meta[64]
    copies = [begin(tok, toks, sems.at[2 * PIECES])]
    for found, at, half in ((own, 0, core), (other, 16, 1 - core)):
        found = [(ref, 0) for ref in found]
        copies += pieces_in(meta, at, found, 0, weights.at[half], sems, at)
    for window in range(2):
        valid = row_valid(meta, core, window, KEYS, LANES)
        aug[window] = jnp.where(
            (lanes(KEYS) == MASK_LANE) & ~valid, MASKED_SCORE, spread[...].astype(F32)
        ).astype(BF16)
        ks[window, TOK:] = jnp.zeros((KEYS - TOK, width), BF16)
        vs[window, TOK:] = jnp.zeros((KEYS - TOK, width), BF16)
    copies[0].wait()
    tokens = toks[...].reshape(2 * TOK, width).astype(F32)
    xhat, _ = moments(tokens)
    finish(copies[1:])
    outs = [begin(weights, w_out, out_sems.at[0])]
    vecs[...] = weights[0, :, width : width + LANES].astype(F32).T[:8]
    normed = (xhat * vecs[0:1] + vecs[1:2]).astype(BF16)
    n1s[...] = normed.reshape(2, TOK, width)
    outs.append(begin(n1s, n1, out_sems.at[1]))
    for mat, (made_in, dest) in enumerate(((qs, q), (ks, k), (vs, v))):
        for start in range(0, width, 256):
            cols = pl.ds(start, 256)
            half, here = columns_of(mat, width, start, 256)
            made = dot(normed, weights[half, :, here])
            if mat != 1:
                made = made + vecs[2 + mat // 2 : 3 + mat // 2, cols]
            made = made.astype(BF16)
            made_in[0, :TOK, cols] = made[:TOK]
            made_in[1, :TOK, cols] = made[TOK:]
        outs.append(begin(made_in, dest, out_sems.at[2 + mat]))

    place = lanes(TOK)
    for step in range(2 * PAIRS):
        window, pair = step // PAIRS, step % PAIRS
        cols = pl.ds(pair * LANES, LANES)
        q2, k2, v2 = qs[window, :, cols], ks[window, :, cols], vs[window, :, cols]
        turned = dot(q2, table[...])
        keys_aug = jnp.concatenate([k2, aug[window]], axis=1)
        parts = []
        for half in range(2):
            rel = relative(turned[:, half * LANES : (half + 1) * LANES])
            high = rel.astype(BF16).astype(F32)
            rel = jnp.where(place < 64, high, rel - high)
            rel = jnp.where(place == MASK_LANE, 1.0, rel).astype(BF16)
            mine = jnp.where(place // 64 == half, q2.astype(F32) * HDIM**-0.5, 0.0).astype(BF16)
            scores = dot_nt(jnp.concatenate([mine, rel], axis=1), keys_aug)
            terms = jnp.exp(scores - jnp.max(scores, axis=-1, keepdims=True))
            soft = terms * (1.0 / jnp.sum(terms, axis=-1, keepdims=True))
            soft = soft.astype(BF16)
            ps[window, 2 * pair + half] = soft
            parts.append(dot(soft, v2))
        atts[window, :, cols] = jnp.where(place < 64, parts[0], parts[1]).astype(BF16)
        heads = pl.ds(2 * pair, 2)
        outs.append(begin(ps.at[window, heads], p.at[window, heads], out_sems.at[len(outs)]))
    outs.append(begin(atts, att, out_sems.at[len(outs)]))
    half, here = columns_of(3, width)
    for window in range(2):
        resid = toks[window].astype(F32) + (dot(atts[window], weights[half, :, here]) + vecs[4:5])
        x1s[window] = resid
        xhat, _ = moments(resid)
        n2s[window] = (xhat * vecs[5:6] + vecs[6:7]).astype(BF16)
        outs.append(begin(x1s.at[window], x1.at[window], out_sems.at[len(outs)]))
        outs.append(begin(n2s.at[window], n2.at[window], out_sems.at[len(outs)]))
    finish(outs)


def attend(meta, tok, table, spread, own, other):
    count, total, width = len(own), len(own) + len(other), tok.shape[-1]
    rows, keys, heads = (2, TOK, width), (2, KEYS, width), (2, HEADS, TOK, KEYS)
    halves = (2, width, 2 * width + LANES)
    outs = [shape(dims, BF16) for dims in (rows, rows, keys, keys, heads, rows, halves)]
    outs += [shape(rows, F32), shape(rows, BF16)]
    scratch = (rows, halves, (2, KEYS, LANES), rows, rows, keys, keys, heads, rows)
    return pl.pallas_call(
        partial(attend_kernel, count, total),
        out_shape=[shape((8, width), F32)] + outs,
        in_specs=[SMEM, HBM, WHOLE, WHOLE] + [HBM] * total,
        out_specs=[WHOLE] + [HBM] * len(outs),
        scratch_shapes=[pltpu.VMEM(dims, BF16) for dims in scratch]
        + [
            pltpu.VMEM(rows, F32),
            pltpu.VMEM(rows, BF16),
            pltpu.SemaphoreType.DMA((2 * PIECES + 1,)),
            pltpu.SemaphoreType.DMA((10 + 2 * PAIRS,)),
        ],
        compiler_params=params(),
        cost_estimate=COST,
        name="attend",
    )(meta, tok, table, spread, *own, *other)


def pieces_out(meta, made, cols, keep, send, sems, first):
    rows = made.shape[0] // PIECES
    copies = []
    for piece in range(PIECES):
        dest = keep if piece < PIECES // 2 else send
        place = pl.multiple_of(meta[32 + piece] * rows, rows)
        at = pl.ds(piece % (PIECES // 2) * rows, rows)
        source = made.at[pl.ds(place, rows), cols]
        copies.append(begin(source, dest.at[at, cols], sems.at[first + len(copies)]))
    return copies


def hidden_fwd_kernel(bases, meta, n2a, n2b, dma, dmb, bias, *refs):
    count = len(bases)
    ins, (keep, send) = list(zip(refs[:count], bases)), refs[count : count + 2]
    w0, n2s, dms, grad, sems, out_sems = refs[count + 2 :]
    width, hidden = w0.shape
    at = PIECES
    copies = [begin(n2a, n2s.at[: 2 * TOK], sems.at[at]), begin(n2b, n2s.at[2 * TOK :], sems.at[at + 1])]
    copies += pieces_in(meta, 0, ins, 0, w0, sems, 0)
    dm_copies = [
        begin(dma, dms.at[: 2 * TOK], sems.at[at + 2]),
        begin(dmb, dms.at[2 * TOK :], sems.at[at + 3]),
    ]
    finish(copies)
    outs = []
    for start in range(0, hidden, CHUNK):
        cols = pl.ds(start, CHUNK)
        inner = dot(n2s[...], w0[:, cols]) + bias[:, cols]
        act = (inner * (0.5 + 0.5 * lax.erf(inner * 0.7071067811865476))).astype(BF16)
        if start == 0:
            finish(dm_copies)
        grad[:, cols] = dot_tn(dms[...], act).astype(BF16)
        if start + CHUNK == hidden - CHUNK:
            outs += pieces_out(meta, grad, pl.ds(0, hidden - CHUNK), keep, send, out_sems, 0)
    outs += pieces_out(meta, grad, pl.ds(hidden - CHUNK, CHUNK), keep, send, out_sems, PIECES)
    finish(outs)


def hidden_fwd(meta, n2a, n2b, dma, dmb, bias, ins):
    refs, bases = zip(*ins)
    width, hidden = n2a.shape[-1], bias.shape[-1]
    return pl.pallas_call(
        partial(hidden_fwd_kernel, bases),
        out_shape=[shape((width // 2, hidden), BF16)] * 2,
        in_specs=[SMEM] + [HBM] * 4 + [WHOLE] + [HBM] * len(refs),
        out_specs=[HBM] * 2,
        scratch_shapes=[
            pltpu.VMEM((width, hidden), BF16),
            pltpu.VMEM((4 * TOK, width), BF16),
            pltpu.VMEM((4 * TOK, width), BF16),
            pltpu.VMEM((width, hidden), BF16),
            pltpu.SemaphoreType.DMA((PIECES + 4,)),
            pltpu.SemaphoreType.DMA((2 * PIECES,)),
        ],
        compiler_params=params(),
        cost_estimate=COST,
        name="hidden_fwd",
    )(meta, n2a, n2b, dma, dmb, bias, *refs)


def hidden_back_kernel(bases0, bases1, meta, n2a, n2b, dma, dmb, bias, *refs):
    count = len(bases0)
    ins0, ins1 = list(zip(refs[:count], bases0)), list(zip(refs[count : 2 * count], bases1))
    refs = refs[2 * count :]
    bias_grad, keep, send, back_own, back_far, acts_out = refs[:6]
    w0, w1, n2s, dms, acts, backs, grad, big, small, sems, out_sems = refs[6:]
    width, hidden = w0.shape
    halves = (pl.ds(0, 2 * TOK), pl.ds(2 * TOK, 2 * TOK))
    at = 2 * PIECES
    copies = [begin(ref, n2s.at[half], sems.at[at + i]) for i, (ref, half) in enumerate(zip((n2a, n2b), halves))]
    copies += pieces_in(meta, 0, ins0, 0, w0, sems, 0)
    at += 2
    later = [begin(ref, dms.at[half], sems.at[at + i]) for i, (ref, half) in enumerate(zip((dma, dmb), halves))]
    later += pieces_in(meta, 0, ins1, 0, w1, sems, PIECES)
    finish(copies)
    outs = []
    for start in range(0, hidden, CHUNK):
        cols = pl.ds(start, CHUNK)
        inner = dot(n2s[...], w0[:, cols]) + bias[:, cols]
        if start == 0:
            finish(later)
        back = dot(dms[...], w1[:, cols])
        cdf = 0.5 + 0.5 * lax.erf(inner * 0.7071067811865476)
        density = jnp.exp(inner * inner * -0.5) * 0.3989422804014327
        acts[:, cols] = (inner * cdf).astype(BF16)
        back_pre = (back * (cdf + inner * density)).astype(BF16)
        backs[:, cols] = back_pre
        bias_grad[:, cols] = jnp.sum(back_pre.astype(F32), axis=0, keepdims=True)
        grad[:, cols] = dot_tn(n2s[...], back_pre).astype(BF16)
    outs = pieces_out(meta, grad, pl.ds(0, hidden), keep, send, out_sems, 0)
    outs.append(begin(acts, acts_out, out_sems.at[len(outs)]))
    small[...] = dot_nt(backs[halves[1]], w0[...]).astype(BF16)
    outs.append(begin(small, back_far, out_sems.at[len(outs)]))
    big[...] = dot_nt(backs[halves[0]], w0[...])
    outs.append(begin(big, back_own, out_sems.at[len(outs)]))
    finish(outs)


def hidden_back(meta, n2a, n2b, dma, dmb, bias, ins0, ins1):
    (refs0, bases0), (refs1, bases1) = zip(*ins0), zip(*ins1)
    width, hidden = n2a.shape[-1], bias.shape[-1]
    one = (2 * TOK, width)
    tall = pltpu.VMEM((4 * TOK, width), BF16)
    wide = pltpu.VMEM((width, hidden), BF16)
    return pl.pallas_call(
        partial(hidden_back_kernel, bases0, bases1),
        out_shape=[shape((1, hidden), F32)]
        + [shape((width // 2, hidden), BF16)] * 2
        + [shape(one, F32), shape(one, BF16), shape((4 * TOK, hidden), BF16)],
        in_specs=[SMEM] + [HBM] * 4 + [WHOLE] + [HBM] * (2 * len(refs0)),
        out_specs=[WHOLE] + [HBM] * 5,
        scratch_shapes=[
            wide,
            wide,
            tall,
            tall,
            pltpu.VMEM((4 * TOK, hidden), BF16),
            pltpu.VMEM((4 * TOK, hidden), BF16),
            wide,
            pltpu.VMEM(one, F32),
            pltpu.VMEM(one, BF16),
            pltpu.SemaphoreType.DMA((2 * PIECES + 4,)),
            pltpu.SemaphoreType.DMA((PIECES + 3,)),
        ],
        compiler_params=params(),
        cost_estimate=COST,
        name="hidden_back",
    )(meta, n2a, n2b, dma, dmb, bias, *refs0, *refs1)


def hidden_out_kernel(bases, meta, acts_in, *refs):
    count = len(bases)
    ins, (own, far) = list(zip(refs[:count], bases)), refs[count : count + 2]
    w1, acts, big, small, sems, out_sems = refs[count + 2 :]
    copies = [begin(acts_in, acts, sems.at[PIECES])]
    copies += pieces_in(meta, 0, ins, 0, w1, sems, 0)
    finish(copies)
    big[...] = dot_nt(acts[: 2 * TOK], w1[...])
    outs = [begin(big, own, out_sems.at[0])]
    small[...] = dot_nt(acts[2 * TOK :], w1[...]).astype(BF16)
    outs.append(begin(small, far, out_sems.at[1]))
    finish(outs)


def hidden_out(meta, acts, width, ins):
    refs, bases = zip(*ins)
    hidden = acts.shape[1]
    one = (2 * TOK, width)
    return pl.pallas_call(
        partial(hidden_out_kernel, bases),
        out_shape=[shape(one, F32), shape(one, BF16)],
        in_specs=[SMEM] + [HBM] * (1 + len(refs)),
        out_specs=[HBM] * 2,
        scratch_shapes=[
            pltpu.VMEM((width, hidden), BF16),
            pltpu.VMEM(acts.shape, BF16),
            pltpu.VMEM(one, F32),
            pltpu.VMEM(one, BF16),
            pltpu.SemaphoreType.DMA((PIECES + 1,)),
            pltpu.SemaphoreType.DMA((2,)),
        ],
        compiler_params=params(),
        cost_estimate=COST,
        name="hidden_out",
    )(meta, acts, *refs)


def unrelative(grads):
    out = []
    for row in range(WIN):
        slab = grads[row * SIDE : (row + 1) * SIDE]
        down = pltpu.roll(slab, row, 1) if row else slab
        across = pltpu.roll(slab, 0, 1, stride=1, stride_axis=0)
        out.append(jnp.where(lanes(SIDE) < 32, down, across))
    return jnp.concatenate(out, axis=0)


def attend_back_kernel(before, count, meta, vecs, gather, table, q, k, v, p, weights, att, n1, *refs):
    start, parts = sum(before), len(before)
    first, last = start == 0, start + count == PAIRS
    if first:
        back_own, back_far, x1, dm = refs[:4]
        norm_sums, bias_sums, table_grad, mine, theirs, dqkv_out, dx1, da = refs[4:12]
        refs = refs[12:]
        owns, fars, x1s, dms, dx1s = refs[-5:]
        refs = refs[:-5]
    else:
        da, refs = refs[0], refs[1:]
        if last:
            earlier, tok, dx1, *changes = refs[:4], *refs[4 : 6 + parts]
            flat, mine, theirs, result = refs[6 + parts : 10 + parts]
            refs = refs[10 + parts :]
            bias_sums, wqkv, toks, dx1s, results, *changed = refs[-5 - parts :]
            refs = refs[: -5 - parts]
        else:
            bias_sums, table_grad, mine, theirs, dqkv_out = refs[:5]
            refs = refs[5:]
    das, wproj, atts, n1s, qs, ks, vs, ps, dat, dqkv, grads, sems, out_sems = refs
    core = meta[64]
    width, cols_here = das.shape[-1], qs.shape[-1]
    rows = width // PIECES
    columns = pl.ds(start * LANES, cols_here)
    tokens = (2 * TOK, width)
    early = []
    if first:
        early = [(back_own, owns), (back_far, fars), (x1, x1s), (dm, dms)]
    else:
        early = [(da, das)]
    early = [begin(ref, dest, sems.at[at]) for at, (ref, dest) in enumerate(early)]
    half, here = columns_of(3, width)
    wait_proj = begin(weights.at[half, columns, here], wproj, sems.at[4])
    wait_att = begin(att, atts, sems.at[5])
    wait_v = begin(v.at[:, :, columns], vs, sems.at[6])
    wait_p = []
    for window in range(2):
        for pair in range(count):
            heads = pl.ds(2 * (start + pair), 2)
            wait_p.append(
                begin(p.at[window, heads], ps.at[window, pl.ds(2 * pair, 2)], sems.at[10 + len(wait_p)])
            )
        if window == 0:
            wait_qk = [
                begin(ref.at[:, :, columns], dest, sems.at[7 + at])
                for at, (ref, dest) in enumerate(((q, qs), (k, ks)))
            ]
    wait_n1 = begin(n1, n1s, sems.at[9])
    if last:
        at = 10 + 2 * count
        ends = [begin(tok, toks, sems.at[at]), begin(dx1, dx1s, sems.at[at + 1])]
        for mat in range(3):
            half, here = columns_of(mat, width)
            ends.append(begin(weights.at[half, :, here], wqkv.at[mat], sems.at[at + 2 + mat]))
        for part in range(parts):
            ends.append(begin(changes[part], changed[part], sems.at[at + 5 + part]))
    outs = []
    finish(early)
    if first:
        total = [jnp.zeros((1, width), F32) for _ in range(4)]
        for window in range(2):
            here = pl.ds(window * TOK, TOK)
            grad = owns[here] + fars[here].astype(F32)
            xhat, inverse = moments(x1s[window])
            out_grad = dms[window].astype(F32)
            dresid = out_grad + norm_back(grad, xhat, inverse, vecs[5:6])
            dx1s[window] = dresid
            rounded = dresid.astype(BF16)
            das[window] = rounded
            for slot, value in enumerate((rounded.astype(F32), grad * xhat, grad, out_grad)):
                total[slot] = total[slot] + jnp.sum(value, axis=0, keepdims=True)
        norm_sums[...] = jnp.concatenate(total, axis=0)
        outs.append(begin(dx1s, dx1, out_sems.at[2 * PIECES]))
        outs.append(begin(das, da, out_sems.at[2 * PIECES + 1]))
    wait_proj.wait()
    dat[...] = dot_nt(das[...].reshape(tokens), wproj[...]).astype(BF16).reshape(2, TOK, cols_here)

    def send(half):
        is_own = core == half
        at = jnp.where(is_own, 32, 48)
        for piece in range(PIECES):
            place = pl.multiple_of(meta[at + piece] * rows, rows)
            source, to = grads.at[half, pl.ds(place, rows), :], pl.ds(piece * rows, rows)
            sem = out_sems.at[half * PIECES + piece]
            copies = [pltpu.make_async_copy(source, ref.at[to, :], sem) for ref in (mine, theirs)]
            pl.when(is_own)(copies[0].start)
            pl.when(~is_own)(copies[1].start)
            outs.append(copies[0])

    wait_att.wait()
    made = dot_tn(atts[...].reshape(tokens), das[:, :, columns].reshape(2 * TOK, cols_here))
    grads[1, :, cols_here:] = made.astype(BF16)
    finish(wait_qk + [wait_v] + wait_p)
    place = lanes(TOK)
    table_sum = jnp.zeros((LANES, LANES), F32)
    for step in range(2 * count):
        window, pair = step // count, step % count
        cols = pl.ds(pair * LANES, LANES)
        q2, k2, v2, dat2 = (ref[window, :, cols] for ref in (qs, ks, vs, dat))
        q8 = (q2.astype(F32) * HDIM**-0.5).astype(BF16)
        k8 = (k2.astype(F32) * HDIM**-0.5).astype(BF16)
        dqs, dks, dvs, dts = [], [], [], []
        for half in range(2):
            soft = ps[window, 2 * pair + half]
            soft32 = soft.astype(F32)
            own_lanes = jnp.where(place // 64 == half, dat2.astype(F32), 0.0).astype(BF16)
            weighted = soft32 * dot_nt(own_lanes, v2)
            ds = (weighted - soft32 * jnp.sum(weighted, axis=-1, keepdims=True)).astype(BF16)
            turned = dot(ds, gather[...]).astype(BF16).astype(F32)
            turned = unrelative(turned).astype(BF16)
            dqs.append(dot(ds, k8) + dot(turned, table[half]))
            dks.append(dot_tn(ds, q8))
            dvs.append(dot_tn(soft, dat2))
            dts.append(dot_tn(turned, q2))
        dqkv[0, window, :, cols] = jnp.where(place < 64, dqs[0], dqs[1]).astype(BF16)
        dqkv[1, window, :, cols] = jnp.where(place < 64, dks[0][:TOK], dks[1][:TOK]).astype(BF16)
        dqkv[2, window, :, cols] = jnp.where(place < 64, dvs[0][:TOK], dvs[1][:TOK]).astype(BF16)
        table_sum = table_sum + jnp.where(lanes(LANES) < 64, dts[0], dts[1])
    if not last:
        table_grad[...] = table_sum
    if not last:
        outs.append(begin(dqkv, dqkv_out, out_sems.at[2 * PIECES + 2]))
    wait_n1.wait()
    for mat in (2, 0, 1):
        change = dqkv[mat].reshape(2 * TOK, cols_here)
        made = dot_tn(n1s[...].reshape(tokens), change)
        grads[mat // 2, :, pl.ds(mat % 2 * cols_here, cols_here)] = made.astype(BF16)
        if mat != 0:
            send(mat // 2)
        if mat != 1:
            bias_sums[mat // 2 : mat // 2 + 1] = jnp.sum(change.astype(F32), axis=0, keepdims=True)
    if last:
        finish(ends)
        total = [jnp.zeros((1, width), F32) for _ in range(2)]
        for window in range(2):
            grad = jnp.zeros((TOK, width), F32)
            at = 0
            for change in (*changed, dqkv):
                here = pl.ds(at, change.shape[-1])
                for mat in range(3):
                    grad = grad + dot_nt(change[mat, window], wqkv[mat, :, here])
                at += change.shape[-1]
            xhat, inverse = moments(toks[window].astype(F32))
            results[window] = dx1s[window] + norm_back(grad, xhat, inverse, vecs[0:1])
            outs.append(begin(results.at[window], result.at[window], out_sems.at[2 * PIECES + window]))
            for slot, value in enumerate((grad * xhat, grad)):
                total[slot] = total[slot] + jnp.sum(value, axis=0, keepdims=True)
        norm2_sums, bias0, table0, hidden_sums = earlier
        pack(meta, total, (bias0, bias_sums), norm2_sums, table0[...] + table_sum, hidden_sums, flat)
    finish(outs)


def pack(meta, norm1, biases, norm2, table, hidden, flat):
    flat[...] = jnp.zeros_like(flat)
    parts = biases[0].shape[1] // LANES
    for row in range(8):
        for at in range(6):
            cols = pl.ds(at * LANES, LANES)
            if row < 2:
                value = norm1[row][:, at * LANES : (at + 1) * LANES]
            elif row < 4:
                ref, place = (biases[0], at) if at < parts else (biases[1], at - parts)
                value = ref[row - 2 : row - 1, pl.ds(place * LANES, LANES)]
            else:
                value = norm2[row - 4 : row - 3, cols]
            block = 6 * row + at
            flat[block // 4 : block // 4 + 1, pl.ds(block % 4 * LANES, LANES)] = value
    for block in range(hidden.shape[1] // LANES):
        value = hidden[:, pl.ds(block * LANES, LANES)]
        for core in range(2):
            at = 12 + 3 * core + block // 4
            flat[at : at + 1, pl.ds(block % 4 * LANES, LANES)] = jnp.where(meta[64] == core, value, 0.0)
    both = table[:64] + pltpu.roll(table[:64], HDIM, 1)
    for group in range(4):
        flat[24:40, pl.ds(group * LANES, LANES)] = both[16 * group : 16 * group + 16]


def unpacked(flat, core):
    vectors = flat[:12].reshape(8, -1)
    hidden = lax.dynamic_slice_in_dim(flat, 12 + 3 * core, 3).reshape(-1)
    table = flat[24:40].reshape(16, 4, LANES).transpose(1, 0, 2).reshape(64, LANES)[:, :HDIM]
    return vectors, hidden, table


def attend_back(before, count, meta, vecs, gather, table, q, k, v, p, weights, att, n1, ins):
    width, cols_here = q.shape[-1], count * LANES
    start, parts = sum(before), len(before)
    first, last = start == 0, start + count == PAIRS
    rows, keys = (2, TOK, width), (2, KEYS, cols_here)
    part, flat = (2, TOK, cols_here), (2 * TOK, width)
    heads = (2, 2 * count, TOK, KEYS)
    small = [shape((2, cols_here), F32), shape((LANES, LANES), F32)]
    large = [shape((width, 2 * cols_here), BF16)] * 2
    large.append(shape(rows, F32) if last else shape((3,) + part, BF16))
    if last:
        small = [shape((SMALL, 2 * cols_here), F32)]
    if first:
        small = [shape((4, width), F32)] + small
        large += [shape(rows, F32), shape(rows, BF16)]
    scratch = [rows, (cols_here, width), rows, rows, part, keys, keys, heads, part, (3,) + part]
    scratch.append((2, width, 2 * cols_here))
    scratch = [pltpu.VMEM(dims, BF16) for dims in scratch]
    scratch += [pltpu.SemaphoreType.DMA((15 + 2 * count + parts,)), pltpu.SemaphoreType.DMA((2 * PIECES + 3,))]
    if first:
        scratch += [
            pltpu.VMEM(flat, F32),
            pltpu.VMEM(flat, BF16),
            pltpu.VMEM(rows, F32),
            pltpu.VMEM(rows, BF16),
            pltpu.VMEM(rows, F32),
        ]
    if last:
        scratch += [
            pltpu.VMEM((2, cols_here), F32),
            pltpu.VMEM((3, width, width), BF16),
            pltpu.VMEM(rows, BF16),
            pltpu.VMEM(rows, F32),
            pltpu.VMEM(rows, F32),
        ] + [pltpu.VMEM((3, 2, TOK, size * LANES), BF16) for size in before]
    return pl.pallas_call(
        partial(attend_back_kernel, before, count),
        out_shape=small + large,
        in_specs=[SMEM] + [WHOLE] * 3 + [HBM] * 8 + [WHOLE if last and at < 4 else HBM for at in range(len(ins) - 1)],
        out_specs=[WHOLE] * len(small) + [HBM] * len(large),
        scratch_shapes=scratch,
        compiler_params=params(),
        cost_estimate=COST,
        name="attend_back",
    )(meta, vecs, gather, table, q, k, v, p, weights, att, n1, *ins)


def grid_of(count):
    return (4, 2, 2) if count == 16 else None


def turn(values, dims, moves):
    pairs = []
    for chip in range(dims[0] * dims[1] * dims[2]):
        for core, (axis, by) in enumerate(moves):
            place = list(np.unravel_index(chip, dims))
            place[axis] = (place[axis] + by) % dims[axis]
            pairs.append((2 * chip + core, 2 * int(np.ravel_multi_index(place, dims)) + core))
    return lax.ppermute(values, ("dp", "mp"), pairs)


ALONG_X, ALONG_Y = ((2, 1),) * 2, ((1, 1),) * 2
FIRST, SECOND = ((2, 1), (1, 1)), ((1, 1), (2, 1))


def along_z(values, dims):
    return [turn(values, dims, ((0, step),) * 2) for step in range(1, dims[0])]


def swap_z(values, dims, by):
    chips = dims[1] * dims[2]
    pairs = [(chip, (chip // chips ^ by) * chips + chip % chips) for chip in range(dims[0] * chips)]
    return lax.ppermute(values, "dp", pairs)


def other_core(values):
    return lax.ppermute(values, "mp", [(0, 1), (1, 0)])


def after(values, *others):
    return lax.optimization_barrier((values, *others))[0]


def stack_kernel(count, *refs):
    ins, out, sems = refs[:count], refs[count], refs[count + 1]
    copies, at = [], 0
    for ref in ins:
        rows = ref.shape[0]
        copies.append(begin(ref, out.at[pl.ds(at, rows)], sems.at[len(copies)]))
        at += rows
    finish(copies)


def stack(*parts):
    rows = sum(part.shape[0] for part in parts)
    return pl.pallas_call(
        partial(stack_kernel, len(parts)),
        out_shape=shape((rows, parts[0].shape[1]), BF16),
        in_specs=[HBM] * len(parts),
        out_specs=HBM,
        scratch_shapes=[pltpu.SemaphoreType.DMA((len(parts),))],
        compiler_params=params(),
        cost_estimate=COST,
        name="stack",
    )(*parts)


class Flow:
    def __init__(self, *came):
        self.came = list(came)


def meet(flows, *values):
    sizes = [len(flow.came) for flow in flows]
    found = list(lax.optimization_barrier((*(part for flow in flows for part in flow.came), *values)))
    for flow, size in zip(flows, sizes):
        flow.came, found = found[:size], found[size:]
    return found


def place_orders(dims, core):
    here = lax.axis_index("dp")
    z, y, x = here // (dims[1] * dims[2]), here // dims[2] % dims[1], here % dims[2]

    def chip(step, inner, outer):
        by_x = jnp.where(core == 0, inner, outer)
        by_y = jnp.where(core == 0, outer, inner)
        return ((z - step) % dims[0] * dims[1] + (y + by_y) % 2) * dims[2] + (x + by_x) % 2

    square = [(inner, outer) for outer in range(2) for inner in range(2)]
    gather = [chip(0, *at) for at in square]
    gather += [chip(step, *at) for at in square for step in range(1, dims[0])]
    scatter = [chip(step, *at) for at in square for step in range(dims[0])]
    return [jnp.stack(found).astype(jnp.int32) for found in (gather, scatter)]


def add(a, b):
    return a.astype(F32) + b.astype(F32)


def staged_kernel(kernel, starts, scalars, *refs):
    count = len(starts)
    meta, refs = refs[:scalars], refs[scalars:]
    total = len(refs) // 2
    held, sems = refs[total : 2 * total], refs[2 * total]
    copies = []
    for ref, start, dest in zip(refs, starts, held):
        if start is not None:
            ref = ref.at[pl.ds(start, dest.shape[0])]
        copies.append(begin(ref, dest, sems.at[len(copies)]))
    finish(copies)
    kernel(*meta, *held)
    finish([begin(held[at], refs[at], sems.at[at]) for at in range(count, total)])


def staged(kernel, outs, *ins, meta=None):
    ins = [part if isinstance(part, tuple) else (part, None, part.shape[0]) for part in ins]
    arrays, starts, rows = zip(*ins)
    scalars = () if meta is None else (meta,)
    held = [pltpu.VMEM((count, *array.shape[1:]), array.dtype) for array, count in zip(arrays, rows)]
    held += [pltpu.VMEM(out.shape, out.dtype) for out in outs]
    return pl.pallas_call(
        partial(staged_kernel, kernel, starts, len(scalars)),
        out_shape=outs,
        in_specs=[SMEM] * len(scalars) + [HBM] * len(arrays),
        out_specs=[HBM] * len(outs),
        scratch_shapes=held + [pltpu.SemaphoreType.DMA((len(held),))],
        compiler_params=params(),
        cost_estimate=COST,
        name="staged",
    )(*scalars, *arrays)


def core_rows_kernel(count, meta, *refs):
    *terms, own, far = refs
    half, width = own.shape[1:]
    one, two = (sum(ref[...].astype(F32) for ref in part) for part in (terms[:count], terms[count:]))
    cut, last = one.shape[1] // 2, two.shape[1] // 2
    for core in range(2):

        def put(ref, at=slice(core * half, (core + 1) * half)):
            for mat in range(2):
                ref[mat, :, :cut] = one[at, mat * cut : (mat + 1) * cut]
                ref[mat, :, cut:] = two[at, mat * last : (mat + 1) * last]

        pl.when(meta[64] == core)(partial(put, own))
        pl.when(meta[64] != core)(partial(put, far))


def last_rows_kernel(meta, near, came, qkv, proj):
    width = proj.shape[1]

    def put(qk, vp):
        qkv[:, :width] = qk[0]
        qkv[:, width : 2 * width] = qk[1]
        qkv[:, 2 * width :] = vp[0]
        proj[...] = vp[1]

    pl.when(meta[64] == 0)(partial(put, near, came))
    pl.when(meta[64] != 0)(partial(put, came, near))


class Scatter(Flow):
    def __init__(self, keep, far, dims):
        super().__init__(turn(far, dims, SECOND))
        self.keep, self.dims, self.sent = keep, dims, far

    def second(self):
        half = self.keep.shape[0] // 2
        send = add(self.keep[half:], self.came[0][half:]).astype(BF16)
        self.near = add(self.keep[:half], self.came[0][:half])
        self.sent = send
        self.came = [turn(send, self.dims, FIRST)]

    def third(self):
        near = self.near + self.came[0].astype(F32)
        rows = near.shape[0] // self.dims[0]
        self.near = near[:rows]
        sends = [near[step * rows : (step + 1) * rows].astype(BF16) for step in range(1, self.dims[0])]
        self.sent = sends[0]
        self.came = [
            turn(send, self.dims, ((0, self.dims[0] - step),) * 2) for step, send in enumerate(sends, 1)
        ]

    def halve(self):
        near = self.near + self.came[0].astype(F32)
        rows = near.shape[0] // self.dims[0]
        parts = [near[step * rows : (step + 1) * rows] for step in range(self.dims[0])]
        even = lax.axis_index("dp") // (self.dims[1] * self.dims[2]) % 2 == 0
        self.near = parts[0]
        self.beside = jnp.where(even, parts[3], parts[1])
        self.sent = jnp.concatenate([parts[2], jnp.where(even, parts[1], parts[3])], axis=0).astype(BF16)
        self.came = [swap_z(self.sent, self.dims, 2)]

    def quarter(self):
        rows = self.near.shape[0]
        came = self.came[0]
        self.near = self.near + came[:rows].astype(F32)
        self.sent = (self.beside + came[rows:].astype(F32)).astype(BF16)
        self.came = [swap_z(self.sent, self.dims, 1)]

    def last(self):
        return sum((part.astype(F32) for part in self.came), self.near)


def constants():
    key = np.arange(KEYS)
    row, col = key // SIDE, key % SIDE
    inside = (row < WIN) & (col < WIN)
    spread = np.zeros((KEYS, LANES), np.float32)
    gather = np.zeros((KEYS, LANES), np.float32)
    for place in key[inside]:
        for base in (0, 64):
            spread[place, base + WIN - 1 + row[place]] = 1.0
            spread[place, base + 32 + WIN - 1 + col[place]] = 1.0
        gather[place, WIN - 1 - row[place]] = 1.0
        gather[place, 32 + WIN - 1 - col[place]] = 1.0
    return spread, gather


def tables(rel_pos_h, rel_pos_w):
    count = rel_pos_h.shape[0]
    gap = jnp.zeros((32 - count, HDIM), BF16)
    turned = jnp.concatenate([rel_pos_h[::-1], gap, rel_pos_w[::-1], gap], axis=0)
    turned = jnp.concatenate([turned, turned], axis=0).T
    none = jnp.zeros_like(turned)
    forward = jnp.concatenate(
        [jnp.concatenate([turned, none], axis=0), jnp.concatenate([none, turned], axis=0)], axis=1
    )
    straight = jnp.concatenate([rel_pos_h, gap, rel_pos_w, gap], axis=0)
    straight = jnp.concatenate([straight, jnp.zeros_like(straight)], axis=0)
    none = jnp.zeros_like(straight)
    backward = jnp.stack(
        [
            jnp.concatenate([straight, none], axis=1),
            jnp.concatenate([none, straight], axis=1),
        ]
    )
    return forward, backward


def padded(values):
    images, rows, _, width = values.shape
    values = jnp.pad(values, ((0, 0), (0, 0), (0, SIDE - WIN), (0, 0)))
    return values.reshape(images, rows * SIDE, width)


def unpadded(values):
    images, _, width = values.shape
    return values.reshape(images, WIN, SIDE, width)[:, :, :WIN]


def local(
    patches,
    norm1_gain,
    norm1_bias,
    qkv_weight,
    qv_bias,
    rel_pos_h,
    rel_pos_w,
    proj_weight,
    proj_bias,
    norm2_gain,
    norm2_bias,
    fc1_weight,
    fc1_bias,
    fc2_weight,
    fc2_bias,
    heights,
    widths,
    out_grad,
):
    width = patches.shape[-1]
    dims = grid_of(lax.axis_size("dp"))
    core = lax.axis_index("mp")
    is_first = core == 0
    spread, gather = constants()

    def prepare(patches, out_grad, heights, rel_pos_h, rel_pos_w):
        if dims is None:
            orders = [jnp.tile(jnp.arange(PIECES, dtype=jnp.int32), 4)]
        else:
            own, far = place_orders(dims, core), place_orders(dims, 1 - core)
            orders = [own[0], far[0], own[1], far[1]]
        meta = jnp.concatenate(
            orders + [core.astype(jnp.int32)[None], heights, widths, jnp.zeros((11,), jnp.int32)]
        )
        row_index = core * WIN + jnp.arange(WIN)
        valid = (row_index[None, :, None] < heights[:, None, None]) & (
            jnp.arange(WIN)[None, None, :] < widths[:, None, None]
        )
        dm = padded(jnp.where(valid[..., None], out_grad, jnp.zeros_like(out_grad)))
        return padded(patches), dm, meta, *tables(rel_pos_h, rel_pos_w)

    wanted = (patches, out_grad, heights, rel_pos_h, rel_pos_w)
    vectors = (norm1_gain, norm1_bias, qv_bias[0], qv_bias[1], proj_bias, norm2_gain, norm2_bias, fc2_bias)
    small = jnp.pad(jnp.stack(vectors, axis=1), ((0, 0), (0, LANES - len(vectors))))
    qk = jnp.concatenate([qkv_weight[:, :width], small, qkv_weight[:, width : 2 * width]], axis=1)
    vp = jnp.concatenate([qkv_weight[:, 2 * width :], small, proj_weight], axis=1)
    if dims is None:
        qk = lax.all_gather(qk, ("dp", "mp"), axis=0, tiled=True)
        vp = lax.all_gather(vp, ("dp", "mp"), axis=0, tiled=True)
        attend_own = [jnp.where(is_first, qk, vp)]
        attend_far = [jnp.where(is_first, vp, qk)]
        tok, dm, meta, table, table_back = prepare(*wanted)
        hidden_in = tuple(
            ((lax.all_gather(part, "dp", axis=0, tiled=True), 0),) for part in (fc1_weight, fc2_weight.T)
        )
    else:
        fc1, fc2 = fc1_weight, fc2_weight.T
        came = other_core(jnp.where(is_first, vp, qk))
        near = jnp.where(is_first, qk, vp)
        block = jnp.concatenate(
            [jnp.where(is_first, near, came), jnp.where(is_first, came, near)], axis=0
        )
        attend_size, size = block.shape[1], fc1.shape[1]
        tok, dm, meta, table, table_back = prepare(*meet([], *wanted, block)[:5])
        own = jnp.concatenate([block, fc1, fc2], axis=1)
        attend_z, beside = Flow(*along_z(block, dims)), Flow(turn(own, dims, FIRST))
        fc1, fc2, tok, dm, table, table_back, meta = meet(
            [attend_z, beside], fc1, fc2, tok, dm, table, table_back, meta
        )

        attend_z = stack(*attend_z.came)
        z_beside = Flow(turn(attend_z, dims, FIRST))
        own = stack(own, *beside.came)
        over = Flow(turn(own, dims, SECOND))
        fc1_z = Flow(*along_z(after(fc1, own), dims))
        (fc2,) = meet([over, z_beside, fc1_z], fc2)

        over = over.came[0]
        attend_z = stack(attend_z, *z_beside.came)
        z_over = Flow(turn(attend_z, dims, SECOND))
        fc1_z = stack(after(fc1_z.came[0], attend_z), *fc1_z.came[1:])
        fc1_beside = Flow(turn(fc1_z, dims, FIRST))
        fc2_z = Flow(*along_z(after(fc2, fc1_z), dims))
        own_attend = jnp.concatenate([own[:, :attend_size], over[:, :attend_size]], axis=0)
        own_attend, attend_z = meet([z_over, fc1_beside, fc2_z], own_attend, attend_z)

        z_over = z_over.came[0]
        far = Flow(*(other_core(part) for part in (own_attend, attend_z, z_over)))
        fc1_z = stack(fc1_z, *fc1_beside.came)
        fc1_over = Flow(turn(fc1_z, dims, SECOND))
        fc2_z = stack(*fc2_z.came)
        fc2_beside = Flow(turn(fc2_z, dims, FIRST))
        tok, fc1_z, fc2_z, dm = meet([far], tok, fc1_z, fc2_z, dm)
        dm_far = Flow(other_core(dm))
        attend_own, attend_far = [own, over, attend_z, z_over], far.came

    vecs, n1, q, k, v, p, att, weights, x1, n2 = attend(
        meta, tok, table, jnp.asarray(spread, BF16), attend_own, attend_far
    )
    n2_far = other_core(n2).reshape(-1, width)
    if dims is None:
        dm_far = other_core(dm)
    else:
        (n2,) = meet([fc1_over, fc2_beside, dm_far], n2)
        (dm_far,) = dm_far.came
        fc2_z = stack(fc2_z, *fc2_beside.came)
        fc2_over = turn(fc2_z, dims, SECOND)
    dm_flat, dm_far = dm.reshape(-1, width), dm_far.reshape(-1, width)
    n2 = n2.reshape(-1, width)
    bias = fc1_bias[None].astype(F32)
    if dims is not None:
        n2 = after(n2, fc2_z)
        hidden_in = [
            ((own, attend_size), (over, attend_size), (fc1_z, 0), (*fc1_over.came, 0)),
            ((own, attend_size + size), (over, attend_size + size), (fc2_z, 0), (fc2_over, 0)),
        ]
    fc2_part = hidden_fwd(meta, n2, n2_far, dm_flat, dm_far, bias, hidden_in[0])
    if dims is not None:
        fc2_part = meet([], *fc2_part, fc2_over)[:2]
        fc2_sum = Scatter(*fc2_part, dims)
    fc1_bias_part, *fc1_part, back_own, back_far, acts = hidden_back(
        meta, n2, n2_far, dm_flat, dm_far, bias, *hidden_in
    )
    back_far = other_core(back_far)
    if dims is not None:
        fc1_part = meet([fc2_sum], *fc1_part)
        fc2_sum.second()
        fc1_sum = Scatter(*fc1_part, dims)
        back_own = after(back_own, fc2_sum.sent)

    shared = (meta, vecs, jnp.asarray(gather, BF16), table_back, q, k, v, p, weights, att, n1)
    half = width // 2
    def block_of(out_own, out_far):
        branch = add(out_own, out_far).reshape(x1.shape) + vecs[7]
        row_index = core * WIN + jnp.arange(WIN)
        valid = (row_index[None, :, None] < heights[:, None, None]) & (
            jnp.arange(WIN)[None, None, :] < widths[:, None, None]
        )
        return jnp.where(valid[..., None], unpadded(x1 + branch), 0.0).astype(BF16)

    def core_rows(wholes):
        whole = jnp.stack(
            [
                jnp.concatenate([part.reshape(part.shape[0], 2, -1)[:, at] for part in wholes], axis=1)
                for at in range(2)
            ]
        )
        rows = whole.shape[1] // 2
        cuts = whole[:, :rows], whole[:, rows:]
        return jnp.where(is_first, *cuts), jnp.where(is_first, *cuts[::-1])

    count0, count1 = BACK_PARTS
    sums2, bias0, table0, mine0, theirs0, change, dx1, da = attend_back(
        (), count0, *shared, (back_own, back_far, x1, dm)
    )
    if dims is not None:
        da, mine0, theirs0 = meet([fc2_sum], da, mine0, theirs0)
        came0 = other_core(theirs0)
        da, mine0 = meet([fc1_sum, fc2_sum], da, mine0)
        fc2_sum.halve()
        fc1_sum.second()
        both = add(mine0, came0).astype(BF16)
        first = Scatter(both[:half], both[half:], dims)
        da = after(da, both)
    flat, mine, theirs, result = attend_back(
        (count0,), count1, *shared, (da, sums2, bias0, table0, fc1_bias_part, tok, dx1, change)
    )
    if dims is None:
        out_own, out_far = hidden_out(meta, acts, width, hidden_in[1])
        result, block_out = unpadded(result), block_of(out_own, other_core(out_far))
        fc1_sum, fc2_sum = (
            lax.psum_scatter(
                jnp.concatenate(parts, axis=0).astype(F32), "dp", scatter_dimension=0, tiled=True
            )
            for parts in (fc1_part, fc2_part)
        )
        wholes = [
            lax.psum_scatter(add(own, other_core(far)), "dp", scatter_dimension=0, tiled=True)
            for own, far in ((mine0, theirs0), (mine, theirs))
        ]
        near, far = core_rows(wholes)
        came = other_core(far)
        flat = lax.psum(flat, ("dp", "mp"))
    else:
        came, flat_came = Flow(other_core(theirs)), Flow(other_core(flat))
        mine, flat, acts, result = meet([fc2_sum, fc1_sum, first], mine, flat, acts, result)
        first.second()
        fc1_sum.halve()
        mine, flat, acts = meet([came, flat_came, first], mine, flat, acts)
        both = add(mine, came.came[0]).astype(BF16)
        second = Scatter(both[:half], both[half:], dims)
        flat = flat + flat_came.came[0]
        flat_came = Flow(turn(flat, dims, SECOND))
        first.halve()
        fc2_sum.came[0] = after(fc2_sum.came[0], first.sent)
        fc2_sum.quarter()
        acts = after(acts, first.sent, second.sent, fc2_sum.sent)
        out_own, out_far = hidden_out(meta, acts, width, hidden_in[1])
        flat, result, out_far = meet([flat_came, second, fc1_sum, fc2_sum], flat, result, out_far)
        late = Flow(other_core(out_far))
        flat = flat + flat_came.came[0]
        flat_came = Flow(turn(flat, dims, FIRST))
        second.second()
        fc1_sum.quarter()
        fc2_sum = fc2_sum.last()
        result = unpadded(result)
        flat, fc2_sum, result = meet([flat_came, first, second, fc1_sum, late], flat, fc2_sum, result)
        flat = flat + flat_came.came[0]
        flat_came = Flow(swap_z(flat, dims, 2))
        second.third()
        first.quarter()
        fc1_sum.near, late.came[0] = meet([], fc1_sum.near, late.came[0], second.sent, first.sent)[:2]
        fc1_sum = fc1_sum.last()
        block_out = block_of(out_own, late.came[0])
        flat, fc1_sum, block_out = meet([flat_came, second, first], flat, fc1_sum, block_out)

        share = shape((2, width // len(FIRST) // dims[0] // dims[1] // dims[2], width), F32)
        near, far = staged(
            partial(core_rows_kernel, 2), [share, share], first.near, *first.came, second.near, *second.came, meta=meta
        )
        came = other_core(far)
        flat = flat + flat_came.came[0]
        flat_came = swap_z(flat, dims, 1)
        flat = flat + after(flat_came, far)
    rows = near.shape[1]
    outs = [shape((rows, 3 * width), F32), shape((rows, width), F32)]
    qkv_grad, proj_grad = staged(last_rows_kernel, outs, near, came, meta=meta)
    vec_sums, fc1_bias_grad, rel = unpacked(flat, core)
    share = norm1_gain.shape[0]
    device = lax.axis_index("dp") * 2 + core
    mine = lax.dynamic_slice_in_dim(vec_sums, device * share, share, axis=1)
    rels = rel_pos_h.shape[0]
    return (
        block_out,
        result,
        mine[0],
        mine[1],
        qkv_grad,
        mine[2:4],
        rel[:rels],
        rel[32 : 32 + rels],
        proj_grad,
        mine[4],
        mine[5],
        mine[6],
        fc1_sum,
        fc1_bias_grad,
        fc2_sum.T,
        mine[7],
    )


def solution(mesh):
    return jax.shard_map(
        local,
        mesh=mesh,
        in_specs=(
            P("dp", "mp", None, None),
            P(("dp", "mp")),
            P(("dp", "mp")),
            P(("dp", "mp"), None),
            P(None, ("dp", "mp")),
            P(),
            P(),
            P(("dp", "mp"), None),
            P(("dp", "mp")),
            P(("dp", "mp")),
            P(("dp", "mp")),
            P("dp", "mp"),
            P("mp"),
            P("mp", "dp"),
            P(("dp", "mp")),
            P("dp"),
            P("dp"),
            P("dp", "mp", None, None),
        ),
        out_specs=(
            P("dp", "mp", None, None),
            P("dp", "mp", None, None),
            P(("dp", "mp")),
            P(("dp", "mp")),
            P(("dp", "mp"), None),
            P(None, ("dp", "mp")),
            P(),
            P(),
            P(("dp", "mp"), None),
            P(("dp", "mp")),
            P(("dp", "mp")),
            P(("dp", "mp")),
            P("dp", "mp"),
            P("mp"),
            P("mp", "dp"),
            P(("dp", "mp")),
        ),
        check_vma=False,
    )
```

```python
from functools import partial

import jax
import jax.numpy as jnp
import numpy as np
from jax import lax
from jax.experimental import pallas as pl
from jax.experimental.pallas import tpu as pltpu
from jax.sharding import PartitionSpec as P

HEADS = 12
HDIM = 64
LANES = 128
PAIRS = HEADS // 2
WIN = 14
SIDE = 16
TOK = WIN * SIDE
KEYS = 256
PIECES = 16
EPSILON = 1e-06
MASKED_SCORE = -1e30
MASK_LANE = 60
SMALL = 48
CHUNK = 512
BACK_PARTS = (4, 2)
F32 = jnp.float32
BF16 = jnp.bfloat16
SMEM = pl.BlockSpec(memory_space=pltpu.SMEM)
HBM = pl.BlockSpec(memory_space=pl.ANY)
WHOLE = pl.BlockSpec(memory_space=pltpu.VMEM)
VMEM_BYTES = 52 * 2**20
COST = pl.CostEstimate(flops=1000, bytes_accessed=1000, transcendentals=0)


def params():
    return pltpu.CompilerParams(vmem_limit_bytes=VMEM_BYTES)


def shape(dims, dtype):
    return jax.ShapeDtypeStruct(dims, dtype)


def dot(a, b):
    return jnp.dot(a, b, preferred_element_type=F32)


def dot_nt(a, b):
    return lax.dot_general(a, b, (((1,), (1,)), ((), ())), preferred_element_type=F32)


def dot_tn(a, b):
    return lax.dot_general(a, b, (((0,), (0,)), ((), ())), preferred_element_type=F32)


def lanes(rows):
    return lax.broadcasted_iota(jnp.int32, (rows, LANES), 1)


def moments(values):
    centered = values - jnp.mean(values, axis=-1, keepdims=True)
    inverse = lax.rsqrt(jnp.mean(centered * centered, axis=-1, keepdims=True) + EPSILON)
    return centered * inverse, inverse


def norm_back(grad, xhat, inverse, gain):
    scaled = grad * gain
    first = jnp.mean(scaled, axis=-1, keepdims=True)
    second = jnp.mean(scaled * xhat, axis=-1, keepdims=True)
    return inverse * (scaled - first - xhat * second)


def begin(source, dest, sem):
    copy = pltpu.make_async_copy(source, dest, sem)
    copy.start()
    return copy


def finish(copies):
    for copy in copies:
        copy.wait()


def pieces_in(meta, at, ins, start, dest, sems, first):
    rows, cols = dest.shape[0] // PIECES, dest.shape[1]
    copies = []
    for ref, base in ins:
        for part in range(ref.shape[0] // rows):
            place = pl.multiple_of(meta[at + len(copies)] * rows, rows)
            source = ref.at[pl.ds(part * rows, rows), pl.ds(base + start, cols)]
            copies.append(begin(source, dest.at[pl.ds(place, rows), :], sems.at[first + len(copies)]))
    return copies


def row_valid(meta, core, window, rows, width):
    place = lax.broadcasted_iota(jnp.int32, (rows, width), 0)
    row, col = place // SIDE, place % SIDE
    inside = (row < WIN) & (col < WIN)
    return inside & (core * WIN + row < meta[65 + window]) & (col < meta[67 + window])


def relative(turned):
    out = []
    for row in range(WIN):
        slab = turned[row * SIDE : (row + 1) * SIDE]
        down = pltpu.roll(slab, row, 1) if row else slab
        across = pltpu.roll(slab, 0, 1, stride=1, stride_axis=0)
        out.append(jnp.where(lanes(SIDE) % 64 < 32, down, across))
    return jnp.concatenate(out, axis=0)


def columns_of(mat, width, start=0, size=None):
    return mat // 2, pl.ds(mat % 2 * (width + LANES) + start, width if size is None else size)


def attend_kernel(count, total, meta, tok, table, spread, *refs):
    own, other = refs[:count], refs[count:total]
    vecs, n1, q, k, v, p, att, w_out, x1, n2 = refs[total : total + 10]
    toks, weights, aug, n1s, qs, ks, vs, ps, atts, x1s, n2s, sems, out_sems = refs[total + 10 :]
    width = toks.shape[-1]
    core = meta[64]
    copies = [begin(tok, toks, sems.at[2 * PIECES])]
    for found, at, half in ((own, 0, core), (other, 16, 1 - core)):
        found = [(ref, 0) for ref in found]
        copies += pieces_in(meta, at, found, 0, weights.at[half], sems, at)
    for window in range(2):
        valid = row_valid(meta, core, window, KEYS, LANES)
        aug[window] = jnp.where(
            (lanes(KEYS) == MASK_LANE) & ~valid, MASKED_SCORE, spread[...].astype(F32)
        ).astype(BF16)
        ks[window, TOK:] = jnp.zeros((KEYS - TOK, width), BF16)
        vs[window, TOK:] = jnp.zeros((KEYS - TOK, width), BF16)
    copies[0].wait()
    tokens = toks[...].reshape(2 * TOK, width).astype(F32)
    xhat, _ = moments(tokens)
    finish(copies[1:])
    outs = [begin(weights, w_out, out_sems.at[0])]
    vecs[...] = weights[0, :, width : width + LANES].astype(F32).T[:8]
    normed = (xhat * vecs[0:1] + vecs[1:2]).astype(BF16)
    n1s[...] = normed.reshape(2, TOK, width)
    outs.append(begin(n1s, n1, out_sems.at[1]))
    for mat, (made_in, dest) in enumerate(((qs, q), (ks, k), (vs, v))):
        for start in range(0, width, 256):
            cols = pl.ds(start, 256)
            half, here = columns_of(mat, width, start, 256)
            made = dot(normed, weights[half, :, here])
            if mat != 1:
                made = made + vecs[2 + mat // 2 : 3 + mat // 2, cols]
            made = made.astype(BF16)
            made_in[0, :TOK, cols] = made[:TOK]
            made_in[1, :TOK, cols] = made[TOK:]
        outs.append(begin(made_in, dest, out_sems.at[2 + mat]))

    place = lanes(TOK)
    for step in range(2 * PAIRS):
        window, pair = step // PAIRS, step % PAIRS
        cols = pl.ds(pair * LANES, LANES)
        q2, k2, v2 = qs[window, :, cols], ks[window, :, cols], vs[window, :, cols]
        turned = dot(q2, table[...])
        keys_aug = jnp.concatenate([k2, aug[window]], axis=1)
        parts = []
        for half in range(2):
            rel = relative(turned[:, half * LANES : (half + 1) * LANES])
            high = rel.astype(BF16).astype(F32)
            rel = jnp.where(place < 64, high, rel - high)
            rel = jnp.where(place == MASK_LANE, 1.0, rel).astype(BF16)
            mine = jnp.where(place // 64 == half, q2.astype(F32) * HDIM**-0.5, 0.0).astype(BF16)
            scores = dot_nt(jnp.concatenate([mine, rel], axis=1), keys_aug)
            terms = jnp.exp(scores - jnp.max(scores, axis=-1, keepdims=True))
            soft = terms * (1.0 / jnp.sum(terms, axis=-1, keepdims=True))
            ps[window, 2 * pair + half] = soft
            parts.append(dot(soft.astype(BF16), v2))
        atts[window, :, cols] = jnp.where(place < 64, parts[0], parts[1]).astype(BF16)
        heads = pl.ds(2 * pair, 2)
        outs.append(begin(ps.at[window, heads], p.at[window, heads], out_sems.at[len(outs)]))
    outs.append(begin(atts, att, out_sems.at[len(outs)]))
    half, here = columns_of(3, width)
    for window in range(2):
        resid = toks[window].astype(F32) + (dot(atts[window], weights[half, :, here]) + vecs[4:5])
        x1s[window] = resid
        xhat, _ = moments(resid)
        n2s[window] = (xhat * vecs[5:6] + vecs[6:7]).astype(BF16)
        outs.append(begin(x1s.at[window], x1.at[window], out_sems.at[len(outs)]))
        outs.append(begin(n2s.at[window], n2.at[window], out_sems.at[len(outs)]))
    finish(outs)


def attend(meta, tok, table, spread, own, other):
    count, total, width = len(own), len(own) + len(other), tok.shape[-1]
    rows, keys, heads = (2, TOK, width), (2, KEYS, width), (2, HEADS, TOK, KEYS)
    halves = (2, width, 2 * width + LANES)
    outs = [shape(dims, F32 if dims == heads else BF16) for dims in (rows, rows, keys, keys, heads, rows, halves)]
    outs += [shape(rows, F32), shape(rows, BF16)]
    scratch = (rows, halves, (2, KEYS, LANES), rows, rows, keys, keys, heads, rows)
    return pl.pallas_call(
        partial(attend_kernel, count, total),
        out_shape=[shape((8, width), F32)] + outs,
        in_specs=[SMEM, HBM, WHOLE, WHOLE] + [HBM] * total,
        out_specs=[WHOLE] + [HBM] * len(outs),
        scratch_shapes=[pltpu.VMEM(dims, F32 if dims == heads else BF16) for dims in scratch]
        + [
            pltpu.VMEM(rows, F32),
            pltpu.VMEM(rows, BF16),
            pltpu.SemaphoreType.DMA((2 * PIECES + 1,)),
            pltpu.SemaphoreType.DMA((10 + 2 * PAIRS,)),
        ],
        compiler_params=params(),
        cost_estimate=COST,
        name="attend",
    )(meta, tok, table, spread, *own, *other)


def pieces_out(meta, made, cols, keep, send, sems, first):
    rows = made.shape[0] // PIECES
    copies = []
    for piece in range(PIECES):
        dest = keep if piece < PIECES // 2 else send
        place = pl.multiple_of(meta[32 + piece] * rows, rows)
        at = pl.ds(piece % (PIECES // 2) * rows, rows)
        source = made.at[pl.ds(place, rows), cols]
        copies.append(begin(source, dest.at[at, cols], sems.at[first + len(copies)]))
    return copies


def hidden_fwd_kernel(bases, meta, n2a, n2b, dma, dmb, bias, *refs):
    count = len(bases)
    ins, (keep, send) = list(zip(refs[:count], bases)), refs[count : count + 2]
    w0, n2s, dms, grad, sems, out_sems = refs[count + 2 :]
    width, hidden = w0.shape
    at = PIECES
    copies = [begin(n2a, n2s.at[: 2 * TOK], sems.at[at]), begin(n2b, n2s.at[2 * TOK :], sems.at[at + 1])]
    copies += pieces_in(meta, 0, ins, 0, w0, sems, 0)
    dm_copies = [
        begin(dma, dms.at[: 2 * TOK], sems.at[at + 2]),
        begin(dmb, dms.at[2 * TOK :], sems.at[at + 3]),
    ]
    finish(copies)
    outs = []
    for start in range(0, hidden, CHUNK):
        cols = pl.ds(start, CHUNK)
        inner = dot(n2s[...], w0[:, cols]) + bias[:, cols]
        act = (inner * (0.5 + 0.5 * lax.erf(inner * 0.7071067811865476))).astype(BF16)
        if start == 0:
            finish(dm_copies)
        grad[:, cols] = dot_tn(dms[...], act).astype(BF16)
        if start + CHUNK == hidden - CHUNK:
            outs += pieces_out(meta, grad, pl.ds(0, hidden - CHUNK), keep, send, out_sems, 0)
    outs += pieces_out(meta, grad, pl.ds(hidden - CHUNK, CHUNK), keep, send, out_sems, PIECES)
    finish(outs)


def hidden_fwd(meta, n2a, n2b, dma, dmb, bias, ins):
    refs, bases = zip(*ins)
    width, hidden = n2a.shape[-1], bias.shape[-1]
    return pl.pallas_call(
        partial(hidden_fwd_kernel, bases),
        out_shape=[shape((width // 2, hidden), BF16)] * 2,
        in_specs=[SMEM] + [HBM] * 4 + [WHOLE] + [HBM] * len(refs),
        out_specs=[HBM] * 2,
        scratch_shapes=[
            pltpu.VMEM((width, hidden), BF16),
            pltpu.VMEM((4 * TOK, width), BF16),
            pltpu.VMEM((4 * TOK, width), BF16),
            pltpu.VMEM((width, hidden), BF16),
            pltpu.SemaphoreType.DMA((PIECES + 4,)),
            pltpu.SemaphoreType.DMA((2 * PIECES,)),
        ],
        compiler_params=params(),
        cost_estimate=COST,
        name="hidden_fwd",
    )(meta, n2a, n2b, dma, dmb, bias, *refs)


def hidden_back_kernel(bases0, bases1, meta, n2a, n2b, dma, dmb, bias, *refs):
    count = len(bases0)
    ins0, ins1 = list(zip(refs[:count], bases0)), list(zip(refs[count : 2 * count], bases1))
    refs = refs[2 * count :]
    bias_grad, keep, send, back_own, back_far, acts_out = refs[:6]
    w0, w1, n2s, dms, acts, backs, grad, big, small, sems, out_sems = refs[6:]
    width, hidden = w0.shape
    halves = (pl.ds(0, 2 * TOK), pl.ds(2 * TOK, 2 * TOK))
    at = 2 * PIECES
    copies = [begin(ref, n2s.at[half], sems.at[at + i]) for i, (ref, half) in enumerate(zip((n2a, n2b), halves))]
    copies += pieces_in(meta, 0, ins0, 0, w0, sems, 0)
    at += 2
    later = [begin(ref, dms.at[half], sems.at[at + i]) for i, (ref, half) in enumerate(zip((dma, dmb), halves))]
    later += pieces_in(meta, 0, ins1, 0, w1, sems, PIECES)
    finish(copies)
    outs = []
    for start in range(0, hidden, CHUNK):
        cols = pl.ds(start, CHUNK)
        inner = dot(n2s[...], w0[:, cols]) + bias[:, cols]
        if start == 0:
            finish(later)
        back = dot(dms[...], w1[:, cols])
        cdf = 0.5 + 0.5 * lax.erf(inner * 0.7071067811865476)
        density = jnp.exp(inner * inner * -0.5) * 0.3989422804014327
        acts[:, cols] = (inner * cdf).astype(BF16)
        back_pre = (back * (cdf + inner * density)).astype(BF16)
        backs[:, cols] = back_pre
        bias_grad[:, cols] = jnp.sum(back_pre.astype(F32), axis=0, keepdims=True)
        grad[:, cols] = dot_tn(n2s[...], back_pre).astype(BF16)
    outs = pieces_out(meta, grad, pl.ds(0, hidden), keep, send, out_sems, 0)
    outs.append(begin(acts, acts_out, out_sems.at[len(outs)]))
    small[...] = dot_nt(backs[halves[1]], w0[...]).astype(BF16)
    outs.append(begin(small, back_far, out_sems.at[len(outs)]))
    big[...] = dot_nt(backs[halves[0]], w0[...])
    outs.append(begin(big, back_own, out_sems.at[len(outs)]))
    finish(outs)


def hidden_back(meta, n2a, n2b, dma, dmb, bias, ins0, ins1):
    (refs0, bases0), (refs1, bases1) = zip(*ins0), zip(*ins1)
    width, hidden = n2a.shape[-1], bias.shape[-1]
    one = (2 * TOK, width)
    tall = pltpu.VMEM((4 * TOK, width), BF16)
    wide = pltpu.VMEM((width, hidden), BF16)
    return pl.pallas_call(
        partial(hidden_back_kernel, bases0, bases1),
        out_shape=[shape((1, hidden), F32)]
        + [shape((width // 2, hidden), BF16)] * 2
        + [shape(one, F32), shape(one, BF16), shape((4 * TOK, hidden), BF16)],
        in_specs=[SMEM] + [HBM] * 4 + [WHOLE] + [HBM] * (2 * len(refs0)),
        out_specs=[WHOLE] + [HBM] * 5,
        scratch_shapes=[
            wide,
            wide,
            tall,
            tall,
            pltpu.VMEM((4 * TOK, hidden), BF16),
            pltpu.VMEM((4 * TOK, hidden), BF16),
            wide,
            pltpu.VMEM(one, F32),
            pltpu.VMEM(one, BF16),
            pltpu.SemaphoreType.DMA((2 * PIECES + 4,)),
            pltpu.SemaphoreType.DMA((PIECES + 3,)),
        ],
        compiler_params=params(),
        cost_estimate=COST,
        name="hidden_back",
    )(meta, n2a, n2b, dma, dmb, bias, *refs0, *refs1)


def hidden_out_kernel(bases, meta, acts_in, *refs):
    count = len(bases)
    ins, (own, far) = list(zip(refs[:count], bases)), refs[count : count + 2]
    w1, acts, big, small, sems, out_sems = refs[count + 2 :]
    copies = [begin(acts_in, acts, sems.at[PIECES])]
    copies += pieces_in(meta, 0, ins, 0, w1, sems, 0)
    finish(copies)
    big[...] = dot_nt(acts[: 2 * TOK], w1[...])
    outs = [begin(big, own, out_sems.at[0])]
    small[...] = dot_nt(acts[2 * TOK :], w1[...]).astype(BF16)
    outs.append(begin(small, far, out_sems.at[1]))
    finish(outs)


def hidden_out(meta, acts, width, ins):
    refs, bases = zip(*ins)
    hidden = acts.shape[1]
    one = (2 * TOK, width)
    return pl.pallas_call(
        partial(hidden_out_kernel, bases),
        out_shape=[shape(one, F32), shape(one, BF16)],
        in_specs=[SMEM] + [HBM] * (1 + len(refs)),
        out_specs=[HBM] * 2,
        scratch_shapes=[
            pltpu.VMEM((width, hidden), BF16),
            pltpu.VMEM(acts.shape, BF16),
            pltpu.VMEM(one, F32),
            pltpu.VMEM(one, BF16),
            pltpu.SemaphoreType.DMA((PIECES + 1,)),
            pltpu.SemaphoreType.DMA((2,)),
        ],
        compiler_params=params(),
        cost_estimate=COST,
        name="hidden_out",
    )(meta, acts, *refs)


def unrelative(grads):
    out = []
    for row in range(WIN):
        slab = grads[row * SIDE : (row + 1) * SIDE]
        down = pltpu.roll(slab, row, 1) if row else slab
        across = pltpu.roll(slab, 0, 1, stride=1, stride_axis=0)
        out.append(jnp.where(lanes(SIDE) < 32, down, across))
    return jnp.concatenate(out, axis=0)


def attend_back_kernel(before, count, meta, vecs, gather, table, q, k, v, p, weights, att, n1, *refs):
    start, parts = sum(before), len(before)
    first, last = start == 0, start + count == PAIRS
    if first:
        back_own, back_far, x1, dm = refs[:4]
        norm_sums, bias_sums, table_grad, mine, theirs, dqkv_out, dx1, da = refs[4:12]
        refs = refs[12:]
        owns, fars, x1s, dms, dx1s = refs[-5:]
        refs = refs[:-5]
    else:
        da, refs = refs[0], refs[1:]
        if last:
            earlier, tok, dx1, *changes = refs[:4], *refs[4 : 6 + parts]
            flat, mine, theirs, result = refs[6 + parts : 10 + parts]
            refs = refs[10 + parts :]
            bias_sums, wqkv, toks, dx1s, results, *changed = refs[-5 - parts :]
            refs = refs[: -5 - parts]
        else:
            bias_sums, table_grad, mine, theirs, dqkv_out = refs[:5]
            refs = refs[5:]
    das, wproj, atts, n1s, qs, ks, vs, ps, dat, dqkv, grads, sems, out_sems = refs
    core = meta[64]
    width, cols_here = das.shape[-1], qs.shape[-1]
    rows = width // PIECES
    columns = pl.ds(start * LANES, cols_here)
    tokens = (2 * TOK, width)
    early = []
    if first:
        early = [(back_own, owns), (back_far, fars), (x1, x1s), (dm, dms)]
    else:
        early = [(da, das)]
    early = [begin(ref, dest, sems.at[at]) for at, (ref, dest) in enumerate(early)]
    half, here = columns_of(3, width)
    wait_proj = begin(weights.at[half, columns, here], wproj, sems.at[4])
    wait_att = begin(att, atts, sems.at[5])
    wait_v = begin(v.at[:, :, columns], vs, sems.at[6])
    wait_p = []
    for window in range(2):
        for pair in range(count):
            heads = pl.ds(2 * (start + pair), 2)
            wait_p.append(
                begin(p.at[window, heads], ps.at[window, pl.ds(2 * pair, 2)], sems.at[10 + len(wait_p)])
            )
        if window == 0:
            wait_qk = [
                begin(ref.at[:, :, columns], dest, sems.at[7 + at])
                for at, (ref, dest) in enumerate(((q, qs), (k, ks)))
            ]
    wait_n1 = begin(n1, n1s, sems.at[9])
    if last:
        at = 10 + 2 * count
        ends = [begin(tok, toks, sems.at[at]), begin(dx1, dx1s, sems.at[at + 1])]
        for mat in range(3):
            half, here = columns_of(mat, width)
            ends.append(begin(weights.at[half, :, here], wqkv.at[mat], sems.at[at + 2 + mat]))
        for part in range(parts):
            ends.append(begin(changes[part], changed[part], sems.at[at + 5 + part]))
    outs = []
    finish(early)
    if first:
        total = [jnp.zeros((1, width), F32) for _ in range(4)]
        for window in range(2):
            here = pl.ds(window * TOK, TOK)
            grad = owns[here] + fars[here].astype(F32)
            xhat, inverse = moments(x1s[window])
            out_grad = dms[window].astype(F32)
            dresid = out_grad + norm_back(grad, xhat, inverse, vecs[5:6])
            dx1s[window] = dresid
            rounded = dresid.astype(BF16)
            das[window] = rounded
            for slot, value in enumerate((rounded.astype(F32), grad * xhat, grad, out_grad)):
                total[slot] = total[slot] + jnp.sum(value, axis=0, keepdims=True)
        norm_sums[...] = jnp.concatenate(total, axis=0)
        outs.append(begin(dx1s, dx1, out_sems.at[2 * PIECES]))
        outs.append(begin(das, da, out_sems.at[2 * PIECES + 1]))
    wait_proj.wait()
    dat[...] = dot_nt(das[...].reshape(tokens), wproj[...]).astype(BF16).reshape(2, TOK, cols_here)

    def send(half):
        is_own = core == half
        at = jnp.where(is_own, 32, 48)
        for piece in range(PIECES):
            place = pl.multiple_of(meta[at + piece] * rows, rows)
            source, to = grads.at[half, pl.ds(place, rows), :], pl.ds(piece * rows, rows)
            sem = out_sems.at[half * PIECES + piece]
            copies = [pltpu.make_async_copy(source, ref.at[to, :], sem) for ref in (mine, theirs)]
            pl.when(is_own)(copies[0].start)
            pl.when(~is_own)(copies[1].start)
            outs.append(copies[0])

    wait_att.wait()
    made = dot_tn(atts[...].reshape(tokens), das[:, :, columns].reshape(2 * TOK, cols_here))
    grads[1, :, cols_here:] = made.astype(BF16)
    finish(wait_qk + [wait_v] + wait_p)
    place = lanes(TOK)
    table_sum = jnp.zeros((LANES, LANES), F32)
    for step in range(2 * count):
        window, pair = step // count, step % count
        cols = pl.ds(pair * LANES, LANES)
        q2, k2, v2, dat2 = (ref[window, :, cols] for ref in (qs, ks, vs, dat))
        q8 = (q2.astype(F32) * HDIM**-0.5).astype(BF16)
        k8 = (k2.astype(F32) * HDIM**-0.5).astype(BF16)
        dqs, dks, dvs, dts = [], [], [], []
        for half in range(2):
            soft32 = ps[window, 2 * pair + half]
            soft = soft32.astype(BF16)
            own_lanes = jnp.where(place // 64 == half, dat2.astype(F32), 0.0).astype(BF16)
            weighted = soft32 * dot_nt(own_lanes, v2)
            ds = (weighted - soft32 * jnp.sum(weighted, axis=-1, keepdims=True)).astype(BF16)
            turned = dot(ds, gather[...]).astype(BF16).astype(F32)
            turned = unrelative(turned).astype(BF16)
            dqs.append(dot(ds, k8) + dot(turned, table[half]))
            dks.append(dot_tn(ds, q8))
            dvs.append(dot_tn(soft, dat2))
            dts.append(dot_tn(turned, q2))
        dqkv[0, window, :, cols] = jnp.where(place < 64, dqs[0], dqs[1]).astype(BF16)
        dqkv[1, window, :, cols] = jnp.where(place < 64, dks[0][:TOK], dks[1][:TOK]).astype(BF16)
        dqkv[2, window, :, cols] = jnp.where(place < 64, dvs[0][:TOK], dvs[1][:TOK]).astype(BF16)
        table_sum = table_sum + jnp.where(lanes(LANES) < 64, dts[0], dts[1])
    if not last:
        table_grad[...] = table_sum
    if not last:
        outs.append(begin(dqkv, dqkv_out, out_sems.at[2 * PIECES + 2]))
    wait_n1.wait()
    for mat in (2, 0, 1):
        change = dqkv[mat].reshape(2 * TOK, cols_here)
        made = dot_tn(n1s[...].reshape(tokens), change)
        grads[mat // 2, :, pl.ds(mat % 2 * cols_here, cols_here)] = made.astype(BF16)
        if mat != 0:
            send(mat // 2)
        if mat != 1:
            bias_sums[mat // 2 : mat // 2 + 1] = jnp.sum(change.astype(F32), axis=0, keepdims=True)
    if last:
        finish(ends)
        total = [jnp.zeros((1, width), F32) for _ in range(2)]
        for window in range(2):
            grad = jnp.zeros((TOK, width), F32)
            at = 0
            for change in (*changed, dqkv):
                here = pl.ds(at, change.shape[-1])
                for mat in range(3):
                    grad = grad + dot_nt(change[mat, window], wqkv[mat, :, here])
                at += change.shape[-1]
            xhat, inverse = moments(toks[window].astype(F32))
            results[window] = dx1s[window] + norm_back(grad, xhat, inverse, vecs[0:1])
            outs.append(begin(results.at[window], result.at[window], out_sems.at[2 * PIECES + window]))
            for slot, value in enumerate((grad * xhat, grad)):
                total[slot] = total[slot] + jnp.sum(value, axis=0, keepdims=True)
        norm2_sums, bias0, table0, hidden_sums = earlier
        pack(meta, total, (bias0, bias_sums), norm2_sums, table0[...] + table_sum, hidden_sums, flat)
    finish(outs)


def pack(meta, norm1, biases, norm2, table, hidden, flat):
    flat[...] = jnp.zeros_like(flat)
    parts = biases[0].shape[1] // LANES
    for row in range(8):
        for at in range(6):
            cols = pl.ds(at * LANES, LANES)
            if row < 2:
                value = norm1[row][:, at * LANES : (at + 1) * LANES]
            elif row < 4:
                ref, place = (biases[0], at) if at < parts else (biases[1], at - parts)
                value = ref[row - 2 : row - 1, pl.ds(place * LANES, LANES)]
            else:
                value = norm2[row - 4 : row - 3, cols]
            block = 6 * row + at
            flat[block // 4 : block // 4 + 1, pl.ds(block % 4 * LANES, LANES)] = value
    for block in range(hidden.shape[1] // LANES):
        value = hidden[:, pl.ds(block * LANES, LANES)]
        for core in range(2):
            at = 12 + 3 * core + block // 4
            flat[at : at + 1, pl.ds(block % 4 * LANES, LANES)] = jnp.where(meta[64] == core, value, 0.0)
    both = table[:64] + pltpu.roll(table[:64], HDIM, 1)
    for group in range(4):
        flat[24:40, pl.ds(group * LANES, LANES)] = both[16 * group : 16 * group + 16]


def unpacked(flat, core):
    vectors = flat[:12].reshape(8, -1)
    hidden = lax.dynamic_slice_in_dim(flat, 12 + 3 * core, 3).reshape(-1)
    table = flat[24:40].reshape(16, 4, LANES).transpose(1, 0, 2).reshape(64, LANES)[:, :HDIM]
    return vectors, hidden, table


def attend_back(before, count, meta, vecs, gather, table, q, k, v, p, weights, att, n1, ins):
    width, cols_here = q.shape[-1], count * LANES
    start, parts = sum(before), len(before)
    first, last = start == 0, start + count == PAIRS
    rows, keys = (2, TOK, width), (2, KEYS, cols_here)
    part, flat = (2, TOK, cols_here), (2 * TOK, width)
    heads = (2, 2 * count, TOK, KEYS)
    small = [shape((2, cols_here), F32), shape((LANES, LANES), F32)]
    large = [shape((width, 2 * cols_here), BF16)] * 2
    large.append(shape(rows, F32) if last else shape((3,) + part, BF16))
    if last:
        small = [shape((SMALL, 2 * cols_here), F32)]
    if first:
        small = [shape((4, width), F32)] + small
        large += [shape(rows, F32), shape(rows, BF16)]
    scratch = [rows, (cols_here, width), rows, rows, part, keys, keys, heads, part, (3,) + part]
    scratch.append((2, width, 2 * cols_here))
    scratch = [pltpu.VMEM(dims, F32 if dims == heads else BF16) for dims in scratch]
    scratch += [pltpu.SemaphoreType.DMA((15 + 2 * count + parts,)), pltpu.SemaphoreType.DMA((2 * PIECES + 3,))]
    if first:
        scratch += [
            pltpu.VMEM(flat, F32),
            pltpu.VMEM(flat, BF16),
            pltpu.VMEM(rows, F32),
            pltpu.VMEM(rows, BF16),
            pltpu.VMEM(rows, F32),
        ]
    if last:
        scratch += [
            pltpu.VMEM((2, cols_here), F32),
            pltpu.VMEM((3, width, width), BF16),
            pltpu.VMEM(rows, BF16),
            pltpu.VMEM(rows, F32),
            pltpu.VMEM(rows, F32),
        ] + [pltpu.VMEM((3, 2, TOK, size * LANES), BF16) for size in before]
    return pl.pallas_call(
        partial(attend_back_kernel, before, count),
        out_shape=small + large,
        in_specs=[SMEM] + [WHOLE] * 3 + [HBM] * 8 + [WHOLE if last and at < 4 else HBM for at in range(len(ins) - 1)],
        out_specs=[WHOLE] * len(small) + [HBM] * len(large),
        scratch_shapes=scratch,
        compiler_params=params(),
        cost_estimate=COST,
        name="attend_back",
    )(meta, vecs, gather, table, q, k, v, p, weights, att, n1, *ins)


def grid_of(count):
    return (4, 2, 2) if count == 16 else None


def turn(values, dims, moves):
    pairs = []
    for chip in range(dims[0] * dims[1] * dims[2]):
        for core, (axis, by) in enumerate(moves):
            place = list(np.unravel_index(chip, dims))
            place[axis] = (place[axis] + by) % dims[axis]
            pairs.append((2 * chip + core, 2 * int(np.ravel_multi_index(place, dims)) + core))
    return lax.ppermute(values, ("dp", "mp"), pairs)


ALONG_X, ALONG_Y = ((2, 1),) * 2, ((1, 1),) * 2
FIRST, SECOND = ((2, 1), (1, 1)), ((1, 1), (2, 1))


def along_z(values, dims):
    return [turn(values, dims, ((0, step),) * 2) for step in range(1, dims[0])]


def swap_z(values, dims, by):
    chips = dims[1] * dims[2]
    pairs = [(chip, (chip // chips ^ by) * chips + chip % chips) for chip in range(dims[0] * chips)]
    return lax.ppermute(values, "dp", pairs)


def other_core(values):
    return lax.ppermute(values, "mp", [(0, 1), (1, 0)])


def after(values, *others):
    return lax.optimization_barrier((values, *others))[0]


def stack_kernel(count, *refs):
    ins, out, sems = refs[:count], refs[count], refs[count + 1]
    copies, at = [], 0
    for ref in ins:
        rows = ref.shape[0]
        copies.append(begin(ref, out.at[pl.ds(at, rows)], sems.at[len(copies)]))
        at += rows
    finish(copies)


def stack(*parts):
    rows = sum(part.shape[0] for part in parts)
    return pl.pallas_call(
        partial(stack_kernel, len(parts)),
        out_shape=shape((rows, parts[0].shape[1]), BF16),
        in_specs=[HBM] * len(parts),
        out_specs=HBM,
        scratch_shapes=[pltpu.SemaphoreType.DMA((len(parts),))],
        compiler_params=params(),
        cost_estimate=COST,
        name="stack",
    )(*parts)


class Flow:
    def __init__(self, *came):
        self.came = list(came)


def meet(flows, *values):
    sizes = [len(flow.came) for flow in flows]
    found = list(lax.optimization_barrier((*(part for flow in flows for part in flow.came), *values)))
    for flow, size in zip(flows, sizes):
        flow.came, found = found[:size], found[size:]
    return found


def place_orders(dims, core):
    here = lax.axis_index("dp")
    z, y, x = here // (dims[1] * dims[2]), here // dims[2] % dims[1], here % dims[2]

    def chip(step, inner, outer):
        by_x = jnp.where(core == 0, inner, outer)
        by_y = jnp.where(core == 0, outer, inner)
        return ((z - step) % dims[0] * dims[1] + (y + by_y) % 2) * dims[2] + (x + by_x) % 2

    square = [(inner, outer) for outer in range(2) for inner in range(2)]
    gather = [chip(0, *at) for at in square]
    gather += [chip(step, *at) for at in square for step in range(1, dims[0])]
    scatter = [chip(step, *at) for at in square for step in range(dims[0])]
    return [jnp.stack(found).astype(jnp.int32) for found in (gather, scatter)]


def add(a, b):
    return a.astype(F32) + b.astype(F32)


def staged_kernel(kernel, starts, scalars, *refs):
    count = len(starts)
    meta, refs = refs[:scalars], refs[scalars:]
    total = len(refs) // 2
    held, sems = refs[total : 2 * total], refs[2 * total]
    copies = []
    for ref, start, dest in zip(refs, starts, held):
        if start is not None:
            ref = ref.at[pl.ds(start, dest.shape[0])]
        copies.append(begin(ref, dest, sems.at[len(copies)]))
    finish(copies)
    kernel(*meta, *held)
    finish([begin(held[at], refs[at], sems.at[at]) for at in range(count, total)])


def staged(kernel, outs, *ins, meta=None):
    ins = [part if isinstance(part, tuple) else (part, None, part.shape[0]) for part in ins]
    arrays, starts, rows = zip(*ins)
    scalars = () if meta is None else (meta,)
    held = [pltpu.VMEM((count, *array.shape[1:]), array.dtype) for array, count in zip(arrays, rows)]
    held += [pltpu.VMEM(out.shape, out.dtype) for out in outs]
    return pl.pallas_call(
        partial(staged_kernel, kernel, starts, len(scalars)),
        out_shape=outs,
        in_specs=[SMEM] * len(scalars) + [HBM] * len(arrays),
        out_specs=[HBM] * len(outs),
        scratch_shapes=held + [pltpu.SemaphoreType.DMA((len(held),))],
        compiler_params=params(),
        cost_estimate=COST,
        name="staged",
    )(*scalars, *arrays)


def core_rows_kernel(count, meta, *refs):
    *terms, own, far = refs
    half, width = own.shape[1:]
    one, two = (sum(ref[...].astype(F32) for ref in part) for part in (terms[:count], terms[count:]))
    cut, last = one.shape[1] // 2, two.shape[1] // 2
    for core in range(2):

        def put(ref, at=slice(core * half, (core + 1) * half)):
            for mat in range(2):
                ref[mat, :, :cut] = one[at, mat * cut : (mat + 1) * cut]
                ref[mat, :, cut:] = two[at, mat * last : (mat + 1) * last]

        pl.when(meta[64] == core)(partial(put, own))
        pl.when(meta[64] != core)(partial(put, far))


def last_rows_kernel(meta, near, came, qkv, proj):
    width = proj.shape[1]

    def put(qk, vp):
        qkv[:, :width] = qk[0]
        qkv[:, width : 2 * width] = qk[1]
        qkv[:, 2 * width :] = vp[0]
        proj[...] = vp[1]

    pl.when(meta[64] == 0)(partial(put, near, came))
    pl.when(meta[64] != 0)(partial(put, came, near))


class Scatter(Flow):
    def __init__(self, keep, far, dims):
        super().__init__(turn(far, dims, SECOND))
        self.keep, self.dims, self.sent = keep, dims, far

    def second(self):
        half = self.keep.shape[0] // 2
        send = add(self.keep[half:], self.came[0][half:]).astype(BF16)
        self.near = add(self.keep[:half], self.came[0][:half])
        self.sent = send
        self.came = [turn(send, self.dims, FIRST)]

    def third(self):
        near = self.near + self.came[0].astype(F32)
        rows = near.shape[0] // self.dims[0]
        self.near = near[:rows]
        sends = [near[step * rows : (step + 1) * rows].astype(BF16) for step in range(1, self.dims[0])]
        self.sent = sends[0]
        self.came = [
            turn(send, self.dims, ((0, self.dims[0] - step),) * 2) for step, send in enumerate(sends, 1)
        ]

    def halve(self):
        near = self.near + self.came[0].astype(F32)
        rows = near.shape[0] // self.dims[0]
        parts = [near[step * rows : (step + 1) * rows] for step in range(self.dims[0])]
        even = lax.axis_index("dp") // (self.dims[1] * self.dims[2]) % 2 == 0
        self.near = parts[0]
        self.beside = jnp.where(even, parts[3], parts[1])
        self.sent = jnp.concatenate([parts[2], jnp.where(even, parts[1], parts[3])], axis=0).astype(BF16)
        self.came = [swap_z(self.sent, self.dims, 2)]

    def quarter(self):
        rows = self.near.shape[0]
        came = self.came[0]
        self.near = self.near + came[:rows].astype(F32)
        self.sent = (self.beside + came[rows:].astype(F32)).astype(BF16)
        self.came = [swap_z(self.sent, self.dims, 1)]

    def last(self):
        return sum((part.astype(F32) for part in self.came), self.near)


def constants():
    key = np.arange(KEYS)
    row, col = key // SIDE, key % SIDE
    inside = (row < WIN) & (col < WIN)
    spread = np.zeros((KEYS, LANES), np.float32)
    gather = np.zeros((KEYS, LANES), np.float32)
    for place in key[inside]:
        for base in (0, 64):
            spread[place, base + WIN - 1 + row[place]] = 1.0
            spread[place, base + 32 + WIN - 1 + col[place]] = 1.0
        gather[place, WIN - 1 - row[place]] = 1.0
        gather[place, 32 + WIN - 1 - col[place]] = 1.0
    return spread, gather


def tables(rel_pos_h, rel_pos_w):
    count = rel_pos_h.shape[0]
    gap = jnp.zeros((32 - count, HDIM), BF16)
    turned = jnp.concatenate([rel_pos_h[::-1], gap, rel_pos_w[::-1], gap], axis=0)
    turned = jnp.concatenate([turned, turned], axis=0).T
    none = jnp.zeros_like(turned)
    forward = jnp.concatenate(
        [jnp.concatenate([turned, none], axis=0), jnp.concatenate([none, turned], axis=0)], axis=1
    )
    straight = jnp.concatenate([rel_pos_h, gap, rel_pos_w, gap], axis=0)
    straight = jnp.concatenate([straight, jnp.zeros_like(straight)], axis=0)
    none = jnp.zeros_like(straight)
    backward = jnp.stack(
        [
            jnp.concatenate([straight, none], axis=1),
            jnp.concatenate([none, straight], axis=1),
        ]
    )
    return forward, backward


def padded(values):
    images, rows, _, width = values.shape
    values = jnp.pad(values, ((0, 0), (0, 0), (0, SIDE - WIN), (0, 0)))
    return values.reshape(images, rows * SIDE, width)


def unpadded(values):
    images, _, width = values.shape
    return values.reshape(images, WIN, SIDE, width)[:, :, :WIN]


def local(
    patches,
    norm1_gain,
    norm1_bias,
    qkv_weight,
    qv_bias,
    rel_pos_h,
    rel_pos_w,
    proj_weight,
    proj_bias,
    norm2_gain,
    norm2_bias,
    fc1_weight,
    fc1_bias,
    fc2_weight,
    fc2_bias,
    heights,
    widths,
    out_grad,
):
    width = patches.shape[-1]
    dims = grid_of(lax.axis_size("dp"))
    core = lax.axis_index("mp")
    is_first = core == 0
    spread, gather = constants()

    def prepare(patches, out_grad, heights, rel_pos_h, rel_pos_w):
        if dims is None:
            orders = [jnp.tile(jnp.arange(PIECES, dtype=jnp.int32), 4)]
        else:
            own, far = place_orders(dims, core), place_orders(dims, 1 - core)
            orders = [own[0], far[0], own[1], far[1]]
        meta = jnp.concatenate(
            orders + [core.astype(jnp.int32)[None], heights, widths, jnp.zeros((11,), jnp.int32)]
        )
        row_index = core * WIN + jnp.arange(WIN)
        valid = (row_index[None, :, None] < heights[:, None, None]) & (
            jnp.arange(WIN)[None, None, :] < widths[:, None, None]
        )
        dm = padded(jnp.where(valid[..., None], out_grad, jnp.zeros_like(out_grad)))
        return padded(patches), dm, meta, *tables(rel_pos_h, rel_pos_w)

    wanted = (patches, out_grad, heights, rel_pos_h, rel_pos_w)
    vectors = (norm1_gain, norm1_bias, qv_bias[0], qv_bias[1], proj_bias, norm2_gain, norm2_bias, fc2_bias)
    small = jnp.pad(jnp.stack(vectors, axis=1), ((0, 0), (0, LANES - len(vectors))))
    qk = jnp.concatenate([qkv_weight[:, :width], small, qkv_weight[:, width : 2 * width]], axis=1)
    vp = jnp.concatenate([qkv_weight[:, 2 * width :], small, proj_weight], axis=1)
    if dims is None:
        qk = lax.all_gather(qk, ("dp", "mp"), axis=0, tiled=True)
        vp = lax.all_gather(vp, ("dp", "mp"), axis=0, tiled=True)
        attend_own = [jnp.where(is_first, qk, vp)]
        attend_far = [jnp.where(is_first, vp, qk)]
        tok, dm, meta, table, table_back = prepare(*wanted)
        hidden_in = tuple(
            ((lax.all_gather(part, "dp", axis=0, tiled=True), 0),) for part in (fc1_weight, fc2_weight.T)
        )
    else:
        fc1, fc2 = fc1_weight, fc2_weight.T
        came = other_core(jnp.where(is_first, vp, qk))
        near = jnp.where(is_first, qk, vp)
        block = jnp.concatenate(
            [jnp.where(is_first, near, came), jnp.where(is_first, came, near)], axis=0
        )
        attend_size, size = block.shape[1], fc1.shape[1]
        tok, dm, meta, table, table_back = prepare(*meet([], *wanted, block)[:5])
        own = jnp.concatenate([block, fc1, fc2], axis=1)
        attend_z, beside = Flow(*along_z(block, dims)), Flow(turn(own, dims, FIRST))
        fc1, fc2, tok, dm, table, table_back, meta = meet(
            [attend_z, beside], fc1, fc2, tok, dm, table, table_back, meta
        )

        attend_z = stack(*attend_z.came)
        z_beside = Flow(turn(attend_z, dims, FIRST))
        own = stack(own, *beside.came)
        over = Flow(turn(own, dims, SECOND))
        fc1_z = Flow(*along_z(after(fc1, own), dims))
        (fc2,) = meet([over, z_beside, fc1_z], fc2)

        over = over.came[0]
        attend_z = stack(attend_z, *z_beside.came)
        z_over = Flow(turn(attend_z, dims, SECOND))
        fc1_z = stack(after(fc1_z.came[0], attend_z), *fc1_z.came[1:])
        fc1_beside = Flow(turn(fc1_z, dims, FIRST))
        fc2_z = Flow(*along_z(after(fc2, fc1_z), dims))
        own_attend = jnp.concatenate([own[:, :attend_size], over[:, :attend_size]], axis=0)
        own_attend, attend_z = meet([z_over, fc1_beside, fc2_z], own_attend, attend_z)

        z_over = z_over.came[0]
        far = Flow(*(other_core(part) for part in (own_attend, attend_z, z_over)))
        fc1_z = stack(fc1_z, *fc1_beside.came)
        fc1_over = Flow(turn(fc1_z, dims, SECOND))
        fc2_z = stack(*fc2_z.came)
        fc2_beside = Flow(turn(fc2_z, dims, FIRST))
        tok, fc1_z, fc2_z, dm = meet([far], tok, fc1_z, fc2_z, dm)
        dm_far = Flow(other_core(dm))
        attend_own, attend_far = [own, over, attend_z, z_over], far.came

    vecs, n1, q, k, v, p, att, weights, x1, n2 = attend(
        meta, tok, table, jnp.asarray(spread, BF16), attend_own, attend_far
    )
    n2_far = other_core(n2).reshape(-1, width)
    if dims is None:
        dm_far = other_core(dm)
    else:
        (n2,) = meet([fc1_over, fc2_beside, dm_far], n2)
        (dm_far,) = dm_far.came
        fc2_z = stack(fc2_z, *fc2_beside.came)
        fc2_over = turn(fc2_z, dims, SECOND)
    dm_flat, dm_far = dm.reshape(-1, width), dm_far.reshape(-1, width)
    n2 = n2.reshape(-1, width)
    bias = fc1_bias[None].astype(F32)
    if dims is not None:
        n2 = after(n2, fc2_z)
        hidden_in = [
            ((own, attend_size), (over, attend_size), (fc1_z, 0), (*fc1_over.came, 0)),
            ((own, attend_size + size), (over, attend_size + size), (fc2_z, 0), (fc2_over, 0)),
        ]
    fc2_part = hidden_fwd(meta, n2, n2_far, dm_flat, dm_far, bias, hidden_in[0])
    if dims is not None:
        fc2_part = meet([], *fc2_part, fc2_over)[:2]
        fc2_sum = Scatter(*fc2_part, dims)
    fc1_bias_part, *fc1_part, back_own, back_far, acts = hidden_back(
        meta, n2, n2_far, dm_flat, dm_far, bias, *hidden_in
    )
    back_far = other_core(back_far)
    if dims is not None:
        fc1_part = meet([fc2_sum], *fc1_part)
        fc2_sum.second()
        fc1_sum = Scatter(*fc1_part, dims)
        back_own = after(back_own, fc2_sum.sent)

    shared = (meta, vecs, jnp.asarray(gather, BF16), table_back, q, k, v, p, weights, att, n1)
    half = width // 2
    def block_of(out_own, out_far):
        branch = add(out_own, out_far).reshape(x1.shape) + vecs[7]
        row_index = core * WIN + jnp.arange(WIN)
        valid = (row_index[None, :, None] < heights[:, None, None]) & (
            jnp.arange(WIN)[None, None, :] < widths[:, None, None]
        )
        return jnp.where(valid[..., None], unpadded(x1 + branch), 0.0).astype(BF16)

    def core_rows(wholes):
        whole = jnp.stack(
            [
                jnp.concatenate([part.reshape(part.shape[0], 2, -1)[:, at] for part in wholes], axis=1)
                for at in range(2)
            ]
        )
        rows = whole.shape[1] // 2
        cuts = whole[:, :rows], whole[:, rows:]
        return jnp.where(is_first, *cuts), jnp.where(is_first, *cuts[::-1])

    count0, count1 = BACK_PARTS
    sums2, bias0, table0, mine0, theirs0, change, dx1, da = attend_back(
        (), count0, *shared, (back_own, back_far, x1, dm)
    )
    if dims is not None:
        da, mine0, theirs0 = meet([fc2_sum], da, mine0, theirs0)
        came0 = other_core(theirs0)
        da, mine0 = meet([fc1_sum, fc2_sum], da, mine0)
        fc2_sum.halve()
        fc1_sum.second()
        both = add(mine0, came0).astype(BF16)
        first = Scatter(both[:half], both[half:], dims)
        da = after(da, both)
    flat, mine, theirs, result = attend_back(
        (count0,), count1, *shared, (da, sums2, bias0, table0, fc1_bias_part, tok, dx1, change)
    )
    if dims is None:
        out_own, out_far = hidden_out(meta, acts, width, hidden_in[1])
        result, block_out = unpadded(result), block_of(out_own, other_core(out_far))
        fc1_sum, fc2_sum = (
            lax.psum_scatter(
                jnp.concatenate(parts, axis=0).astype(F32), "dp", scatter_dimension=0, tiled=True
            )
            for parts in (fc1_part, fc2_part)
        )
        wholes = [
            lax.psum_scatter(add(own, other_core(far)), "dp", scatter_dimension=0, tiled=True)
            for own, far in ((mine0, theirs0), (mine, theirs))
        ]
        near, far = core_rows(wholes)
        came = other_core(far)
        flat = lax.psum(flat, ("dp", "mp"))
    else:
        came, flat_came = Flow(other_core(theirs)), Flow(other_core(flat))
        mine, flat, acts, result = meet([fc2_sum, fc1_sum, first], mine, flat, acts, result)
        first.second()
        fc1_sum.halve()
        mine, flat, acts = meet([came, flat_came, first], mine, flat, acts)
        both = add(mine, came.came[0]).astype(BF16)
        second = Scatter(both[:half], both[half:], dims)
        flat = flat + flat_came.came[0]
        flat_came = Flow(turn(flat, dims, SECOND))
        first.halve()
        fc2_sum.came[0] = after(fc2_sum.came[0], first.sent)
        fc2_sum.quarter()
        acts = after(acts, first.sent, second.sent, fc2_sum.sent)
        out_own, out_far = hidden_out(meta, acts, width, hidden_in[1])
        flat, result, out_far = meet([flat_came, second, fc1_sum, fc2_sum], flat, result, out_far)
        late = Flow(other_core(out_far))
        flat = flat + flat_came.came[0]
        flat_came = Flow(turn(flat, dims, FIRST))
        second.second()
        fc1_sum.quarter()
        fc2_sum = fc2_sum.last()
        result = unpadded(result)
        flat, fc2_sum, result = meet([flat_came, first, second, fc1_sum, late], flat, fc2_sum, result)
        flat = flat + flat_came.came[0]
        flat_came = Flow(swap_z(flat, dims, 2))
        second.third()
        first.quarter()
        fc1_sum.near, late.came[0] = meet([], fc1_sum.near, late.came[0], second.sent, first.sent)[:2]
        fc1_sum = fc1_sum.last()
        block_out = block_of(out_own, late.came[0])
        flat, fc1_sum, block_out = meet([flat_came, second, first], flat, fc1_sum, block_out)

        share = shape((2, width // len(FIRST) // dims[0] // dims[1] // dims[2], width), F32)
        near, far = staged(
            partial(core_rows_kernel, 2), [share, share], first.near, *first.came, second.near, *second.came, meta=meta
        )
        came = other_core(far)
        flat = flat + flat_came.came[0]
        flat_came = swap_z(flat, dims, 1)
        flat = flat + after(flat_came, far)
    rows = near.shape[1]
    outs = [shape((rows, 3 * width), F32), shape((rows, width), F32)]
    qkv_grad, proj_grad = staged(last_rows_kernel, outs, near, came, meta=meta)
    vec_sums, fc1_bias_grad, rel = unpacked(flat, core)
    share = norm1_gain.shape[0]
    device = lax.axis_index("dp") * 2 + core
    mine = lax.dynamic_slice_in_dim(vec_sums, device * share, share, axis=1)
    rels = rel_pos_h.shape[0]
    return (
        block_out,
        result,
        mine[0],
        mine[1],
        qkv_grad,
        mine[2:4],
        rel[:rels],
        rel[32 : 32 + rels],
        proj_grad,
        mine[4],
        mine[5],
        mine[6],
        fc1_sum,
        fc1_bias_grad,
        fc2_sum.T,
        mine[7],
    )


def solution(mesh):
    return jax.shard_map(
        local,
        mesh=mesh,
        in_specs=(
            P("dp", "mp", None, None),
            P(("dp", "mp")),
            P(("dp", "mp")),
            P(("dp", "mp"), None),
            P(None, ("dp", "mp")),
            P(),
            P(),
            P(("dp", "mp"), None),
            P(("dp", "mp")),
            P(("dp", "mp")),
            P(("dp", "mp")),
            P("dp", "mp"),
            P("mp"),
            P("mp", "dp"),
            P(("dp", "mp")),
            P("dp"),
            P("dp"),
            P("dp", "mp", None, None),
        ),
        out_specs=(
            P("dp", "mp", None, None),
            P("dp", "mp", None, None),
            P(("dp", "mp")),
            P(("dp", "mp")),
            P(("dp", "mp"), None),
            P(None, ("dp", "mp")),
            P(),
            P(),
            P(("dp", "mp"), None),
            P(("dp", "mp")),
            P(("dp", "mp")),
            P(("dp", "mp")),
            P("dp", "mp"),
            P("mp"),
            P("mp", "dp"),
            P(("dp", "mp")),
        ),
        check_vma=False,
    )
```

```python
from functools import partial

import jax
import jax.numpy as jnp
import numpy as np
from jax import lax
from jax.experimental import pallas as pl
from jax.experimental.pallas import tpu as pltpu
from jax.sharding import PartitionSpec as P

HEADS = 12
HDIM = 64
LANES = 128
PAIRS = HEADS // 2
WIN = 14
SIDE = 16
TOK = WIN * SIDE
KEYS = 256
PIECES = 16
EPSILON = 1e-06
MASKED_SCORE = -1e30
MASK_LANE = 60
SMALL = 48
CHUNK = 512
BACK_PARTS = (4, 2)
F32 = jnp.float32
BF16 = jnp.bfloat16
SMEM = pl.BlockSpec(memory_space=pltpu.SMEM)
HBM = pl.BlockSpec(memory_space=pl.ANY)
WHOLE = pl.BlockSpec(memory_space=pltpu.VMEM)
VMEM_BYTES = 52 * 2**20
COST = pl.CostEstimate(flops=1000, bytes_accessed=1000, transcendentals=0)


def params():
    return pltpu.CompilerParams(vmem_limit_bytes=VMEM_BYTES)


def shape(dims, dtype):
    return jax.ShapeDtypeStruct(dims, dtype)


def dot(a, b):
    return jnp.dot(a, b, preferred_element_type=F32)


def dot_nt(a, b):
    return lax.dot_general(a, b, (((1,), (1,)), ((), ())), preferred_element_type=F32)


def dot_tn(a, b):
    return lax.dot_general(a, b, (((0,), (0,)), ((), ())), preferred_element_type=F32)


def lanes(rows):
    return lax.broadcasted_iota(jnp.int32, (rows, LANES), 1)


def moments(values):
    centered = values - jnp.mean(values, axis=-1, keepdims=True)
    inverse = lax.rsqrt(jnp.mean(centered * centered, axis=-1, keepdims=True) + EPSILON)
    return centered * inverse, inverse


def norm_back(grad, xhat, inverse, gain):
    scaled = grad * gain
    first = jnp.mean(scaled, axis=-1, keepdims=True)
    second = jnp.mean(scaled * xhat, axis=-1, keepdims=True)
    return inverse * (scaled - first - xhat * second)


def begin(source, dest, sem):
    copy = pltpu.make_async_copy(source, dest, sem)
    copy.start()
    return copy


def finish(copies):
    for copy in copies:
        copy.wait()


def pieces_in(meta, at, ins, start, dest, sems, first):
    rows, cols = dest.shape[0] // PIECES, dest.shape[1]
    copies = []
    for ref, base in ins:
        for part in range(ref.shape[0] // rows):
            place = pl.multiple_of(meta[at + len(copies)] * rows, rows)
            source = ref.at[pl.ds(part * rows, rows), pl.ds(base + start, cols)]
            copies.append(begin(source, dest.at[pl.ds(place, rows), :], sems.at[first + len(copies)]))
    return copies


def row_valid(meta, core, window, rows, width):
    place = lax.broadcasted_iota(jnp.int32, (rows, width), 0)
    row, col = place // SIDE, place % SIDE
    inside = (row < WIN) & (col < WIN)
    return inside & (core * WIN + row < meta[65 + window]) & (col < meta[67 + window])


def relative(turned):
    out = []
    for row in range(WIN):
        slab = turned[row * SIDE : (row + 1) * SIDE]
        down = pltpu.roll(slab, row, 1) if row else slab
        across = pltpu.roll(slab, 0, 1, stride=1, stride_axis=0)
        out.append(jnp.where(lanes(SIDE) % 64 < 32, down, across))
    return jnp.concatenate(out, axis=0)


def columns_of(mat, width, start=0, size=None):
    return mat // 2, pl.ds(mat % 2 * (width + LANES) + start, width if size is None else size)


def attend_kernel(count, total, meta, tok, table, spread, *refs):
    own, other = refs[:count], refs[count:total]
    vecs, n1, q, k, v, p, att, w_out, x1, n2 = refs[total : total + 10]
    toks, weights, aug, n1s, qs, ks, vs, ps, atts, x1s, n2s, sems, out_sems = refs[total + 10 :]
    width = toks.shape[-1]
    core = meta[64]
    copies = [begin(tok, toks, sems.at[2 * PIECES])]
    for found, at, half in ((own, 0, core), (other, 16, 1 - core)):
        found = [(ref, 0) for ref in found]
        copies += pieces_in(meta, at, found, 0, weights.at[half], sems, at)
    for window in range(2):
        valid = row_valid(meta, core, window, KEYS, LANES)
        aug[window] = jnp.where(
            (lanes(KEYS) == MASK_LANE) & ~valid, MASKED_SCORE, spread[...].astype(F32)
        ).astype(BF16)
        ks[window, TOK:] = jnp.zeros((KEYS - TOK, width), BF16)
        vs[window, TOK:] = jnp.zeros((KEYS - TOK, width), BF16)
    copies[0].wait()
    tokens = toks[...].reshape(2 * TOK, width).astype(F32)
    xhat, _ = moments(tokens)
    finish(copies[1:])
    outs = [begin(weights, w_out, out_sems.at[0])]
    vecs[...] = weights[0, :, width : width + LANES].astype(F32).T[:8]
    normed = (xhat * vecs[0:1] + vecs[1:2]).astype(BF16)
    n1s[...] = normed.reshape(2, TOK, width)
    outs.append(begin(n1s, n1, out_sems.at[1]))
    for mat, (made_in, dest) in enumerate(((qs, q), (ks, k), (vs, v))):
        for start in range(0, width, 256):
            cols = pl.ds(start, 256)
            half, here = columns_of(mat, width, start, 256)
            made = dot(normed, weights[half, :, here])
            if mat != 1:
                made = made + vecs[2 + mat // 2 : 3 + mat // 2, cols]
            made = made.astype(BF16)
            made_in[0, :TOK, cols] = made[:TOK]
            made_in[1, :TOK, cols] = made[TOK:]
        outs.append(begin(made_in, dest, out_sems.at[2 + mat]))

    place = lanes(TOK)
    for step in range(2 * PAIRS):
        window, pair = step // PAIRS, step % PAIRS
        cols = pl.ds(pair * LANES, LANES)
        q2, k2, v2 = qs[window, :, cols], ks[window, :, cols], vs[window, :, cols]
        turned = dot(q2, table[...])
        keys_aug = jnp.concatenate([k2, aug[window]], axis=1)
        parts = []
        for half in range(2):
            rel = relative(turned[:, half * LANES : (half + 1) * LANES])
            high = rel.astype(BF16).astype(F32)
            rel = jnp.where(place < 64, high, rel - high)
            rel = jnp.where(place == MASK_LANE, 1.0, rel).astype(BF16)
            mine = jnp.where(place // 64 == half, q2.astype(F32) * HDIM**-0.5, 0.0).astype(BF16)
            scores = dot_nt(jnp.concatenate([mine, rel], axis=1), keys_aug)
            terms = jnp.exp(scores - jnp.max(scores, axis=-1, keepdims=True))
            soft = terms * (1.0 / jnp.sum(terms, axis=-1, keepdims=True))
            ps[window, 2 * pair + half] = soft
            parts.append(dot(soft.astype(BF16), v2))
        atts[window, :, cols] = jnp.where(place < 64, parts[0], parts[1]).astype(BF16)
        heads = pl.ds(2 * pair, 2)
        outs.append(begin(ps.at[window, heads], p.at[window, heads], out_sems.at[len(outs)]))
    outs.append(begin(atts, att, out_sems.at[len(outs)]))
    half, here = columns_of(3, width)
    for window in range(2):
        resid = toks[window].astype(F32) + (dot(atts[window], weights[half, :, here]) + vecs[4:5])
        x1s[window] = resid
        xhat, _ = moments(resid)
        n2s[window] = (xhat * vecs[5:6] + vecs[6:7]).astype(BF16)
        outs.append(begin(x1s.at[window], x1.at[window], out_sems.at[len(outs)]))
        outs.append(begin(n2s.at[window], n2.at[window], out_sems.at[len(outs)]))
    finish(outs)


def attend(meta, tok, table, spread, own, other):
    count, total, width = len(own), len(own) + len(other), tok.shape[-1]
    rows, keys, heads = (2, TOK, width), (2, KEYS, width), (2, HEADS, TOK, KEYS)
    halves = (2, width, 2 * width + LANES)
    outs = [shape(dims, F32 if dims == heads else BF16) for dims in (rows, rows, keys, keys, heads, rows, halves)]
    outs += [shape(rows, F32), shape(rows, BF16)]
    scratch = (rows, halves, (2, KEYS, LANES), rows, rows, keys, keys, heads, rows)
    return pl.pallas_call(
        partial(attend_kernel, count, total),
        out_shape=[shape((8, width), F32)] + outs,
        in_specs=[SMEM, HBM, WHOLE, WHOLE] + [HBM] * total,
        out_specs=[WHOLE] + [HBM] * len(outs),
        scratch_shapes=[pltpu.VMEM(dims, F32 if dims == heads else BF16) for dims in scratch]
        + [
            pltpu.VMEM(rows, F32),
            pltpu.VMEM(rows, BF16),
            pltpu.SemaphoreType.DMA((2 * PIECES + 1,)),
            pltpu.SemaphoreType.DMA((10 + 2 * PAIRS,)),
        ],
        compiler_params=params(),
        cost_estimate=COST,
        name="attend",
    )(meta, tok, table, spread, *own, *other)


def pieces_out(meta, made, cols, keep, send, sems, first):
    rows = made.shape[0] // PIECES
    copies = []
    for piece in range(PIECES):
        dest = keep if piece < PIECES // 2 else send
        place = pl.multiple_of(meta[80 + piece] * rows, rows)
        at = pl.ds(piece % (PIECES // 2) * rows, rows)
        source = made.at[pl.ds(place, rows), cols]
        copies.append(begin(source, dest.at[at, cols], sems.at[first + len(copies)]))
    return copies


def hidden_fwd_kernel(bases, meta, n2a, n2b, dma, dmb, bias, *refs):
    count = len(bases)
    ins, (keep, send) = list(zip(refs[:count], bases)), refs[count : count + 2]
    w0, n2s, dms, grad, sems, out_sems = refs[count + 2 :]
    width, hidden = w0.shape
    at = PIECES
    copies = [begin(n2a, n2s.at[: 2 * TOK], sems.at[at]), begin(n2b, n2s.at[2 * TOK :], sems.at[at + 1])]
    copies += pieces_in(meta, 0, ins, 0, w0, sems, 0)
    dm_copies = [
        begin(dma, dms.at[: 2 * TOK], sems.at[at + 2]),
        begin(dmb, dms.at[2 * TOK :], sems.at[at + 3]),
    ]
    finish(copies)
    outs = []
    for start in range(0, hidden, CHUNK):
        cols = pl.ds(start, CHUNK)
        inner = dot(n2s[...], w0[:, cols]) + bias[:, cols]
        act = (inner * (0.5 + 0.5 * lax.erf(inner * 0.7071067811865476))).astype(BF16)
        if start == 0:
            finish(dm_copies)
        grad[:, cols] = dot_tn(dms[...], act).astype(BF16)
        if start + CHUNK == hidden - CHUNK:
            outs += pieces_out(meta, grad, pl.ds(0, hidden - CHUNK), keep, send, out_sems, 0)
    outs += pieces_out(meta, grad, pl.ds(hidden - CHUNK, CHUNK), keep, send, out_sems, PIECES)
    finish(outs)


def hidden_fwd(meta, n2a, n2b, dma, dmb, bias, ins):
    refs, bases = zip(*ins)
    width, hidden = n2a.shape[-1], bias.shape[-1]
    return pl.pallas_call(
        partial(hidden_fwd_kernel, bases),
        out_shape=[shape((width // 2, hidden), BF16)] * 2,
        in_specs=[SMEM] + [HBM] * 4 + [WHOLE] + [HBM] * len(refs),
        out_specs=[HBM] * 2,
        scratch_shapes=[
            pltpu.VMEM((width, hidden), BF16),
            pltpu.VMEM((4 * TOK, width), BF16),
            pltpu.VMEM((4 * TOK, width), BF16),
            pltpu.VMEM((width, hidden), BF16),
            pltpu.SemaphoreType.DMA((PIECES + 4,)),
            pltpu.SemaphoreType.DMA((2 * PIECES,)),
        ],
        compiler_params=params(),
        cost_estimate=COST,
        name="hidden_fwd",
    )(meta, n2a, n2b, dma, dmb, bias, *refs)


def hidden_back_kernel(bases0, bases1, meta, n2a, n2b, dma, dmb, bias, *refs):
    count = len(bases0)
    ins0, ins1 = list(zip(refs[:count], bases0)), list(zip(refs[count : 2 * count], bases1))
    refs = refs[2 * count :]
    bias_grad, keep, send, back_own, back_far, acts_out = refs[:6]
    w0, w1, n2s, dms, acts, backs, grad, big, small, sems, out_sems = refs[6:]
    width, hidden = w0.shape
    halves = (pl.ds(0, 2 * TOK), pl.ds(2 * TOK, 2 * TOK))
    at = 2 * PIECES
    copies = [begin(ref, n2s.at[half], sems.at[at + i]) for i, (ref, half) in enumerate(zip((n2a, n2b), halves))]
    copies += pieces_in(meta, 0, ins0, 0, w0, sems, 0)
    at += 2
    later = [begin(ref, dms.at[half], sems.at[at + i]) for i, (ref, half) in enumerate(zip((dma, dmb), halves))]
    later += pieces_in(meta, 0, ins1, 0, w1, sems, PIECES)
    finish(copies)
    outs = []
    for start in range(0, hidden, CHUNK):
        cols = pl.ds(start, CHUNK)
        inner = dot(n2s[...], w0[:, cols]) + bias[:, cols]
        if start == 0:
            finish(later)
        back = dot(dms[...], w1[:, cols])
        cdf = 0.5 + 0.5 * lax.erf(inner * 0.7071067811865476)
        density = jnp.exp(inner * inner * -0.5) * 0.3989422804014327
        acts[:, cols] = (inner * cdf).astype(BF16)
        back_pre = (back * (cdf + inner * density)).astype(BF16)
        backs[:, cols] = back_pre
        bias_grad[:, cols] = jnp.sum(back_pre.astype(F32), axis=0, keepdims=True)
        grad[:, cols] = dot_tn(n2s[...], back_pre).astype(BF16)
    outs = pieces_out(meta, grad, pl.ds(0, hidden), keep, send, out_sems, 0)
    outs.append(begin(acts, acts_out, out_sems.at[len(outs)]))
    small[...] = dot_nt(backs[halves[1]], w0[...]).astype(BF16)
    outs.append(begin(small, back_far, out_sems.at[len(outs)]))
    big[...] = dot_nt(backs[halves[0]], w0[...])
    outs.append(begin(big, back_own, out_sems.at[len(outs)]))
    finish(outs)


def hidden_back(meta, n2a, n2b, dma, dmb, bias, ins0, ins1):
    (refs0, bases0), (refs1, bases1) = zip(*ins0), zip(*ins1)
    width, hidden = n2a.shape[-1], bias.shape[-1]
    one = (2 * TOK, width)
    tall = pltpu.VMEM((4 * TOK, width), BF16)
    wide = pltpu.VMEM((width, hidden), BF16)
    return pl.pallas_call(
        partial(hidden_back_kernel, bases0, bases1),
        out_shape=[shape((1, hidden), F32)]
        + [shape((width // 2, hidden), BF16)] * 2
        + [shape(one, F32), shape(one, BF16), shape((4 * TOK, hidden), BF16)],
        in_specs=[SMEM] + [HBM] * 4 + [WHOLE] + [HBM] * (2 * len(refs0)),
        out_specs=[WHOLE] + [HBM] * 5,
        scratch_shapes=[
            wide,
            wide,
            tall,
            tall,
            pltpu.VMEM((4 * TOK, hidden), BF16),
            pltpu.VMEM((4 * TOK, hidden), BF16),
            wide,
            pltpu.VMEM(one, F32),
            pltpu.VMEM(one, BF16),
            pltpu.SemaphoreType.DMA((2 * PIECES + 4,)),
            pltpu.SemaphoreType.DMA((PIECES + 3,)),
        ],
        compiler_params=params(),
        cost_estimate=COST,
        name="hidden_back",
    )(meta, n2a, n2b, dma, dmb, bias, *refs0, *refs1)


def hidden_out_kernel(bases, meta, acts_in, *refs):
    count = len(bases)
    ins, (own, far) = list(zip(refs[:count], bases)), refs[count : count + 2]
    w1, acts, big, small, sems, out_sems = refs[count + 2 :]
    copies = [begin(acts_in, acts, sems.at[PIECES])]
    copies += pieces_in(meta, 0, ins, 0, w1, sems, 0)
    finish(copies)
    big[...] = dot_nt(acts[: 2 * TOK], w1[...])
    outs = [begin(big, own, out_sems.at[0])]
    small[...] = dot_nt(acts[2 * TOK :], w1[...]).astype(BF16)
    outs.append(begin(small, far, out_sems.at[1]))
    finish(outs)


def hidden_out(meta, acts, width, ins):
    refs, bases = zip(*ins)
    hidden = acts.shape[1]
    one = (2 * TOK, width)
    return pl.pallas_call(
        partial(hidden_out_kernel, bases),
        out_shape=[shape(one, F32), shape(one, BF16)],
        in_specs=[SMEM] + [HBM] * (1 + len(refs)),
        out_specs=[HBM] * 2,
        scratch_shapes=[
            pltpu.VMEM((width, hidden), BF16),
            pltpu.VMEM(acts.shape, BF16),
            pltpu.VMEM(one, F32),
            pltpu.VMEM(one, BF16),
            pltpu.SemaphoreType.DMA((PIECES + 1,)),
            pltpu.SemaphoreType.DMA((2,)),
        ],
        compiler_params=params(),
        cost_estimate=COST,
        name="hidden_out",
    )(meta, acts, *refs)


def unrelative(grads):
    out = []
    for row in range(WIN):
        slab = grads[row * SIDE : (row + 1) * SIDE]
        down = pltpu.roll(slab, row, 1) if row else slab
        across = pltpu.roll(slab, 0, 1, stride=1, stride_axis=0)
        out.append(jnp.where(lanes(SIDE) < 32, down, across))
    return jnp.concatenate(out, axis=0)


def attend_back_kernel(before, count, meta, vecs, gather, table, q, k, v, p, weights, att, n1, *refs):
    start, parts = sum(before), len(before)
    first, last = start == 0, start + count == PAIRS
    if first:
        back_own, back_far, x1, dm = refs[:4]
        norm_sums, bias_sums, table_grad, mine, theirs, dqkv_out, dx1, da = refs[4:12]
        refs = refs[12:]
        owns, fars, x1s, dms, dx1s = refs[-5:]
        refs = refs[:-5]
    else:
        da, refs = refs[0], refs[1:]
        if last:
            earlier, tok, dx1, *changes = refs[:4], *refs[4 : 6 + parts]
            flat, mine, theirs, result = refs[6 + parts : 10 + parts]
            refs = refs[10 + parts :]
            bias_sums, wqkv, toks, dx1s, results, *changed = refs[-5 - parts :]
            refs = refs[: -5 - parts]
        else:
            bias_sums, table_grad, mine, theirs, dqkv_out = refs[:5]
            refs = refs[5:]
    das, wproj, atts, n1s, qs, ks, vs, ps, dat, dqkv, grads, sems, out_sems = refs
    core = meta[64]
    width, cols_here = das.shape[-1], qs.shape[-1]
    rows = width // PIECES
    columns = pl.ds(start * LANES, cols_here)
    tokens = (2 * TOK, width)
    early = []
    if first:
        early = [(back_own, owns), (back_far, fars), (x1, x1s), (dm, dms)]
    else:
        early = [(da, das)]
    early = [begin(ref, dest, sems.at[at]) for at, (ref, dest) in enumerate(early)]
    half, here = columns_of(3, width)
    wait_proj = begin(weights.at[half, columns, here], wproj, sems.at[4])
    wait_att = begin(att, atts, sems.at[5])
    wait_v = begin(v.at[:, :, columns], vs, sems.at[6])
    wait_p = []
    for window in range(2):
        for pair in range(count):
            heads = pl.ds(2 * (start + pair), 2)
            wait_p.append(
                begin(p.at[window, heads], ps.at[window, pl.ds(2 * pair, 2)], sems.at[10 + len(wait_p)])
            )
        if window == 0:
            wait_qk = [
                begin(ref.at[:, :, columns], dest, sems.at[7 + at])
                for at, (ref, dest) in enumerate(((q, qs), (k, ks)))
            ]
    wait_n1 = begin(n1, n1s, sems.at[9])
    if last:
        at = 10 + 2 * count
        ends = [begin(tok, toks, sems.at[at]), begin(dx1, dx1s, sems.at[at + 1])]
        for mat in range(3):
            half, here = columns_of(mat, width)
            ends.append(begin(weights.at[half, :, here], wqkv.at[mat], sems.at[at + 2 + mat]))
        for part in range(parts):
            ends.append(begin(changes[part], changed[part], sems.at[at + 5 + part]))
    outs = []
    finish(early)
    if first:
        total = [jnp.zeros((1, width), F32) for _ in range(4)]
        for window in range(2):
            here = pl.ds(window * TOK, TOK)
            grad = owns[here] + fars[here].astype(F32)
            xhat, inverse = moments(x1s[window])
            out_grad = dms[window].astype(F32)
            dresid = out_grad + norm_back(grad, xhat, inverse, vecs[5:6])
            dx1s[window] = dresid
            rounded = dresid.astype(BF16)
            das[window] = rounded
            for slot, value in enumerate((rounded.astype(F32), grad * xhat, grad, out_grad)):
                total[slot] = total[slot] + jnp.sum(value, axis=0, keepdims=True)
        norm_sums[...] = jnp.concatenate(total, axis=0)
        outs.append(begin(dx1s, dx1, out_sems.at[2 * PIECES]))
        outs.append(begin(das, da, out_sems.at[2 * PIECES + 1]))
    wait_proj.wait()
    dat[...] = dot_nt(das[...].reshape(tokens), wproj[...]).astype(BF16).reshape(2, TOK, cols_here)

    def send(half):
        is_own = core == half
        at = jnp.where(is_own, 32, 48) if last else jnp.where(is_own, 80, 96)
        for piece in range(PIECES):
            place = pl.multiple_of(meta[at + piece] * rows, rows)
            source, to = grads.at[half, pl.ds(place, rows), :], pl.ds(piece * rows, rows)
            sem = out_sems.at[half * PIECES + piece]
            copies = [pltpu.make_async_copy(source, ref.at[to, :], sem) for ref in (mine, theirs)]
            pl.when(is_own)(copies[0].start)
            pl.when(~is_own)(copies[1].start)
            outs.append(copies[0])

    wait_att.wait()
    made = dot_tn(atts[...].reshape(tokens), das[:, :, columns].reshape(2 * TOK, cols_here))
    grads[1, :, cols_here:] = made.astype(BF16)
    finish(wait_qk + [wait_v] + wait_p)
    place = lanes(TOK)
    table_sum = jnp.zeros((LANES, LANES), F32)
    for step in range(2 * count):
        window, pair = step // count, step % count
        cols = pl.ds(pair * LANES, LANES)
        q2, k2, v2, dat2 = (ref[window, :, cols] for ref in (qs, ks, vs, dat))
        q8 = (q2.astype(F32) * HDIM**-0.5).astype(BF16)
        k8 = (k2.astype(F32) * HDIM**-0.5).astype(BF16)
        dqs, dks, dvs, dts = [], [], [], []
        for half in range(2):
            soft32 = ps[window, 2 * pair + half]
            soft = soft32.astype(BF16)
            own_lanes = jnp.where(place // 64 == half, dat2.astype(F32), 0.0).astype(BF16)
            weighted = soft32 * dot_nt(own_lanes, v2)
            ds = (weighted - soft32 * jnp.sum(weighted, axis=-1, keepdims=True)).astype(BF16)
            turned = dot(ds, gather[...]).astype(BF16).astype(F32)
            turned = unrelative(turned).astype(BF16)
            dqs.append(dot(ds, k8) + dot(turned, table[half]))
            dks.append(dot_tn(ds, q8))
            dvs.append(dot_tn(soft, dat2))
            dts.append(dot_tn(turned, q2))
        dqkv[0, window, :, cols] = jnp.where(place < 64, dqs[0], dqs[1]).astype(BF16)
        dqkv[1, window, :, cols] = jnp.where(place < 64, dks[0][:TOK], dks[1][:TOK]).astype(BF16)
        dqkv[2, window, :, cols] = jnp.where(place < 64, dvs[0][:TOK], dvs[1][:TOK]).astype(BF16)
        table_sum = table_sum + jnp.where(lanes(LANES) < 64, dts[0], dts[1])
    if not last:
        table_grad[...] = table_sum
    if not last:
        outs.append(begin(dqkv, dqkv_out, out_sems.at[2 * PIECES + 2]))
    wait_n1.wait()
    for mat in (2, 0, 1):
        change = dqkv[mat].reshape(2 * TOK, cols_here)
        made = dot_tn(n1s[...].reshape(tokens), change)
        grads[mat // 2, :, pl.ds(mat % 2 * cols_here, cols_here)] = made.astype(BF16)
        if mat != 0:
            send(mat // 2)
        if mat != 1:
            bias_sums[mat // 2 : mat // 2 + 1] = jnp.sum(change.astype(F32), axis=0, keepdims=True)
    if last:
        finish(ends)
        total = [jnp.zeros((1, width), F32) for _ in range(2)]
        for window in range(2):
            grad = jnp.zeros((TOK, width), F32)
            at = 0
            for change in (*changed, dqkv):
                here = pl.ds(at, change.shape[-1])
                for mat in range(3):
                    grad = grad + dot_nt(change[mat, window], wqkv[mat, :, here])
                at += change.shape[-1]
            xhat, inverse = moments(toks[window].astype(F32))
            results[window] = dx1s[window] + norm_back(grad, xhat, inverse, vecs[0:1])
            outs.append(begin(results.at[window], result.at[window], out_sems.at[2 * PIECES + window]))
            for slot, value in enumerate((grad * xhat, grad)):
                total[slot] = total[slot] + jnp.sum(value, axis=0, keepdims=True)
        norm2_sums, bias0, table0, hidden_sums = earlier
        pack(meta, total, (bias0, bias_sums), norm2_sums, table0[...] + table_sum, hidden_sums, flat)
    finish(outs)


def pack(meta, norm1, biases, norm2, table, hidden, flat):
    flat[...] = jnp.zeros_like(flat)
    parts = biases[0].shape[1] // LANES
    for row in range(8):
        for at in range(6):
            cols = pl.ds(at * LANES, LANES)
            if row < 2:
                value = norm1[row][:, at * LANES : (at + 1) * LANES]
            elif row < 4:
                ref, place = (biases[0], at) if at < parts else (biases[1], at - parts)
                value = ref[row - 2 : row - 1, pl.ds(place * LANES, LANES)]
            else:
                value = norm2[row - 4 : row - 3, cols]
            block = 6 * row + at
            flat[block // 4 : block // 4 + 1, pl.ds(block % 4 * LANES, LANES)] = value
    for block in range(hidden.shape[1] // LANES):
        value = hidden[:, pl.ds(block * LANES, LANES)]
        for core in range(2):
            at = 12 + 3 * core + block // 4
            flat[at : at + 1, pl.ds(block % 4 * LANES, LANES)] = jnp.where(meta[64] == core, value, 0.0)
    both = table[:64] + pltpu.roll(table[:64], HDIM, 1)
    for group in range(4):
        flat[24:40, pl.ds(group * LANES, LANES)] = both[16 * group : 16 * group + 16]


def unpacked(flat, core):
    vectors = flat[:12].reshape(8, -1)
    hidden = lax.dynamic_slice_in_dim(flat, 12 + 3 * core, 3).reshape(-1)
    table = flat[24:40].reshape(16, 4, LANES).transpose(1, 0, 2).reshape(64, LANES)[:, :HDIM]
    return vectors, hidden, table


def attend_back(before, count, meta, vecs, gather, table, q, k, v, p, weights, att, n1, ins):
    width, cols_here = q.shape[-1], count * LANES
    start, parts = sum(before), len(before)
    first, last = start == 0, start + count == PAIRS
    rows, keys = (2, TOK, width), (2, KEYS, cols_here)
    part, flat = (2, TOK, cols_here), (2 * TOK, width)
    heads = (2, 2 * count, TOK, KEYS)
    small = [shape((2, cols_here), F32), shape((LANES, LANES), F32)]
    large = [shape((width, 2 * cols_here), BF16)] * 2
    large.append(shape(rows, F32) if last else shape((3,) + part, BF16))
    if last:
        small = [shape((SMALL, 2 * cols_here), F32)]
    if first:
        small = [shape((4, width), F32)] + small
        large += [shape(rows, F32), shape(rows, BF16)]
    scratch = [rows, (cols_here, width), rows, rows, part, keys, keys, heads, part, (3,) + part]
    scratch.append((2, width, 2 * cols_here))
    scratch = [pltpu.VMEM(dims, F32 if dims == heads else BF16) for dims in scratch]
    scratch += [pltpu.SemaphoreType.DMA((15 + 2 * count + parts,)), pltpu.SemaphoreType.DMA((2 * PIECES + 3,))]
    if first:
        scratch += [
            pltpu.VMEM(flat, F32),
            pltpu.VMEM(flat, BF16),
            pltpu.VMEM(rows, F32),
            pltpu.VMEM(rows, BF16),
            pltpu.VMEM(rows, F32),
        ]
    if last:
        scratch += [
            pltpu.VMEM((2, cols_here), F32),
            pltpu.VMEM((3, width, width), BF16),
            pltpu.VMEM(rows, BF16),
            pltpu.VMEM(rows, F32),
            pltpu.VMEM(rows, F32),
        ] + [pltpu.VMEM((3, 2, TOK, size * LANES), BF16) for size in before]
    return pl.pallas_call(
        partial(attend_back_kernel, before, count),
        out_shape=small + large,
        in_specs=[SMEM] + [WHOLE] * 3 + [HBM] * 8 + [WHOLE if last and at < 4 else HBM for at in range(len(ins) - 1)],
        out_specs=[WHOLE] * len(small) + [HBM] * len(large),
        scratch_shapes=scratch,
        compiler_params=params(),
        cost_estimate=COST,
        name="attend_back",
    )(meta, vecs, gather, table, q, k, v, p, weights, att, n1, *ins)


def grid_of(count):
    return (4, 2, 2) if count == 16 else None


def turn(values, dims, moves):
    pairs = []
    for chip in range(dims[0] * dims[1] * dims[2]):
        for core, (axis, by) in enumerate(moves):
            place = list(np.unravel_index(chip, dims))
            place[axis] = (place[axis] + by) % dims[axis]
            pairs.append((2 * chip + core, 2 * int(np.ravel_multi_index(place, dims)) + core))
    return lax.ppermute(values, ("dp", "mp"), pairs)


ALONG_X, ALONG_Y = ((2, 1),) * 2, ((1, 1),) * 2
FIRST, SECOND = ((2, 1), (1, 1)), ((1, 1), (2, 1))


def along_z(values, dims):
    return [turn(values, dims, ((0, step),) * 2) for step in range(1, dims[0])]


def swap_z(values, dims, by):
    chips = dims[1] * dims[2]
    pairs = [(chip, (chip // chips ^ by) * chips + chip % chips) for chip in range(dims[0] * chips)]
    return lax.ppermute(values, "dp", pairs)


def other_core(values):
    return lax.ppermute(values, "mp", [(0, 1), (1, 0)])


def after(values, *others):
    return lax.optimization_barrier((values, *others))[0]


def stack_kernel(count, *refs):
    ins, out, sems = refs[:count], refs[count], refs[count + 1]
    copies, at = [], 0
    for ref in ins:
        rows = ref.shape[0]
        copies.append(begin(ref, out.at[pl.ds(at, rows)], sems.at[len(copies)]))
        at += rows
    finish(copies)


def stack(*parts):
    rows = sum(part.shape[0] for part in parts)
    return pl.pallas_call(
        partial(stack_kernel, len(parts)),
        out_shape=shape((rows, parts[0].shape[1]), BF16),
        in_specs=[HBM] * len(parts),
        out_specs=HBM,
        scratch_shapes=[pltpu.SemaphoreType.DMA((len(parts),))],
        compiler_params=params(),
        cost_estimate=COST,
        name="stack",
    )(*parts)


class Flow:
    def __init__(self, *came):
        self.came = list(came)


def meet(flows, *values):
    sizes = [len(flow.came) for flow in flows]
    found = list(lax.optimization_barrier((*(part for flow in flows for part in flow.came), *values)))
    for flow, size in zip(flows, sizes):
        flow.came, found = found[:size], found[size:]
    return found


def place_orders(dims, core):
    here = lax.axis_index("dp")
    z, y, x = here // (dims[1] * dims[2]), here // dims[2] % dims[1], here % dims[2]

    def chip(at_z, inner, outer):
        by_x = jnp.where(core == 0, inner, outer)
        by_y = jnp.where(core == 0, outer, inner)
        return (at_z * dims[1] + (y + by_y) % 2) * dims[2] + (x + by_x) % 2

    back = [(z - step) % dims[0] for step in range(dims[0])]
    pairs = [z ^ step for step in range(dims[0])]

    square = [(inner, outer) for outer in range(2) for inner in range(2)]
    gather = [chip(z, *at) for at in square]
    gather += [chip(place, *at) for at in square for place in back[1:]]
    scatter = [chip(place, *at) for at in square for place in back]
    halving = [chip(place, *at) for at in square for place in pairs]
    return [jnp.stack(found).astype(jnp.int32) for found in (gather, scatter, halving)]


def add(a, b):
    return a.astype(F32) + b.astype(F32)


def staged_kernel(kernel, starts, scalars, *refs):
    count = len(starts)
    meta, refs = refs[:scalars], refs[scalars:]
    total = len(refs) // 2
    held, sems = refs[total : 2 * total], refs[2 * total]
    copies = []
    for ref, start, dest in zip(refs, starts, held):
        if start is not None:
            ref = ref.at[pl.ds(start, dest.shape[0])]
        copies.append(begin(ref, dest, sems.at[len(copies)]))
    finish(copies)
    kernel(*meta, *held)
    finish([begin(held[at], refs[at], sems.at[at]) for at in range(count, total)])


def staged(kernel, outs, *ins, meta=None):
    ins = [part if isinstance(part, tuple) else (part, None, part.shape[0]) for part in ins]
    arrays, starts, rows = zip(*ins)
    scalars = () if meta is None else (meta,)
    held = [pltpu.VMEM((count, *array.shape[1:]), array.dtype) for array, count in zip(arrays, rows)]
    held += [pltpu.VMEM(out.shape, out.dtype) for out in outs]
    return pl.pallas_call(
        partial(staged_kernel, kernel, starts, len(scalars)),
        out_shape=outs,
        in_specs=[SMEM] * len(scalars) + [HBM] * len(arrays),
        out_specs=[HBM] * len(outs),
        scratch_shapes=held + [pltpu.SemaphoreType.DMA((len(held),))],
        compiler_params=params(),
        cost_estimate=COST,
        name="staged",
    )(*scalars, *arrays)


def core_rows_kernel(count, meta, *refs):
    *terms, own, far = refs
    half, width = own.shape[1:]
    one, two = (sum(ref[...].astype(F32) for ref in part) for part in (terms[:count], terms[count:]))
    cut, last = one.shape[1] // 2, two.shape[1] // 2
    for core in range(2):

        def put(ref, at=slice(core * half, (core + 1) * half)):
            for mat in range(2):
                ref[mat, :, :cut] = one[at, mat * cut : (mat + 1) * cut]
                ref[mat, :, cut:] = two[at, mat * last : (mat + 1) * last]

        pl.when(meta[64] == core)(partial(put, own))
        pl.when(meta[64] != core)(partial(put, far))


def last_rows_kernel(meta, near, came, qkv, proj):
    width = proj.shape[1]

    def put(qk, vp):
        qkv[:, :width] = qk[0]
        qkv[:, width : 2 * width] = qk[1]
        qkv[:, 2 * width :] = vp[0]
        proj[...] = vp[1]

    pl.when(meta[64] == 0)(partial(put, near, came))
    pl.when(meta[64] != 0)(partial(put, came, near))


class Scatter(Flow):
    def __init__(self, keep, far, dims):
        super().__init__(turn(far, dims, SECOND))
        self.keep, self.dims, self.sent = keep, dims, far

    def second(self):
        half = self.keep.shape[0] // 2
        send = add(self.keep[half:], self.came[0][half:]).astype(BF16)
        self.near = add(self.keep[:half], self.came[0][:half])
        self.sent = send
        self.came = [turn(send, self.dims, FIRST)]

    def third(self):
        near = self.near + self.came[0].astype(F32)
        rows = near.shape[0] // self.dims[0]
        self.near = near[:rows]
        sends = [near[step * rows : (step + 1) * rows].astype(BF16) for step in range(1, self.dims[0])]
        self.sent = sends[0]
        self.came = [
            turn(send, self.dims, ((0, self.dims[0] - step),) * 2) for step, send in enumerate(sends, 1)
        ]

    def halve(self):
        near = self.near + self.came[0].astype(F32)
        rows = near.shape[0] // self.dims[0]
        self.near, self.beside = near[:rows], near[rows : 2 * rows]
        self.sent = near[2 * rows :].astype(BF16)
        self.came = [swap_z(self.sent, self.dims, 2)]

    def quarter(self):
        rows = self.near.shape[0]
        came = self.came[0]
        self.near = self.near + came[:rows].astype(F32)
        self.sent = (self.beside + came[rows:].astype(F32)).astype(BF16)
        self.came = [swap_z(self.sent, self.dims, 1)]

    def last(self):
        return sum((part.astype(F32) for part in self.came), self.near)


def constants():
    key = np.arange(KEYS)
    row, col = key // SIDE, key % SIDE
    inside = (row < WIN) & (col < WIN)
    spread = np.zeros((KEYS, LANES), np.float32)
    gather = np.zeros((KEYS, LANES), np.float32)
    for place in key[inside]:
        for base in (0, 64):
            spread[place, base + WIN - 1 + row[place]] = 1.0
            spread[place, base + 32 + WIN - 1 + col[place]] = 1.0
        gather[place, WIN - 1 - row[place]] = 1.0
        gather[place, 32 + WIN - 1 - col[place]] = 1.0
    return spread, gather


def tables(rel_pos_h, rel_pos_w):
    count = rel_pos_h.shape[0]
    gap = jnp.zeros((32 - count, HDIM), BF16)
    turned = jnp.concatenate([rel_pos_h[::-1], gap, rel_pos_w[::-1], gap], axis=0)
    turned = jnp.concatenate([turned, turned], axis=0).T
    none = jnp.zeros_like(turned)
    forward = jnp.concatenate(
        [jnp.concatenate([turned, none], axis=0), jnp.concatenate([none, turned], axis=0)], axis=1
    )
    straight = jnp.concatenate([rel_pos_h, gap, rel_pos_w, gap], axis=0)
    straight = jnp.concatenate([straight, jnp.zeros_like(straight)], axis=0)
    none = jnp.zeros_like(straight)
    backward = jnp.stack(
        [
            jnp.concatenate([straight, none], axis=1),
            jnp.concatenate([none, straight], axis=1),
        ]
    )
    return forward, backward


def padded(values):
    images, rows, _, width = values.shape
    values = jnp.pad(values, ((0, 0), (0, 0), (0, SIDE - WIN), (0, 0)))
    return values.reshape(images, rows * SIDE, width)


def unpadded(values):
    images, _, width = values.shape
    return values.reshape(images, WIN, SIDE, width)[:, :, :WIN]


def local(
    patches,
    norm1_gain,
    norm1_bias,
    qkv_weight,
    qv_bias,
    rel_pos_h,
    rel_pos_w,
    proj_weight,
    proj_bias,
    norm2_gain,
    norm2_bias,
    fc1_weight,
    fc1_bias,
    fc2_weight,
    fc2_bias,
    heights,
    widths,
    out_grad,
):
    width = patches.shape[-1]
    dims = grid_of(lax.axis_size("dp"))
    core = lax.axis_index("mp")
    is_first = core == 0
    spread, gather = constants()

    def prepare(patches, out_grad, heights, rel_pos_h, rel_pos_w):
        if dims is None:
            orders = [jnp.tile(jnp.arange(PIECES, dtype=jnp.int32), 4)]
            halving = [orders[0][: 2 * PIECES]]
        else:
            own, far = place_orders(dims, core), place_orders(dims, 1 - core)
            orders = [own[0], far[0], own[1], far[1]]
            halving = [own[2], far[2]]
        meta = jnp.concatenate(
            orders + [core.astype(jnp.int32)[None], heights, widths, jnp.zeros((11,), jnp.int32)] + halving
        )
        row_index = core * WIN + jnp.arange(WIN)
        valid = (row_index[None, :, None] < heights[:, None, None]) & (
            jnp.arange(WIN)[None, None, :] < widths[:, None, None]
        )
        dm = padded(jnp.where(valid[..., None], out_grad, jnp.zeros_like(out_grad)))
        return padded(patches), dm, meta, *tables(rel_pos_h, rel_pos_w)

    wanted = (patches, out_grad, heights, rel_pos_h, rel_pos_w)
    vectors = (norm1_gain, norm1_bias, qv_bias[0], qv_bias[1], proj_bias, norm2_gain, norm2_bias, fc2_bias)
    small = jnp.pad(jnp.stack(vectors, axis=1), ((0, 0), (0, LANES - len(vectors))))
    qk = jnp.concatenate([qkv_weight[:, :width], small, qkv_weight[:, width : 2 * width]], axis=1)
    vp = jnp.concatenate([qkv_weight[:, 2 * width :], small, proj_weight], axis=1)
    if dims is None:
        qk = lax.all_gather(qk, ("dp", "mp"), axis=0, tiled=True)
        vp = lax.all_gather(vp, ("dp", "mp"), axis=0, tiled=True)
        attend_own = [jnp.where(is_first, qk, vp)]
        attend_far = [jnp.where(is_first, vp, qk)]
        tok, dm, meta, table, table_back = prepare(*wanted)
        hidden_in = tuple(
            ((lax.all_gather(part, "dp", axis=0, tiled=True), 0),) for part in (fc1_weight, fc2_weight.T)
        )
    else:
        fc1, fc2 = fc1_weight, fc2_weight.T
        came = other_core(jnp.where(is_first, vp, qk))
        near = jnp.where(is_first, qk, vp)
        block = jnp.concatenate(
            [jnp.where(is_first, near, came), jnp.where(is_first, came, near)], axis=0
        )
        attend_size, size = block.shape[1], fc1.shape[1]
        tok, dm, meta, table, table_back = prepare(*meet([], *wanted, block)[:5])
        own = jnp.concatenate([block, fc1, fc2], axis=1)
        attend_z, beside = Flow(*along_z(block, dims)), Flow(turn(own, dims, FIRST))
        fc1, fc2, tok, dm, table, table_back, meta = meet(
            [attend_z, beside], fc1, fc2, tok, dm, table, table_back, meta
        )

        attend_z = stack(*attend_z.came)
        z_beside = Flow(turn(attend_z, dims, FIRST))
        own = stack(own, *beside.came)
        over = Flow(turn(own, dims, SECOND))
        fc1_z = Flow(*along_z(after(fc1, own), dims))
        (fc2,) = meet([over, z_beside, fc1_z], fc2)

        over = over.came[0]
        attend_z = stack(attend_z, *z_beside.came)
        z_over = Flow(turn(attend_z, dims, SECOND))
        fc1_z = stack(after(fc1_z.came[0], attend_z), *fc1_z.came[1:])
        fc1_beside = Flow(turn(fc1_z, dims, FIRST))
        fc2_z = Flow(*along_z(after(fc2, fc1_z), dims))
        own_attend = jnp.concatenate([own[:, :attend_size], over[:, :attend_size]], axis=0)
        own_attend, attend_z = meet([z_over, fc1_beside, fc2_z], own_attend, attend_z)

        z_over = z_over.came[0]
        far = Flow(*(other_core(part) for part in (own_attend, attend_z, z_over)))
        fc1_z = stack(fc1_z, *fc1_beside.came)
        fc1_over = Flow(turn(fc1_z, dims, SECOND))
        fc2_z = stack(*fc2_z.came)
        fc2_beside = Flow(turn(fc2_z, dims, FIRST))
        tok, fc1_z, fc2_z, dm = meet([far], tok, fc1_z, fc2_z, dm)
        dm_far = Flow(other_core(dm))
        attend_own, attend_far = [own, over, attend_z, z_over], far.came

    vecs, n1, q, k, v, p, att, weights, x1, n2 = attend(
        meta, tok, table, jnp.asarray(spread, BF16), attend_own, attend_far
    )
    n2_far = other_core(n2).reshape(-1, width)
    if dims is None:
        dm_far = other_core(dm)
    else:
        (n2,) = meet([fc1_over, fc2_beside, dm_far], n2)
        (dm_far,) = dm_far.came
        fc2_z = stack(fc2_z, *fc2_beside.came)
        fc2_over = turn(fc2_z, dims, SECOND)
    dm_flat, dm_far = dm.reshape(-1, width), dm_far.reshape(-1, width)
    n2 = n2.reshape(-1, width)
    bias = fc1_bias[None].astype(F32)
    if dims is not None:
        n2 = after(n2, fc2_z)
        hidden_in = [
            ((own, attend_size), (over, attend_size), (fc1_z, 0), (*fc1_over.came, 0)),
            ((own, attend_size + size), (over, attend_size + size), (fc2_z, 0), (fc2_over, 0)),
        ]
    fc2_part = hidden_fwd(meta, n2, n2_far, dm_flat, dm_far, bias, hidden_in[0])
    if dims is not None:
        fc2_part = meet([], *fc2_part, fc2_over)[:2]
        fc2_sum = Scatter(*fc2_part, dims)
    fc1_bias_part, *fc1_part, back_own, back_far, acts = hidden_back(
        meta, n2, n2_far, dm_flat, dm_far, bias, *hidden_in
    )
    back_far = other_core(back_far)
    if dims is not None:
        fc1_part = meet([fc2_sum], *fc1_part)
        fc2_sum.second()
        fc1_sum = Scatter(*fc1_part, dims)
        back_own = after(back_own, fc2_sum.sent)

    shared = (meta, vecs, jnp.asarray(gather, BF16), table_back, q, k, v, p, weights, att, n1)
    half = width // 2
    def block_of(out_own, out_far):
        branch = add(out_own, out_far).reshape(x1.shape) + vecs[7]
        row_index = core * WIN + jnp.arange(WIN)
        valid = (row_index[None, :, None] < heights[:, None, None]) & (
            jnp.arange(WIN)[None, None, :] < widths[:, None, None]
        )
        return jnp.where(valid[..., None], unpadded(x1 + branch), 0.0).astype(BF16)

    def core_rows(wholes):
        whole = jnp.stack(
            [
                jnp.concatenate([part.reshape(part.shape[0], 2, -1)[:, at] for part in wholes], axis=1)
                for at in range(2)
            ]
        )
        rows = whole.shape[1] // 2
        cuts = whole[:, :rows], whole[:, rows:]
        return jnp.where(is_first, *cuts), jnp.where(is_first, *cuts[::-1])

    count0, count1 = BACK_PARTS
    sums2, bias0, table0, mine0, theirs0, change, dx1, da = attend_back(
        (), count0, *shared, (back_own, back_far, x1, dm)
    )
    if dims is not None:
        da, mine0, theirs0 = meet([fc2_sum], da, mine0, theirs0)
        came0 = other_core(theirs0)
        da, mine0 = meet([fc1_sum, fc2_sum], da, mine0)
        fc2_sum.halve()
        fc1_sum.second()
        both = add(mine0, came0).astype(BF16)
        first = Scatter(both[:half], both[half:], dims)
        da = after(da, both)
    flat, mine, theirs, result = attend_back(
        (count0,), count1, *shared, (da, sums2, bias0, table0, fc1_bias_part, tok, dx1, change)
    )
    if dims is None:
        out_own, out_far = hidden_out(meta, acts, width, hidden_in[1])
        result, block_out = unpadded(result), block_of(out_own, other_core(out_far))
        fc1_sum, fc2_sum = (
            lax.psum_scatter(
                jnp.concatenate(parts, axis=0).astype(F32), "dp", scatter_dimension=0, tiled=True
            )
            for parts in (fc1_part, fc2_part)
        )
        wholes = [
            lax.psum_scatter(add(own, other_core(far)), "dp", scatter_dimension=0, tiled=True)
            for own, far in ((mine0, theirs0), (mine, theirs))
        ]
        near, far = core_rows(wholes)
        came = other_core(far)
        flat = lax.psum(flat, ("dp", "mp"))
    else:
        came, flat_came = Flow(other_core(theirs)), Flow(other_core(flat))
        mine, flat, acts, result = meet([fc2_sum, fc1_sum, first], mine, flat, acts, result)
        first.second()
        fc1_sum.halve()
        mine, flat, acts = meet([came, flat_came, first], mine, flat, acts)
        both = add(mine, came.came[0]).astype(BF16)
        second = Scatter(both[:half], both[half:], dims)
        flat = flat + flat_came.came[0]
        flat_came = Flow(turn(flat, dims, SECOND))
        first.halve()
        fc2_sum.came[0] = after(fc2_sum.came[0], first.sent)
        fc2_sum.quarter()
        acts = after(acts, first.sent, second.sent, fc2_sum.sent)
        out_own, out_far = hidden_out(meta, acts, width, hidden_in[1])
        flat, result, out_far = meet([flat_came, second, fc1_sum, fc2_sum], flat, result, out_far)
        late = Flow(other_core(out_far))
        flat = flat + flat_came.came[0]
        flat_came = Flow(turn(flat, dims, FIRST))
        second.second()
        fc1_sum.quarter()
        fc2_sum = fc2_sum.last()
        result = unpadded(result)
        flat, fc2_sum, result = meet([flat_came, first, second, fc1_sum, late], flat, fc2_sum, result)
        flat = flat + flat_came.came[0]
        flat_came = Flow(swap_z(flat, dims, 2))
        second.third()
        first.quarter()
        fc1_sum.near, late.came[0] = meet([], fc1_sum.near, late.came[0], second.sent, first.sent)[:2]
        fc1_sum = fc1_sum.last()
        block_out = block_of(out_own, late.came[0])
        flat, fc1_sum, block_out = meet([flat_came, second, first], flat, fc1_sum, block_out)

        share = shape((2, width // len(FIRST) // dims[0] // dims[1] // dims[2], width), F32)
        near, far = staged(
            partial(core_rows_kernel, 2), [share, share], first.near, *first.came, second.near, *second.came, meta=meta
        )
        came = other_core(far)
        flat = flat + flat_came.came[0]
        flat_came = swap_z(flat, dims, 1)
        flat = flat + after(flat_came, far)
    rows = near.shape[1]
    outs = [shape((rows, 3 * width), F32), shape((rows, width), F32)]
    qkv_grad, proj_grad = staged(last_rows_kernel, outs, near, came, meta=meta)
    vec_sums, fc1_bias_grad, rel = unpacked(flat, core)
    share = norm1_gain.shape[0]
    device = lax.axis_index("dp") * 2 + core
    mine = lax.dynamic_slice_in_dim(vec_sums, device * share, share, axis=1)
    rels = rel_pos_h.shape[0]
    return (
        block_out,
        result,
        mine[0],
        mine[1],
        qkv_grad,
        mine[2:4],
        rel[:rels],
        rel[32 : 32 + rels],
        proj_grad,
        mine[4],
        mine[5],
        mine[6],
        fc1_sum,
        fc1_bias_grad,
        fc2_sum.T,
        mine[7],
    )


def solution(mesh):
    return jax.shard_map(
        local,
        mesh=mesh,
        in_specs=(
            P("dp", "mp", None, None),
            P(("dp", "mp")),
            P(("dp", "mp")),
            P(("dp", "mp"), None),
            P(None, ("dp", "mp")),
            P(),
            P(),
            P(("dp", "mp"), None),
            P(("dp", "mp")),
            P(("dp", "mp")),
            P(("dp", "mp")),
            P("dp", "mp"),
            P("mp"),
            P("mp", "dp"),
            P(("dp", "mp")),
            P("dp"),
            P("dp"),
            P("dp", "mp", None, None),
        ),
        out_specs=(
            P("dp", "mp", None, None),
            P("dp", "mp", None, None),
            P(("dp", "mp")),
            P(("dp", "mp")),
            P(("dp", "mp"), None),
            P(None, ("dp", "mp")),
            P(),
            P(),
            P(("dp", "mp"), None),
            P(("dp", "mp")),
            P(("dp", "mp")),
            P(("dp", "mp")),
            P("dp", "mp"),
            P("mp"),
            P("mp", "dp"),
            P(("dp", "mp")),
        ),
        check_vma=False,
    )
```

```python
from functools import partial

import jax
import jax.numpy as jnp
import numpy as np
from jax import lax
from jax.experimental import pallas as pl
from jax.experimental.pallas import tpu as pltpu
from jax.sharding import PartitionSpec as P

HEADS = 12
HDIM = 64
LANES = 128
PAIRS = HEADS // 2
WIN = 14
SIDE = 16
TOK = WIN * SIDE
KEYS = 256
PIECES = 16
EPSILON = 1e-06
MASKED_SCORE = -1e30
MASK_LANE = 60
SMALL = 48
CHUNK = 512
BACK_PARTS = (4, 2)
F32 = jnp.float32
BF16 = jnp.bfloat16
SMEM = pl.BlockSpec(memory_space=pltpu.SMEM)
HBM = pl.BlockSpec(memory_space=pl.ANY)
WHOLE = pl.BlockSpec(memory_space=pltpu.VMEM)
VMEM_BYTES = 52 * 2**20
COST = pl.CostEstimate(flops=1000, bytes_accessed=1000, transcendentals=0)


def params():
    return pltpu.CompilerParams(vmem_limit_bytes=VMEM_BYTES)


def shape(dims, dtype):
    return jax.ShapeDtypeStruct(dims, dtype)


def dot(a, b):
    return jnp.dot(a, b, preferred_element_type=F32)


def dot_nt(a, b):
    return lax.dot_general(a, b, (((1,), (1,)), ((), ())), preferred_element_type=F32)


def dot_tn(a, b):
    return lax.dot_general(a, b, (((0,), (0,)), ((), ())), preferred_element_type=F32)


def lanes(rows):
    return lax.broadcasted_iota(jnp.int32, (rows, LANES), 1)


def moments(values):
    centered = values - jnp.mean(values, axis=-1, keepdims=True)
    inverse = lax.rsqrt(jnp.mean(centered * centered, axis=-1, keepdims=True) + EPSILON)
    return centered * inverse, inverse


def norm_back(grad, xhat, inverse, gain):
    scaled = grad * gain
    first = jnp.mean(scaled, axis=-1, keepdims=True)
    second = jnp.mean(scaled * xhat, axis=-1, keepdims=True)
    return inverse * (scaled - first - xhat * second)


def begin(source, dest, sem):
    copy = pltpu.make_async_copy(source, dest, sem)
    copy.start()
    return copy


def finish(copies):
    for copy in copies:
        copy.wait()


def pieces_in(meta, at, ins, start, dest, sems, first):
    rows, cols = dest.shape[0] // PIECES, dest.shape[1]
    copies = []
    for ref, base in ins:
        for part in range(ref.shape[0] // rows):
            place = pl.multiple_of(meta[at + len(copies)] * rows, rows)
            source = ref.at[pl.ds(part * rows, rows), pl.ds(base + start, cols)]
            copies.append(begin(source, dest.at[pl.ds(place, rows), :], sems.at[first + len(copies)]))
    return copies


def row_valid(meta, core, window, rows, width):
    place = lax.broadcasted_iota(jnp.int32, (rows, width), 0)
    row, col = place // SIDE, place % SIDE
    inside = (row < WIN) & (col < WIN)
    return inside & (core * WIN + row < meta[65 + window]) & (col < meta[67 + window])


def relative(turned):
    out = []
    for row in range(WIN):
        slab = turned[row * SIDE : (row + 1) * SIDE]
        down = pltpu.roll(slab, row, 1) if row else slab
        across = pltpu.roll(slab, 0, 1, stride=1, stride_axis=0)
        out.append(jnp.where(lanes(SIDE) % 64 < 32, down, across))
    return jnp.concatenate(out, axis=0)


def columns_of(mat, width, start=0, size=None):
    return mat // 2, pl.ds(mat % 2 * (width + LANES) + start, width if size is None else size)


def attend_kernel(count, total, meta, tok, table, spread, *refs):
    own, other = refs[:count], refs[count:total]
    vecs, n1, q, k, v, p, att, w_out, x1, n2 = refs[total : total + 10]
    toks, weights, aug, n1s, qs, ks, vs, ps, atts, x1s, n2s, sems, out_sems = refs[total + 10 :]
    width = toks.shape[-1]
    core = meta[64]
    copies = [begin(tok, toks, sems.at[2 * PIECES])]
    for found, at, half in ((own, 0, core), (other, 16, 1 - core)):
        found = [(ref, 0) for ref in found]
        copies += pieces_in(meta, at, found, 0, weights.at[half], sems, at)
    for window in range(2):
        valid = row_valid(meta, core, window, KEYS, LANES)
        aug[window] = jnp.where(
            (lanes(KEYS) == MASK_LANE) & ~valid, MASKED_SCORE, spread[...].astype(F32)
        ).astype(BF16)
        ks[window, TOK:] = jnp.zeros((KEYS - TOK, width), BF16)
        vs[window, TOK:] = jnp.zeros((KEYS - TOK, width), BF16)
    copies[0].wait()
    tokens = toks[...].reshape(2 * TOK, width).astype(F32)
    xhat, _ = moments(tokens)
    finish(copies[1:])
    outs = [begin(weights, w_out, out_sems.at[0])]
    vecs[...] = weights[0, :, width : width + LANES].astype(F32).T[:8]
    normed = (xhat * vecs[0:1] + vecs[1:2]).astype(BF16)
    n1s[...] = normed.reshape(2, TOK, width)
    outs.append(begin(n1s, n1, out_sems.at[1]))
    for mat, (made_in, dest) in enumerate(((qs, q), (ks, k), (vs, v))):
        for start in range(0, width, 256):
            cols = pl.ds(start, 256)
            half, here = columns_of(mat, width, start, 256)
            made = dot(normed, weights[half, :, here])
            if mat != 1:
                made = made + vecs[2 + mat // 2 : 3 + mat // 2, cols]
            made = made.astype(BF16)
            made_in[0, :TOK, cols] = made[:TOK]
            made_in[1, :TOK, cols] = made[TOK:]
        outs.append(begin(made_in, dest, out_sems.at[2 + mat]))

    place = lanes(TOK)
    for step in range(2 * PAIRS):
        window, pair = step // PAIRS, step % PAIRS
        cols = pl.ds(pair * LANES, LANES)
        q2, k2, v2 = qs[window, :, cols], ks[window, :, cols], vs[window, :, cols]
        turned = dot(q2, table[...])
        keys_aug = jnp.concatenate([k2, aug[window]], axis=1)
        parts = []
        for half in range(2):
            rel = relative(turned[:, half * LANES : (half + 1) * LANES])
            high = rel.astype(BF16).astype(F32)
            rel = jnp.where(place < 64, high, rel - high)
            rel = jnp.where(place == MASK_LANE, 1.0, rel).astype(BF16)
            mine = jnp.where(place // 64 == half, q2.astype(F32) * HDIM**-0.5, 0.0).astype(BF16)
            scores = dot_nt(jnp.concatenate([mine, rel], axis=1), keys_aug)
            terms = jnp.exp(scores - jnp.max(scores, axis=-1, keepdims=True))
            soft = terms * (1.0 / jnp.sum(terms, axis=-1, keepdims=True))
            ps[window, 2 * pair + half] = soft
            parts.append(dot(soft.astype(BF16), v2))
        atts[window, :, cols] = jnp.where(place < 64, parts[0], parts[1]).astype(BF16)
        heads = pl.ds(2 * pair, 2)
        outs.append(begin(ps.at[window, heads], p.at[window, heads], out_sems.at[len(outs)]))
    outs.append(begin(atts, att, out_sems.at[len(outs)]))
    half, here = columns_of(3, width)
    for window in range(2):
        resid = toks[window].astype(F32) + (dot(atts[window], weights[half, :, here]) + vecs[4:5])
        x1s[window] = resid
        xhat, _ = moments(resid)
        n2s[window] = (xhat * vecs[5:6] + vecs[6:7]).astype(BF16)
        outs.append(begin(x1s.at[window], x1.at[window], out_sems.at[len(outs)]))
        outs.append(begin(n2s.at[window], n2.at[window], out_sems.at[len(outs)]))
    finish(outs)


def attend(meta, tok, table, spread, own, other):
    count, total, width = len(own), len(own) + len(other), tok.shape[-1]
    rows, keys, heads = (2, TOK, width), (2, KEYS, width), (2, HEADS, TOK, KEYS)
    halves = (2, width, 2 * width + LANES)
    outs = [shape(dims, F32 if dims == heads else BF16) for dims in (rows, rows, keys, keys, heads, rows, halves)]
    outs += [shape(rows, F32), shape(rows, BF16)]
    scratch = (rows, halves, (2, KEYS, LANES), rows, rows, keys, keys, heads, rows)
    return pl.pallas_call(
        partial(attend_kernel, count, total),
        out_shape=[shape((8, width), F32)] + outs,
        in_specs=[SMEM, HBM, WHOLE, WHOLE] + [HBM] * total,
        out_specs=[WHOLE] + [HBM] * len(outs),
        scratch_shapes=[pltpu.VMEM(dims, F32 if dims == heads else BF16) for dims in scratch]
        + [
            pltpu.VMEM(rows, F32),
            pltpu.VMEM(rows, BF16),
            pltpu.SemaphoreType.DMA((2 * PIECES + 1,)),
            pltpu.SemaphoreType.DMA((10 + 2 * PAIRS,)),
        ],
        compiler_params=params(),
        cost_estimate=COST,
        name="attend",
    )(meta, tok, table, spread, *own, *other)


def pieces_out(meta, made, cols, keep, send, sems, first):
    rows = made.shape[0] // PIECES
    copies = []
    for piece in range(PIECES):
        dest = keep if piece < PIECES // 2 else send
        place = pl.multiple_of(meta[80 + piece] * rows, rows)
        at = pl.ds(piece % (PIECES // 2) * rows, rows)
        source = made.at[pl.ds(place, rows), cols]
        copies.append(begin(source, dest.at[at, cols], sems.at[first + len(copies)]))
    return copies


def hidden_fwd_kernel(bases, meta, n2a, n2b, dma, dmb, bias, *refs):
    count = len(bases)
    ins, (keep, send) = list(zip(refs[:count], bases)), refs[count : count + 2]
    w0, n2s, dms, grad, sems, out_sems = refs[count + 2 :]
    width, hidden = w0.shape
    at = PIECES
    copies = [begin(n2a, n2s.at[: 2 * TOK], sems.at[at]), begin(n2b, n2s.at[2 * TOK :], sems.at[at + 1])]
    copies += pieces_in(meta, 0, ins, 0, w0, sems, 0)
    dm_copies = [
        begin(dma, dms.at[: 2 * TOK], sems.at[at + 2]),
        begin(dmb, dms.at[2 * TOK :], sems.at[at + 3]),
    ]
    finish(copies)
    outs = []
    for start in range(0, hidden, CHUNK):
        cols = pl.ds(start, CHUNK)
        inner = dot(n2s[...], w0[:, cols]) + bias[:, cols]
        act = (inner * (0.5 + 0.5 * lax.erf(inner * 0.7071067811865476))).astype(BF16)
        if start == 0:
            finish(dm_copies)
        grad[:, cols] = dot_tn(dms[...], act).astype(BF16)
        if start + CHUNK == hidden - CHUNK:
            outs += pieces_out(meta, grad, pl.ds(0, hidden - CHUNK), keep, send, out_sems, 0)
    outs += pieces_out(meta, grad, pl.ds(hidden - CHUNK, CHUNK), keep, send, out_sems, PIECES)
    finish(outs)


def hidden_fwd(meta, n2a, n2b, dma, dmb, bias, ins):
    refs, bases = zip(*ins)
    width, hidden = n2a.shape[-1], bias.shape[-1]
    return pl.pallas_call(
        partial(hidden_fwd_kernel, bases),
        out_shape=[shape((width // 2, hidden), BF16)] * 2,
        in_specs=[SMEM] + [HBM] * 4 + [WHOLE] + [HBM] * len(refs),
        out_specs=[HBM] * 2,
        scratch_shapes=[
            pltpu.VMEM((width, hidden), BF16),
            pltpu.VMEM((4 * TOK, width), BF16),
            pltpu.VMEM((4 * TOK, width), BF16),
            pltpu.VMEM((width, hidden), BF16),
            pltpu.SemaphoreType.DMA((PIECES + 4,)),
            pltpu.SemaphoreType.DMA((2 * PIECES,)),
        ],
        compiler_params=params(),
        cost_estimate=COST,
        name="hidden_fwd",
    )(meta, n2a, n2b, dma, dmb, bias, *refs)


def hidden_back_kernel(bases0, bases1, meta, n2a, n2b, dma, dmb, bias, *refs):
    count = len(bases0)
    ins0, ins1 = list(zip(refs[:count], bases0)), list(zip(refs[count : 2 * count], bases1))
    refs = refs[2 * count :]
    bias_grad, keep, send, back_own, back_far, acts_out = refs[:6]
    w0, w1, n2s, dms, acts, backs, grad, big, small, sems, out_sems = refs[6:]
    width, hidden = w0.shape
    halves = (pl.ds(0, 2 * TOK), pl.ds(2 * TOK, 2 * TOK))
    at = 2 * PIECES
    copies = [begin(ref, n2s.at[half], sems.at[at + i]) for i, (ref, half) in enumerate(zip((n2a, n2b), halves))]
    copies += pieces_in(meta, 0, ins0, 0, w0, sems, 0)
    at += 2
    later = [begin(ref, dms.at[half], sems.at[at + i]) for i, (ref, half) in enumerate(zip((dma, dmb), halves))]
    later += pieces_in(meta, 0, ins1, 0, w1, sems, PIECES)
    finish(copies)
    outs = []
    for start in range(0, hidden, CHUNK):
        cols = pl.ds(start, CHUNK)
        inner = dot(n2s[...], w0[:, cols]) + bias[:, cols]
        if start == 0:
            finish(later)
        back = dot(dms[...], w1[:, cols])
        cdf = 0.5 + 0.5 * lax.erf(inner * 0.7071067811865476)
        density = jnp.exp(inner * inner * -0.5) * 0.3989422804014327
        acts[:, cols] = (inner * cdf).astype(BF16)
        back_pre = (back * (cdf + inner * density)).astype(BF16)
        backs[:, cols] = back_pre
        bias_grad[:, cols] = jnp.sum(back_pre.astype(F32), axis=0, keepdims=True)
        grad[:, cols] = dot_tn(n2s[...], back_pre).astype(BF16)
    outs = pieces_out(meta, grad, pl.ds(0, hidden), keep, send, out_sems, 0)
    outs.append(begin(acts, acts_out, out_sems.at[len(outs)]))
    small[...] = dot_nt(backs[halves[1]], w0[...]).astype(BF16)
    outs.append(begin(small, back_far, out_sems.at[len(outs)]))
    big[...] = dot_nt(backs[halves[0]], w0[...])
    outs.append(begin(big, back_own, out_sems.at[len(outs)]))
    finish(outs)


def hidden_back(meta, n2a, n2b, dma, dmb, bias, ins0, ins1):
    (refs0, bases0), (refs1, bases1) = zip(*ins0), zip(*ins1)
    width, hidden = n2a.shape[-1], bias.shape[-1]
    one = (2 * TOK, width)
    tall = pltpu.VMEM((4 * TOK, width), BF16)
    wide = pltpu.VMEM((width, hidden), BF16)
    return pl.pallas_call(
        partial(hidden_back_kernel, bases0, bases1),
        out_shape=[shape((1, hidden), F32)]
        + [shape((width // 2, hidden), BF16)] * 2
        + [shape(one, F32), shape(one, BF16), shape((4 * TOK, hidden), BF16)],
        in_specs=[SMEM] + [HBM] * 4 + [WHOLE] + [HBM] * (2 * len(refs0)),
        out_specs=[WHOLE] + [HBM] * 5,
        scratch_shapes=[
            wide,
            wide,
            tall,
            tall,
            pltpu.VMEM((4 * TOK, hidden), BF16),
            pltpu.VMEM((4 * TOK, hidden), BF16),
            wide,
            pltpu.VMEM(one, F32),
            pltpu.VMEM(one, BF16),
            pltpu.SemaphoreType.DMA((2 * PIECES + 4,)),
            pltpu.SemaphoreType.DMA((PIECES + 3,)),
        ],
        compiler_params=params(),
        cost_estimate=COST,
        name="hidden_back",
    )(meta, n2a, n2b, dma, dmb, bias, *refs0, *refs1)


def hidden_out_kernel(bases, meta, acts_in, *refs):
    count = len(bases)
    ins, (own, far) = list(zip(refs[:count], bases)), refs[count : count + 2]
    w1, acts, big, small, sems, out_sems = refs[count + 2 :]
    copies = [begin(acts_in, acts, sems.at[PIECES])]
    copies += pieces_in(meta, 0, ins, 0, w1, sems, 0)
    finish(copies)
    big[...] = dot_nt(acts[: 2 * TOK], w1[...])
    outs = [begin(big, own, out_sems.at[0])]
    small[...] = dot_nt(acts[2 * TOK :], w1[...]).astype(BF16)
    outs.append(begin(small, far, out_sems.at[1]))
    finish(outs)


def hidden_out(meta, acts, width, ins):
    refs, bases = zip(*ins)
    hidden = acts.shape[1]
    one = (2 * TOK, width)
    return pl.pallas_call(
        partial(hidden_out_kernel, bases),
        out_shape=[shape(one, F32), shape(one, BF16)],
        in_specs=[SMEM] + [HBM] * (1 + len(refs)),
        out_specs=[HBM] * 2,
        scratch_shapes=[
            pltpu.VMEM((width, hidden), BF16),
            pltpu.VMEM(acts.shape, BF16),
            pltpu.VMEM(one, F32),
            pltpu.VMEM(one, BF16),
            pltpu.SemaphoreType.DMA((PIECES + 1,)),
            pltpu.SemaphoreType.DMA((2,)),
        ],
        compiler_params=params(),
        cost_estimate=COST,
        name="hidden_out",
    )(meta, acts, *refs)


def unrelative(grads):
    out = []
    for row in range(WIN):
        slab = grads[row * SIDE : (row + 1) * SIDE]
        down = pltpu.roll(slab, row, 1) if row else slab
        across = pltpu.roll(slab, 0, 1, stride=1, stride_axis=0)
        out.append(jnp.where(lanes(SIDE) < 32, down, across))
    return jnp.concatenate(out, axis=0)


def attend_back_kernel(before, count, meta, vecs, gather, table, q, k, v, p, weights, att, n1, *refs):
    start, parts = sum(before), len(before)
    first, last = start == 0, start + count == PAIRS
    if first:
        back_own, back_far, x1, dm = refs[:4]
        norm_sums, bias_sums, table_grad, mine, theirs, dqkv_out, dx1, da = refs[4:12]
        refs = refs[12:]
        owns, fars, x1s, dms, dx1s = refs[-5:]
        refs = refs[:-5]
    else:
        da, refs = refs[0], refs[1:]
        if last:
            earlier, tok, dx1, *changes = refs[:4], *refs[4 : 6 + parts]
            flat, mine, theirs, result = refs[6 + parts : 10 + parts]
            refs = refs[10 + parts :]
            bias_sums, wqkv, toks, dx1s, results, *changed = refs[-5 - parts :]
            refs = refs[: -5 - parts]
        else:
            bias_sums, table_grad, mine, theirs, dqkv_out = refs[:5]
            refs = refs[5:]
    das, wproj, atts, n1s, qs, ks, vs, ps, dat, dqkv, grads, sems, out_sems = refs
    core = meta[64]
    width, cols_here = das.shape[-1], qs.shape[-1]
    rows = width // PIECES
    columns = pl.ds(start * LANES, cols_here)
    tokens = (2 * TOK, width)
    early = []
    if first:
        early = [(back_own, owns), (back_far, fars), (x1, x1s), (dm, dms)]
    else:
        early = [(da, das)]
    early = [begin(ref, dest, sems.at[at]) for at, (ref, dest) in enumerate(early)]
    half, here = columns_of(3, width)
    wait_proj = begin(weights.at[half, columns, here], wproj, sems.at[4])
    wait_att = begin(att, atts, sems.at[5])
    wait_v = begin(v.at[:, :, columns], vs, sems.at[6])
    wait_p = []
    for window in range(2):
        for pair in range(count):
            heads = pl.ds(2 * (start + pair), 2)
            wait_p.append(
                begin(p.at[window, heads], ps.at[window, pl.ds(2 * pair, 2)], sems.at[10 + len(wait_p)])
            )
        if window == 0:
            wait_qk = [
                begin(ref.at[:, :, columns], dest, sems.at[7 + at])
                for at, (ref, dest) in enumerate(((q, qs), (k, ks)))
            ]
    wait_n1 = begin(n1, n1s, sems.at[9])
    if last:
        at = 10 + 2 * count
        ends = [begin(tok, toks, sems.at[at]), begin(dx1, dx1s, sems.at[at + 1])]
        for mat in range(3):
            half, here = columns_of(mat, width)
            ends.append(begin(weights.at[half, :, here], wqkv.at[mat], sems.at[at + 2 + mat]))
        for part in range(parts):
            ends.append(begin(changes[part], changed[part], sems.at[at + 5 + part]))
    outs = []
    finish(early)
    if first:
        total = [jnp.zeros((1, width), F32) for _ in range(4)]
        for window in range(2):
            here = pl.ds(window * TOK, TOK)
            grad = owns[here] + fars[here].astype(F32)
            xhat, inverse = moments(x1s[window])
            out_grad = dms[window].astype(F32)
            dresid = out_grad + norm_back(grad, xhat, inverse, vecs[5:6])
            dx1s[window] = dresid
            rounded = dresid.astype(BF16)
            das[window] = rounded
            for slot, value in enumerate((rounded.astype(F32), grad * xhat, grad, out_grad)):
                total[slot] = total[slot] + jnp.sum(value, axis=0, keepdims=True)
        norm_sums[...] = jnp.concatenate(total, axis=0)
        outs.append(begin(dx1s, dx1, out_sems.at[2 * PIECES]))
        outs.append(begin(das, da, out_sems.at[2 * PIECES + 1]))
    wait_proj.wait()
    dat[...] = dot_nt(das[...].reshape(tokens), wproj[...]).astype(BF16).reshape(2, TOK, cols_here)

    def send(half):
        is_own = core == half
        at = jnp.where(is_own, 32, 48) if last else jnp.where(is_own, 80, 96)
        for piece in range(PIECES):
            place = pl.multiple_of(meta[at + piece] * rows, rows)
            source, to = grads.at[half, pl.ds(place, rows), :], pl.ds(piece * rows, rows)
            sem = out_sems.at[half * PIECES + piece]
            copies = [pltpu.make_async_copy(source, ref.at[to, :], sem) for ref in (mine, theirs)]
            pl.when(is_own)(copies[0].start)
            pl.when(~is_own)(copies[1].start)
            outs.append(copies[0])

    wait_att.wait()
    made = dot_tn(atts[...].reshape(tokens), das[:, :, columns].reshape(2 * TOK, cols_here))
    grads[1, :, cols_here:] = made.astype(BF16)
    finish(wait_qk + [wait_v] + wait_p)
    place = lanes(TOK)
    table_sum = jnp.zeros((LANES, LANES), F32)
    for step in range(2 * count):
        window, pair = step // count, step % count
        cols = pl.ds(pair * LANES, LANES)
        q2, k2, v2, dat2 = (ref[window, :, cols] for ref in (qs, ks, vs, dat))
        q8 = (q2.astype(F32) * HDIM**-0.5).astype(BF16)
        k8 = (k2.astype(F32) * HDIM**-0.5).astype(BF16)
        dqs, dks, dvs, dts = [], [], [], []
        for half in range(2):
            soft32 = ps[window, 2 * pair + half]
            soft = soft32.astype(BF16)
            own_lanes = jnp.where(place // 64 == half, dat2.astype(F32), 0.0).astype(BF16)
            weighted = soft32 * dot_nt(own_lanes, v2)
            ds = (weighted - soft32 * jnp.sum(weighted, axis=-1, keepdims=True)).astype(BF16)
            turned = dot(ds, gather[...]).astype(BF16).astype(F32)
            turned = unrelative(turned).astype(BF16)
            dqs.append(dot(ds, k8) + dot(turned, table[half]))
            dks.append(dot_tn(ds, q8))
            dvs.append(dot_tn(soft, dat2))
            dts.append(dot_tn(turned, q2))
        dqkv[0, window, :, cols] = jnp.where(place < 64, dqs[0], dqs[1]).astype(BF16)
        dqkv[1, window, :, cols] = jnp.where(place < 64, dks[0][:TOK], dks[1][:TOK]).astype(BF16)
        dqkv[2, window, :, cols] = jnp.where(place < 64, dvs[0][:TOK], dvs[1][:TOK]).astype(BF16)
        table_sum = table_sum + jnp.where(lanes(LANES) < 64, dts[0], dts[1])
    if not last:
        table_grad[...] = table_sum
    if not last:
        outs.append(begin(dqkv, dqkv_out, out_sems.at[2 * PIECES + 2]))
    wait_n1.wait()
    for mat in (2, 0, 1):
        change = dqkv[mat].reshape(2 * TOK, cols_here)
        made = dot_tn(n1s[...].reshape(tokens), change)
        grads[mat // 2, :, pl.ds(mat % 2 * cols_here, cols_here)] = made.astype(BF16)
        if mat != 0:
            send(mat // 2)
        if mat != 1:
            bias_sums[mat // 2 : mat // 2 + 1] = jnp.sum(change.astype(F32), axis=0, keepdims=True)
    if last:
        finish(ends)
        total = [jnp.zeros((1, width), F32) for _ in range(2)]
        for window in range(2):
            grad = jnp.zeros((TOK, width), F32)
            at = 0
            for change in (*changed, dqkv):
                here = pl.ds(at, change.shape[-1])
                for mat in range(3):
                    grad = grad + dot_nt(change[mat, window], wqkv[mat, :, here])
                at += change.shape[-1]
            xhat, inverse = moments(toks[window].astype(F32))
            results[window] = dx1s[window] + norm_back(grad, xhat, inverse, vecs[0:1])
            outs.append(begin(results.at[window], result.at[window], out_sems.at[2 * PIECES + window]))
            for slot, value in enumerate((grad * xhat, grad)):
                total[slot] = total[slot] + jnp.sum(value, axis=0, keepdims=True)
        norm2_sums, bias0, table0, hidden_sums = earlier
        pack(meta, total, (bias0, bias_sums), norm2_sums, table0[...] + table_sum, hidden_sums, flat)
    finish(outs)


def pack(meta, norm1, biases, norm2, table, hidden, flat):
    flat[...] = jnp.zeros_like(flat)
    parts = biases[0].shape[1] // LANES
    for row in range(8):
        for at in range(6):
            cols = pl.ds(at * LANES, LANES)
            if row < 2:
                value = norm1[row][:, at * LANES : (at + 1) * LANES]
            elif row < 4:
                ref, place = (biases[0], at) if at < parts else (biases[1], at - parts)
                value = ref[row - 2 : row - 1, pl.ds(place * LANES, LANES)]
            else:
                value = norm2[row - 4 : row - 3, cols]
            block = 6 * row + at
            flat[block // 4 : block // 4 + 1, pl.ds(block % 4 * LANES, LANES)] = value
    for block in range(hidden.shape[1] // LANES):
        value = hidden[:, pl.ds(block * LANES, LANES)]
        for core in range(2):
            at = 12 + 3 * core + block // 4
            flat[at : at + 1, pl.ds(block % 4 * LANES, LANES)] = jnp.where(meta[64] == core, value, 0.0)
    both = table[:64] + pltpu.roll(table[:64], HDIM, 1)
    for group in range(4):
        flat[24:40, pl.ds(group * LANES, LANES)] = both[16 * group : 16 * group + 16]


def unpacked(flat, core):
    vectors = flat[:12].reshape(8, -1)
    hidden = lax.dynamic_slice_in_dim(flat, 12 + 3 * core, 3).reshape(-1)
    table = flat[24:40].reshape(16, 4, LANES).transpose(1, 0, 2).reshape(64, LANES)[:, :HDIM]
    return vectors, hidden, table


def attend_back(before, count, meta, vecs, gather, table, q, k, v, p, weights, att, n1, ins):
    width, cols_here = q.shape[-1], count * LANES
    start, parts = sum(before), len(before)
    first, last = start == 0, start + count == PAIRS
    rows, keys = (2, TOK, width), (2, KEYS, cols_here)
    part, flat = (2, TOK, cols_here), (2 * TOK, width)
    heads = (2, 2 * count, TOK, KEYS)
    small = [shape((2, cols_here), F32), shape((LANES, LANES), F32)]
    large = [shape((width, 2 * cols_here), BF16)] * 2
    large.append(shape(rows, F32) if last else shape((3,) + part, BF16))
    if last:
        small = [shape((SMALL, 2 * cols_here), F32)]
    if first:
        small = [shape((4, width), F32)] + small
        large += [shape(rows, F32), shape(rows, BF16)]
    scratch = [rows, (cols_here, width), rows, rows, part, keys, keys, heads, part, (3,) + part]
    scratch.append((2, width, 2 * cols_here))
    scratch = [pltpu.VMEM(dims, F32 if dims == heads else BF16) for dims in scratch]
    scratch += [pltpu.SemaphoreType.DMA((15 + 2 * count + parts,)), pltpu.SemaphoreType.DMA((2 * PIECES + 3,))]
    if first:
        scratch += [
            pltpu.VMEM(flat, F32),
            pltpu.VMEM(flat, BF16),
            pltpu.VMEM(rows, F32),
            pltpu.VMEM(rows, BF16),
            pltpu.VMEM(rows, F32),
        ]
    if last:
        scratch += [
            pltpu.VMEM((2, cols_here), F32),
            pltpu.VMEM((3, width, width), BF16),
            pltpu.VMEM(rows, BF16),
            pltpu.VMEM(rows, F32),
            pltpu.VMEM(rows, F32),
        ] + [pltpu.VMEM((3, 2, TOK, size * LANES), BF16) for size in before]
    return pl.pallas_call(
        partial(attend_back_kernel, before, count),
        out_shape=small + large,
        in_specs=[SMEM] + [WHOLE] * 3 + [HBM] * 8 + [WHOLE if last and at < 4 else HBM for at in range(len(ins) - 1)],
        out_specs=[WHOLE] * len(small) + [HBM] * len(large),
        scratch_shapes=scratch,
        compiler_params=params(),
        cost_estimate=COST,
        name="attend_back",
    )(meta, vecs, gather, table, q, k, v, p, weights, att, n1, *ins)


def grid_of(count):
    return (4, 2, 2) if count == 16 else None


def turn(values, dims, moves):
    pairs = []
    for chip in range(dims[0] * dims[1] * dims[2]):
        for core, (axis, by) in enumerate(moves):
            place = list(np.unravel_index(chip, dims))
            place[axis] = (place[axis] + by) % dims[axis]
            pairs.append((2 * chip + core, 2 * int(np.ravel_multi_index(place, dims)) + core))
    return lax.ppermute(values, ("dp", "mp"), pairs)


ALONG_X, ALONG_Y = ((2, 1),) * 2, ((1, 1),) * 2
FIRST, SECOND = ((2, 1), (1, 1)), ((1, 1), (2, 1))


def along_z(values, dims):
    return [turn(values, dims, ((0, step),) * 2) for step in range(1, dims[0])]


def swap_z(values, dims, by):
    chips = dims[1] * dims[2]
    pairs = [(chip, (chip // chips ^ by) * chips + chip % chips) for chip in range(dims[0] * chips)]
    return lax.ppermute(values, "dp", pairs)


def other_core(values):
    return lax.ppermute(values, "mp", [(0, 1), (1, 0)])


def after(values, *others):
    return lax.optimization_barrier((values, *others))[0]


def stack_kernel(count, *refs):
    ins, out, sems = refs[:count], refs[count], refs[count + 1]
    copies, at = [], 0
    for ref in ins:
        rows = ref.shape[0]
        copies.append(begin(ref, out.at[pl.ds(at, rows)], sems.at[len(copies)]))
        at += rows
    finish(copies)


def stack(*parts):
    rows = sum(part.shape[0] for part in parts)
    return pl.pallas_call(
        partial(stack_kernel, len(parts)),
        out_shape=shape((rows, parts[0].shape[1]), BF16),
        in_specs=[HBM] * len(parts),
        out_specs=HBM,
        scratch_shapes=[pltpu.SemaphoreType.DMA((len(parts),))],
        compiler_params=params(),
        cost_estimate=COST,
        name="stack",
    )(*parts)


class Flow:
    def __init__(self, *came):
        self.came = list(came)


def meet(flows, *values):
    sizes = [len(flow.came) for flow in flows]
    found = list(lax.optimization_barrier((*(part for flow in flows for part in flow.came), *values)))
    for flow, size in zip(flows, sizes):
        flow.came, found = found[:size], found[size:]
    return found


def place_orders(dims, core):
    here = lax.axis_index("dp")
    z, y, x = here // (dims[1] * dims[2]), here // dims[2] % dims[1], here % dims[2]

    def chip(at_z, inner, outer):
        by_x = jnp.where(core == 0, inner, outer)
        by_y = jnp.where(core == 0, outer, inner)
        return (at_z * dims[1] + (y + by_y) % 2) * dims[2] + (x + by_x) % 2

    back = [(z - step) % dims[0] for step in range(dims[0])]
    pairs = [z ^ step for step in range(dims[0])]

    square = [(inner, outer) for outer in range(2) for inner in range(2)]
    gather = [chip(z, *at) for at in square]
    gather += [chip(place, *at) for at in square for place in back[1:]]
    scatter = [chip(place, *at) for at in square for place in back]
    halving = [chip(place, *at) for at in square for place in pairs]
    return [jnp.stack(found).astype(jnp.int32) for found in (gather, scatter, halving)]


def add(a, b):
    return a.astype(F32) + b.astype(F32)


def staged_kernel(kernel, starts, scalars, *refs):
    count = len(starts)
    meta, refs = refs[:scalars], refs[scalars:]
    total = len(refs) // 2
    held, sems = refs[total : 2 * total], refs[2 * total]
    copies = []
    for ref, start, dest in zip(refs, starts, held):
        if start is not None:
            ref = ref.at[pl.ds(start, dest.shape[0])]
        copies.append(begin(ref, dest, sems.at[len(copies)]))
    finish(copies)
    kernel(*meta, *held)
    finish([begin(held[at], refs[at], sems.at[at]) for at in range(count, total)])


def staged(kernel, outs, *ins, meta=None):
    ins = [part if isinstance(part, tuple) else (part, None, part.shape[0]) for part in ins]
    arrays, starts, rows = zip(*ins)
    scalars = () if meta is None else (meta,)
    held = [pltpu.VMEM((count, *array.shape[1:]), array.dtype) for array, count in zip(arrays, rows)]
    held += [pltpu.VMEM(out.shape, out.dtype) for out in outs]
    return pl.pallas_call(
        partial(staged_kernel, kernel, starts, len(scalars)),
        out_shape=outs,
        in_specs=[SMEM] * len(scalars) + [HBM] * len(arrays),
        out_specs=[HBM] * len(outs),
        scratch_shapes=held + [pltpu.SemaphoreType.DMA((len(held),))],
        compiler_params=params(),
        cost_estimate=COST,
        name="staged",
    )(*scalars, *arrays)


def core_rows_kernel(count, meta, *refs):
    *terms, own, far = refs
    half, width = own.shape[1:]
    one, two = (sum(ref[...].astype(F32) for ref in part) for part in (terms[:count], terms[count:]))
    cut, last = one.shape[1] // 2, two.shape[1] // 2
    for core in range(2):

        def put(ref, at=slice(core * half, (core + 1) * half)):
            for mat in range(2):
                ref[mat, :, :cut] = one[at, mat * cut : (mat + 1) * cut]
                ref[mat, :, cut:] = two[at, mat * last : (mat + 1) * last]

        pl.when(meta[64] == core)(partial(put, own))
        pl.when(meta[64] != core)(partial(put, far))


def last_rows_kernel(meta, near, came, qkv, proj):
    width = proj.shape[1]

    def put(qk, vp):
        qkv[:, :width] = qk[0]
        qkv[:, width : 2 * width] = qk[1]
        qkv[:, 2 * width :] = vp[0]
        proj[...] = vp[1]

    pl.when(meta[64] == 0)(partial(put, near, came))
    pl.when(meta[64] != 0)(partial(put, came, near))


class Scatter(Flow):
    def __init__(self, keep, far, dims):
        super().__init__(turn(far, dims, SECOND))
        self.keep, self.dims, self.sent = keep, dims, far

    def second(self):
        half = self.keep.shape[0] // 2
        send = add(self.keep[half:], self.came[0][half:]).astype(BF16)
        self.near = add(self.keep[:half], self.came[0][:half])
        self.sent = send
        self.came = [turn(send, self.dims, FIRST)]

    def third(self):
        near = self.near + self.came[0].astype(F32)
        rows = near.shape[0] // self.dims[0]
        self.near = near[:rows]
        sends = [near[step * rows : (step + 1) * rows].astype(BF16) for step in range(1, self.dims[0])]
        self.sent = sends[0]
        self.came = [
            turn(send, self.dims, ((0, self.dims[0] - step),) * 2) for step, send in enumerate(sends, 1)
        ]

    def halve(self):
        near = self.near + self.came[0].astype(F32)
        rows = near.shape[0] // self.dims[0]
        self.near, self.beside = near[:rows], near[rows : 2 * rows]
        self.sent = near[2 * rows :].astype(BF16)
        self.came = [swap_z(self.sent, self.dims, 2)]

    def quarter(self):
        rows = self.near.shape[0]
        came = self.came[0]
        self.near = self.near + came[:rows].astype(F32)
        self.sent = (self.beside + came[rows:].astype(F32)).astype(BF16)
        self.came = [swap_z(self.sent, self.dims, 1)]

    def last(self):
        return sum((part.astype(F32) for part in self.came), self.near)


def constants():
    key = np.arange(KEYS)
    row, col = key // SIDE, key % SIDE
    inside = (row < WIN) & (col < WIN)
    spread = np.zeros((KEYS, LANES), np.float32)
    gather = np.zeros((KEYS, LANES), np.float32)
    for place in key[inside]:
        for base in (0, 64):
            spread[place, base + WIN - 1 + row[place]] = 1.0
            spread[place, base + 32 + WIN - 1 + col[place]] = 1.0
        gather[place, WIN - 1 - row[place]] = 1.0
        gather[place, 32 + WIN - 1 - col[place]] = 1.0
    return spread, gather


def tables(rel_pos_h, rel_pos_w):
    count = rel_pos_h.shape[0]
    gap = jnp.zeros((32 - count, HDIM), BF16)
    turned = jnp.concatenate([rel_pos_h[::-1], gap, rel_pos_w[::-1], gap], axis=0)
    turned = jnp.concatenate([turned, turned], axis=0).T
    none = jnp.zeros_like(turned)
    forward = jnp.concatenate(
        [jnp.concatenate([turned, none], axis=0), jnp.concatenate([none, turned], axis=0)], axis=1
    )
    straight = jnp.concatenate([rel_pos_h, gap, rel_pos_w, gap], axis=0)
    straight = jnp.concatenate([straight, jnp.zeros_like(straight)], axis=0)
    none = jnp.zeros_like(straight)
    backward = jnp.stack(
        [
            jnp.concatenate([straight, none], axis=1),
            jnp.concatenate([none, straight], axis=1),
        ]
    )
    return forward, backward


def padded(values):
    images, rows, _, width = values.shape
    values = jnp.pad(values, ((0, 0), (0, 0), (0, SIDE - WIN), (0, 0)))
    return values.reshape(images, rows * SIDE, width)


def unpadded(values):
    images, _, width = values.shape
    return values.reshape(images, WIN, SIDE, width)[:, :, :WIN]


def local(
    patches,
    norm1_gain,
    norm1_bias,
    qkv_weight,
    qv_bias,
    rel_pos_h,
    rel_pos_w,
    proj_weight,
    proj_bias,
    norm2_gain,
    norm2_bias,
    fc1_weight,
    fc1_bias,
    fc2_weight,
    fc2_bias,
    heights,
    widths,
    out_grad,
):
    width = patches.shape[-1]
    dims = grid_of(lax.axis_size("dp"))
    core = lax.axis_index("mp")
    is_first = core == 0
    spread, gather = constants()

    def prepare(patches, out_grad, heights, rel_pos_h, rel_pos_w):
        if dims is None:
            orders = [jnp.tile(jnp.arange(PIECES, dtype=jnp.int32), 4)]
            halving = [orders[0][: 2 * PIECES]]
        else:
            own, far = place_orders(dims, core), place_orders(dims, 1 - core)
            orders = [own[0], far[0], own[1], far[1]]
            halving = [own[2], far[2]]
        meta = jnp.concatenate(
            orders + [core.astype(jnp.int32)[None], heights, widths, jnp.zeros((11,), jnp.int32)] + halving
        )
        row_index = core * WIN + jnp.arange(WIN)
        valid = (row_index[None, :, None] < heights[:, None, None]) & (
            jnp.arange(WIN)[None, None, :] < widths[:, None, None]
        )
        dm = padded(jnp.where(valid[..., None], out_grad, jnp.zeros_like(out_grad)))
        return padded(patches), dm, meta, *tables(rel_pos_h, rel_pos_w)

    wanted = (patches, out_grad, heights, rel_pos_h, rel_pos_w)
    vectors = (norm1_gain, norm1_bias, qv_bias[0], qv_bias[1], proj_bias, norm2_gain, norm2_bias, fc2_bias)
    small = jnp.pad(jnp.stack(vectors, axis=1), ((0, 0), (0, LANES - len(vectors))))
    qk = jnp.concatenate([qkv_weight[:, :width], small, qkv_weight[:, width : 2 * width]], axis=1)
    vp = jnp.concatenate([qkv_weight[:, 2 * width :], small, proj_weight], axis=1)
    if dims is None:
        qk = lax.all_gather(qk, ("dp", "mp"), axis=0, tiled=True)
        vp = lax.all_gather(vp, ("dp", "mp"), axis=0, tiled=True)
        attend_own = [jnp.where(is_first, qk, vp)]
        attend_far = [jnp.where(is_first, vp, qk)]
        tok, dm, meta, table, table_back = prepare(*wanted)
        hidden_in = tuple(
            ((lax.all_gather(part, "dp", axis=0, tiled=True), 0),) for part in (fc1_weight, fc2_weight.T)
        )
    else:
        fc1, fc2 = fc1_weight, fc2_weight.T
        came = other_core(jnp.where(is_first, vp, qk))
        near = jnp.where(is_first, qk, vp)
        block = jnp.concatenate(
            [jnp.where(is_first, near, came), jnp.where(is_first, came, near)], axis=0
        )
        attend_size, size = block.shape[1], fc1.shape[1]
        tok, dm, meta, table, table_back = prepare(*meet([], *wanted, block)[:5])
        own = jnp.concatenate([block, fc1, fc2], axis=1)
        attend_z, beside = Flow(*along_z(block, dims)), Flow(turn(own, dims, FIRST))
        fc1, fc2, tok, dm, table, table_back, meta = meet(
            [attend_z, beside], fc1, fc2, tok, dm, table, table_back, meta
        )

        attend_z = stack(*attend_z.came)
        z_beside = Flow(turn(attend_z, dims, FIRST))
        own = stack(own, *beside.came)
        over = Flow(turn(own, dims, SECOND))
        fc1_z = Flow(*along_z(after(fc1, own), dims))
        (fc2,) = meet([over, z_beside, fc1_z], fc2)

        over = over.came[0]
        attend_z = stack(attend_z, *z_beside.came)
        z_over = Flow(turn(attend_z, dims, SECOND))
        fc1_z = stack(after(fc1_z.came[0], attend_z), *fc1_z.came[1:])
        fc1_beside = Flow(turn(fc1_z, dims, FIRST))
        fc2_z = Flow(*along_z(after(fc2, fc1_z), dims))
        own_attend = jnp.concatenate([own[:, :attend_size], over[:, :attend_size]], axis=0)
        own_attend, attend_z = meet([z_over, fc1_beside, fc2_z], own_attend, attend_z)

        z_over = z_over.came[0]
        far = Flow(*(other_core(part) for part in (own_attend, attend_z, z_over)))
        fc1_z = stack(fc1_z, *fc1_beside.came)
        fc1_over = Flow(turn(fc1_z, dims, SECOND))
        fc2_z = stack(*fc2_z.came)
        fc2_beside = Flow(turn(fc2_z, dims, FIRST))
        tok, fc1_z, fc2_z, dm = meet([far], tok, fc1_z, fc2_z, dm)
        dm_far = Flow(other_core(dm))
        attend_own, attend_far = [own, over, attend_z, z_over], far.came

    vecs, n1, q, k, v, p, att, weights, x1, n2 = attend(
        meta, tok, table, jnp.asarray(spread, BF16), attend_own, attend_far
    )
    n2_far = other_core(n2).reshape(-1, width)
    if dims is None:
        dm_far = other_core(dm)
    else:
        (n2,) = meet([fc1_over, fc2_beside, dm_far], n2)
        (dm_far,) = dm_far.came
        fc2_z = stack(fc2_z, *fc2_beside.came)
        fc2_over = turn(fc2_z, dims, SECOND)
    dm_flat, dm_far = dm.reshape(-1, width), dm_far.reshape(-1, width)
    n2 = n2.reshape(-1, width)
    bias = fc1_bias[None].astype(F32)
    if dims is not None:
        n2 = after(n2, fc2_z)
        hidden_in = [
            ((own, attend_size), (over, attend_size), (fc1_z, 0), (*fc1_over.came, 0)),
            ((own, attend_size + size), (over, attend_size + size), (fc2_z, 0), (fc2_over, 0)),
        ]
    fc2_part = hidden_fwd(meta, n2, n2_far, dm_flat, dm_far, bias, hidden_in[0])
    if dims is not None:
        fc2_part = meet([], *fc2_part, fc2_over)[:2]
        fc2_sum = Scatter(*fc2_part, dims)
    fc1_bias_part, *fc1_part, back_own, back_far, acts = hidden_back(
        meta, n2, n2_far, dm_flat, dm_far, bias, *hidden_in
    )
    back_far = other_core(back_far)
    if dims is not None:
        fc1_part = meet([fc2_sum], *fc1_part)
        fc2_sum.second()
        fc1_sum = Scatter(*fc1_part, dims)
        back_own = after(back_own, fc2_sum.sent)

    shared = (meta, vecs, jnp.asarray(gather, BF16), table_back, q, k, v, p, weights, att, n1)
    half = width // 2
    def block_of(out_own, out_far):
        branch = add(out_own, out_far).reshape(x1.shape) + vecs[7]
        row_index = core * WIN + jnp.arange(WIN)
        valid = (row_index[None, :, None] < heights[:, None, None]) & (
            jnp.arange(WIN)[None, None, :] < widths[:, None, None]
        )
        return jnp.where(valid[..., None], unpadded(x1 + branch), 0.0).astype(BF16)

    def core_rows(wholes):
        whole = jnp.stack(
            [
                jnp.concatenate([part.reshape(part.shape[0], 2, -1)[:, at] for part in wholes], axis=1)
                for at in range(2)
            ]
        )
        rows = whole.shape[1] // 2
        cuts = whole[:, :rows], whole[:, rows:]
        return jnp.where(is_first, *cuts), jnp.where(is_first, *cuts[::-1])

    count0, count1 = BACK_PARTS
    sums2, bias0, table0, mine0, theirs0, change, dx1, da = attend_back(
        (), count0, *shared, (back_own, back_far, x1, dm)
    )
    if dims is not None:
        da, mine0, theirs0 = meet([fc2_sum], da, mine0, theirs0)
        came0 = other_core(theirs0)
        da, mine0 = meet([fc1_sum, fc2_sum], da, mine0)
        fc2_sum.halve()
        fc1_sum.second()
        both = add(mine0, came0).astype(BF16)
        first = Scatter(both[:half], both[half:], dims)
        da = after(da, both)
    flat, mine, theirs, result = attend_back(
        (count0,), count1, *shared, (da, sums2, bias0, table0, fc1_bias_part, tok, dx1, change)
    )
    if dims is None:
        out_own, out_far = hidden_out(meta, acts, width, hidden_in[1])
        result, block_out = unpadded(result), block_of(out_own, other_core(out_far))
        fc1_sum, fc2_sum = (
            lax.psum_scatter(
                jnp.concatenate(parts, axis=0).astype(F32), "dp", scatter_dimension=0, tiled=True
            )
            for parts in (fc1_part, fc2_part)
        )
        wholes = [
            lax.psum_scatter(add(own, other_core(far)), "dp", scatter_dimension=0, tiled=True)
            for own, far in ((mine0, theirs0), (mine, theirs))
        ]
        near, far = core_rows(wholes)
        came = other_core(far)
        flat = lax.psum(flat, ("dp", "mp"))
    else:
        came, flat_came = Flow(other_core(theirs)), Flow(other_core(flat))
        mine, flat, acts, result = meet([fc2_sum, fc1_sum, first], mine, flat, acts, result)
        first.second()
        fc1_sum.halve()
        mine, flat, acts = meet([came, flat_came, first], mine, flat, acts)
        both = add(mine, came.came[0]).astype(BF16)
        second = Scatter(both[:half], both[half:], dims)
        flat = flat + flat_came.came[0]
        flat_came = Flow(turn(flat, dims, SECOND))
        first.halve()
        fc2_sum.came[0] = after(fc2_sum.came[0], first.sent)
        fc2_sum.quarter()
        acts = after(acts, first.sent, second.sent, fc2_sum.sent)
        out_own, out_far = hidden_out(meta, acts, width, hidden_in[1])
        flat, result, out_far = meet([flat_came, second, fc1_sum, fc2_sum], flat, result, out_far)
        late = Flow(other_core(out_far))
        flat = flat + flat_came.came[0]
        flat_came = Flow(turn(flat, dims, FIRST))
        second.second()
        fc1_sum.came[0] = after(fc1_sum.came[0], second.sent)
        fc1_sum.quarter()
        fc2_sum = fc2_sum.last()
        result = unpadded(result)
        flat, fc2_sum, result = meet([flat_came, first, second, fc1_sum, late], flat, fc2_sum, result)
        flat = flat + flat_came.came[0]
        flat_came = Flow(swap_z(flat, dims, 2))
        second.third()
        first.came[0] = after(first.came[0], second.sent, flat)
        first.quarter()
        fc1_sum.near, late.came[0] = meet([], fc1_sum.near, late.came[0], second.sent, first.sent)[:2]
        fc1_sum = fc1_sum.last()
        block_out = block_of(out_own, late.came[0])
        flat, fc1_sum, block_out = meet([flat_came, second, first], flat, fc1_sum, block_out)

        share = shape((2, width // len(FIRST) // dims[0] // dims[1] // dims[2], width), F32)
        near, far = staged(
            partial(core_rows_kernel, 2), [share, share], first.near, *first.came, second.near, *second.came, meta=meta
        )
        came = other_core(far)
        flat = flat + flat_came.came[0]
        flat_came = swap_z(flat, dims, 1)
        flat = flat + after(flat_came, far)
    rows = near.shape[1]
    outs = [shape((rows, 3 * width), F32), shape((rows, width), F32)]
    qkv_grad, proj_grad = staged(last_rows_kernel, outs, near, came, meta=meta)
    vec_sums, fc1_bias_grad, rel = unpacked(flat, core)
    share = norm1_gain.shape[0]
    device = lax.axis_index("dp") * 2 + core
    mine = lax.dynamic_slice_in_dim(vec_sums, device * share, share, axis=1)
    rels = rel_pos_h.shape[0]
    return (
        block_out,
        result,
        mine[0],
        mine[1],
        qkv_grad,
        mine[2:4],
        rel[:rels],
        rel[32 : 32 + rels],
        proj_grad,
        mine[4],
        mine[5],
        mine[6],
        fc1_sum,
        fc1_bias_grad,
        fc2_sum.T,
        mine[7],
    )


def solution(mesh):
    return jax.shard_map(
        local,
        mesh=mesh,
        in_specs=(
            P("dp", "mp", None, None),
            P(("dp", "mp")),
            P(("dp", "mp")),
            P(("dp", "mp"), None),
            P(None, ("dp", "mp")),
            P(),
            P(),
            P(("dp", "mp"), None),
            P(("dp", "mp")),
            P(("dp", "mp")),
            P(("dp", "mp")),
            P("dp", "mp"),
            P("mp"),
            P("mp", "dp"),
            P(("dp", "mp")),
            P("dp"),
            P("dp"),
            P("dp", "mp", None, None),
        ),
        out_specs=(
            P("dp", "mp", None, None),
            P("dp", "mp", None, None),
            P(("dp", "mp")),
            P(("dp", "mp")),
            P(("dp", "mp"), None),
            P(None, ("dp", "mp")),
            P(),
            P(),
            P(("dp", "mp"), None),
            P(("dp", "mp")),
            P(("dp", "mp")),
            P(("dp", "mp")),
            P("dp", "mp"),
            P("mp"),
            P("mp", "dp"),
            P(("dp", "mp")),
        ),
        check_vma=False,
    )
```

```python
from functools import partial

import jax
import jax.numpy as jnp
import numpy as np
from jax import lax
from jax.experimental import pallas as pl
from jax.experimental.pallas import tpu as pltpu
from jax.sharding import PartitionSpec as P

HEADS = 12
HDIM = 64
LANES = 128
PAIRS = HEADS // 2
WIN = 14
SIDE = 16
TOK = WIN * SIDE
KEYS = 256
PIECES = 16
EPSILON = 1e-06
MASKED_SCORE = -1e30
MASK_LANE = 60
SMALL = 48
CHUNK = 512
BACK_PARTS = (4, 2)
F32 = jnp.float32
BF16 = jnp.bfloat16
SMEM = pl.BlockSpec(memory_space=pltpu.SMEM)
HBM = pl.BlockSpec(memory_space=pl.ANY)
WHOLE = pl.BlockSpec(memory_space=pltpu.VMEM)
VMEM_BYTES = 52 * 2**20
COST = pl.CostEstimate(flops=1000, bytes_accessed=1000, transcendentals=0)


def params():
    return pltpu.CompilerParams(vmem_limit_bytes=VMEM_BYTES)


def shape(dims, dtype):
    return jax.ShapeDtypeStruct(dims, dtype)


def dot(a, b):
    return jnp.dot(a, b, preferred_element_type=F32)


def dot_nt(a, b):
    return lax.dot_general(a, b, (((1,), (1,)), ((), ())), preferred_element_type=F32)


def dot_tn(a, b):
    return lax.dot_general(a, b, (((0,), (0,)), ((), ())), preferred_element_type=F32)


def lanes(rows):
    return lax.broadcasted_iota(jnp.int32, (rows, LANES), 1)


def moments(values):
    centered = values - jnp.mean(values, axis=-1, keepdims=True)
    inverse = lax.rsqrt(jnp.mean(centered * centered, axis=-1, keepdims=True) + EPSILON)
    return centered * inverse, inverse


def norm_back(grad, xhat, inverse, gain):
    scaled = grad * gain
    first = jnp.mean(scaled, axis=-1, keepdims=True)
    second = jnp.mean(scaled * xhat, axis=-1, keepdims=True)
    return inverse * (scaled - first - xhat * second)


def begin(source, dest, sem):
    copy = pltpu.make_async_copy(source, dest, sem)
    copy.start()
    return copy


def finish(copies):
    for copy in copies:
        copy.wait()


def pieces_in(meta, at, ins, start, dest, sems, first):
    rows, cols = dest.shape[0] // PIECES, dest.shape[1]
    copies = []
    for ref, base in ins:
        for part in range(ref.shape[0] // rows):
            place = pl.multiple_of(meta[at + len(copies)] * rows, rows)
            source = ref.at[pl.ds(part * rows, rows), pl.ds(base + start, cols)]
            copies.append(begin(source, dest.at[pl.ds(place, rows), :], sems.at[first + len(copies)]))
    return copies


def row_valid(meta, core, window, rows, width):
    place = lax.broadcasted_iota(jnp.int32, (rows, width), 0)
    row, col = place // SIDE, place % SIDE
    inside = (row < WIN) & (col < WIN)
    return inside & (core * WIN + row < meta[65 + window]) & (col < meta[67 + window])


def relative(turned):
    out = []
    for row in range(WIN):
        slab = turned[row * SIDE : (row + 1) * SIDE]
        down = pltpu.roll(slab, row, 1) if row else slab
        across = pltpu.roll(slab, 0, 1, stride=1, stride_axis=0)
        out.append(jnp.where(lanes(SIDE) % 64 < 32, down, across))
    return jnp.concatenate(out, axis=0)


def columns_of(mat, width, start=0, size=None):
    return mat // 2, pl.ds(mat % 2 * (width + LANES) + start, width if size is None else size)


def attend_kernel(count, total, meta, tok, table, spread, *refs):
    own, other = refs[:count], refs[count:total]
    vecs, n1, q, k, v, p, att, w_out, x1, n2 = refs[total : total + 10]
    toks, weights, aug, n1s, qs, ks, vs, ps, atts, x1s, n2s, sems, out_sems = refs[total + 10 :]
    width = toks.shape[-1]
    core = meta[64]
    copies = [begin(tok, toks, sems.at[2 * PIECES])]
    for found, at, half in ((own, 0, core), (other, 16, 1 - core)):
        found = [(ref, 0) for ref in found]
        copies += pieces_in(meta, at, found, 0, weights.at[half], sems, at)
    for window in range(2):
        valid = row_valid(meta, core, window, KEYS, LANES)
        aug[window] = jnp.where(
            (lanes(KEYS) == MASK_LANE) & ~valid, MASKED_SCORE, spread[...].astype(F32)
        ).astype(BF16)
        ks[window, TOK:] = jnp.zeros((KEYS - TOK, width), BF16)
        vs[window, TOK:] = jnp.zeros((KEYS - TOK, width), BF16)
    copies[0].wait()
    tokens = toks[...].reshape(2 * TOK, width).astype(F32)
    xhat, _ = moments(tokens)
    finish(copies[1:])
    outs = [begin(weights, w_out, out_sems.at[0])]
    vecs[...] = weights[0, :, width : width + LANES].astype(F32).T[:8]
    normed = (xhat * vecs[0:1] + vecs[1:2]).astype(BF16)
    n1s[...] = normed.reshape(2, TOK, width)
    outs.append(begin(n1s, n1, out_sems.at[1]))
    for mat, (made_in, dest) in enumerate(((qs, q), (ks, k), (vs, v))):
        for start in range(0, width, 256):
            cols = pl.ds(start, 256)
            half, here = columns_of(mat, width, start, 256)
            made = dot(normed, weights[half, :, here])
            if mat != 1:
                made = made + vecs[2 + mat // 2 : 3 + mat // 2, cols]
            made = made.astype(BF16)
            made_in[0, :TOK, cols] = made[:TOK]
            made_in[1, :TOK, cols] = made[TOK:]
        outs.append(begin(made_in, dest, out_sems.at[2 + mat]))

    place = lanes(TOK)
    for step in range(2 * PAIRS):
        window, pair = step // PAIRS, step % PAIRS
        cols = pl.ds(pair * LANES, LANES)
        q2, k2, v2 = qs[window, :, cols], ks[window, :, cols], vs[window, :, cols]
        turned = dot(q2, table[...])
        keys_aug = jnp.concatenate([k2, aug[window]], axis=1)
        parts = []
        for half in range(2):
            rel = relative(turned[:, half * LANES : (half + 1) * LANES])
            high = rel.astype(BF16).astype(F32)
            rel = jnp.where(place < 64, high, rel - high)
            rel = jnp.where(place == MASK_LANE, 1.0, rel).astype(BF16)
            mine = jnp.where(place // 64 == half, q2.astype(F32) * HDIM**-0.5, 0.0).astype(BF16)
            scores = dot_nt(jnp.concatenate([mine, rel], axis=1), keys_aug)
            terms = jnp.exp(scores - jnp.max(scores, axis=-1, keepdims=True))
            soft = terms * (1.0 / jnp.sum(terms, axis=-1, keepdims=True))
            ps[window, 2 * pair + half] = soft
            parts.append(dot(soft.astype(BF16), v2))
        atts[window, :, cols] = jnp.where(place < 64, parts[0], parts[1]).astype(BF16)
        heads = pl.ds(2 * pair, 2)
        outs.append(begin(ps.at[window, heads], p.at[window, heads], out_sems.at[len(outs)]))
    outs.append(begin(atts, att, out_sems.at[len(outs)]))
    half, here = columns_of(3, width)
    for window in range(2):
        resid = toks[window].astype(F32) + (dot(atts[window], weights[half, :, here]) + vecs[4:5])
        x1s[window] = resid
        xhat, _ = moments(resid)
        n2s[window] = (xhat * vecs[5:6] + vecs[6:7]).astype(BF16)
        outs.append(begin(x1s.at[window], x1.at[window], out_sems.at[len(outs)]))
        outs.append(begin(n2s.at[window], n2.at[window], out_sems.at[len(outs)]))
    finish(outs)


def attend(meta, tok, table, spread, own, other):
    count, total, width = len(own), len(own) + len(other), tok.shape[-1]
    rows, keys, heads = (2, TOK, width), (2, KEYS, width), (2, HEADS, TOK, KEYS)
    halves = (2, width, 2 * width + LANES)
    outs = [shape(dims, F32 if dims == heads else BF16) for dims in (rows, rows, keys, keys, heads, rows, halves)]
    outs += [shape(rows, F32), shape(rows, BF16)]
    scratch = (rows, halves, (2, KEYS, LANES), rows, rows, keys, keys, heads, rows)
    return pl.pallas_call(
        partial(attend_kernel, count, total),
        out_shape=[shape((8, width), F32)] + outs,
        in_specs=[SMEM, HBM, WHOLE, WHOLE] + [HBM] * total,
        out_specs=[WHOLE] + [HBM] * len(outs),
        scratch_shapes=[pltpu.VMEM(dims, F32 if dims == heads else BF16) for dims in scratch]
        + [
            pltpu.VMEM(rows, F32),
            pltpu.VMEM(rows, BF16),
            pltpu.SemaphoreType.DMA((2 * PIECES + 1,)),
            pltpu.SemaphoreType.DMA((10 + 2 * PAIRS,)),
        ],
        compiler_params=params(),
        cost_estimate=COST,
        name="attend",
    )(meta, tok, table, spread, *own, *other)


def pieces_out(meta, made, cols, keep, send, sems, first):
    rows = made.shape[0] // PIECES
    copies = []
    for piece in range(PIECES):
        dest = keep if piece < PIECES // 2 else send
        place = pl.multiple_of(meta[80 + piece] * rows, rows)
        at = pl.ds(piece % (PIECES // 2) * rows, rows)
        source = made.at[pl.ds(place, rows), cols]
        copies.append(begin(source, dest.at[at, cols], sems.at[first + len(copies)]))
    return copies


def hidden_fwd_kernel(bases, meta, n2a, n2b, dma, dmb, bias, *refs):
    count = len(bases)
    ins, (keep, send) = list(zip(refs[:count], bases)), refs[count : count + 2]
    w0, n2s, dms, grad, sems, out_sems = refs[count + 2 :]
    width, hidden = w0.shape
    at = PIECES
    copies = [begin(n2a, n2s.at[: 2 * TOK], sems.at[at]), begin(n2b, n2s.at[2 * TOK :], sems.at[at + 1])]
    copies += pieces_in(meta, 0, ins, 0, w0, sems, 0)
    dm_copies = [
        begin(dma, dms.at[: 2 * TOK], sems.at[at + 2]),
        begin(dmb, dms.at[2 * TOK :], sems.at[at + 3]),
    ]
    finish(copies)
    outs = []
    for start in range(0, hidden, CHUNK):
        cols = pl.ds(start, CHUNK)
        inner = dot(n2s[...], w0[:, cols]) + bias[:, cols]
        act = (inner * (0.5 + 0.5 * lax.erf(inner * 0.7071067811865476))).astype(BF16)
        if start == 0:
            finish(dm_copies)
        grad[:, cols] = dot_tn(dms[...], act).astype(BF16)
        if start + CHUNK == hidden - CHUNK:
            outs += pieces_out(meta, grad, pl.ds(0, hidden - CHUNK), keep, send, out_sems, 0)
    outs += pieces_out(meta, grad, pl.ds(hidden - CHUNK, CHUNK), keep, send, out_sems, PIECES)
    finish(outs)


def hidden_fwd(meta, n2a, n2b, dma, dmb, bias, ins):
    refs, bases = zip(*ins)
    width, hidden = n2a.shape[-1], bias.shape[-1]
    return pl.pallas_call(
        partial(hidden_fwd_kernel, bases),
        out_shape=[shape((width // 2, hidden), BF16)] * 2,
        in_specs=[SMEM] + [HBM] * 4 + [WHOLE] + [HBM] * len(refs),
        out_specs=[HBM] * 2,
        scratch_shapes=[
            pltpu.VMEM((width, hidden), BF16),
            pltpu.VMEM((4 * TOK, width), BF16),
            pltpu.VMEM((4 * TOK, width), BF16),
            pltpu.VMEM((width, hidden), BF16),
            pltpu.SemaphoreType.DMA((PIECES + 4,)),
            pltpu.SemaphoreType.DMA((2 * PIECES,)),
        ],
        compiler_params=params(),
        cost_estimate=COST,
        name="hidden_fwd",
    )(meta, n2a, n2b, dma, dmb, bias, *refs)


def hidden_back_kernel(bases0, bases1, meta, n2a, n2b, dma, dmb, bias, *refs):
    count = len(bases0)
    ins0, ins1 = list(zip(refs[:count], bases0)), list(zip(refs[count : 2 * count], bases1))
    refs = refs[2 * count :]
    bias_grad, keep, send, back_own, back_far, acts_out = refs[:6]
    w0, w1, n2s, dms, acts, backs, grad, big, small, sems, out_sems = refs[6:]
    width, hidden = w0.shape
    halves = (pl.ds(0, 2 * TOK), pl.ds(2 * TOK, 2 * TOK))
    at = 2 * PIECES
    copies = [begin(ref, n2s.at[half], sems.at[at + i]) for i, (ref, half) in enumerate(zip((n2a, n2b), halves))]
    copies += pieces_in(meta, 0, ins0, 0, w0, sems, 0)
    at += 2
    later = [begin(ref, dms.at[half], sems.at[at + i]) for i, (ref, half) in enumerate(zip((dma, dmb), halves))]
    later += pieces_in(meta, 0, ins1, 0, w1, sems, PIECES)
    finish(copies)
    outs = []
    for start in range(0, hidden, CHUNK):
        cols = pl.ds(start, CHUNK)
        inner = dot(n2s[...], w0[:, cols]) + bias[:, cols]
        if start == 0:
            finish(later)
        back = dot(dms[...], w1[:, cols])
        cdf = 0.5 + 0.5 * lax.erf(inner * 0.7071067811865476)
        density = jnp.exp(inner * inner * -0.5) * 0.3989422804014327
        acts[:, cols] = (inner * cdf).astype(BF16)
        back_pre = (back * (cdf + inner * density)).astype(BF16)
        backs[:, cols] = back_pre
        bias_grad[:, cols] = jnp.sum(back_pre.astype(F32), axis=0, keepdims=True)
        grad[:, cols] = dot_tn(n2s[...], back_pre).astype(BF16)
    outs = pieces_out(meta, grad, pl.ds(0, hidden), keep, send, out_sems, 0)
    outs.append(begin(acts, acts_out, out_sems.at[len(outs)]))
    small[...] = dot_nt(backs[halves[1]], w0[...]).astype(BF16)
    outs.append(begin(small, back_far, out_sems.at[len(outs)]))
    big[...] = dot_nt(backs[halves[0]], w0[...])
    outs.append(begin(big, back_own, out_sems.at[len(outs)]))
    finish(outs)


def hidden_back(meta, n2a, n2b, dma, dmb, bias, ins0, ins1):
    (refs0, bases0), (refs1, bases1) = zip(*ins0), zip(*ins1)
    width, hidden = n2a.shape[-1], bias.shape[-1]
    one = (2 * TOK, width)
    tall = pltpu.VMEM((4 * TOK, width), BF16)
    wide = pltpu.VMEM((width, hidden), BF16)
    return pl.pallas_call(
        partial(hidden_back_kernel, bases0, bases1),
        out_shape=[shape((1, hidden), F32)]
        + [shape((width // 2, hidden), BF16)] * 2
        + [shape(one, F32), shape(one, BF16), shape((4 * TOK, hidden), BF16)],
        in_specs=[SMEM] + [HBM] * 4 + [WHOLE] + [HBM] * (2 * len(refs0)),
        out_specs=[WHOLE] + [HBM] * 5,
        scratch_shapes=[
            wide,
            wide,
            tall,
            tall,
            pltpu.VMEM((4 * TOK, hidden), BF16),
            pltpu.VMEM((4 * TOK, hidden), BF16),
            wide,
            pltpu.VMEM(one, F32),
            pltpu.VMEM(one, BF16),
            pltpu.SemaphoreType.DMA((2 * PIECES + 4,)),
            pltpu.SemaphoreType.DMA((PIECES + 3,)),
        ],
        compiler_params=params(),
        cost_estimate=COST,
        name="hidden_back",
    )(meta, n2a, n2b, dma, dmb, bias, *refs0, *refs1)


def hidden_out_kernel(bases, meta, acts_in, *refs):
    count = len(bases)
    ins, (own, far) = list(zip(refs[:count], bases)), refs[count : count + 2]
    w1, acts, big, small, sems, out_sems = refs[count + 2 :]
    copies = [begin(acts_in, acts, sems.at[PIECES])]
    copies += pieces_in(meta, 0, ins, 0, w1, sems, 0)
    finish(copies)
    big[...] = dot_nt(acts[: 2 * TOK], w1[...])
    outs = [begin(big, own, out_sems.at[0])]
    small[...] = dot_nt(acts[2 * TOK :], w1[...]).astype(BF16)
    outs.append(begin(small, far, out_sems.at[1]))
    finish(outs)


def hidden_out(meta, acts, width, ins):
    refs, bases = zip(*ins)
    hidden = acts.shape[1]
    one = (2 * TOK, width)
    return pl.pallas_call(
        partial(hidden_out_kernel, bases),
        out_shape=[shape(one, F32), shape(one, BF16)],
        in_specs=[SMEM] + [HBM] * (1 + len(refs)),
        out_specs=[HBM] * 2,
        scratch_shapes=[
            pltpu.VMEM((width, hidden), BF16),
            pltpu.VMEM(acts.shape, BF16),
            pltpu.VMEM(one, F32),
            pltpu.VMEM(one, BF16),
            pltpu.SemaphoreType.DMA((PIECES + 1,)),
            pltpu.SemaphoreType.DMA((2,)),
        ],
        compiler_params=params(),
        cost_estimate=COST,
        name="hidden_out",
    )(meta, acts, *refs)


def unrelative(grads):
    out = []
    for row in range(WIN):
        slab = grads[row * SIDE : (row + 1) * SIDE]
        down = pltpu.roll(slab, row, 1) if row else slab
        across = pltpu.roll(slab, 0, 1, stride=1, stride_axis=0)
        out.append(jnp.where(lanes(SIDE) < 32, down, across))
    return jnp.concatenate(out, axis=0)


def attend_back_kernel(before, count, meta, vecs, gather, table, q, k, v, p, weights, att, n1, *refs):
    start, parts = sum(before), len(before)
    first, last = start == 0, start + count == PAIRS
    if first:
        back_own, back_far, x1, dm = refs[:4]
        norm_sums, bias_sums, table_grad, mine, theirs, dqkv_out, dx1, da = refs[4:12]
        refs = refs[12:]
        owns, fars, x1s, dms, dx1s = refs[-5:]
        refs = refs[:-5]
    else:
        da, refs = refs[0], refs[1:]
        if last:
            earlier, tok, dx1, *changes = refs[:4], *refs[4 : 6 + parts]
            flat, mine, theirs, result = refs[6 + parts : 10 + parts]
            refs = refs[10 + parts :]
            bias_sums, wqkv, toks, dx1s, results, *changed = refs[-5 - parts :]
            refs = refs[: -5 - parts]
        else:
            bias_sums, table_grad, mine, theirs, dqkv_out = refs[:5]
            refs = refs[5:]
    das, wproj, atts, n1s, qs, ks, vs, ps, dat, dqkv, grads, sems, out_sems = refs
    core = meta[64]
    width, cols_here = das.shape[-1], qs.shape[-1]
    rows = width // PIECES
    columns = pl.ds(start * LANES, cols_here)
    tokens = (2 * TOK, width)
    early = []
    if first:
        early = [(back_own, owns), (back_far, fars), (x1, x1s), (dm, dms)]
    else:
        early = [(da, das)]
    early = [begin(ref, dest, sems.at[at]) for at, (ref, dest) in enumerate(early)]
    half, here = columns_of(3, width)
    wait_proj = begin(weights.at[half, columns, here], wproj, sems.at[4])
    wait_att = begin(att, atts, sems.at[5])
    wait_v = begin(v.at[:, :, columns], vs, sems.at[6])
    wait_p = []
    for window in range(2):
        for pair in range(count):
            heads = pl.ds(2 * (start + pair), 2)
            wait_p.append(
                begin(p.at[window, heads], ps.at[window, pl.ds(2 * pair, 2)], sems.at[10 + len(wait_p)])
            )
        if window == 0:
            wait_qk = [
                begin(ref.at[:, :, columns], dest, sems.at[7 + at])
                for at, (ref, dest) in enumerate(((q, qs), (k, ks)))
            ]
    wait_n1 = begin(n1, n1s, sems.at[9])
    if last:
        at = 10 + 2 * count
        ends = [begin(tok, toks, sems.at[at]), begin(dx1, dx1s, sems.at[at + 1])]
        for mat in range(3):
            half, here = columns_of(mat, width)
            ends.append(begin(weights.at[half, :, here], wqkv.at[mat], sems.at[at + 2 + mat]))
        for part in range(parts):
            ends.append(begin(changes[part], changed[part], sems.at[at + 5 + part]))
    outs = []
    finish(early)
    if first:
        total = [jnp.zeros((1, width), F32) for _ in range(4)]
        for window in range(2):
            here = pl.ds(window * TOK, TOK)
            grad = owns[here] + fars[here].astype(F32)
            xhat, inverse = moments(x1s[window])
            out_grad = dms[window].astype(F32)
            dresid = out_grad + norm_back(grad, xhat, inverse, vecs[5:6])
            dx1s[window] = dresid
            rounded = dresid.astype(BF16)
            das[window] = rounded
            for slot, value in enumerate((rounded.astype(F32), grad * xhat, grad, out_grad)):
                total[slot] = total[slot] + jnp.sum(value, axis=0, keepdims=True)
        norm_sums[...] = jnp.concatenate(total, axis=0)
        outs.append(begin(dx1s, dx1, out_sems.at[2 * PIECES]))
        outs.append(begin(das, da, out_sems.at[2 * PIECES + 1]))
    wait_proj.wait()
    dat[...] = dot_nt(das[...].reshape(tokens), wproj[...]).astype(BF16).reshape(2, TOK, cols_here)

    def send(half):
        is_own = core == half
        at = jnp.where(is_own, 32, 48) if last else jnp.where(is_own, 80, 96)
        for piece in range(PIECES):
            place = pl.multiple_of(meta[at + piece] * rows, rows)
            source, to = grads.at[half, pl.ds(place, rows), :], pl.ds(piece * rows, rows)
            sem = out_sems.at[half * PIECES + piece]
            copies = [pltpu.make_async_copy(source, ref.at[to, :], sem) for ref in (mine, theirs)]
            pl.when(is_own)(copies[0].start)
            pl.when(~is_own)(copies[1].start)
            outs.append(copies[0])

    wait_att.wait()
    made = dot_tn(atts[...].reshape(tokens), das[:, :, columns].reshape(2 * TOK, cols_here))
    grads[1, :, cols_here:] = made.astype(BF16)
    finish(wait_qk + [wait_v] + wait_p)
    place = lanes(TOK)
    table_sum = jnp.zeros((LANES, LANES), F32)
    for step in range(2 * count):
        window, pair = step // count, step % count
        cols = pl.ds(pair * LANES, LANES)
        q2, k2, v2, dat2 = (ref[window, :, cols] for ref in (qs, ks, vs, dat))
        q8 = (q2.astype(F32) * HDIM**-0.5).astype(BF16)
        k8 = (k2.astype(F32) * HDIM**-0.5).astype(BF16)
        dqs, dks, dvs, dts = [], [], [], []
        for half in range(2):
            soft32 = ps[window, 2 * pair + half]
            soft = soft32.astype(BF16)
            own_lanes = jnp.where(place // 64 == half, dat2.astype(F32), 0.0).astype(BF16)
            weighted = soft32 * dot_nt(own_lanes, v2)
            ds = (weighted - soft32 * jnp.sum(weighted, axis=-1, keepdims=True)).astype(BF16)
            turned = dot(ds, gather[...]).astype(BF16).astype(F32)
            turned = unrelative(turned).astype(BF16)
            dqs.append(dot(ds, k8) + dot(turned, table[half]))
            dks.append(dot_tn(ds, q8))
            dvs.append(dot_tn(soft, dat2))
            dts.append(dot_tn(turned, q2))
        dqkv[0, window, :, cols] = jnp.where(place < 64, dqs[0], dqs[1]).astype(BF16)
        dqkv[1, window, :, cols] = jnp.where(place < 64, dks[0][:TOK], dks[1][:TOK]).astype(BF16)
        dqkv[2, window, :, cols] = jnp.where(place < 64, dvs[0][:TOK], dvs[1][:TOK]).astype(BF16)
        table_sum = table_sum + jnp.where(lanes(LANES) < 64, dts[0], dts[1])
    if not last:
        table_grad[...] = table_sum
    if not last:
        outs.append(begin(dqkv, dqkv_out, out_sems.at[2 * PIECES + 2]))
    wait_n1.wait()
    for mat in (2, 0, 1):
        change = dqkv[mat].reshape(2 * TOK, cols_here)
        made = dot_tn(n1s[...].reshape(tokens), change)
        grads[mat // 2, :, pl.ds(mat % 2 * cols_here, cols_here)] = made.astype(BF16)
        if mat != 0:
            send(mat // 2)
        if mat != 1:
            bias_sums[mat // 2 : mat // 2 + 1] = jnp.sum(change.astype(F32), axis=0, keepdims=True)
    if last:
        finish(ends)
        total = [jnp.zeros((1, width), F32) for _ in range(2)]
        for window in range(2):
            grad = jnp.zeros((TOK, width), F32)
            at = 0
            for change in (*changed, dqkv):
                here = pl.ds(at, change.shape[-1])
                for mat in range(3):
                    grad = grad + dot_nt(change[mat, window], wqkv[mat, :, here])
                at += change.shape[-1]
            xhat, inverse = moments(toks[window].astype(F32))
            results[window] = dx1s[window] + norm_back(grad, xhat, inverse, vecs[0:1])
            outs.append(begin(results.at[window], result.at[window], out_sems.at[2 * PIECES + window]))
            for slot, value in enumerate((grad * xhat, grad)):
                total[slot] = total[slot] + jnp.sum(value, axis=0, keepdims=True)
        norm2_sums, bias0, table0, hidden_sums = earlier
        pack(meta, total, (bias0, bias_sums), norm2_sums, table0[...] + table_sum, hidden_sums, flat)
    finish(outs)


def pack(meta, norm1, biases, norm2, table, hidden, flat):
    flat[...] = jnp.zeros_like(flat)
    parts = biases[0].shape[1] // LANES
    for row in range(8):
        for at in range(6):
            cols = pl.ds(at * LANES, LANES)
            if row < 2:
                value = norm1[row][:, at * LANES : (at + 1) * LANES]
            elif row < 4:
                ref, place = (biases[0], at) if at < parts else (biases[1], at - parts)
                value = ref[row - 2 : row - 1, pl.ds(place * LANES, LANES)]
            else:
                value = norm2[row - 4 : row - 3, cols]
            block = 6 * row + at
            flat[block // 4 : block // 4 + 1, pl.ds(block % 4 * LANES, LANES)] = value
    for block in range(hidden.shape[1] // LANES):
        value = hidden[:, pl.ds(block * LANES, LANES)]
        for core in range(2):
            at = 12 + 3 * core + block // 4
            flat[at : at + 1, pl.ds(block % 4 * LANES, LANES)] = jnp.where(meta[64] == core, value, 0.0)
    both = table[:64] + pltpu.roll(table[:64], HDIM, 1)
    for group in range(4):
        flat[24:40, pl.ds(group * LANES, LANES)] = both[16 * group : 16 * group + 16]


def unpacked(flat, core):
    vectors = flat[:12].reshape(8, -1)
    hidden = lax.dynamic_slice_in_dim(flat, 12 + 3 * core, 3).reshape(-1)
    table = flat[24:40].reshape(16, 4, LANES).transpose(1, 0, 2).reshape(64, LANES)[:, :HDIM]
    return vectors, hidden, table


def attend_back(before, count, meta, vecs, gather, table, q, k, v, p, weights, att, n1, ins):
    width, cols_here = q.shape[-1], count * LANES
    start, parts = sum(before), len(before)
    first, last = start == 0, start + count == PAIRS
    rows, keys = (2, TOK, width), (2, KEYS, cols_here)
    part, flat = (2, TOK, cols_here), (2 * TOK, width)
    heads = (2, 2 * count, TOK, KEYS)
    small = [shape((2, cols_here), F32), shape((LANES, LANES), F32)]
    large = [shape((width, 2 * cols_here), BF16)] * 2
    large.append(shape(rows, F32) if last else shape((3,) + part, BF16))
    if last:
        small = [shape((SMALL, 2 * cols_here), F32)]
    if first:
        small = [shape((4, width), F32)] + small
        large += [shape(rows, F32), shape(rows, BF16)]
    scratch = [rows, (cols_here, width), rows, rows, part, keys, keys, heads, part, (3,) + part]
    scratch.append((2, width, 2 * cols_here))
    scratch = [pltpu.VMEM(dims, F32 if dims == heads else BF16) for dims in scratch]
    scratch += [pltpu.SemaphoreType.DMA((15 + 2 * count + parts,)), pltpu.SemaphoreType.DMA((2 * PIECES + 3,))]
    if first:
        scratch += [
            pltpu.VMEM(flat, F32),
            pltpu.VMEM(flat, BF16),
            pltpu.VMEM(rows, F32),
            pltpu.VMEM(rows, BF16),
            pltpu.VMEM(rows, F32),
        ]
    if last:
        scratch += [
            pltpu.VMEM((2, cols_here), F32),
            pltpu.VMEM((3, width, width), BF16),
            pltpu.VMEM(rows, BF16),
            pltpu.VMEM(rows, F32),
            pltpu.VMEM(rows, F32),
        ] + [pltpu.VMEM((3, 2, TOK, size * LANES), BF16) for size in before]
    return pl.pallas_call(
        partial(attend_back_kernel, before, count),
        out_shape=small + large,
        in_specs=[SMEM] + [WHOLE] * 3 + [HBM] * 8 + [WHOLE if last and at < 4 else HBM for at in range(len(ins) - 1)],
        out_specs=[WHOLE] * len(small) + [HBM] * len(large),
        scratch_shapes=scratch,
        compiler_params=params(),
        cost_estimate=COST,
        name="attend_back",
    )(meta, vecs, gather, table, q, k, v, p, weights, att, n1, *ins)


def grid_of(count):
    return (4, 2, 2) if count == 16 else None


def turn(values, dims, moves):
    pairs = []
    for chip in range(dims[0] * dims[1] * dims[2]):
        for core, (axis, by) in enumerate(moves):
            place = list(np.unravel_index(chip, dims))
            place[axis] = (place[axis] + by) % dims[axis]
            pairs.append((2 * chip + core, 2 * int(np.ravel_multi_index(place, dims)) + core))
    return lax.ppermute(values, ("dp", "mp"), pairs)


ALONG_X, ALONG_Y = ((2, 1),) * 2, ((1, 1),) * 2
FIRST, SECOND = ((2, 1), (1, 1)), ((1, 1), (2, 1))


def along_z(values, dims):
    return [turn(values, dims, ((0, step),) * 2) for step in range(1, dims[0])]


def swap_z(values, dims, by):
    chips = dims[1] * dims[2]
    pairs = [(chip, (chip // chips ^ by) * chips + chip % chips) for chip in range(dims[0] * chips)]
    return lax.ppermute(values, "dp", pairs)


def other_core(values):
    return lax.ppermute(values, "mp", [(0, 1), (1, 0)])


def after(values, *others):
    return lax.optimization_barrier((values, *others))[0]


def stack_kernel(count, *refs):
    ins, out, sems = refs[:count], refs[count], refs[count + 1]
    copies, at = [], 0
    for ref in ins:
        rows = ref.shape[0]
        copies.append(begin(ref, out.at[pl.ds(at, rows)], sems.at[len(copies)]))
        at += rows
    finish(copies)


def stack(*parts):
    rows = sum(part.shape[0] for part in parts)
    return pl.pallas_call(
        partial(stack_kernel, len(parts)),
        out_shape=shape((rows, parts[0].shape[1]), BF16),
        in_specs=[HBM] * len(parts),
        out_specs=HBM,
        scratch_shapes=[pltpu.SemaphoreType.DMA((len(parts),))],
        compiler_params=params(),
        cost_estimate=COST,
        name="stack",
    )(*parts)


class Flow:
    def __init__(self, *came):
        self.came = list(came)


def meet(flows, *values):
    sizes = [len(flow.came) for flow in flows]
    found = list(lax.optimization_barrier((*(part for flow in flows for part in flow.came), *values)))
    for flow, size in zip(flows, sizes):
        flow.came, found = found[:size], found[size:]
    return found


def place_orders(dims, core):
    here = lax.axis_index("dp")
    z, y, x = here // (dims[1] * dims[2]), here // dims[2] % dims[1], here % dims[2]

    def chip(at_z, inner, outer):
        by_x = jnp.where(core == 0, inner, outer)
        by_y = jnp.where(core == 0, outer, inner)
        return (at_z * dims[1] + (y + by_y) % 2) * dims[2] + (x + by_x) % 2

    back = [(z - step) % dims[0] for step in range(dims[0])]
    pairs = [z ^ step for step in range(dims[0])]

    square = [(inner, outer) for outer in range(2) for inner in range(2)]
    gather = [chip(z, *at) for at in square]
    gather += [chip(place, *at) for at in square for place in back[1:]]
    scatter = [chip(place, *at) for at in square for place in back]
    halving = [chip(place, *at) for at in square for place in pairs]
    return [jnp.stack(found).astype(jnp.int32) for found in (gather, scatter, halving)]


def add(a, b):
    return a.astype(F32) + b.astype(F32)


def staged_kernel(kernel, starts, scalars, *refs):
    count = len(starts)
    meta, refs = refs[:scalars], refs[scalars:]
    total = len(refs) // 2
    held, sems = refs[total : 2 * total], refs[2 * total]
    copies = []
    for ref, start, dest in zip(refs, starts, held):
        if start is not None:
            ref = ref.at[pl.ds(start, dest.shape[0])]
        copies.append(begin(ref, dest, sems.at[len(copies)]))
    finish(copies)
    kernel(*meta, *held)
    finish([begin(held[at], refs[at], sems.at[at]) for at in range(count, total)])


def staged(kernel, outs, *ins, meta=None):
    ins = [part if isinstance(part, tuple) else (part, None, part.shape[0]) for part in ins]
    arrays, starts, rows = zip(*ins)
    scalars = () if meta is None else (meta,)
    held = [pltpu.VMEM((count, *array.shape[1:]), array.dtype) for array, count in zip(arrays, rows)]
    held += [pltpu.VMEM(out.shape, out.dtype) for out in outs]
    return pl.pallas_call(
        partial(staged_kernel, kernel, starts, len(scalars)),
        out_shape=outs,
        in_specs=[SMEM] * len(scalars) + [HBM] * len(arrays),
        out_specs=[HBM] * len(outs),
        scratch_shapes=held + [pltpu.SemaphoreType.DMA((len(held),))],
        compiler_params=params(),
        cost_estimate=COST,
        name="staged",
    )(*scalars, *arrays)


def core_rows_kernel(count, meta, *refs):
    *terms, own, far = refs
    half, width = own.shape[1:]
    one, two = (sum(ref[...].astype(F32) for ref in part) for part in (terms[:count], terms[count:]))
    cut, last = one.shape[1] // 2, two.shape[1] // 2
    for core in range(2):

        def put(ref, at=slice(core * half, (core + 1) * half)):
            for mat in range(2):
                ref[mat, :, :cut] = one[at, mat * cut : (mat + 1) * cut]
                ref[mat, :, cut:] = two[at, mat * last : (mat + 1) * last]

        pl.when(meta[64] == core)(partial(put, own))
        pl.when(meta[64] != core)(partial(put, far))


def last_rows_kernel(meta, near, came, qkv, proj):
    width = proj.shape[1]

    def put(qk, vp):
        qkv[:, :width] = qk[0]
        qkv[:, width : 2 * width] = qk[1]
        qkv[:, 2 * width :] = vp[0]
        proj[...] = vp[1]

    pl.when(meta[64] == 0)(partial(put, near, came))
    pl.when(meta[64] != 0)(partial(put, came, near))


class Scatter(Flow):
    def __init__(self, keep, far, dims):
        super().__init__(turn(far, dims, SECOND))
        self.keep, self.dims, self.sent = keep, dims, far

    def second(self):
        half = self.keep.shape[0] // 2
        send = add(self.keep[half:], self.came[0][half:]).astype(BF16)
        self.near = add(self.keep[:half], self.came[0][:half])
        self.sent = send
        self.came = [turn(send, self.dims, FIRST)]

    def third(self):
        near = self.near + self.came[0].astype(F32)
        rows = near.shape[0] // self.dims[0]
        self.near = near[:rows]
        sends = [near[step * rows : (step + 1) * rows].astype(BF16) for step in range(1, self.dims[0])]
        self.sent = sends[0]
        self.came = [
            turn(send, self.dims, ((0, self.dims[0] - step),) * 2) for step, send in enumerate(sends, 1)
        ]

    def halve(self):
        near = self.near + self.came[0].astype(F32)
        rows = near.shape[0] // self.dims[0]
        self.near, self.beside = near[:rows], near[rows : 2 * rows]
        self.sent = near[2 * rows :].astype(BF16)
        self.came = [swap_z(self.sent, self.dims, 2)]

    def quarter(self):
        rows = self.near.shape[0]
        came = self.came[0]
        self.near = self.near + came[:rows].astype(F32)
        self.sent = (self.beside + came[rows:].astype(F32)).astype(BF16)
        self.came = [swap_z(self.sent, self.dims, 1)]

    def last(self):
        return sum((part.astype(F32) for part in self.came), self.near)


def constants():
    key = np.arange(KEYS)
    row, col = key // SIDE, key % SIDE
    inside = (row < WIN) & (col < WIN)
    spread = np.zeros((KEYS, LANES), np.float32)
    gather = np.zeros((KEYS, LANES), np.float32)
    for place in key[inside]:
        for base in (0, 64):
            spread[place, base + WIN - 1 + row[place]] = 1.0
            spread[place, base + 32 + WIN - 1 + col[place]] = 1.0
        gather[place, WIN - 1 - row[place]] = 1.0
        gather[place, 32 + WIN - 1 - col[place]] = 1.0
    return spread, gather


def tables(rel_pos_h, rel_pos_w):
    count = rel_pos_h.shape[0]
    gap = jnp.zeros((32 - count, HDIM), BF16)
    turned = jnp.concatenate([rel_pos_h[::-1], gap, rel_pos_w[::-1], gap], axis=0)
    turned = jnp.concatenate([turned, turned], axis=0).T
    none = jnp.zeros_like(turned)
    forward = jnp.concatenate(
        [jnp.concatenate([turned, none], axis=0), jnp.concatenate([none, turned], axis=0)], axis=1
    )
    straight = jnp.concatenate([rel_pos_h, gap, rel_pos_w, gap], axis=0)
    straight = jnp.concatenate([straight, jnp.zeros_like(straight)], axis=0)
    none = jnp.zeros_like(straight)
    backward = jnp.stack(
        [
            jnp.concatenate([straight, none], axis=1),
            jnp.concatenate([none, straight], axis=1),
        ]
    )
    return forward, backward


def padded(values):
    images, rows, _, width = values.shape
    values = jnp.pad(values, ((0, 0), (0, 0), (0, SIDE - WIN), (0, 0)))
    return values.reshape(images, rows * SIDE, width)


def unpadded(values):
    images, _, width = values.shape
    return values.reshape(images, WIN, SIDE, width)[:, :, :WIN]


def local(
    patches,
    norm1_gain,
    norm1_bias,
    qkv_weight,
    qv_bias,
    rel_pos_h,
    rel_pos_w,
    proj_weight,
    proj_bias,
    norm2_gain,
    norm2_bias,
    fc1_weight,
    fc1_bias,
    fc2_weight,
    fc2_bias,
    heights,
    widths,
    out_grad,
):
    width = patches.shape[-1]
    dims = grid_of(lax.axis_size("dp"))
    core = lax.axis_index("mp")
    is_first = core == 0
    spread, gather = constants()

    def prepare(patches, out_grad, heights, rel_pos_h, rel_pos_w):
        if dims is None:
            orders = [jnp.tile(jnp.arange(PIECES, dtype=jnp.int32), 4)]
            halving = [orders[0][: 2 * PIECES]]
        else:
            own, far = place_orders(dims, core), place_orders(dims, 1 - core)
            orders = [own[0], far[0], own[1], far[1]]
            halving = [own[2], far[2]]
        meta = jnp.concatenate(
            orders + [core.astype(jnp.int32)[None], heights, widths, jnp.zeros((11,), jnp.int32)] + halving
        )
        row_index = core * WIN + jnp.arange(WIN)
        valid = (row_index[None, :, None] < heights[:, None, None]) & (
            jnp.arange(WIN)[None, None, :] < widths[:, None, None]
        )
        dm = padded(jnp.where(valid[..., None], out_grad, jnp.zeros_like(out_grad)))
        return padded(patches), dm, meta, *tables(rel_pos_h, rel_pos_w)

    wanted = (patches, out_grad, heights, rel_pos_h, rel_pos_w)
    vectors = (norm1_gain, norm1_bias, qv_bias[0], qv_bias[1], proj_bias, norm2_gain, norm2_bias, fc2_bias)
    small = jnp.pad(jnp.stack(vectors, axis=1), ((0, 0), (0, LANES - len(vectors))))
    qk = jnp.concatenate([qkv_weight[:, :width], small, qkv_weight[:, width : 2 * width]], axis=1)
    vp = jnp.concatenate([qkv_weight[:, 2 * width :], small, proj_weight], axis=1)
    if dims is None:
        qk = lax.all_gather(qk, ("dp", "mp"), axis=0, tiled=True)
        vp = lax.all_gather(vp, ("dp", "mp"), axis=0, tiled=True)
        attend_own = [jnp.where(is_first, qk, vp)]
        attend_far = [jnp.where(is_first, vp, qk)]
        tok, dm, meta, table, table_back = prepare(*wanted)
        hidden_in = tuple(
            ((lax.all_gather(part, "dp", axis=0, tiled=True), 0),) for part in (fc1_weight, fc2_weight.T)
        )
    else:
        fc1, fc2 = fc1_weight, fc2_weight.T
        came = other_core(jnp.where(is_first, vp, qk))
        near = jnp.where(is_first, qk, vp)
        block = jnp.concatenate(
            [jnp.where(is_first, near, came), jnp.where(is_first, came, near)], axis=0
        )
        attend_size, size = block.shape[1], fc1.shape[1]
        tok, dm, meta, table, table_back = prepare(*meet([], *wanted, block)[:5])
        own = jnp.concatenate([block, fc1, fc2], axis=1)
        attend_z, beside = Flow(*along_z(block, dims)), Flow(turn(own, dims, FIRST))
        fc1, fc2, tok, dm, table, table_back, meta = meet(
            [attend_z, beside], fc1, fc2, tok, dm, table, table_back, meta
        )

        attend_z = stack(*attend_z.came)
        z_beside = Flow(turn(attend_z, dims, FIRST))
        own = stack(own, *beside.came)
        over = Flow(turn(own, dims, SECOND))
        fc1_z = Flow(*along_z(after(fc1, own), dims))
        (fc2,) = meet([over, z_beside, fc1_z], fc2)

        over = over.came[0]
        attend_z = stack(attend_z, *z_beside.came)
        z_over = Flow(turn(attend_z, dims, SECOND))
        fc1_z = stack(after(fc1_z.came[0], attend_z), *fc1_z.came[1:])
        fc1_beside = Flow(turn(fc1_z, dims, FIRST))
        fc2_z = Flow(*along_z(after(fc2, fc1_z), dims))
        own_attend = jnp.concatenate([own[:, :attend_size], over[:, :attend_size]], axis=0)
        own_attend, attend_z = meet([z_over, fc1_beside, fc2_z], own_attend, attend_z)

        z_over = z_over.came[0]
        far = Flow(*(other_core(part) for part in (own_attend, attend_z, z_over)))
        fc1_z = stack(fc1_z, *fc1_beside.came)
        fc1_over = Flow(turn(fc1_z, dims, SECOND))
        fc2_z = stack(*fc2_z.came)
        fc2_beside = Flow(turn(fc2_z, dims, FIRST))
        tok, fc1_z, fc2_z = meet([far], tok, fc1_z, fc2_z)
        attend_own, attend_far = [own, over, attend_z, z_over], far.came

    vecs, n1, q, k, v, p, att, weights, x1, n2 = attend(
        meta, tok, table, jnp.asarray(spread, BF16), attend_own, attend_far
    )
    n2_far = other_core(n2).reshape(-1, width)
    if dims is None:
        dm_far = other_core(dm)
    else:
        n2, dm = meet([fc1_over, fc2_beside], n2, dm)
        dm_far = other_core(dm)
        fc2_z = stack(fc2_z, *fc2_beside.came)
        fc2_over = turn(fc2_z, dims, SECOND)
    dm_flat, dm_far = dm.reshape(-1, width), dm_far.reshape(-1, width)
    n2 = n2.reshape(-1, width)
    bias = fc1_bias[None].astype(F32)
    if dims is not None:
        n2 = after(n2, fc2_z)
        hidden_in = [
            ((own, attend_size), (over, attend_size), (fc1_z, 0), (*fc1_over.came, 0)),
            ((own, attend_size + size), (over, attend_size + size), (fc2_z, 0), (fc2_over, 0)),
        ]
    fc2_part = hidden_fwd(meta, n2, n2_far, dm_flat, dm_far, bias, hidden_in[0])
    if dims is not None:
        fc2_part = meet([], *fc2_part, fc2_over)[:2]
        fc2_sum = Scatter(*fc2_part, dims)
    fc1_bias_part, *fc1_part, back_own, back_far, acts = hidden_back(
        meta, n2, n2_far, dm_flat, dm_far, bias, *hidden_in
    )
    back_far = other_core(back_far)
    if dims is not None:
        fc1_part = meet([fc2_sum], *fc1_part)
        fc2_sum.second()
        fc1_sum = Scatter(*fc1_part, dims)
        back_own = after(back_own, fc2_sum.sent)

    shared = (meta, vecs, jnp.asarray(gather, BF16), table_back, q, k, v, p, weights, att, n1)
    half = width // 2
    def block_of(out_own, out_far):
        branch = add(out_own, out_far).reshape(x1.shape) + vecs[7]
        row_index = core * WIN + jnp.arange(WIN)
        valid = (row_index[None, :, None] < heights[:, None, None]) & (
            jnp.arange(WIN)[None, None, :] < widths[:, None, None]
        )
        return jnp.where(valid[..., None], unpadded(x1 + branch), 0.0).astype(BF16)

    def core_rows(wholes):
        whole = jnp.stack(
            [
                jnp.concatenate([part.reshape(part.shape[0], 2, -1)[:, at] for part in wholes], axis=1)
                for at in range(2)
            ]
        )
        rows = whole.shape[1] // 2
        cuts = whole[:, :rows], whole[:, rows:]
        return jnp.where(is_first, *cuts), jnp.where(is_first, *cuts[::-1])

    count0, count1 = BACK_PARTS
    sums2, bias0, table0, mine0, theirs0, change, dx1, da = attend_back(
        (), count0, *shared, (back_own, back_far, x1, dm)
    )
    if dims is not None:
        da, mine0, theirs0 = meet([fc2_sum], da, mine0, theirs0)
        came0 = other_core(theirs0)
        da, mine0 = meet([fc1_sum, fc2_sum], da, mine0)
        fc2_sum.halve()
        fc1_sum.second()
        both = add(mine0, came0).astype(BF16)
        first = Scatter(both[:half], both[half:], dims)
        da = after(da, both)
    flat, mine, theirs, result = attend_back(
        (count0,), count1, *shared, (da, sums2, bias0, table0, fc1_bias_part, tok, dx1, change)
    )
    if dims is None:
        out_own, out_far = hidden_out(meta, acts, width, hidden_in[1])
        result, block_out = unpadded(result), block_of(out_own, other_core(out_far))
        fc1_sum, fc2_sum = (
            lax.psum_scatter(
                jnp.concatenate(parts, axis=0).astype(F32), "dp", scatter_dimension=0, tiled=True
            )
            for parts in (fc1_part, fc2_part)
        )
        wholes = [
            lax.psum_scatter(add(own, other_core(far)), "dp", scatter_dimension=0, tiled=True)
            for own, far in ((mine0, theirs0), (mine, theirs))
        ]
        near, far = core_rows(wholes)
        came = other_core(far)
        flat = lax.psum(flat, ("dp", "mp"))
    else:
        came, flat_came = Flow(other_core(theirs)), Flow(other_core(flat))
        mine, flat, acts, result = meet([fc2_sum, fc1_sum, first], mine, flat, acts, result)
        first.second()
        fc1_sum.halve()
        mine, flat, acts = meet([came, flat_came, first], mine, flat, acts)
        both = add(mine, came.came[0]).astype(BF16)
        second = Scatter(both[:half], both[half:], dims)
        flat = flat + flat_came.came[0]
        flat_came = Flow(turn(flat, dims, SECOND))
        first.halve()
        fc2_sum.came[0] = after(fc2_sum.came[0], first.sent)
        fc2_sum.quarter()
        acts = after(acts, first.sent, second.sent, fc2_sum.sent)
        out_own, out_far = hidden_out(meta, acts, width, hidden_in[1])
        flat, result, out_far = meet([flat_came, second, fc1_sum, fc2_sum], flat, result, out_far)
        late = Flow(other_core(out_far))
        flat = flat + flat_came.came[0]
        flat_came = Flow(turn(flat, dims, FIRST))
        second.second()
        fc1_sum.came[0] = after(fc1_sum.came[0], second.sent)
        fc1_sum.quarter()
        fc2_sum = fc2_sum.last()
        result = unpadded(result)
        flat, fc2_sum, result = meet([flat_came, first, second, fc1_sum, late], flat, fc2_sum, result)
        flat = flat + flat_came.came[0]
        flat_came = Flow(swap_z(flat, dims, 2))
        second.third()
        first.came[0] = after(first.came[0], second.sent, flat)
        first.quarter()
        fc1_sum.near, late.came[0] = meet([], fc1_sum.near, late.came[0], second.sent, first.sent)[:2]
        fc1_sum = fc1_sum.last()
        block_out = block_of(out_own, late.came[0])
        flat, fc1_sum, block_out = meet([flat_came, second, first], flat, fc1_sum, block_out)

        share = shape((2, width // len(FIRST) // dims[0] // dims[1] // dims[2], width), F32)
        near, far = staged(
            partial(core_rows_kernel, 2), [share, share], first.near, *first.came, second.near, *second.came, meta=meta
        )
        came = other_core(far)
        flat = flat + flat_came.came[0]
        flat_came = swap_z(flat, dims, 1)
        flat = flat + after(flat_came, far)
    rows = near.shape[1]
    outs = [shape((rows, 3 * width), F32), shape((rows, width), F32)]
    qkv_grad, proj_grad = staged(last_rows_kernel, outs, near, came, meta=meta)
    vec_sums, fc1_bias_grad, rel = unpacked(flat, core)
    share = norm1_gain.shape[0]
    device = lax.axis_index("dp") * 2 + core
    mine = lax.dynamic_slice_in_dim(vec_sums, device * share, share, axis=1)
    rels = rel_pos_h.shape[0]
    return (
        block_out,
        result,
        mine[0],
        mine[1],
        qkv_grad,
        mine[2:4],
        rel[:rels],
        rel[32 : 32 + rels],
        proj_grad,
        mine[4],
        mine[5],
        mine[6],
        fc1_sum,
        fc1_bias_grad,
        fc2_sum.T,
        mine[7],
    )


def solution(mesh):
    return jax.shard_map(
        local,
        mesh=mesh,
        in_specs=(
            P("dp", "mp", None, None),
            P(("dp", "mp")),
            P(("dp", "mp")),
            P(("dp", "mp"), None),
            P(None, ("dp", "mp")),
            P(),
            P(),
            P(("dp", "mp"), None),
            P(("dp", "mp")),
            P(("dp", "mp")),
            P(("dp", "mp")),
            P("dp", "mp"),
            P("mp"),
            P("mp", "dp"),
            P(("dp", "mp")),
            P("dp"),
            P("dp"),
            P("dp", "mp", None, None),
        ),
        out_specs=(
            P("dp", "mp", None, None),
            P("dp", "mp", None, None),
            P(("dp", "mp")),
            P(("dp", "mp")),
            P(("dp", "mp"), None),
            P(None, ("dp", "mp")),
            P(),
            P(),
            P(("dp", "mp"), None),
            P(("dp", "mp")),
            P(("dp", "mp")),
            P(("dp", "mp")),
            P("dp", "mp"),
            P("mp"),
            P("mp", "dp"),
            P(("dp", "mp")),
        ),
        check_vma=False,
    )
```
